32 devices in a mesh: shard: 4 (over z), ctx: 2 (over x), tensor: 4 (over y, core).
Axes of the slice: x: 2, y: 2, z: 4, core: 2. Of those that a mesh axis runs over, the one named last changes fastest.
Arguments:
- tokens: bfloat16 [8192, 2048], P(('shard', 'ctx')), may hold values from -6 to 6
- cotangent: bfloat16 [8192, 2048], P(('shard', 'ctx')), may hold values from -6 to 6
- seq_len: int32 [4], P('shard'), may hold values from 1024 to 2048
- block_slot: int32 [4, 16], P('shard'), may hold values from 0 to 15, each once within a row
- attn_gain: bfloat16 [2048], P(('shard', 'ctx')), may hold values from 0.099609375 to 1.8984375
- w_query: bfloat16 [2048, 2048], P(('shard', 'ctx'), 'tensor'), may hold values from -0.125 to 0.125
- w_key: bfloat16 [2048, 2048], P(('shard', 'ctx'), 'tensor'), may hold values from -0.125 to 0.125
- w_value: bfloat16 [2048, 2048], P(('shard', 'ctx'), 'tensor'), may hold values from -0.125 to 0.125
- w_out: bfloat16 [2048, 2048], P('tensor', ('shard', 'ctx')), may hold values from -1.5 to 1.5
- mlp_gain: bfloat16 [2048], P(('shard', 'ctx')), may hold values from 0.099609375 to 1.8984375
- w_gate: bfloat16 [2048, 8192], P(('shard', 'ctx'), 'tensor'), may hold values from -0.125 to 0.125
- w_up: bfloat16 [2048, 8192], P(('shard', 'ctx'), 'tensor'), may hold values from -0.125 to 0.125
- w_down: bfloat16 [8192, 2048], P('tensor', ('shard', 'ctx')), may hold values from -0.0625 to 0.0625
Outputs:
- out: bfloat16 [8192, 2048], P(('shard', 'ctx'))
- grad_x: bfloat16 [8192, 2048], P(('shard', 'ctx'))
- grad_attn_gain: float32 [2048], P(('shard', 'ctx'))
- grad_w_query: float32 [2048, 2048], P(('shard', 'ctx'), 'tensor')
- grad_w_key: float32 [2048, 2048], P(('shard', 'ctx'), 'tensor')
- grad_w_value: float32 [2048, 2048], P(('shard', 'ctx'), 'tensor')
- grad_w_out: float32 [2048, 2048], P('tensor', ('shard', 'ctx'))
- grad_mlp_gain: float32 [2048], P(('shard', 'ctx'))
- grad_w_gate: float32 [2048, 8192], P(('shard', 'ctx'), 'tensor')
- grad_w_up: float32 [2048, 8192], P(('shard', 'ctx'), 'tensor')
- grad_w_down: float32 [8192, 2048], P('tensor', ('shard', 'ctx'))
The draws below stay inside these ranges and needn't reach their ends.
Inputs may be any that keep to these rules, and one draw needn't show every extreme that they name: Rows of a sequence at positions from seq_len on are padding. `block_slot`: each row is a permutation of the sequence's 16 slots; slot j holds rows j * 128 to (j + 1) * 128 - 1 of the sequence.
All inputs are finite; a program needn't handle non-finite values.
Results may differ from the reference program's by a relative error of at most 0.024.
Values may be sent and summed in bfloat16 or wider, within the bound.
A program may use at most 256 MiB of HBM per device.

```python
import jax
import jax.numpy as jnp
from jax import lax

D = 2048
HEADS = 32
HDIM = 64
FF = 8192
BLK = 128
GBLK = 16
GROUPS = 4
TOKENS = 8192


def with_ends(array, own_key, smallest, high):
    longest = array.shape.index(max(array.shape))
    spots = []
    for shift in (0, 1):
        where = [jax.random.randint(jax.random.fold_in(own_key, axis), (), 0, length) for axis, length in enumerate(array.shape)]
        where[longest] = (where[longest] + shift) % array.shape[longest]
        spots.append(tuple(where))
    return array.at[spots[0]].set(smallest).at[spots[1]].set(high)


def shard_levels(stream_key, extent, shards, least, largest):
    loudness, own = 1.0, jax.random.fold_in(stream_key, 6)
    for dim, blocks in shards:
        heights = jnp.exp(jax.random.uniform(jax.random.fold_in(own, dim), (blocks,), jnp.float32, least / len(shards), largest / len(shards)))
        loudness = loudness * jnp.repeat(heights, extent[dim] // blocks).reshape([-1 if axis == dim else 1 for axis in range(len(extent))])
    return loudness


def scatter_about(own_key, dims, deviation, most, shards=(), kind=jnp.bfloat16):
    values = deviation * jax.random.normal(own_key, dims, jnp.float32)
    if shards:
        values = values * shard_levels(own_key, dims, shards, -0.22, 0.18)
    return jnp.clip(values, -most, most).astype(kind)


def setup_inputs(seed: int = 0) -> dict:
    key_of = jax.random.split(jax.random.key(seed), 14)
    return {
        "tokens": scatter_about(key_of[0], (TOKENS, D), 1.0, 6.0, ((0, 8),)),
        "cotangent": scatter_about(key_of[1], (TOKENS, D), 1.0, 6.0, ((0, 8),)),
        "seq_len": with_ends(jax.random.randint(key_of[2], (GROUPS,), GBLK * BLK // 2, GBLK * BLK + 1), jax.random.fold_in(key_of[2], 1), GBLK * BLK // 2, GBLK * BLK).astype(jnp.int32),
        "block_slot": jax.vmap(lambda own: jax.random.permutation(own, GBLK))(jax.random.split(key_of[3], GROUPS)).reshape((GROUPS, GBLK)).astype(jnp.int32),
        "attn_gain": jnp.clip(1.0 + 0.18 * jax.random.normal(key_of[4], (D,), jnp.float32), 0.099609375, 1.8984375).astype(jnp.bfloat16),
        "w_query": scatter_about(key_of[5], (D, D), D ** -0.5, 0.125, ((0, 8), (1, 4))),
        "w_key": scatter_about(key_of[6], (D, D), D ** -0.5, 0.125, ((0, 8), (1, 4))),
        "w_value": scatter_about(key_of[7], (D, D), D ** -0.5, 0.125, ((0, 8), (1, 4))),
        "w_out": scatter_about(key_of[8], (D, D), (max(4, D // 128)) ** -0.5, 1.5, ((0, 4), (1, 8))),
        "mlp_gain": jnp.clip(1.0 + 0.18 * jax.random.normal(key_of[9], (D,), jnp.float32), 0.099609375, 1.8984375).astype(jnp.bfloat16),
        "w_gate": scatter_about(key_of[10], (D, FF), D ** -0.5, 0.125, ((0, 8), (1, 4))),
        "w_up": scatter_about(key_of[11], (D, FF), D ** -0.5, 0.125, ((0, 8), (1, 4))),
        "w_down": scatter_about(key_of[12], (FF, D), FF ** -0.5, 0.0625, ((0, 4), (1, 8))),
    }


EPS = 1e-05
THETA = 130000.0
NEG = -1e+30

@jax.custom_vjp
def low(v):
    return lax.optimization_barrier(v.astype(jnp.bfloat16)).astype(jnp.float32)

@jax.custom_vjp
def low_back(v):
    return v

def low_keep(v):
    return (low(v), None)

def low_pass(kept, grad):
    return (grad,)

def back_keep(v):
    return (v, None)

def back_low(kept, grad):
    return (low(grad),)
low.defvjp(low_keep, low_pass)
low_back.defvjp(back_keep, back_low)

def block_layout(live_len, block_slot, block_len):
    slot_count = block_slot.shape[0]
    order = jnp.arange(slot_count, dtype=jnp.int32)
    placed = (block_slot[:, None] == order[None, :]).astype(jnp.int32)
    slot_within = lax.optimization_barrier(jnp.sum(placed * order[:, None], axis=0)).astype(jnp.int32)
    offsets = jnp.arange(block_len, dtype=jnp.int32)
    row_pos = (slot_within[:, None] * block_len + offsets[None, :]).reshape(-1).astype(jnp.int32)
    row_live = row_pos < live_len
    return (row_pos, row_live)

def rope_tables(positions, half_dim):
    freqs = THETA ** (-jnp.arange(half_dim, dtype=jnp.float32) / half_dim)
    angles = positions.astype(jnp.float32)[:, None] * freqs[None, :]
    return (jnp.cos(angles), jnp.sin(angles))

def rotate(values, cosines, sines, head_count):
    row_count = values.shape[0]
    paired = values.reshape(row_count, head_count, 2, -1)
    first = paired[:, :, 0]
    second = paired[:, :, 1]
    cos_wide = cosines[:, None]
    sin_wide = sines[:, None]
    turned = jnp.stack([first * cos_wide - second * sin_wide, second * cos_wide + first * sin_wide], axis=2)
    return turned.reshape(row_count, -1)

def rms_norm(values, gain):
    scale = lax.rsqrt(lax.optimization_barrier(jnp.mean(values * values, axis=-1, keepdims=True)) + EPS)
    return values * scale * gain

def matmul(left, right):
    return jnp.dot(left, right, precision=lax.Precision.HIGHEST, preferred_element_type=jnp.float32)

def forward(inputs, attn_gain, w_query, w_key, w_value, w_out, mlp_gain, w_gate, w_up, w_down, row_pos, row_live):
    row_count = inputs.shape[0]
    n_one = low(rms_norm(inputs, attn_gain))
    cosines, sines = rope_tables(row_pos, HDIM // 2)
    queries = low(rotate(low_back(matmul(n_one, w_query)), cosines, sines, HEADS))
    keys = low(rotate(low_back(matmul(n_one, w_key)), cosines, sines, HEADS))
    values = low(low_back(matmul(n_one, w_value)))
    key_heads = keys.reshape(row_count, HEADS, HDIM)
    value_heads = values.reshape(row_count, HEADS, HDIM)
    q_rows = min(512, row_count)
    q_blocks = row_count // q_rows

    def attend(packed):
        query_part, pos_part = packed
        raw = jnp.einsum('qhd,khd->hqk', query_part, key_heads, precision=lax.Precision.HIGHEST) * 0.125
        scores = low_back(raw)
        allowed = (row_pos[None, :] <= pos_part[:, None]) & row_live[None, :]
        scores = jnp.where(allowed[None], scores, NEG)
        attn_prob = low(jax.nn.softmax(scores, axis=-1))
        mixed = jnp.einsum('hqk,khd->qhd', attn_prob, value_heads, precision=lax.Precision.HIGHEST)
        return low_back(mixed).reshape(q_rows, HEADS * HDIM)
    mixed_all = lax.map(jax.checkpoint(attend), (queries.reshape(q_blocks, q_rows, HEADS, HDIM), row_pos.reshape(q_blocks, q_rows)))
    attn_out = low(mixed_all.reshape(row_count, HEADS * HDIM))
    hidden_res = inputs + low_back(matmul(attn_out, w_out))
    n_two = low(rms_norm(hidden_res, mlp_gain))
    gate_pre = low_back(matmul(n_two, w_gate))
    up_proj = low_back(matmul(n_two, w_up))
    activated = low(jax.nn.silu(gate_pre) * up_proj)
    return hidden_res + low_back(matmul(activated, w_down))

def reference(tokens, cotangent, seq_len, block_slot, attn_gain, w_query, w_key, w_value, w_out, mlp_gain, w_gate, w_up, w_down):
    params = tuple((param.astype(jnp.float32) for param in (attn_gain, w_query, w_key, w_value, w_out, mlp_gain, w_gate, w_up, w_down)))
    group_rows = GBLK * BLK
    inputs = tokens.astype(jnp.float32).reshape(GROUPS, group_rows, D)
    grads_top = cotangent.astype(jnp.float32).reshape(GROUPS, group_rows, D)

    def per_group(running, packed):
        group_in, group_grad, live_len, slot_row = packed
        row_pos, row_live = block_layout(live_len, slot_row, BLK)

        def layer(group_values, *weights):
            return forward(group_values, *weights, row_pos, row_live)
        outputs, pullback = jax.vjp(layer, group_in, *params)
        grads = pullback(group_grad)
        running = tuple((acc + update for acc, update in zip(running, grads[1:])))
        return (running, (outputs.astype(jnp.bfloat16), grads[0].astype(jnp.bfloat16)))
    start = tuple((jnp.zeros(param.shape, jnp.float32) for param in params))
    totals, (outputs, grad_inputs) = lax.scan(per_group, start, (inputs, grads_top, seq_len, block_slot))
    return (outputs.reshape(TOKENS, D), grad_inputs.reshape(TOKENS, D), totals[0], totals[1], totals[2], totals[3], totals[4], totals[5], totals[6], totals[7], totals[8])
```

```python
import functools

import jax
import jax.numpy as jnp
from jax import lax
from jax.experimental import pallas as pl
from jax.experimental.pallas import tpu as pltpu
from jax.sharding import PartitionSpec as P

HDIM = 64
BLK = 128
EPS = 1e-05
THETA = 130000.0
NEG = -1e30
LEVEL = ("ctx", "tensor")
BF = jnp.bfloat16
F32 = jnp.float32
QT = 512

NT = (((1,), (1,)), ((), ()))
TN = (((0,), (0,)), ((), ()))


def mm(left, right, dims=None):
    if dims is None:
        return jnp.dot(left, right, preferred_element_type=F32)
    return lax.dot_general(left, right, dims, preferred_element_type=F32)


def swap(value, group, bit):
    return lax.ppermute(value, LEVEL, [(i, i ^ bit) for i in range(group)])


def level_bits(ctx, tensor):
    bits_y = []
    bit = 2
    while bit < tensor:
        bits_y.append(bit)
        bit *= 2
    bits_x = []
    bit = tensor
    while bit < ctx * tensor:
        bits_x.append(bit)
        bit *= 2
    return bits_y, bits_x


def level_gather(block, ctx, tensor, axis=0):
    group = ctx * tensor
    bits_y, bits_x = level_bits(ctx, tensor)
    half = block.shape[axis] // 2
    whole = {0: block, 1: swap(block, group, 1)}
    parts = [lax.slice_in_dim(block, 0, half, axis=axis), lax.slice_in_dim(block, half, 2 * half, axis=axis)]
    found = [{0: parts[0]}, {0: parts[1]}]
    for which, order in enumerate((bits_x + bits_y, bits_y + bits_x)):
        have = [(0, parts[which])]
        for bit in order:
            sent = jnp.concatenate([v for _, v in have], axis=axis) if len(have) > 1 else have[0][1]
            got = swap(sent, group, bit)
            core = swap(got, group, 1)
            new = []
            for i, (k, _) in enumerate(have):
                piece = lax.slice_in_dim(got, i * half, (i + 1) * half, axis=axis)
                new.append((k | bit, piece))
                found[which][k | bit] = piece
                found[which][k | bit | 1] = lax.slice_in_dim(core, i * half, (i + 1) * half, axis=axis)
            have = have + new
    out = []
    for k in range(group):
        if k in whole:
            out.append(whole[k])
        else:
            out.append(jnp.concatenate([found[0][k], found[1][k]], axis=axis))
    return out


def plus(a, b):
    return (a.astype(F32) + b.astype(F32)).astype(BF)


def level_sum(blocks, ctx, tensor):
    group = ctx * tensor
    bits_y, bits_x = level_bits(ctx, tensor)
    rows = blocks[0].shape[0]
    half = rows // 2
    evens = list(range(0, group, 2))
    got = swap(jnp.concatenate([blocks[k | 1] for k in evens], axis=0), group, 1)
    chip = {k: plus(blocks[k], got[i * rows : (i + 1) * rows]) for i, k in enumerate(evens)}
    done = []
    for which, order in enumerate((bits_x + bits_y, bits_y + bits_x)):
        have = {k: v[which * half : (which + 1) * half] for k, v in chip.items()}
        for bit in order:
            leave = sorted(k for k in have if k & bit)
            got = swap(jnp.concatenate([have[k] for k in leave], axis=0), group, bit)
            for i, k in enumerate(leave):
                piece = got[i * half : (i + 1) * half]
                own = have[k ^ bit]
                have[k ^ bit] = plus(own, piece) if len(leave) > 1 else own.astype(F32) + piece.astype(F32)
                del have[k]
        done.append(have[0])
    return jnp.concatenate(done, axis=0)


def level_exchange(blocks, group):
    return [blocks[0]] + [swap(blocks[k], group, k) for k in range(1, group)]


def chain_gather(own, shards):
    here = lax.axis_index("shard")
    ups, downs = [], []
    up = down = own
    for k in range(1, shards):
        up = lax.ppermute(up, "shard", [(i, i + 1) for i in range(k - 1, shards - 1)])
        down = lax.ppermute(down, "shard", [(i, i - 1) for i in range(1, shards - k + 1)])
        ups.append(up)
        downs.append(down)
    rel = [own]
    for k in range(1, shards):
        rel.append(jnp.where(here >= k, ups[k - 1], downs[shards - k - 1]))
    return rel


def in_order(rel, shards):
    here = lax.axis_index("shard")
    order = (here - jnp.arange(shards)) % shards
    return jnp.take(jnp.stack(rel, axis=0), order, axis=0)


def chain_sum(terms, shards):
    here = lax.axis_index("shard")

    def term(index):
        return lax.dynamic_index_in_dim(terms, jnp.clip(index, 0, shards - 1), 0, keepdims=False)

    up = down = None
    for k in range(1, shards):
        send = term(here + shards - k)
        send = send if up is None else plus(send, up)
        up = lax.ppermute(send, "shard", [(i, i + 1) for i in range(0, k)])
        send = term(here - (shards - k))
        send = send if down is None else plus(send, down)
        down = lax.ppermute(send, "shard", [(i, i - 1) for i in range(shards - k, shards)])
    return term(here).astype(F32) + up.astype(F32) + down.astype(F32)


def qkv_kernel(tok_ref, gain_ref, w_ref, n_ref, out_ref):
    x = tok_ref[...].astype(F32)
    scale = lax.rsqrt(jnp.mean(x * x, axis=-1, keepdims=True) + EPS)
    n = (x * scale * gain_ref[...]).astype(BF)
    n_ref[...] = n
    out_ref[...] = mm(n, w_ref[...])


def qkv_call(tok, gain, weights):
    rows, width = tok.shape
    cols = weights.shape[1]
    tile = 256
    return pl.pallas_call(
        qkv_kernel,
        grid=(rows // tile,),
        in_specs=[
            pl.BlockSpec((tile, width), lambda i: (i, 0)),
            pl.BlockSpec((1, width), lambda i: (0, 0)),
            pl.BlockSpec((width, cols), lambda i: (0, 0)),
        ],
        out_specs=[
            pl.BlockSpec((tile, width), lambda i: (i, 0)),
            pl.BlockSpec((tile, cols), lambda i: (i, 0)),
        ],
        out_shape=[
            jax.ShapeDtypeStruct((rows, width), BF),
            jax.ShapeDtypeStruct((rows, cols), F32),
        ],
        compiler_params=pltpu.CompilerParams(vmem_limit_bytes=48 * 1024 * 1024),
        cost_estimate=pl.CostEstimate(
            flops=2 * rows * width * cols, bytes_accessed=rows * width * 4 + rows * cols * 4 + width * cols * 2, transcendentals=0
        ),
        name="norm_qkv",
    )(tok, gain, weights)


def turn(u, cos, sin):
    lane = lax.broadcasted_iota(jnp.int32, u.shape, 1)
    width = u.shape[1]
    ahead = pltpu.roll(u, width - HDIM // 2, axis=1)
    behind = pltpu.roll(u, HDIM // 2, axis=1)
    other = jnp.where(lane % HDIM < HDIM // 2, ahead, behind)
    return u * cos + other * sin


def wide(table, cols):
    reps = cols // table.shape[1]
    return jnp.concatenate([table] * reps, axis=1) if reps > 1 else table


def attend_kernel(slots, lin_ref, cos_ref, sin_ref, o_slot, qs, ks, vs, os, stats):
    rows, cols = qs.shape
    heads = cols // HDIM

    def fill(b, carry):
        src = pl.ds(pl.multiple_of(slots[b] * BLK, BLK), BLK)
        dst = pl.ds(pl.multiple_of(b * BLK, BLK), BLK)
        cos = wide(cos_ref[dst, :], cols)
        sin = wide(sin_ref[dst, :], cols)
        qs[dst, :] = turn(lin_ref[src, 0:cols], cos, sin).astype(BF)
        ks[dst, :] = turn(lin_ref[src, cols : 2 * cols], cos, sin).astype(BF)
        vs[dst, :] = lin_ref[src, 2 * cols : 3 * cols].astype(BF)
        return carry

    lax.fori_loop(0, rows // BLK, fill, 0)
    live = slots[rows // BLK]
    tiles = rows // QT
    for t in range(tiles):
        ext = (t + 1) * QT
        lane = lax.broadcasted_iota(jnp.int32, (QT, cols), 1) // HDIM
        qpos = lax.broadcasted_iota(jnp.int32, (QT, QT), 0)
        kpos = lax.broadcasted_iota(jnp.int32, (QT, QT), 1)
        diag = jnp.where(kpos <= qpos, 0.0, NEG)
        dead = jnp.where(lax.broadcasted_iota(jnp.int32, (1, ext), 1) < live, 0.0, NEG)

        def head(h, acc):
            q = jnp.where(lane == h, qs[t * QT : ext, :] * BF(0.125), BF(0))
            s = mm(q, ks[0:ext, :], NT) + dead
            last = s[:, t * QT :] + diag
            s = jnp.concatenate([s[:, : t * QT], last], axis=1) if t else last
            top = jnp.max(s, axis=1, keepdims=True)
            p = jnp.exp(s - top)
            total = jnp.sum(p, axis=1, keepdims=True)
            mixed = mm(p.astype(BF), vs[0:ext, :]) / total
            note = jnp.broadcast_to(top + jnp.log(total), (QT, 128))
            stats[pl.ds(h, 1), t * QT : ext] = jnp.transpose(note)[0:1, :]
            return jnp.where(lane == h, mixed, acc)

        acc = lax.fori_loop(0, heads, head, jnp.zeros((QT, cols), F32))
        out = acc.astype(BF)
        os[t * QT : ext, :] = out
        for i in range(QT // BLK):
            dst = pl.ds(pl.multiple_of(slots[t * (QT // BLK) + i] * BLK, BLK), BLK)
            o_slot[dst, :] = out[i * BLK : (i + 1) * BLK, :]


def full_spec(shape):
    return pl.BlockSpec(shape, lambda *_: (0,) * len(shape))


def attend_call(slots, lin, cos, sin):
    rows = lin.shape[0]
    cols = lin.shape[1] // 3
    heads = cols // HDIM
    piece = jax.ShapeDtypeStruct((rows, cols), BF)
    return pl.pallas_call(
        attend_kernel,
        grid_spec=pltpu.PrefetchScalarGridSpec(
            num_scalar_prefetch=1,
            grid=(1,),
            in_specs=[full_spec(lin.shape), full_spec(cos.shape), full_spec(sin.shape)],
            out_specs=[full_spec((rows, cols))] * 5 + [full_spec((8, rows))],
        ),
        out_shape=[piece] * 5 + [jax.ShapeDtypeStruct((8, rows), F32)],
        compiler_params=pltpu.CompilerParams(vmem_limit_bytes=56 * 1024 * 1024),
        cost_estimate=pl.CostEstimate(
            flops=heads * rows * rows * HDIM * 8, bytes_accessed=rows * cols * 22, transcendentals=heads * rows * rows // 2
        ),
        name="attend",
    )(slots, lin, cos, sin)


def attend_back_kernel(slots, qs, ks, vs, os, stats, go_ref, cos_ref, sin_ref, out_ref, go, delta, dq):
    rows, cols = qs.shape
    heads = cols // HDIM

    def fill(b, carry):
        src = pl.ds(pl.multiple_of(slots[b] * BLK, BLK), BLK)
        dst = pl.ds(pl.multiple_of(b * BLK, BLK), BLK)
        go[dst, :] = go_ref[src, :]
        return carry

    lax.fori_loop(0, rows // BLK, fill, 0)
    pick = (
        lax.broadcasted_iota(jnp.int32, (8, cols), 0) == lax.broadcasted_iota(jnp.int32, (8, cols), 1) // HDIM
    ).astype(F32)
    for t in range(rows // QT):
        part = slice(t * QT, (t + 1) * QT)
        both = go[part, :].astype(F32) * os[part, :].astype(F32)
        delta[:, part] = lax.dot_general(
            pick, both, NT, precision=lax.Precision.HIGHEST, preferred_element_type=F32
        )
    dq[...] = jnp.zeros_like(dq)
    live = slots[rows // BLK]
    tiles = rows // QT

    def store(t, column, value, sign):
        cos = wide(cos_ref[t * QT : (t + 1) * QT, :], cols)
        sin = wide(sin_ref[t * QT : (t + 1) * QT, :], cols)
        done = (turn(value, cos, -sin) if sign else value).astype(BF)
        for i in range(QT // BLK):
            dst = pl.ds(pl.multiple_of(slots[t * (QT // BLK) + i] * BLK, BLK), BLK)
            out_ref[dst, column * cols : (column + 1) * cols] = done[i * BLK : (i + 1) * BLK, :]

    for t in range(tiles):
        begin = t * QT
        count = rows - begin
        lane_k = lax.broadcasted_iota(jnp.int32, (QT, cols), 1) // HDIM
        lane_q = lax.broadcasted_iota(jnp.int32, (count, cols), 1) // HDIM
        kpos = lax.broadcasted_iota(jnp.int32, (QT, QT), 0)
        qpos = lax.broadcasted_iota(jnp.int32, (QT, QT), 1)
        diag = jnp.where(kpos <= qpos, 0.0, NEG)
        dead = jnp.where(lax.broadcasted_iota(jnp.int32, (QT, 1), 0) + begin < live, 0.0, NEG)

        def head(h, carry):
            dk, dv = carry
            kt = ks[begin : begin + QT, :]
            qm = jnp.where(lane_q == h, qs[begin:, :] * BF(0.125), BF(0))
            gm = jnp.where(lane_q == h, go[begin:, :], BF(0))
            s = mm(kt, qm, NT) + dead
            first = s[:, :QT] + diag
            s = jnp.concatenate([first, s[:, QT:]], axis=1) if count > QT else first
            p = jnp.exp(s - stats[pl.ds(h, 1), begin:])
            dp = mm(vs[begin : begin + QT, :], gm, NT)
            ds = (p * (dp - delta[pl.ds(h, 1), begin:])).astype(BF)
            km = jnp.where(lane_k == h, kt * BF(0.125), BF(0))
            dq[begin:, :] += mm(ds, km, TN)
            return dk + mm(ds, qm), dv + mm(p.astype(BF), gm)

        zero = jnp.zeros((QT, cols), F32)
        dk, dv = lax.fori_loop(0, heads, head, (zero, zero))
        store(t, 1, dk, True)
        store(t, 2, dv, False)
    for t in range(tiles):
        store(t, 0, dq[t * QT : (t + 1) * QT, :], True)


def attend_back_call(slots, qs, ks, vs, os, stats, go, cos, sin):
    rows, cols = qs.shape
    heads = cols // HDIM
    return pl.pallas_call(
        attend_back_kernel,
        grid_spec=pltpu.PrefetchScalarGridSpec(
            num_scalar_prefetch=1,
            grid=(1,),
            in_specs=[full_spec(qs.shape)] * 4
            + [full_spec(stats.shape), full_spec(go.shape), full_spec(cos.shape), full_spec(sin.shape)],
            out_specs=full_spec((rows, 3 * cols)),
            scratch_shapes=[
                pltpu.VMEM((rows, cols), BF),
                pltpu.VMEM((8, rows), F32),
                pltpu.VMEM((rows, cols), F32),
            ],
        ),
        out_shape=jax.ShapeDtypeStruct((rows, 3 * cols), BF),
        compiler_params=pltpu.CompilerParams(vmem_limit_bytes=60 * 1024 * 1024),
        cost_estimate=pl.CostEstimate(
            flops=heads * rows * rows * HDIM * 20, bytes_accessed=rows * cols * 18, transcendentals=heads * rows * rows // 2
        ),
        name="attend_back",
    )(slots, qs, ks, vs, os, stats, go, cos, sin)


def per_device(
    shards, ctx, tensor, tokens, cotangent, seq_len, block_slot, attn_gain, w_query, w_key, w_value, w_out, mlp_gain, w_gate, w_up, w_down
):
    group = ctx * tensor
    my_x = lax.axis_index("ctx")
    my_t = lax.axis_index("tensor")
    my_z = lax.axis_index("shard")
    me = my_x * tensor + my_t
    width = tokens.shape[1]
    own_rows = tokens.shape[0] // tensor
    level_rows = own_rows * group
    slots_each = own_rows // BLK
    d_own = w_query.shape[0]
    cols = w_query.shape[1] // ctx
    ff = w_gate.shape[1] // ctx
    rel = jnp.arange(group, dtype=jnp.int32)
    swap_x = [(i, i ^ 1) for i in range(ctx)]

    slot = block_slot[0]
    place = ((slot // slots_each) ^ me) * slots_each + slot % slots_each
    slots = jnp.concatenate([place, seq_len]).astype(jnp.int32)

    def level_rows_of(array):
        local = jnp.take(array.reshape(tensor, own_rows, width), my_t ^ jnp.arange(tensor), axis=0)
        blocks = [local[k] for k in range(tensor)]
        half = own_rows // 2
        have = [(0, blocks[0])]
        got = swap(blocks[0], group, tensor)
        far = {tensor: got}
        bit = tensor // 2
        while bit >= 1:
            keys = sorted(far)
            sent = jnp.concatenate([far[k] for k in keys], axis=0) if len(keys) > 1 else far[keys[0]]
            got = swap(sent, group, bit)
            for i, k in enumerate(keys):
                far[k | bit] = got[i * own_rows : (i + 1) * own_rows]
            bit //= 2
        return jnp.concatenate([local.reshape(tensor * own_rows, width)] + [far[tensor + k] for k in range(tensor)], axis=0), blocks[0]

    def x_halves(array, axis):
        size = array.shape[axis] // ctx
        mine = lax.dynamic_slice_in_dim(array, my_x * size, size, axis=axis)
        other = lax.dynamic_slice_in_dim(array, (1 - my_x) * size, size, axis=axis)
        return mine, other

    def x_join(mine, got, axis):
        return jnp.where(
            my_x == 0, jnp.concatenate([mine, got], axis=axis), jnp.concatenate([got, mine], axis=axis)
        )

    gains = jnp.stack([attn_gain, mlp_gain], axis=0)
    gains = x_join(gains, lax.ppermute(gains, "ctx", swap_x), 1)
    gains = in_order(chain_gather(gains, shards), shards)
    gains = jnp.transpose(gains, (1, 0, 2)).reshape(2, width).astype(F32)
    gain_one, gain_two = gains[0:1], gains[1:2]

    halves = [x_halves(w, 1) for w in (w_query, w_key, w_value)]
    mine = jnp.concatenate([a for a, _ in halves], axis=1)
    got = lax.ppermute(jnp.concatenate([b for _, b in halves], axis=1), "ctx", swap_x)
    w_qkv = in_order(chain_gather(x_join(mine, got, 0), shards), shards).reshape(width, 3 * cols)

    tok, tok_own = level_rows_of(tokens)

    angle_at = jnp.arange(level_rows, dtype=F32)
    lane = jnp.arange(128)
    freqs = THETA ** (-(lane % (HDIM // 2)).astype(F32) / (HDIM // 2))
    angles = angle_at[:, None] * freqs[None, :]
    cos = jnp.cos(angles)
    sin = jnp.sin(angles) * jnp.where(lane % HDIM < HDIM // 2, -1.0, 1.0)
    n_one, lin = qkv_call(tok, gain_one, w_qkv)
    o_slot, qs, ks, vs, os, stats = attend_call(slots, lin, cos, sin)

    head_order = jnp.arange(group)
    head_owner = (head_order % ctx) * tensor + head_order // ctx
    got = level_exchange([o_slot[k * own_rows : (k + 1) * own_rows] for k in range(group)], group)
    attn_rows = jnp.take(jnp.stack(got, axis=0), head_owner ^ me, axis=0)
    attn_rows = jnp.transpose(attn_rows, (1, 0, 2)).reshape(own_rows, width)

    pieces = jnp.stack(chain_gather(w_out, shards), axis=0)
    every = jnp.stack(level_gather(pieces, ctx, tensor, axis=1), axis=0)
    every = jnp.take(every, rel ^ me, axis=0)
    every = jnp.take(every, (my_z - jnp.arange(shards)) % shards, axis=1)
    every = every.reshape(ctx, tensor, shards, w_out.shape[0], d_own)
    w_out_all = jnp.transpose(every, (1, 3, 2, 0, 4)).reshape(width, width)

    x_own = tok_own.astype(F32)
    hidden_res = x_own + mm(attn_rows, w_out_all)
    scale_two = lax.rsqrt(jnp.mean(hidden_res * hidden_res, axis=-1, keepdims=True) + EPS)
    normed_two = hidden_res * scale_two
    n_two_own = (normed_two * gain_two).astype(BF)
    n_two = jnp.concatenate(level_gather(n_two_own, ctx, tensor), axis=0)
    cot, cot_own = level_rows_of(cotangent)

    chunks = 2
    fc = ff // chunks
    w_down_t = w_down.T
    chunk_grads = []
    gu_all, hid_all, w_gu_all, w_dt_all = [], [], [], []
    for c in range(chunks):
        mine_parts, other_parts = [], []
        for w in (w_gate, w_up, w_down_t):
            mine_parts.append(lax.dynamic_slice_in_dim(w, my_x * ff + c * fc, fc, axis=1))
            other_parts.append(lax.dynamic_slice_in_dim(w, (1 - my_x) * ff + c * fc, fc, axis=1))
        mine = jnp.concatenate(mine_parts, axis=1)
        got = lax.ppermute(jnp.concatenate(other_parts, axis=1), "ctx", swap_x)
        weights = in_order(chain_gather(x_join(mine, got, 0), shards), shards).reshape(width, 3 * fc)
        w_gu, w_dt = weights[:, : 2 * fc], weights[:, 2 * fc :]
        gate_up = mm(n_two, w_gu)
        gate, up = gate_up[:, :fc], gate_up[:, fc:]
        sig = jax.nn.sigmoid(gate)
        act = gate * sig
        hidden = (act * up).astype(BF)
        d_hidden = mm(cot, w_dt)
        d_gate = (d_hidden * up * sig * (1.0 + gate * (1.0 - sig))).astype(BF)
        d_up = (d_hidden * act).astype(BF)
        d_gu = jnp.concatenate([d_gate, d_up], axis=1)
        grad_gu = mm(n_two, d_gu, TN).astype(BF)
        grad_dt = mm(cot, hidden, TN).astype(BF)
        chunk_grads.append(jnp.concatenate([grad_gu, grad_dt], axis=1))
        gu_all.append(d_gu)
        hid_all.append(hidden)
        w_gu_all.append(w_gu)
        w_dt_all.append(w_dt)
    d_gu = jnp.concatenate(gu_all, axis=1)
    hidden = jnp.concatenate(hid_all, axis=1)
    w_gu = jnp.concatenate(w_gu_all, axis=1)
    w_dt = jnp.concatenate(w_dt_all, axis=1)

    def row_blocks(array):
        return [array[k * own_rows : (k + 1) * own_rows] for k in range(group)]

    d_n_two = level_sum(row_blocks(mm(d_gu, w_gu, NT).astype(BF)), ctx, tensor)
    out_own = hidden_res + level_sum(row_blocks(mm(hidden, w_dt, NT).astype(BF)), ctx, tensor)

    def tensor_rows(own):
        have = [(0, own)]
        bit = tensor // 2
        while bit >= 1:
            sent = jnp.concatenate([v for _, v in have], axis=0) if len(have) > 1 else have[0][1]
            got = swap(sent, group, bit)
            have = have + [(k | bit, got[i * own_rows : (i + 1) * own_rows]) for i, (k, _) in enumerate(have)]
            bit //= 2
        have = [v for _, v in sorted(have, key=lambda e: e[0])]
        ordered = jnp.take(jnp.stack(have, axis=0), my_t ^ jnp.arange(tensor), axis=0)
        return ordered.reshape(tensor * own_rows, width)

    result = tensor_rows(out_own.astype(BF))

    def mlp_sums(chunk):
        total = chain_sum(chunk.reshape(shards, ctx * d_own, 3 * fc), shards)
        mine, other = x_halves(total, 0)
        got = lax.ppermute(other.astype(BF), "ctx", swap_x).astype(F32)
        return mine, got

    cot_f = cot_own.astype(F32)
    scaled = d_n_two * gain_two
    inner = jnp.mean(scaled * normed_two, axis=-1, keepdims=True)
    d_h = cot_f + scale_two * (scaled - normed_two * inner)
    gain_two_part = jnp.sum(d_n_two * normed_two, axis=0)
    d_h_low = d_h.astype(BF)
    d_attn = mm(d_h_low, w_out_all, NT).astype(BF)
    blocks = jnp.transpose(d_attn.reshape(own_rows, group, cols), (1, 0, 2))
    owner_rel = rel ^ me
    col_of = (owner_rel % tensor) * ctx + owner_rel // tensor
    blocks = jnp.take(blocks, col_of, axis=0)
    go = jnp.concatenate(level_exchange([blocks[k] for k in range(group)], group), axis=0)
    d_qkv = attend_back_call(slots, qs, ks, vs, os, stats, go, cos, sin)

    d_h_all = jnp.concatenate(level_gather(d_h_low, ctx, tensor), axis=0)
    grad_wo = mm(d_h_all, o_slot, TN).astype(BF)
    grad_wqkv = mm(n_one, d_qkv, TN).astype(BF)
    d_n_one = level_sum(row_blocks(mm(d_qkv, w_qkv, NT).astype(BF)), ctx, tensor)
    x_scale = lax.rsqrt(jnp.mean(x_own * x_own, axis=-1, keepdims=True) + EPS)
    x_normed = x_own * x_scale
    scaled = d_n_one * gain_one
    inner = jnp.mean(scaled * x_normed, axis=-1, keepdims=True)
    d_x = d_h + x_scale * (scaled - x_normed * inner)
    gain_one_part = jnp.sum(d_n_one * x_normed, axis=0)
    grad_x = tensor_rows(d_x.astype(BF))

    def spread(parts, axis):
        mine = jnp.concatenate([m for m, _ in parts], axis=axis) if len(parts) > 1 else parts[0][0]
        got = jnp.concatenate([g for _, g in parts], axis=axis) if len(parts) > 1 else parts[0][1]
        return x_join(mine, got, axis)

    sums = [mlp_sums(g) for g in chunk_grads]
    grad_gate = spread([(m[:, :fc], g[:, :fc]) for m, g in sums], 1)
    grad_up = spread([(m[:, fc : 2 * fc], g[:, fc : 2 * fc]) for m, g in sums], 1)
    grad_down = spread([(m[:, 2 * fc :], g[:, 2 * fc :]) for m, g in sums], 1).T

    def attn_sums(array):
        total = chain_sum(array.reshape(shards, ctx * d_own, array.shape[1]), shards)
        mine, other = x_halves(total, 0)
        got = lax.ppermute(other.astype(BF), "ctx", swap_x).astype(F32)
        return mine, got

    mine, got = attn_sums(grad_wo)
    grad_out = x_join(mine, got, 1).T
    mine, got = attn_sums(grad_wqkv)
    grad_q = x_join(mine[:, :cols], got[:, :cols], 1)
    grad_k = x_join(mine[:, cols : 2 * cols], got[:, cols : 2 * cols], 1)
    grad_v = x_join(mine[:, 2 * cols :], got[:, 2 * cols :], 1)

    def gain_sum(part):
        total = lax.psum(part, ("shard", "ctx", "tensor"))
        return lax.dynamic_slice_in_dim(total, (my_z * ctx + my_x) * d_own, d_own)

    grad_gain_two = gain_sum(gain_two_part)
    grad_gain_one = gain_sum(gain_one_part)
    return (
        result,
        grad_x,
        grad_gain_one,
        grad_q,
        grad_k,
        grad_v,
        grad_out,
        grad_gain_two,
        grad_gate,
        grad_up,
        grad_down,
    )


def solution(mesh):
    rows = P(("shard", "ctx"), None)
    gain = P(("shard", "ctx"))
    into = P(("shard", "ctx"), "tensor")
    back = P("tensor", ("shard", "ctx"))
    sizes = mesh.shape
    return jax.shard_map(
        functools.partial(per_device, sizes["shard"], sizes["ctx"], sizes["tensor"]),
        mesh=mesh,
        in_specs=(rows, rows, P("shard"), P("shard", None), gain, into, into, into, back, gain, into, into, back),
        out_specs=(rows, rows, gain, into, into, into, back, gain, into, into, back),
        check_vma=False,
    )
```

```python
import functools

import jax
import jax.numpy as jnp
from jax import lax
from jax.experimental import pallas as pl
from jax.experimental.pallas import tpu as pltpu
from jax.sharding import PartitionSpec as P

HDIM = 64
BLK = 128
EPS = 1e-05
THETA = 130000.0
NEG = -1e30
LEVEL = ("ctx", "tensor")
BF = jnp.bfloat16
F32 = jnp.float32
QT = 512

NT = (((1,), (1,)), ((), ()))
TN = (((0,), (0,)), ((), ()))


def mm(left, right, dims=None):
    if dims is None:
        return jnp.dot(left, right, preferred_element_type=F32)
    return lax.dot_general(left, right, dims, preferred_element_type=F32)


def swap(value, group, bit):
    return lax.ppermute(value, LEVEL, [(i, i ^ bit) for i in range(group)])


def level_bits(ctx, tensor):
    bits_y = []
    bit = 2
    while bit < tensor:
        bits_y.append(bit)
        bit *= 2
    bits_x = []
    bit = tensor
    while bit < ctx * tensor:
        bits_x.append(bit)
        bit *= 2
    return bits_y, bits_x


def level_gather(block, ctx, tensor, axis=0):
    group = ctx * tensor
    bits_y, bits_x = level_bits(ctx, tensor)
    half = block.shape[axis] // 2
    whole = {0: block, 1: swap(block, group, 1)}
    parts = [lax.slice_in_dim(block, 0, half, axis=axis), lax.slice_in_dim(block, half, 2 * half, axis=axis)]
    found = [{0: parts[0]}, {0: parts[1]}]
    for which, order in enumerate((bits_x + bits_y, bits_y + bits_x)):
        have = [(0, parts[which])]
        for bit in order:
            sent = jnp.concatenate([v for _, v in have], axis=axis) if len(have) > 1 else have[0][1]
            got = swap(sent, group, bit)
            core = swap(got, group, 1)
            new = []
            for i, (k, _) in enumerate(have):
                piece = lax.slice_in_dim(got, i * half, (i + 1) * half, axis=axis)
                new.append((k | bit, piece))
                found[which][k | bit] = piece
                found[which][k | bit | 1] = lax.slice_in_dim(core, i * half, (i + 1) * half, axis=axis)
            have = have + new
    out = []
    for k in range(group):
        if k in whole:
            out.append(whole[k])
        else:
            out.append(jnp.concatenate([found[0][k], found[1][k]], axis=axis))
    return out


def plus(a, b):
    return (a.astype(F32) + b.astype(F32)).astype(BF)


def level_sum(blocks, ctx, tensor):
    group = ctx * tensor
    bits_y, bits_x = level_bits(ctx, tensor)
    rows = blocks[0].shape[0]
    half = rows // 2
    evens = list(range(0, group, 2))
    got = swap(jnp.concatenate([blocks[k | 1] for k in evens], axis=0), group, 1)
    chip = {k: plus(blocks[k], got[i * rows : (i + 1) * rows]) for i, k in enumerate(evens)}
    done = []
    for which, order in enumerate((bits_x + bits_y, bits_y + bits_x)):
        have = {k: v[which * half : (which + 1) * half] for k, v in chip.items()}
        for bit in order:
            leave = sorted(k for k in have if k & bit)
            got = swap(jnp.concatenate([have[k] for k in leave], axis=0), group, bit)
            for i, k in enumerate(leave):
                piece = got[i * half : (i + 1) * half]
                own = have[k ^ bit]
                have[k ^ bit] = plus(own, piece) if len(leave) > 1 else own.astype(F32) + piece.astype(F32)
                del have[k]
        done.append(have[0])
    return jnp.concatenate(done, axis=0)


def level_exchange(blocks, group):
    return [blocks[0]] + [swap(blocks[k], group, k) for k in range(1, group)]


def chain_gather(own, shards):
    here = lax.axis_index("shard")
    ups, downs = [], []
    up = down = own
    for k in range(1, shards):
        up = lax.ppermute(up, "shard", [(i, i + 1) for i in range(k - 1, shards - 1)])
        down = lax.ppermute(down, "shard", [(i, i - 1) for i in range(1, shards - k + 1)])
        ups.append(up)
        downs.append(down)
    rel = [own]
    for k in range(1, shards):
        rel.append(jnp.where(here >= k, ups[k - 1], downs[shards - k - 1]))
    return rel


def in_order(rel, shards):
    here = lax.axis_index("shard")
    order = (here - jnp.arange(shards)) % shards
    return jnp.take(jnp.stack(rel, axis=0), order, axis=0)


def chain_sum(terms, shards):
    here = lax.axis_index("shard")

    def term(index):
        return lax.dynamic_index_in_dim(terms, jnp.clip(index, 0, shards - 1), 0, keepdims=False)

    up = down = None
    for k in range(1, shards):
        send = term(here + shards - k)
        send = send if up is None else plus(send, up)
        up = lax.ppermute(send, "shard", [(i, i + 1) for i in range(0, k)])
        send = term(here - (shards - k))
        send = send if down is None else plus(send, down)
        down = lax.ppermute(send, "shard", [(i, i - 1) for i in range(shards - k, shards)])
    return term(here).astype(F32) + up.astype(F32) + down.astype(F32)


def qkv_kernel(tok_ref, gain_ref, w_ref, n_ref, out_ref):
    x = tok_ref[...].astype(F32)
    scale = lax.rsqrt(jnp.mean(x * x, axis=-1, keepdims=True) + EPS)
    n = (x * scale * gain_ref[...]).astype(BF)
    n_ref[...] = n
    out_ref[...] = mm(n, w_ref[...])


def qkv_call(tok, gain, weights):
    rows, width = tok.shape
    cols = weights.shape[1]
    tile = 256
    return pl.pallas_call(
        qkv_kernel,
        grid=(rows // tile,),
        in_specs=[
            pl.BlockSpec((tile, width), lambda i: (i, 0)),
            pl.BlockSpec((1, width), lambda i: (0, 0)),
            pl.BlockSpec((width, cols), lambda i: (0, 0)),
        ],
        out_specs=[
            pl.BlockSpec((tile, width), lambda i: (i, 0)),
            pl.BlockSpec((tile, cols), lambda i: (i, 0)),
        ],
        out_shape=[
            jax.ShapeDtypeStruct((rows, width), BF),
            jax.ShapeDtypeStruct((rows, cols), F32),
        ],
        compiler_params=pltpu.CompilerParams(vmem_limit_bytes=48 * 1024 * 1024),
        cost_estimate=pl.CostEstimate(
            flops=2 * rows * width * cols, bytes_accessed=rows * width * 4 + rows * cols * 4 + width * cols * 2, transcendentals=0
        ),
        name="norm_qkv",
    )(tok, gain, weights)


def turn(u, cos, sin):
    lane = lax.broadcasted_iota(jnp.int32, u.shape, 1)
    width = u.shape[1]
    ahead = pltpu.roll(u, width - HDIM // 2, axis=1)
    behind = pltpu.roll(u, HDIM // 2, axis=1)
    other = jnp.where(lane % HDIM < HDIM // 2, ahead, behind)
    return u * cos + other * sin


def wide(table, cols):
    reps = cols // table.shape[1]
    return jnp.concatenate([table] * reps, axis=1) if reps > 1 else table


def attend_kernel(slots, lin_ref, cos_ref, sin_ref, o_slot, qs, ks, vs, os, stats):
    rows, cols = qs.shape
    heads = cols // HDIM

    def fill(b, carry):
        src = pl.ds(pl.multiple_of(slots[b] * BLK, BLK), BLK)
        dst = pl.ds(pl.multiple_of(b * BLK, BLK), BLK)
        cos = wide(cos_ref[dst, :], cols)
        sin = wide(sin_ref[dst, :], cols)
        qs[dst, :] = turn(lin_ref[src, 0:cols], cos, sin).astype(BF)
        ks[dst, :] = turn(lin_ref[src, cols : 2 * cols], cos, sin).astype(BF)
        vs[dst, :] = lin_ref[src, 2 * cols : 3 * cols].astype(BF)
        return carry

    lax.fori_loop(0, rows // BLK, fill, 0)
    live = slots[rows // BLK]
    tiles = rows // QT
    for t in range(tiles):
        ext = (t + 1) * QT
        lane = lax.broadcasted_iota(jnp.int32, (QT, cols), 1) // HDIM
        qpos = lax.broadcasted_iota(jnp.int32, (QT, QT), 0)
        kpos = lax.broadcasted_iota(jnp.int32, (QT, QT), 1)
        diag = jnp.where(kpos <= qpos, 0.0, NEG)
        dead = jnp.where(lax.broadcasted_iota(jnp.int32, (1, ext), 1) < live, 0.0, NEG)

        def head(h, acc):
            q = jnp.where(lane == h, qs[t * QT : ext, :] * BF(0.125), BF(0))
            s = mm(q, ks[0:ext, :], NT) + dead
            last = s[:, t * QT :] + diag
            s = jnp.concatenate([s[:, : t * QT], last], axis=1) if t else last
            top = jnp.max(s, axis=1, keepdims=True)
            p = jnp.exp(s - top)
            total = jnp.sum(p, axis=1, keepdims=True)
            mixed = mm(p.astype(BF), vs[0:ext, :]) / total
            note = jnp.broadcast_to(top + jnp.log(total), (QT, 128))
            stats[pl.ds(h, 1), t * QT : ext] = jnp.transpose(note)[0:1, :]
            return jnp.where(lane == h, mixed, acc)

        acc = lax.fori_loop(0, heads, head, jnp.zeros((QT, cols), F32))
        out = acc.astype(BF)
        os[t * QT : ext, :] = out
        for i in range(QT // BLK):
            dst = pl.ds(pl.multiple_of(slots[t * (QT // BLK) + i] * BLK, BLK), BLK)
            o_slot[dst, :] = out[i * BLK : (i + 1) * BLK, :]


def full_spec(shape):
    return pl.BlockSpec(shape, lambda *_: (0,) * len(shape))


def attend_call(slots, lin, cos, sin):
    rows = lin.shape[0]
    cols = lin.shape[1] // 3
    heads = cols // HDIM
    piece = jax.ShapeDtypeStruct((rows, cols), BF)
    return pl.pallas_call(
        attend_kernel,
        grid_spec=pltpu.PrefetchScalarGridSpec(
            num_scalar_prefetch=1,
            grid=(1,),
            in_specs=[full_spec(lin.shape), full_spec(cos.shape), full_spec(sin.shape)],
            out_specs=[full_spec((rows, cols))] * 5 + [full_spec((8, rows))],
        ),
        out_shape=[piece] * 5 + [jax.ShapeDtypeStruct((8, rows), F32)],
        compiler_params=pltpu.CompilerParams(vmem_limit_bytes=56 * 1024 * 1024),
        cost_estimate=pl.CostEstimate(
            flops=heads * rows * rows * HDIM * 8, bytes_accessed=rows * cols * 22, transcendentals=heads * rows * rows // 2
        ),
        name="attend",
    )(slots, lin, cos, sin)


def attend_back_kernel(slots, qs, ks, vs, os, stats, go_ref, cos_ref, sin_ref, out_ref, go, delta, dq):
    rows, cols = qs.shape
    heads = cols // HDIM

    def fill(b, carry):
        src = pl.ds(pl.multiple_of(slots[b] * BLK, BLK), BLK)
        dst = pl.ds(pl.multiple_of(b * BLK, BLK), BLK)
        go[dst, :] = go_ref[src, :]
        return carry

    lax.fori_loop(0, rows // BLK, fill, 0)
    pick = (
        lax.broadcasted_iota(jnp.int32, (8, cols), 0) == lax.broadcasted_iota(jnp.int32, (8, cols), 1) // HDIM
    ).astype(F32)
    for t in range(rows // QT):
        part = slice(t * QT, (t + 1) * QT)
        both = go[part, :].astype(F32) * os[part, :].astype(F32)
        delta[:, part] = lax.dot_general(
            pick, both, NT, precision=lax.Precision.HIGHEST, preferred_element_type=F32
        )
    dq[...] = jnp.zeros_like(dq)
    live = slots[rows // BLK]
    tiles = rows // QT

    def store(t, column, value, sign):
        cos = wide(cos_ref[t * QT : (t + 1) * QT, :], cols)
        sin = wide(sin_ref[t * QT : (t + 1) * QT, :], cols)
        done = (turn(value, cos, -sin) if sign else value).astype(BF)
        for i in range(QT // BLK):
            dst = pl.ds(pl.multiple_of(slots[t * (QT // BLK) + i] * BLK, BLK), BLK)
            out_ref[dst, column * cols : (column + 1) * cols] = done[i * BLK : (i + 1) * BLK, :]

    for t in range(tiles):
        begin = t * QT
        count = rows - begin
        lane_k = lax.broadcasted_iota(jnp.int32, (QT, cols), 1) // HDIM
        lane_q = lax.broadcasted_iota(jnp.int32, (count, cols), 1) // HDIM
        kpos = lax.broadcasted_iota(jnp.int32, (QT, QT), 0)
        qpos = lax.broadcasted_iota(jnp.int32, (QT, QT), 1)
        diag = jnp.where(kpos <= qpos, 0.0, NEG)
        dead = jnp.where(lax.broadcasted_iota(jnp.int32, (QT, 1), 0) + begin < live, 0.0, NEG)

        def head(h, carry):
            dk, dv = carry
            kt = ks[begin : begin + QT, :]
            qm = jnp.where(lane_q == h, qs[begin:, :] * BF(0.125), BF(0))
            gm = jnp.where(lane_q == h, go[begin:, :], BF(0))
            s = mm(kt, qm, NT) + dead
            first = s[:, :QT] + diag
            s = jnp.concatenate([first, s[:, QT:]], axis=1) if count > QT else first
            p = jnp.exp(s - stats[pl.ds(h, 1), begin:])
            dp = mm(vs[begin : begin + QT, :], gm, NT)
            ds = (p * (dp - delta[pl.ds(h, 1), begin:])).astype(BF)
            km = jnp.where(lane_k == h, kt * BF(0.125), BF(0))
            dq[begin:, :] += mm(ds, km, TN)
            return dk + mm(ds, qm), dv + mm(p.astype(BF), gm)

        zero = jnp.zeros((QT, cols), F32)
        dk, dv = lax.fori_loop(0, heads, head, (zero, zero))
        store(t, 1, dk, True)
        store(t, 2, dv, False)
    for t in range(tiles):
        store(t, 0, dq[t * QT : (t + 1) * QT, :], True)


def attend_back_call(slots, qs, ks, vs, os, stats, go, cos, sin):
    rows, cols = qs.shape
    heads = cols // HDIM
    return pl.pallas_call(
        attend_back_kernel,
        grid_spec=pltpu.PrefetchScalarGridSpec(
            num_scalar_prefetch=1,
            grid=(1,),
            in_specs=[full_spec(qs.shape)] * 4
            + [full_spec(stats.shape), full_spec(go.shape), full_spec(cos.shape), full_spec(sin.shape)],
            out_specs=full_spec((rows, 3 * cols)),
            scratch_shapes=[
                pltpu.VMEM((rows, cols), BF),
                pltpu.VMEM((8, rows), F32),
                pltpu.VMEM((rows, cols), F32),
            ],
        ),
        out_shape=jax.ShapeDtypeStruct((rows, 3 * cols), BF),
        compiler_params=pltpu.CompilerParams(vmem_limit_bytes=60 * 1024 * 1024),
        cost_estimate=pl.CostEstimate(
            flops=heads * rows * rows * HDIM * 20, bytes_accessed=rows * cols * 18, transcendentals=heads * rows * rows // 2
        ),
        name="attend_back",
    )(slots, qs, ks, vs, os, stats, go, cos, sin)


def flip(index, bit):
    return index + bit - 2 * bit * ((index // bit) % 2)


def mlp_kernel(
    dims, n_own, cot_in, wg, wu, wd,
    dn_out, out_out, mine_out, got_out, g_hbm, r_hbm,
    n2, cot, wgu_v, wd_v, hid, dgu, left_t, gt, st, ost, fin, away,
    lev_send, lev_recv, x_own, x_send, x_recv, a_send, a_recv, g_sem, s_sem, rs_send, rs_recv, fx_send, fx_recv, o_sem, c_sem,
):
    shards, ctx, tensor, chunks, fc, rows_own, d_own = dims
    group = ctx * tensor
    rows, width = n2.shape
    dz = ctx * d_own
    ff = chunks * fc
    z = lax.axis_index("shard")
    x = lax.axis_index("ctx")
    t = lax.axis_index("tensor")
    bits_y, bits_x = level_bits(ctx, tensor)

    def mesh_id(bit):
        return (z, x, flip(t, bit)) if bit < tensor else (z, 1 - x, t)

    def above():
        return (z + 1, x, t)

    def below():
        return (z - 1, x, t)

    barrier = pltpu.get_barrier_semaphore()
    partners = [1] + bits_y + bits_x
    for bit in partners:
        pl.semaphore_signal(barrier, inc=1, device_id=mesh_id(bit), device_id_type=pl.DeviceIdType.MESH)

    @pl.when(z < shards - 1)
    def _():
        pl.semaphore_signal(barrier, inc=1, device_id=above(), device_id_type=pl.DeviceIdType.MESH)

    @pl.when(z > 0)
    def _():
        pl.semaphore_signal(barrier, inc=1, device_id=below(), device_id_type=pl.DeviceIdType.MESH)

    peers = len(partners) + (z + shards - 1) // shards + (2 * shards - 2 - z) // shards
    pl.semaphore_wait(barrier, peers)

    here_too = (z, x, flip(t, 1))

    def remote(src, dst, send, recv, where):
        return pltpu.make_async_remote_copy(
            src_ref=src, dst_ref=dst, send_sem=send, recv_sem=recv, device_id=where, device_id_type=pl.DeviceIdType.MESH
        )

    def x_copies(c, own):
        half = x if own else 1 - x
        low_c = pl.multiple_of(half * ff + c * fc, fc)
        d_at = pl.ds(pl.multiple_of((z * ctx + x) * d_own, d_own), d_own)
        pairs = [
            (wg.at[:, pl.ds(low_c, fc)], wgu_v.at[c, d_at, pl.ds(0, fc)]),
            (wu.at[:, pl.ds(low_c, fc)], wgu_v.at[c, d_at, pl.ds(fc, fc)]),
            (wd.at[pl.ds(low_c, fc), :], wd_v.at[pl.ds(pl.multiple_of(c * fc, fc), fc), d_at]),
        ]
        if own:
            return [pltpu.make_async_copy(a, b, x_own.at[c, i]) for i, (a, b) in enumerate(pairs)]
        return [remote(a, b, x_send.at[c, i], x_recv.at[c, i], (z, 1 - x, t)) for i, (a, b) in enumerate(pairs)]

    def x_landed(c):
        d_at = pl.ds(pl.multiple_of((z * ctx + 1 - x) * d_own, d_own), d_own)
        lands = [
            wgu_v.at[c, d_at, pl.ds(0, fc)],
            wgu_v.at[c, d_at, pl.ds(fc, fc)],
            wd_v.at[pl.ds(pl.multiple_of(c * fc, fc), fc), d_at],
        ]
        return [remote(a, a, x_send.at[c, i], x_recv.at[c, i], here_too) for i, a in enumerate(lands)]

    def hop(c, way, k, b, wait=False):
        at = pl.ds(pl.multiple_of(b * dz, dz), dz)
        parts = [wgu_v.at[c, at, :], wd_v.at[pl.ds(pl.multiple_of(c * fc, fc), fc), at]]
        where = here_too if wait else above() if way == 0 else below()
        return [remote(p, p, a_send.at[c, way, k, i], a_recv.at[c, way, k, i], where) for i, p in enumerate(parts)]

    def hop_start(c, k):
        @pl.when((z >= k - 1) & (z < shards - 1))
        def _():
            for d in hop(c, 0, k - 1, z - (k - 1)):
                d.start()

        @pl.when((z + k - 1 <= shards - 1) & (z > 0))
        def _():
            for d in hop(c, 1, k - 1, z + (k - 1)):
                d.start()

    def hop_sent(c, k):
        @pl.when((z >= k - 1) & (z < shards - 1))
        def _():
            for d in hop(c, 0, k - 1, z - (k - 1)):
                d.wait_send()

        @pl.when((z + k - 1 <= shards - 1) & (z > 0))
        def _():
            for d in hop(c, 1, k - 1, z + (k - 1)):
                d.wait_send()

    def hop_wait(c, k):
        @pl.when(z >= k)
        def _():
            for d in hop(c, 0, k - 1, z - k, True):
                d.wait_recv()

        @pl.when(z + k <= shards - 1)
        def _():
            for d in hop(c, 1, k - 1, z + k, True):
                d.wait_recv()

    def x_start(c):
        for d in x_copies(c, False):
            d.start()
        for d in x_copies(c, True):
            d.start()

    x_start(0)

    half = rows_own // 2

    def lev(src_k, dst_k, part, sem, bit):
        if part is None:
            s = pl.ds(src_k * rows_own, rows_own)
            e = pl.ds(dst_k * rows_own, rows_own)
        else:
            s = pl.ds(src_k * rows_own + part * half, half)
            e = pl.ds(dst_k * rows_own + part * half, half)
        return remote(n2.at[s, :], n2.at[e, :], lev_send.at[sem], lev_recv.at[sem], mesh_id(bit))

    cot_copy = pltpu.make_async_copy(cot_in, cot, c_sem.at[0])
    own_copy = pltpu.make_async_copy(n_own, n2.at[pl.ds(0, rows_own), :], c_sem.at[1])
    own_copy.start()
    cot_copy.start()
    own_copy.wait()
    sem = 0
    started = []

    def go(src_k, dst_k, part, bit):
        nonlocal sem
        d = lev(src_k, dst_k, part, sem, bit)
        d.start()
        sem += 1
        started.append(d)
        return d

    first = go(0, 1, None, 1)
    have = [[0], [0]]
    orders = [bits_x + bits_y, bits_y + bits_x]
    core_moves = [first]
    arrived = {}
    stages = len(orders[0])
    pending = []
    for stage in range(stages):
        now = []
        for part in (0, 1):
            bit = orders[part][stage]
            for k in have[part]:
                now.append((part, k | bit, go(k, k | bit, part, bit)))
        for part in (0, 1):
            bit = orders[part][stage]
            have[part] = have[part] + [k | bit for k in have[part]]
        pending.append(now)
        if stage == 0:
            for c in range(1, chunks):
                x_start(c)
            for d in x_copies(0, True):
                d.wait()
            for d in x_landed(0):
                d.wait_recv()
            hop_start(0, 1)
        for part, k, d in now:
            d.wait_recv()
            arrived[k] = arrived.get(k, 0) + 1
            if arrived[k] == 2:
                core_moves.append(go(k, k | 1, None, 1))

    def ag_round(r, top):
        for k in range(shards - 1, 0, -1):
            if k > top:
                continue
            c = r - k + 1

            @pl.when((c >= 0) & (c < chunks))
            def _(c=c, k=k):
                if k == 1:
                    for d in x_copies(c, True):
                        d.wait()
                    for d in x_landed(c):
                        d.wait_recv()
                else:
                    hop_wait(c, k - 1)
                hop_start(c, k)

    for r in range(1, shards - 1):
        ag_round(jnp.int32(r), shards - 1)
    for d in core_moves:
        d.wait_recv()
    cot_copy.wait()

    def block_of(i):
        down = shards - 1 - i
        down = down - jnp.where(down <= z, 1, 0)
        up = i + jnp.where(i >= z, 1, 0)
        return jnp.where(i == shards - 1, z, jnp.where(2 * z < shards, down, up))

    def g_copy(c, d, slot):
        return pltpu.make_async_copy(gt.at[slot], g_hbm.at[c, d], g_sem.at[slot])

    def rs_send_copy(src, c, way, d, wait=False):
        where = here_too if wait else above() if way == 0 else below()
        return remote(src, r_hbm.at[c, way, d], rs_send.at[c, way, d], rs_recv.at[c, way, d], where)

    combos = [(way, k) for k in range(2, shards) for way in (0, 1)]

    def target(way, k):
        return z + shards - k if way == 0 else z - (shards - k)

    def sends(way, k):
        if way == 0:
            return z < k
        return z >= shards - k

    def starts(way):
        return z == 0 if way == 0 else z == shards - 1

    def runs(way):
        return z != 0 if way == 0 else z != shards - 1

    def rs_step(s):
        for way in (0, 1):
            for k in range(1, shards):
                c = s - (k - 1)

                @pl.when((c >= 0) & (c < chunks) & starts(way))
                def _(c=c, way=way, k=k):
                    d = target(way, k)
                    rs_send_copy(g_hbm.at[c, d], c, way, d).start()

        for i, (way, k) in enumerate(combos):
            c = s - (k - 1)

            @pl.when((c >= 0) & (c < chunks) & sends(way, k) & runs(way))
            def _(c=c, way=way, k=k, i=i):
                d = target(way, k)

                @pl.when(c >= 1)
                def _():
                    rs_send_copy(st.at[2 * i], c - 1, way, d).wait_send()

                rs_send_copy(st.at[2 * i], c, way, d, True).wait_recv()
                pltpu.make_async_copy(g_hbm.at[c, d], st.at[2 * i], s_sem.at[2 * i]).start()
                pltpu.make_async_copy(r_hbm.at[c, way, d], st.at[2 * i + 1], s_sem.at[2 * i + 1]).start()

        last = 2 * len(combos)
        c_fin = s - (shards - 1)

        @pl.when((c_fin >= 0) & (c_fin < chunks))
        def _():
            pltpu.make_async_copy(g_hbm.at[c_fin, z], st.at[last], s_sem.at[last]).start()
            for way in (0, 1):
                slot = last + 1 + way

                @pl.when(runs(way))
                def _(way=way, slot=slot):
                    rs_send_copy(st.at[slot], c_fin, way, z, True).wait_recv()
                    pltpu.make_async_copy(r_hbm.at[c_fin, way, z], st.at[slot], s_sem.at[slot]).start()

                @pl.when(starts(way))
                def _(slot=slot):
                    st[slot] = jnp.zeros(st.shape[1:], BF)

        for i, (way, k) in enumerate(combos):
            c = s - (k - 1)

            @pl.when((c >= 0) & (c < chunks) & sends(way, k) & runs(way))
            def _(c=c, way=way, k=k, i=i):
                d = target(way, k)
                pltpu.make_async_copy(g_hbm.at[c, d], st.at[2 * i], s_sem.at[2 * i]).wait()
                pltpu.make_async_copy(r_hbm.at[c, way, d], st.at[2 * i + 1], s_sem.at[2 * i + 1]).wait()
                st[2 * i] = (st[2 * i].astype(F32) + st[2 * i + 1].astype(F32)).astype(BF)
                rs_send_copy(st.at[2 * i], c, way, d).start()

        @pl.when((c_fin >= 0) & (c_fin < chunks))
        def _():
            pltpu.make_async_copy(g_hbm.at[c_fin, z], st.at[last], s_sem.at[last]).wait()
            for way in (0, 1):
                slot = last + 1 + way

                @pl.when(runs(way))
                def _(way=way, slot=slot):
                    pltpu.make_async_copy(r_hbm.at[c_fin, way, z], st.at[slot], s_sem.at[slot]).wait()

            @pl.when(c_fin >= 1)
            def _():
                pltpu.make_async_copy(fin, mine_out.at[c_fin - 1], c_sem.at[2]).wait()
                fin_copy(c_fin - 1).wait_send()

            total = st[last].astype(F32) + st[last + 1].astype(F32) + st[last + 2].astype(F32)
            low, high = total[:, :d_own], total[:, d_own:]
            fin[...] = jnp.where(x == 0, low, high)
            away[...] = jnp.where(x == 0, high, low).astype(BF)
            pltpu.make_async_copy(fin, mine_out.at[c_fin], c_sem.at[2]).start()
            fin_copy(c_fin).start()

    def fin_copy(c):
        return remote(away, got_out.at[c], fx_send.at[c], fx_recv.at[c], (z, 1 - x, t))

    tile = 512

    def phase_one(c):
        def body(r, carry):
            at = pl.ds(pl.multiple_of(r * tile, tile), tile)
            gu = mm(n2[at, :], wgu_v[c])
            dh = mm(cot[at, :], wd_v[pl.ds(pl.multiple_of(c * fc, fc), fc), :], NT)
            gate, up = gu[:, :fc], gu[:, fc:]
            sig = 1.0 / (1.0 + jnp.exp(-gate))
            act = gate * sig
            h = (act * up).astype(BF)
            dg = (dh * up * sig * (1.0 + gate * (1.0 - sig))).astype(BF)
            du = (dh * act).astype(BF)
            hid[c, at, :] = h
            dgu[c, at, 0:fc] = dg
            dgu[c, at, fc : 2 * fc] = du
            left_t[0:fc, at] = h.T
            left_t[fc : 2 * fc, at] = dg.T
            left_t[2 * fc : 3 * fc, at] = du.T
            return carry

        lax.fori_loop(0, rows // tile, body, 0)

    def phase_two(c):
        def body(i, carry):
            d = block_of(i)
            slot = i % 2
            at = pl.ds(pl.multiple_of(d * dz, dz), dz)

            @pl.when(i >= 2)
            def _():
                g_copy(c, block_of(i - 2), slot).wait()

            gt[slot, 0:fc, :] = mm(left_t[0:fc, :], cot[:, at]).astype(BF)
            gt[slot, fc : 3 * fc, :] = mm(left_t[fc : 3 * fc, :], n2[:, at]).astype(BF)
            g_copy(c, d, slot).start()
            return carry

        lax.fori_loop(0, shards, body, 0)
        for i in (shards - 2, shards - 1):
            g_copy(c, block_of(jnp.int32(i)), i % 2).wait()

    ot = 256
    units = rows // ot

    def tail_unit(u):
        at = pl.ds(pl.multiple_of((u % units) * ot, ot), ot)
        slot = u % 2

        @pl.when(u >= 2)
        def _():
            pltpu.make_async_copy(ost.at[slot], dn_out.at[at, :], o_sem.at[slot]).wait()

        @pl.when(u < units)
        def _():
            for n in range(width // 512):
                cols = slice(n * 512, (n + 1) * 512)
                acc = jnp.zeros((ot, 512), F32)
                for c in range(chunks):
                    acc = acc + mm(dgu[c, at, :], wgu_v[c, cols, :], NT)
                ost[slot, :, cols] = acc.astype(BF)
            pltpu.make_async_copy(ost.at[slot], dn_out.at[at, :], o_sem.at[slot]).start()

        @pl.when(u >= units)
        def _():
            for n in range(width // 512):
                cols = slice(n * 512, (n + 1) * 512)
                acc = jnp.zeros((ot, 512), F32)
                for c in range(chunks):
                    acc = acc + mm(hid[c, at, :], wd_v[c * fc : (c + 1) * fc, cols])
                ost[slot, :, cols] = acc.astype(BF)
            pltpu.make_async_copy(ost.at[slot], out_out.at[at, :], o_sem.at[slot]).start()

    tail_slots = shards - 1
    per_slot = -(-2 * units // tail_slots)

    def slot_body(s, carry):
        @pl.when(s < chunks)
        def _():
            hop_wait(s, shards - 1)
            phase_one(s)
            ag_round(s + shards - 1, shards - 1)
            phase_two(s)

        @pl.when(s >= chunks)
        def _():
            first_u = (s - chunks) * per_slot
            last_u = jnp.minimum(first_u + per_slot, 2 * units)

            def body(u, carry):
                tail_unit(u)
                return carry

            lax.fori_loop(first_u, last_u, body, 0)

        rs_step(s)
        return carry

    lax.fori_loop(0, chunks + tail_slots, slot_body, 0)

    for u in (2 * units - 2, 2 * units - 1):
        at = pl.ds((u % units) * ot, ot)
        pltpu.make_async_copy(ost.at[u % 2], out_out.at[at, :], o_sem.at[u % 2]).wait()
    for d in started:
        d.wait_send()
    for c in range(chunks):
        for d in x_copies(c, False):
            d.wait_send()
        for k in range(1, shards):
            hop_sent(c, k)
    for way in (0, 1):
        for k in range(1, shards):

            @pl.when(starts(way))
            def _(way=way, k=k):
                d = target(way, k)
                for c in range(chunks):
                    rs_send_copy(g_hbm.at[c, d], c, way, d).wait_send()

    for i, (way, k) in enumerate(combos):

        @pl.when(sends(way, k) & runs(way))
        def _(way=way, k=k, i=i):
            rs_send_copy(st.at[2 * i], chunks - 1, way, target(way, k)).wait_send()

    pltpu.make_async_copy(fin, mine_out.at[chunks - 1], c_sem.at[2]).wait()
    fin_copy(chunks - 1).wait_send()
    for c in range(chunks):
        fin_copy(c).wait_recv()


def mlp_call(shards, ctx, tensor, n_own, cot, wg, wu, wd):
    rows_own, width = n_own.shape
    group = ctx * tensor
    rows = rows_own * group
    d_own = wg.shape[0]
    ff = wg.shape[1] // ctx
    fc = 256
    chunks = ff // fc
    dz = ctx * d_own
    any_spec = pl.BlockSpec(memory_space=pl.ANY)
    bits_y, bits_x = level_bits(ctx, tensor)
    halves = 2 ** (len(bits_y) + len(bits_x)) - 1
    moves = 2 * halves + halves + 1
    stage = 4 * (shards - 2) + 3
    dims = (shards, ctx, tensor, chunks, fc, rows_own, d_own)
    dma = pltpu.SemaphoreType.DMA
    return pl.pallas_call(
        functools.partial(mlp_kernel, dims),
        in_specs=[any_spec] * 5,
        out_specs=[any_spec] * 6,
        out_shape=[
            jax.ShapeDtypeStruct((rows, width), BF),
            jax.ShapeDtypeStruct((rows, width), BF),
            jax.ShapeDtypeStruct((chunks, 3 * fc, d_own), F32),
            jax.ShapeDtypeStruct((chunks, 3 * fc, d_own), BF),
            jax.ShapeDtypeStruct((chunks, shards, 3 * fc, dz), BF),
            jax.ShapeDtypeStruct((chunks, 2, shards, 3 * fc, dz), BF),
        ],
        scratch_shapes=[
            pltpu.VMEM((rows, width), BF),
            pltpu.VMEM((rows, width), BF),
            pltpu.VMEM((chunks, width, 2 * fc), BF),
            pltpu.VMEM((ff, width), BF),
            pltpu.VMEM((chunks, rows, fc), BF),
            pltpu.VMEM((chunks, rows, 2 * fc), BF),
            pltpu.VMEM((3 * fc, rows), BF),
            pltpu.VMEM((2, 3 * fc, dz), BF),
            pltpu.VMEM((stage, 3 * fc, dz), BF),
            pltpu.VMEM((2, 256, width), BF),
            pltpu.VMEM((3 * fc, d_own), F32),
            pltpu.VMEM((3 * fc, d_own), BF),
            dma((moves,)),
            dma((moves,)),
            dma((chunks, 3)),
            dma((chunks, 3)),
            dma((chunks, 3)),
            dma((chunks, 2, shards - 1, 2)),
            dma((chunks, 2, shards - 1, 2)),
            dma((2,)),
            dma((stage,)),
            dma((chunks, 2, shards)),
            dma((chunks, 2, shards)),
            dma((chunks,)),
            dma((chunks,)),
            dma((2,)),
            dma((3,)),
        ],
        compiler_params=pltpu.CompilerParams(
            collective_id=1, has_side_effects=True, vmem_limit_bytes=63 * 1024 * 1024
        ),
        cost_estimate=pl.CostEstimate(
            flops=18 * rows * width * ff, bytes_accessed=100 * 1024 * 1024, transcendentals=rows * ff
        ),
        name="feed_forward",
    )(n_own, cot, wg, wu, wd)


def per_device(
    shards, ctx, tensor, tokens, cotangent, seq_len, block_slot, attn_gain, w_query, w_key, w_value, w_out, mlp_gain, w_gate, w_up, w_down
):
    group = ctx * tensor
    my_x = lax.axis_index("ctx")
    my_t = lax.axis_index("tensor")
    my_z = lax.axis_index("shard")
    me = my_x * tensor + my_t
    width = tokens.shape[1]
    own_rows = tokens.shape[0] // tensor
    level_rows = own_rows * group
    slots_each = own_rows // BLK
    d_own = w_query.shape[0]
    cols = w_query.shape[1] // ctx
    ff = w_gate.shape[1] // ctx
    rel = jnp.arange(group, dtype=jnp.int32)
    swap_x = [(i, i ^ 1) for i in range(ctx)]

    slot = block_slot[0]
    place = ((slot // slots_each) ^ me) * slots_each + slot % slots_each
    slots = jnp.concatenate([place, seq_len]).astype(jnp.int32)

    def level_rows_of(array):
        local = jnp.take(array.reshape(tensor, own_rows, width), my_t ^ jnp.arange(tensor), axis=0)
        blocks = [local[k] for k in range(tensor)]
        half = own_rows // 2
        have = [(0, blocks[0])]
        got = swap(blocks[0], group, tensor)
        far = {tensor: got}
        bit = tensor // 2
        while bit >= 1:
            keys = sorted(far)
            sent = jnp.concatenate([far[k] for k in keys], axis=0) if len(keys) > 1 else far[keys[0]]
            got = swap(sent, group, bit)
            for i, k in enumerate(keys):
                far[k | bit] = got[i * own_rows : (i + 1) * own_rows]
            bit //= 2
        return jnp.concatenate([local.reshape(tensor * own_rows, width)] + [far[tensor + k] for k in range(tensor)], axis=0), blocks[0]

    def x_halves(array, axis):
        size = array.shape[axis] // ctx
        mine = lax.dynamic_slice_in_dim(array, my_x * size, size, axis=axis)
        other = lax.dynamic_slice_in_dim(array, (1 - my_x) * size, size, axis=axis)
        return mine, other

    def x_join(mine, got, axis):
        return jnp.where(
            my_x == 0, jnp.concatenate([mine, got], axis=axis), jnp.concatenate([got, mine], axis=axis)
        )

    gains = jnp.stack([attn_gain, mlp_gain], axis=0)
    gains = x_join(gains, lax.ppermute(gains, "ctx", swap_x), 1)
    gains = in_order(chain_gather(gains, shards), shards)
    gains = jnp.transpose(gains, (1, 0, 2)).reshape(2, width).astype(F32)
    gain_one, gain_two = gains[0:1], gains[1:2]

    halves = [x_halves(w, 1) for w in (w_query, w_key, w_value)]
    mine = jnp.concatenate([a for a, _ in halves], axis=1)
    got = lax.ppermute(jnp.concatenate([b for _, b in halves], axis=1), "ctx", swap_x)
    w_qkv = in_order(chain_gather(x_join(mine, got, 0), shards), shards).reshape(width, 3 * cols)

    tok, tok_own = level_rows_of(tokens)

    angle_at = jnp.arange(level_rows, dtype=F32)
    lane = jnp.arange(128)
    freqs = THETA ** (-(lane % (HDIM // 2)).astype(F32) / (HDIM // 2))
    angles = angle_at[:, None] * freqs[None, :]
    cos = jnp.cos(angles)
    sin = jnp.sin(angles) * jnp.where(lane % HDIM < HDIM // 2, -1.0, 1.0)
    n_one, lin = qkv_call(tok, gain_one, w_qkv)
    o_slot, qs, ks, vs, os, stats = attend_call(slots, lin, cos, sin)

    head_order = jnp.arange(group)
    head_owner = (head_order % ctx) * tensor + head_order // ctx
    got = level_exchange([o_slot[k * own_rows : (k + 1) * own_rows] for k in range(group)], group)
    attn_rows = jnp.take(jnp.stack(got, axis=0), head_owner ^ me, axis=0)
    attn_rows = jnp.transpose(attn_rows, (1, 0, 2)).reshape(own_rows, width)

    pieces = jnp.stack(chain_gather(w_out, shards), axis=0)
    every = jnp.stack(level_gather(pieces, ctx, tensor, axis=1), axis=0)
    every = jnp.take(every, rel ^ me, axis=0)
    every = jnp.take(every, (my_z - jnp.arange(shards)) % shards, axis=1)
    every = every.reshape(ctx, tensor, shards, w_out.shape[0], d_own)
    w_out_all = jnp.transpose(every, (1, 3, 2, 0, 4)).reshape(width, width)

    x_own = tok_own.astype(F32)
    hidden_res = x_own + mm(attn_rows, w_out_all)
    scale_two = lax.rsqrt(jnp.mean(hidden_res * hidden_res, axis=-1, keepdims=True) + EPS)
    normed_two = hidden_res * scale_two
    n_two_own = (normed_two * gain_two).astype(BF)
    cot, cot_own = level_rows_of(cotangent)
    dn_part, out_part, ff_mine, ff_got, _, _ = mlp_call(shards, ctx, tensor, n_two_own, cot, w_gate, w_up, w_down)

    def row_blocks(array):
        return [array[k * own_rows : (k + 1) * own_rows] for k in range(group)]

    d_n_two = level_sum(row_blocks(dn_part), ctx, tensor)
    out_own = hidden_res + level_sum(row_blocks(out_part), ctx, tensor)

    def tensor_rows(own):
        have = [(0, own)]
        bit = tensor // 2
        while bit >= 1:
            sent = jnp.concatenate([v for _, v in have], axis=0) if len(have) > 1 else have[0][1]
            got = swap(sent, group, bit)
            have = have + [(k | bit, got[i * own_rows : (i + 1) * own_rows]) for i, (k, _) in enumerate(have)]
            bit //= 2
        have = [v for _, v in sorted(have, key=lambda e: e[0])]
        ordered = jnp.take(jnp.stack(have, axis=0), my_t ^ jnp.arange(tensor), axis=0)
        return ordered.reshape(tensor * own_rows, width)

    result = tensor_rows(out_own.astype(BF))

    cot_f = cot_own.astype(F32)
    scaled = d_n_two * gain_two
    inner = jnp.mean(scaled * normed_two, axis=-1, keepdims=True)
    d_h = cot_f + scale_two * (scaled - normed_two * inner)
    gain_two_part = jnp.sum(d_n_two * normed_two, axis=0)
    d_h_low = d_h.astype(BF)
    d_attn = mm(d_h_low, w_out_all, NT).astype(BF)
    blocks = jnp.transpose(d_attn.reshape(own_rows, group, cols), (1, 0, 2))
    owner_rel = rel ^ me
    col_of = (owner_rel % tensor) * ctx + owner_rel // tensor
    blocks = jnp.take(blocks, col_of, axis=0)
    go = jnp.concatenate(level_exchange([blocks[k] for k in range(group)], group), axis=0)
    d_qkv = attend_back_call(slots, qs, ks, vs, os, stats, go, cos, sin)

    d_h_all = jnp.concatenate(level_gather(d_h_low, ctx, tensor), axis=0)
    grad_wo = mm(d_h_all, o_slot, TN).astype(BF)
    grad_wqkv = mm(n_one, d_qkv, TN).astype(BF)
    d_n_one = level_sum(row_blocks(mm(d_qkv, w_qkv, NT).astype(BF)), ctx, tensor)
    x_scale = lax.rsqrt(jnp.mean(x_own * x_own, axis=-1, keepdims=True) + EPS)
    x_normed = x_own * x_scale
    scaled = d_n_one * gain_one
    inner = jnp.mean(scaled * x_normed, axis=-1, keepdims=True)
    d_x = d_h + x_scale * (scaled - x_normed * inner)
    gain_one_part = jnp.sum(d_n_one * x_normed, axis=0)
    grad_x = tensor_rows(d_x.astype(BF))

    chunks = ff_mine.shape[0]
    fc = ff // chunks
    mine = ff_mine.reshape(chunks, 3, fc, d_own)
    got = ff_got.reshape(chunks, 3, fc, d_own).astype(F32)

    def spread(i):
        return x_join(mine[:, i].reshape(ff, d_own), got[:, i].reshape(ff, d_own), 0)

    grad_down = spread(0)
    grad_gate = spread(1).T
    grad_up = spread(2).T

    def attn_sums(array):
        total = chain_sum(array.reshape(shards, ctx * d_own, array.shape[1]), shards)
        mine, other = x_halves(total, 0)
        got = lax.ppermute(other.astype(BF), "ctx", swap_x).astype(F32)
        return mine, got

    mine, got = attn_sums(grad_wo)
    grad_out = x_join(mine, got, 1).T
    mine, got = attn_sums(grad_wqkv)
    grad_q = x_join(mine[:, :cols], got[:, :cols], 1)
    grad_k = x_join(mine[:, cols : 2 * cols], got[:, cols : 2 * cols], 1)
    grad_v = x_join(mine[:, 2 * cols :], got[:, 2 * cols :], 1)

    def gain_sum(part):
        total = lax.psum(part, ("shard", "ctx", "tensor"))
        return lax.dynamic_slice_in_dim(total, (my_z * ctx + my_x) * d_own, d_own)

    grad_gain_two = gain_sum(gain_two_part)
    grad_gain_one = gain_sum(gain_one_part)
    return (
        result,
        grad_x,
        grad_gain_one,
        grad_q,
        grad_k,
        grad_v,
        grad_out,
        grad_gain_two,
        grad_gate,
        grad_up,
        grad_down,
    )


def solution(mesh):
    rows = P(("shard", "ctx"), None)
    gain = P(("shard", "ctx"))
    into = P(("shard", "ctx"), "tensor")
    back = P("tensor", ("shard", "ctx"))
    sizes = mesh.shape
    return jax.shard_map(
        functools.partial(per_device, sizes["shard"], sizes["ctx"], sizes["tensor"]),
        mesh=mesh,
        in_specs=(rows, rows, P("shard"), P("shard", None), gain, into, into, into, back, gain, into, into, back),
        out_specs=(rows, rows, gain, into, into, into, back, gain, into, into, back),
        check_vma=False,
    )
```

```python
import functools

import jax
import jax.numpy as jnp
from jax import lax
from jax.experimental import pallas as pl
from jax.experimental.pallas import tpu as pltpu
from jax.sharding import PartitionSpec as P

HDIM = 64
BLK = 128
EPS = 1e-05
THETA = 130000.0
NEG = -1e30
LEVEL = ("ctx", "tensor")
BF = jnp.bfloat16
F32 = jnp.float32
QT = 512

NT = (((1,), (1,)), ((), ()))
TN = (((0,), (0,)), ((), ()))


def mm(left, right, dims=None):
    if dims is None:
        return jnp.dot(left, right, preferred_element_type=F32)
    return lax.dot_general(left, right, dims, preferred_element_type=F32)


def swap(value, group, bit):
    return lax.ppermute(value, LEVEL, [(i, i ^ bit) for i in range(group)])


def level_bits(ctx, tensor):
    bits_y = []
    bit = 2
    while bit < tensor:
        bits_y.append(bit)
        bit *= 2
    bits_x = []
    bit = tensor
    while bit < ctx * tensor:
        bits_x.append(bit)
        bit *= 2
    return bits_y, bits_x


def level_gather(block, ctx, tensor, axis=0):
    group = ctx * tensor
    bits_y, bits_x = level_bits(ctx, tensor)
    half = block.shape[axis] // 2
    whole = {0: block, 1: swap(block, group, 1)}
    parts = [lax.slice_in_dim(block, 0, half, axis=axis), lax.slice_in_dim(block, half, 2 * half, axis=axis)]
    found = [{0: parts[0]}, {0: parts[1]}]
    for which, order in enumerate((bits_x + bits_y, bits_y + bits_x)):
        have = [(0, parts[which])]
        for bit in order:
            sent = jnp.concatenate([v for _, v in have], axis=axis) if len(have) > 1 else have[0][1]
            got = swap(sent, group, bit)
            core = swap(got, group, 1)
            new = []
            for i, (k, _) in enumerate(have):
                piece = lax.slice_in_dim(got, i * half, (i + 1) * half, axis=axis)
                new.append((k | bit, piece))
                found[which][k | bit] = piece
                found[which][k | bit | 1] = lax.slice_in_dim(core, i * half, (i + 1) * half, axis=axis)
            have = have + new
    out = []
    for k in range(group):
        if k in whole:
            out.append(whole[k])
        else:
            out.append(jnp.concatenate([found[0][k], found[1][k]], axis=axis))
    return out


def plus(a, b):
    return (a.astype(F32) + b.astype(F32)).astype(BF)


def level_sum(blocks, ctx, tensor):
    group = ctx * tensor
    bits_y, bits_x = level_bits(ctx, tensor)
    rows = blocks[0].shape[0]
    half = rows // 2
    evens = list(range(0, group, 2))
    got = swap(jnp.concatenate([blocks[k | 1] for k in evens], axis=0), group, 1)
    chip = {k: plus(blocks[k], got[i * rows : (i + 1) * rows]) for i, k in enumerate(evens)}
    done = []
    for which, order in enumerate((bits_x + bits_y, bits_y + bits_x)):
        have = {k: v[which * half : (which + 1) * half] for k, v in chip.items()}
        for bit in order:
            leave = sorted(k for k in have if k & bit)
            got = swap(jnp.concatenate([have[k] for k in leave], axis=0), group, bit)
            for i, k in enumerate(leave):
                piece = got[i * half : (i + 1) * half]
                own = have[k ^ bit]
                have[k ^ bit] = plus(own, piece) if len(leave) > 1 else own.astype(F32) + piece.astype(F32)
                del have[k]
        done.append(have[0])
    return jnp.concatenate(done, axis=0)


def level_exchange(blocks, group):
    return [blocks[0]] + [swap(blocks[k], group, k) for k in range(1, group)]


def chain_gather(own, shards):
    here = lax.axis_index("shard")
    ups, downs = [], []
    up = down = own
    for k in range(1, shards):
        up = lax.ppermute(up, "shard", [(i, i + 1) for i in range(k - 1, shards - 1)])
        down = lax.ppermute(down, "shard", [(i, i - 1) for i in range(1, shards - k + 1)])
        ups.append(up)
        downs.append(down)
    rel = [own]
    for k in range(1, shards):
        rel.append(jnp.where(here >= k, ups[k - 1], downs[shards - k - 1]))
    return rel


def in_order(rel, shards):
    here = lax.axis_index("shard")
    order = (here - jnp.arange(shards)) % shards
    return jnp.take(jnp.stack(rel, axis=0), order, axis=0)


def chain_sum(terms, shards):
    here = lax.axis_index("shard")

    def term(index):
        return lax.dynamic_index_in_dim(terms, jnp.clip(index, 0, shards - 1), 0, keepdims=False)

    up = down = None
    for k in range(1, shards):
        send = term(here + shards - k)
        send = send if up is None else plus(send, up)
        up = lax.ppermute(send, "shard", [(i, i + 1) for i in range(0, k)])
        send = term(here - (shards - k))
        send = send if down is None else plus(send, down)
        down = lax.ppermute(send, "shard", [(i, i - 1) for i in range(shards - k, shards)])
    return term(here).astype(F32) + up.astype(F32) + down.astype(F32)


def turn(u, cos, sin):
    lane = lax.broadcasted_iota(jnp.int32, u.shape, 1)
    width = u.shape[1]
    ahead = pltpu.roll(u, width - HDIM // 2, axis=1)
    behind = pltpu.roll(u, HDIM // 2, axis=1)
    other = jnp.where(lane % HDIM < HDIM // 2, ahead, behind)
    return u * cos + other * sin


def wide(table, cols):
    reps = cols // table.shape[1]
    return jnp.concatenate([table] * reps, axis=1) if reps > 1 else table


def full_spec(shape):
    return pl.BlockSpec(shape, lambda *_: (0,) * len(shape))


def attend_back_kernel(slots, qs, ks, vs, os, stats, go_ref, cos_ref, sin_ref, out_ref, go, delta, dq):
    rows, cols = qs.shape
    heads = cols // HDIM

    def fill(b, carry):
        src = pl.ds(pl.multiple_of(slots[b] * BLK, BLK), BLK)
        dst = pl.ds(pl.multiple_of(b * BLK, BLK), BLK)
        go[dst, :] = go_ref[src, :]
        return carry

    lax.fori_loop(0, rows // BLK, fill, 0)
    pick = (
        lax.broadcasted_iota(jnp.int32, (8, cols), 0) == lax.broadcasted_iota(jnp.int32, (8, cols), 1) // HDIM
    ).astype(F32)
    for t in range(rows // QT):
        part = slice(t * QT, (t + 1) * QT)
        both = go[part, :].astype(F32) * os[part, :].astype(F32)
        delta[:, part] = lax.dot_general(
            pick, both, NT, precision=lax.Precision.HIGHEST, preferred_element_type=F32
        )
    dq[...] = jnp.zeros_like(dq)
    live = slots[rows // BLK]
    tiles = rows // QT

    def store(t, column, value, sign):
        cos = wide(cos_ref[t * QT : (t + 1) * QT, :], cols)
        sin = wide(sin_ref[t * QT : (t + 1) * QT, :], cols)
        done = (turn(value, cos, -sin) if sign else value).astype(BF)
        for i in range(QT // BLK):
            dst = pl.ds(pl.multiple_of(slots[t * (QT // BLK) + i] * BLK, BLK), BLK)
            out_ref[dst, column * cols : (column + 1) * cols] = done[i * BLK : (i + 1) * BLK, :]

    for t in range(tiles):
        begin = t * QT
        count = rows - begin
        lane_k = lax.broadcasted_iota(jnp.int32, (QT, cols), 1) // HDIM
        lane_q = lax.broadcasted_iota(jnp.int32, (count, cols), 1) // HDIM
        kpos = lax.broadcasted_iota(jnp.int32, (QT, QT), 0)
        qpos = lax.broadcasted_iota(jnp.int32, (QT, QT), 1)
        diag = jnp.where(kpos <= qpos, 0.0, NEG)
        dead = jnp.where(lax.broadcasted_iota(jnp.int32, (QT, 1), 0) + begin < live, 0.0, NEG)

        def head(h, carry):
            dk, dv = carry
            kt = ks[begin : begin + QT, :]
            qm = jnp.where(lane_q == h, qs[begin:, :] * BF(0.125), BF(0))
            gm = jnp.where(lane_q == h, go[begin:, :], BF(0))
            s = mm(kt, qm, NT) + dead
            first = s[:, :QT] + diag
            s = jnp.concatenate([first, s[:, QT:]], axis=1) if count > QT else first
            p = jnp.exp(s - stats[pl.ds(h, 1), begin:])
            dp = mm(vs[begin : begin + QT, :], gm, NT)
            ds = (p * (dp - delta[pl.ds(h, 1), begin:])).astype(BF)
            km = jnp.where(lane_k == h, kt * BF(0.125), BF(0))
            dq[begin:, :] += mm(ds, km, TN)
            return dk + mm(ds, qm), dv + mm(p.astype(BF), gm)

        zero = jnp.zeros((QT, cols), F32)
        dk, dv = lax.fori_loop(0, heads, head, (zero, zero))
        store(t, 1, dk, True)
        store(t, 2, dv, False)
    for t in range(tiles):
        store(t, 0, dq[t * QT : (t + 1) * QT, :], True)


def attend_back_call(slots, qs, ks, vs, os, stats, go, cos, sin):
    rows, cols = qs.shape
    heads = cols // HDIM
    return pl.pallas_call(
        attend_back_kernel,
        grid_spec=pltpu.PrefetchScalarGridSpec(
            num_scalar_prefetch=1,
            grid=(1,),
            in_specs=[full_spec(qs.shape)] * 4
            + [full_spec(stats.shape), full_spec(go.shape), full_spec(cos.shape), full_spec(sin.shape)],
            out_specs=full_spec((rows, 3 * cols)),
            scratch_shapes=[
                pltpu.VMEM((rows, cols), BF),
                pltpu.VMEM((8, rows), F32),
                pltpu.VMEM((rows, cols), F32),
            ],
        ),
        out_shape=jax.ShapeDtypeStruct((rows, 3 * cols), BF),
        compiler_params=pltpu.CompilerParams(vmem_limit_bytes=60 * 1024 * 1024),
        cost_estimate=pl.CostEstimate(
            flops=heads * rows * rows * HDIM * 20, bytes_accessed=rows * cols * 18, transcendentals=heads * rows * rows // 2
        ),
        name="attend_back",
    )(slots, qs, ks, vs, os, stats, go, cos, sin)


def flip(index, bit):
    return index + bit - 2 * bit * ((index // bit) % 2)


class Place:
    def __init__(self, shards, ctx, tensor):
        self.shards, self.ctx, self.tensor = shards, ctx, tensor
        self.group = ctx * tensor
        self.z = lax.axis_index("shard")
        self.x = lax.axis_index("ctx")
        self.t = lax.axis_index("tensor")
        self.bits_y, self.bits_x = level_bits(ctx, tensor)

    def peer(self, offset):
        t, x = self.t, self.x
        bit = 1
        while bit < self.group:
            if offset & bit:
                if bit < self.tensor:
                    t = flip(t, bit)
                else:
                    x = 1 - x
            bit *= 2
        return x, t

    def peer_id(self, offset):
        x, t = self.peer(offset)
        return (self.z, x, t)

    def above(self):
        return (self.z + 1, self.x, self.t)

    def below(self):
        return (self.z - 1, self.x, self.t)

    def meet(self, offsets, chain=True):
        barrier = pltpu.get_barrier_semaphore()
        z, shards = self.z, self.shards
        for k in offsets:
            pl.semaphore_signal(barrier, inc=1, device_id=self.peer_id(k), device_id_type=pl.DeviceIdType.MESH)
        peers = len(offsets)
        if chain:

            @pl.when(z < shards - 1)
            def _():
                pl.semaphore_signal(barrier, inc=1, device_id=self.above(), device_id_type=pl.DeviceIdType.MESH)

            @pl.when(z > 0)
            def _():
                pl.semaphore_signal(barrier, inc=1, device_id=self.below(), device_id_type=pl.DeviceIdType.MESH)

            peers = peers + (z + shards - 1) // shards + (2 * shards - 2 - z) // shards
        pl.semaphore_wait(barrier, peers)


class Move:
    def __init__(self, out, due, goes, comes):
        self.out, self.due, self.goes, self.comes = out, due, goes, comes

    def _run(self, cond, fn):
        if cond is None:
            fn()
        else:
            pl.when(cond)(fn)

    def start(self):
        self._run(self.goes, self.out.start)

    def come(self):
        self._run(self.comes, self.due.wait_recv)

    def sent(self):
        self._run(self.goes, self.out.wait_send)


class Links:
    def __init__(self, place, send_sems, recv_sems):
        self.place, self.send_sems, self.recv_sems = place, send_sems, recv_sems
        self.moves = []

    def send(self, src, dst, where, land=None, goes=None, comes=None, start=True):
        i = len(self.moves)
        land = dst if land is None else land
        safe = self.place.peer_id(1)

        def copy(a, b, w):
            return pltpu.make_async_remote_copy(
                src_ref=a,
                dst_ref=b,
                send_sem=self.send_sems.at[i],
                recv_sem=self.recv_sems.at[i],
                device_id=w,
                device_id_type=pl.DeviceIdType.MESH,
            )

        move = Move(copy(src, dst, where), copy(land, land, safe), goes, comes)
        self.moves.append(move)
        if start:
            move.start()
        return move

    def all_sent(self):
        for m in self.moves:
            m.sent()


    def chain(self, parts):
        p = self.place
        z, shards = p.z, p.shards
        due = []
        for k in range(1, shards):
            for m in due:
                m.come()
            due = []
            up = zip(parts(z - (k - 1)), parts(z - k))
            for src, land in up:
                due.append(self.send(src, src, p.above(), land, (z >= k - 1) & (z < shards - 1), z >= k))
            down = zip(parts(z + (k - 1)), parts(z + k))
            for src, land in down:
                due.append(
                    self.send(src, src, p.below(), land, (z + k - 1 <= shards - 1) & (z > 0), z + k <= shards - 1)
                )
            yield
        for m in due:
            m.come()

    def spread(self, part, absolute=False):
        p = self.place

        def put(k, bit, h):
            return self.send(part(k, h), part(k if absolute else k | bit, h), p.peer_id(bit), part(k | bit, h))

        cores = [put(0, 1, None)]
        have = [[0], [0]]
        found = {}
        orders = [p.bits_x + p.bits_y, p.bits_y + p.bits_x]
        for stage in range(len(orders[0])):
            step = []
            for h in (0, 1):
                bit = orders[h][stage]
                step += [(k | bit, put(k, bit, h)) for k in have[h]]
                have[h] = have[h] + [k | bit for k in have[h]]
            yield
            for k, m in step:
                m.come()
                found[k] = found.get(k, 0) + 1
                if found[k] == 2:
                    cores.append(put(k, 1, None))
        yield
        for m in cores:
            m.come()

    def rows(self, source, keep, own_rows, log):
        p = self.place

        def slot(k):
            return keep.at[pl.ds(k * own_rows, own_rows), :]

        mine = source.at[pl.ds(pl.multiple_of(p.t * own_rows, own_rows), own_rows), :]
        first = self.send(mine, slot(p.tensor), p.peer_id(p.tensor))
        log.append(first)
        yield
        first.come()
        far = [p.tensor]
        for bit in p.bits_y:
            step = [self.send(slot(k), slot(k | bit), p.peer_id(bit)) for k in far]
            log += step
            yield
            for m in step:
                m.come()
            far = far + [k | bit for k in far]
        last = [self.send(slot(k), slot(k | 1), p.peer_id(1)) for k in far]
        log += last
        yield
        for m in last:
            m.come()


def drain(*gens):
    for g in gens:
        for _ in g:
            pass


def first_kernel(
    dims, place_s, at_s, live_s, tokens, cotangent, gains_in, wq, wk, wv, w_out, wg, wu, wd, cos_ref, sin_ref,
    n_one_out, w_qkv_out, w_o_out, cot_out, gu_out, d_out, n_own_out, h_out, gains, qs, ks, vs, os, stats, o_rel,
    n_one, w_qkv, w_o, qkv_rel, attn_rows, h_own, n_own, x_keep,
    send_sems, recv_sems, own_sems,
):
    shards, ctx, tensor, fc, own_rows, d_own = dims
    p = Place(shards, ctx, tensor)
    z, x, t = p.z, p.x, p.t
    group = p.group
    rows, width = n_one.shape
    cols = qs.shape[1]
    heads = cols // HDIM
    ff = wg.shape[1] // ctx
    dz = ctx * d_own
    links = Links(p, send_sems, recv_sems)
    own_count = [0]

    def own(src, dst):
        i = own_count[0]
        own_count[0] += 1
        c = pltpu.make_async_copy(src, dst, own_sems.at[i])
        c.start()
        return c

    p.meet(list(range(1, group)))

    def d_at(xx):
        return pl.ds(pl.multiple_of((z * ctx + xx) * d_own, d_own), d_own)

    def z_at(b):
        return pl.ds(pl.multiple_of(b * dz, dz), dz)

    def part_cols(xx, size):
        return pl.ds(pl.multiple_of(xx * size, size), size)

    across = p.peer_id(tensor)

    wo_rows = w_out.shape[0]

    def o_at(tt, xx, zz):
        return w_o.at[xx, pl.ds(pl.multiple_of(tt * wo_rows, wo_rows), wo_rows), pl.ds(pl.multiple_of(zz * d_own, d_own), d_own)]

    own_o = own(w_out, o_at(t, x, z))
    own_gain = own(gains_in, gains.at[:, d_at(x)])
    own_w = [own(w.at[:, part_cols(x, cols)], w_qkv.at[d_at(x), i * cols : (i + 1) * cols]) for i, w in enumerate((wq, wk, wv))]
    own_gain.wait()
    gain_x = links.send(gains.at[:, d_at(x)], gains.at[:, d_at(x)], across, gains.at[:, d_at(1 - x)])
    qkv_x = [
        links.send(
            w.at[:, part_cols(1 - x, cols)],
            w_qkv.at[d_at(x), i * cols : (i + 1) * cols],
            across,
            w_qkv.at[d_at(1 - x), i * cols : (i + 1) * cols],
        )
        for i, w in enumerate((wq, wk, wv))
    ]
    tok_log = []
    tok_rows = links.rows(tokens, n_one, own_rows, tok_log)
    next(tok_rows)
    own_tok = []
    for k in range(tensor):
        _, tt = p.peer(k)
        src = tokens.at[pl.ds(pl.multiple_of(tt * own_rows, own_rows), own_rows), :]
        own_tok.append(own(src, n_one.at[pl.ds(k * own_rows, own_rows), :]))
    own_o.wait()
    o_chain = links.chain(lambda b: [o_at(t, x, b)])
    next(o_chain)
    gain_x.come()
    gain_chain = links.chain(lambda b: [gains.at[:, z_at(b)]])
    next(gain_chain)
    next(o_chain, None)
    for c in own_w:
        c.wait()
    for m in qkv_x:
        m.come()
    next(gain_chain, None)
    qkv_chain = links.chain(lambda b: [w_qkv.at[z_at(b), :]])
    next(qkv_chain)

    gu_pairs = [(wg, 0), (wu, 1)]

    def gu_place(xx, i):
        return gu_out.at[d_at(xx), i * fc : (i + 1) * fc]

    ff_own = [own(w.at[:, pl.ds(pl.multiple_of(x * ff, fc), fc)], gu_place(x, i)) for w, i in gu_pairs]
    ff_own.append(own(wd.at[pl.ds(pl.multiple_of(x * ff, fc), fc), :], d_out.at[:, d_at(x)]))
    ff_x = [
        links.send(w.at[:, pl.ds(pl.multiple_of((1 - x) * ff, fc), fc)], gu_place(x, i), across, gu_place(1 - x, i))
        for w, i in gu_pairs
    ]
    ff_x.append(
        links.send(wd.at[pl.ds(pl.multiple_of((1 - x) * ff, fc), fc), :], d_out.at[:, d_at(x)], across, d_out.at[:, d_at(1 - x)])
    )
    drain(gain_chain)
    drain(o_chain)
    for c in own_tok:
        c.wait()
    x_keep[...] = n_one[0:own_rows, :]
    next(tok_rows, None)

    def o_part(k, h):
        xx, tt = p.peer(k)
        size = wo_rows if h is None else wo_rows // 2
        start = tt * wo_rows + (0 if h is None else h * size)
        return w_o.at[xx, pl.ds(pl.multiple_of(start, size), size), :]

    o_spread = links.spread(o_part, absolute=True)
    next(o_spread)

    def norm(r, carry):
        at = pl.ds(pl.multiple_of(r * own_rows, own_rows), own_rows)
        v = n_one[at, :].astype(F32)
        scale = lax.rsqrt(jnp.mean(v * v, axis=-1, keepdims=True) + EPS)
        n_one[at, :] = (v * scale * gains[0:1, :]).astype(BF)
        return carry

    next(qkv_chain, None)
    lax.fori_loop(0, tensor, norm, 0)
    for c in ff_own:
        c.wait()
    for m in ff_x:
        m.come()
    next(tok_rows, None)
    next(qkv_chain, None)
    ff_chain = links.chain(lambda b: [gu_out.at[z_at(b), :], d_out.at[:, z_at(b)]])
    next(ff_chain)
    drain(tok_rows)
    for m in tok_log:
        m.sent()
    lax.fori_loop(tensor, group, norm, 0)
    out_n = own(n_one, n_one_out)
    next(o_spread, None)
    drain(qkv_chain)
    next(ff_chain, None)
    out_w = own(w_qkv, w_qkv_out)

    def project(r, carry):
        at = pl.ds(pl.multiple_of(r * own_rows, own_rows), own_rows)
        lin = mm(n_one[at, :], w_qkv[...])
        per = own_rows // BLK
        for i in range(per):
            where = pl.ds(pl.multiple_of(r * own_rows + i * BLK, BLK), BLK)
            cos, sin = wide(cos_ref[where, :], cols), wide(sin_ref[where, :], cols)
            part = lin[i * BLK : (i + 1) * BLK, :]
            dst = pl.ds(pl.multiple_of(r * own_rows + i * BLK, BLK), BLK)
            qkv_rel[dst, 0:cols] = turn(part[:, 0:cols], cos, sin).astype(BF)
            qkv_rel[dst, cols : 2 * cols] = turn(part[:, cols : 2 * cols], cos, sin).astype(BF)
            qkv_rel[dst, 2 * cols : 3 * cols] = part[:, 2 * cols : 3 * cols].astype(BF)
        return carry

    lax.fori_loop(0, group, project, 0)
    next(o_spread, None)

    def fill(b, carry):
        dst = pl.ds(pl.multiple_of(b * BLK, BLK), BLK)
        found = picked(qkv_rel, place_s[b])
        qs[dst, :] = found[:, 0:cols]
        ks[dst, :] = found[:, cols : 2 * cols]
        vs[dst, :] = found[:, 2 * cols : 3 * cols]
        return carry

    lax.fori_loop(0, rows // BLK, fill, 0)
    cot_rows = links.rows(cotangent, cot_out, own_rows, [])
    next(cot_rows)
    own_cot = []
    for k in range(tensor):
        _, tt = p.peer(k)
        src = cotangent.at[pl.ds(pl.multiple_of(tt * own_rows, own_rows), own_rows), :]
        own_cot.append(own(src, cot_out.at[pl.ds(k * own_rows, own_rows), :]))
    live = live_s[0]
    for tile in range(rows // QT):
        attend_tile(tile, live, qs, ks, vs, os, stats)
        next(ff_chain, None)
        next(o_spread, None)
        next(cot_rows, None)

    def back_to_rows(j, carry):
        dst = pl.ds(pl.multiple_of(j * BLK, BLK), BLK)
        o_rel[dst, :] = picked(os, at_s[j])
        return carry

    lax.fori_loop(0, rows // BLK, back_to_rows, 0)

    def head_at(k):
        xx, tt = p.peer(k)
        return attn_rows.at[:, pl.ds(pl.multiple_of((tt * ctx + xx) * cols, cols), cols)]

    swaps = [
        links.send(o_rel.at[pl.ds(k * own_rows, own_rows), :], head_at(0), p.peer_id(k), head_at(k)) for k in range(1, group)
    ]
    own_heads = own(o_rel.at[pl.ds(0, own_rows), :], head_at(0))
    drain(o_spread)
    out_o = own(w_o, w_o_out)
    own_heads.wait()
    for m in swaps:
        m.come()
    for xx in range(ctx):
        span = shards * d_own
        mixed = mm(attn_rows[...], w_o[xx])
        for zz in range(shards):
            at = slice((zz * ctx + xx) * d_own, (zz * ctx + xx + 1) * d_own)
            h_own[:, at] = x_keep[:, at].astype(F32) + mixed[:, zz * d_own : (zz + 1) * d_own]
    h = h_own[...]
    scale = lax.rsqrt(jnp.mean(h * h, axis=-1, keepdims=True) + EPS)
    n_own[...] = (h * scale * gains[1:2, :]).astype(BF)
    out_h = own(h_own, h_out)
    out_own = own(n_own, n_own_out)
    drain(ff_chain)
    drain(cot_rows)
    for c in own_cot:
        c.wait()
    for m in links.moves:
        if m not in tok_log:
            m.sent()
    for c in (out_n, out_w, out_o, out_h, out_own):
        c.wait()


def picked(ref, block):
    found = ref[0:BLK, :]
    for j in range(1, ref.shape[0] // BLK):
        found = jnp.where(block == j, ref[j * BLK : (j + 1) * BLK, :], found)
    return found


def attend_tile(t, live, qs, ks, vs, os, stats):
    rows, cols = qs.shape
    heads = cols // HDIM
    ext = (t + 1) * QT
    lane = lax.broadcasted_iota(jnp.int32, (QT, cols), 1) // HDIM
    qpos = lax.broadcasted_iota(jnp.int32, (QT, QT), 0)
    kpos = lax.broadcasted_iota(jnp.int32, (QT, QT), 1)
    diag = jnp.where(kpos <= qpos, 0.0, NEG)
    dead = jnp.where(lax.broadcasted_iota(jnp.int32, (1, ext), 1) < live, 0.0, NEG)

    def head(h, acc):
        q = jnp.where(lane == h, qs[t * QT : ext, :] * BF(0.125), BF(0))
        s = mm(q, ks[0:ext, :], NT) + dead
        last = s[:, t * QT :] + diag
        s = jnp.concatenate([s[:, : t * QT], last], axis=1) if t else last
        top = jnp.max(s, axis=1, keepdims=True)
        e = jnp.exp(s - top)
        total = jnp.sum(e, axis=1, keepdims=True)
        mixed = mm(e.astype(BF), vs[0:ext, :]) / total
        note = jnp.broadcast_to(top + jnp.log(total), (QT, 128))
        stats[pl.ds(h, 1), t * QT : ext] = jnp.transpose(note)[0:1, :]
        return jnp.where(lane == h, mixed, acc)

    acc = lax.fori_loop(0, heads, head, jnp.zeros((QT, cols), F32))
    os[t * QT : ext, :] = acc.astype(BF)


def first_call(shards, ctx, tensor, place, at, live, tokens, cotangent, gains, wq, wk, wv, w_out, wg, wu, wd, cos, sin):
    width = tokens.shape[1]
    own_rows = tokens.shape[0] // tensor
    group = ctx * tensor
    rows = own_rows * group
    d_own = wq.shape[0]
    cols = wq.shape[1] // ctx
    fc = 256
    dims = (shards, ctx, tensor, fc, own_rows, d_own)
    any_spec = pl.BlockSpec(memory_space=pl.ANY)
    smem = pl.BlockSpec(memory_space=pltpu.SMEM)
    vmem = pl.BlockSpec(memory_space=pltpu.VMEM)
    piece = jax.ShapeDtypeStruct((rows, cols), BF)
    moves = 400
    dma = pltpu.SemaphoreType.DMA
    return pl.pallas_call(
        functools.partial(first_kernel, dims),
        in_specs=[smem] * 3 + [any_spec] * 10 + [vmem] * 2,
        out_specs=[any_spec] * 8 + [vmem] * 7,
        out_shape=[
            jax.ShapeDtypeStruct((rows, width), BF),
            jax.ShapeDtypeStruct((width, 3 * cols), BF),
            jax.ShapeDtypeStruct((ctx, width, shards * d_own), BF),
            jax.ShapeDtypeStruct((rows, width), BF),
            jax.ShapeDtypeStruct((width, 2 * fc), BF),
            jax.ShapeDtypeStruct((fc, width), BF),
            jax.ShapeDtypeStruct((own_rows, width), BF),
            jax.ShapeDtypeStruct((own_rows, width), F32),
            jax.ShapeDtypeStruct((8, width), F32),
            piece,
            piece,
            piece,
            piece,
            jax.ShapeDtypeStruct((8, rows), F32),
            piece,
        ],
        scratch_shapes=[
            pltpu.VMEM((rows, width), BF),
            pltpu.VMEM((width, 3 * cols), BF),
            pltpu.VMEM((ctx, width, shards * d_own), BF),
            pltpu.VMEM((rows, 3 * cols), BF),
            pltpu.VMEM((own_rows, width), BF),
            pltpu.VMEM((own_rows, width), F32),
            pltpu.VMEM((own_rows, width), BF),
            pltpu.VMEM((own_rows, width), BF),
            dma((moves,)),
            dma((moves,)),
            dma((40,)),
        ],
        compiler_params=pltpu.CompilerParams(
            collective_id=0, has_side_effects=True, vmem_limit_bytes=62 * 1024 * 1024
        ),
        cost_estimate=pl.CostEstimate(
            flops=2 * rows * width * cols * 4, bytes_accessed=64 * 1024 * 1024, transcendentals=rows * rows * cols // HDIM
        ),
        name="first",
    )(place, at, live, tokens, cotangent, gains, wq, wk, wv, w_out, wg, wu, wd, cos, sin)


def mlp_kernel(
    dims, n_own, cot_in, wg, wu, wd, gu_pre, d_pre,
    dn_out, out_out, mine_out, got_out, g_hbm, r_hbm,
    n2, cot, wgu_v, wd_v, hid, dgu, left_t, gt, st, ost, fin, away,
    lev_send, lev_recv, x_own, x_send, x_recv, a_send, a_recv, g_sem, s_sem, rs_send, rs_recv, fx_send, fx_recv, o_sem, c_sem,
):
    shards, ctx, tensor, chunks, fc, rows_own, d_own = dims
    group = ctx * tensor
    rows, width = n2.shape
    dz = ctx * d_own
    ff = chunks * fc
    z = lax.axis_index("shard")
    x = lax.axis_index("ctx")
    t = lax.axis_index("tensor")
    bits_y, bits_x = level_bits(ctx, tensor)

    p = Place(shards, ctx, tensor)
    above, below = p.above, p.below
    p.meet([1] + bits_y + bits_x)

    here_too = (z, x, flip(t, 1))

    def remote(src, dst, send, recv, where):
        return pltpu.make_async_remote_copy(
            src_ref=src, dst_ref=dst, send_sem=send, recv_sem=recv, device_id=where, device_id_type=pl.DeviceIdType.MESH
        )

    def x_copies(c, own):
        half = x if own else 1 - x
        low_c = pl.multiple_of(half * ff + c * fc, fc)
        d_at = pl.ds(pl.multiple_of((z * ctx + x) * d_own, d_own), d_own)
        pairs = [
            (wg.at[:, pl.ds(low_c, fc)], wgu_v.at[c, d_at, pl.ds(0, fc)]),
            (wu.at[:, pl.ds(low_c, fc)], wgu_v.at[c, d_at, pl.ds(fc, fc)]),
            (wd.at[pl.ds(low_c, fc), :], wd_v.at[pl.ds(pl.multiple_of(c * fc, fc), fc), d_at]),
        ]
        if own:
            return [pltpu.make_async_copy(a, b, x_own.at[c, i]) for i, (a, b) in enumerate(pairs)]
        return [remote(a, b, x_send.at[c, i], x_recv.at[c, i], (z, 1 - x, t)) for i, (a, b) in enumerate(pairs)]

    def x_landed(c):
        d_at = pl.ds(pl.multiple_of((z * ctx + 1 - x) * d_own, d_own), d_own)
        lands = [
            wgu_v.at[c, d_at, pl.ds(0, fc)],
            wgu_v.at[c, d_at, pl.ds(fc, fc)],
            wd_v.at[pl.ds(pl.multiple_of(c * fc, fc), fc), d_at],
        ]
        return [remote(a, a, x_send.at[c, i], x_recv.at[c, i], here_too) for i, a in enumerate(lands)]

    def hop(c, way, k, b, wait=False):
        at = pl.ds(pl.multiple_of(b * dz, dz), dz)
        parts = [wgu_v.at[c, at, :], wd_v.at[pl.ds(pl.multiple_of(c * fc, fc), fc), at]]
        where = here_too if wait else above() if way == 0 else below()
        return [remote(p, p, a_send.at[c, way, k, i], a_recv.at[c, way, k, i], where) for i, p in enumerate(parts)]

    def hop_start(c, k):
        @pl.when((z >= k - 1) & (z < shards - 1))
        def _():
            for d in hop(c, 0, k - 1, z - (k - 1)):
                d.start()

        @pl.when((z + k - 1 <= shards - 1) & (z > 0))
        def _():
            for d in hop(c, 1, k - 1, z + (k - 1)):
                d.start()

    def hop_sent(c, k):
        @pl.when((z >= k - 1) & (z < shards - 1))
        def _():
            for d in hop(c, 0, k - 1, z - (k - 1)):
                d.wait_send()

        @pl.when((z + k - 1 <= shards - 1) & (z > 0))
        def _():
            for d in hop(c, 1, k - 1, z + (k - 1)):
                d.wait_send()

    def hop_wait(c, k):
        @pl.when(z >= k)
        def _():
            for d in hop(c, 0, k - 1, z - k, True):
                d.wait_recv()

        @pl.when(z + k <= shards - 1)
        def _():
            for d in hop(c, 1, k - 1, z + k, True):
                d.wait_recv()

    def x_start(c):
        for d in x_copies(c, False):
            d.start()
        for d in x_copies(c, True):
            d.start()

    x_start(1)
    pre_copies = [
        pltpu.make_async_copy(gu_pre, wgu_v.at[0], x_own.at[0, 0]),
        pltpu.make_async_copy(d_pre, wd_v.at[pl.ds(0, fc), :], x_own.at[0, 1]),
    ]
    for d in pre_copies:
        d.start()

    half = rows_own // 2
    links = Links(p, lev_send, lev_recv)
    cot_copy = pltpu.make_async_copy(cot_in, cot, c_sem.at[0])
    own_copy = pltpu.make_async_copy(n_own, n2.at[pl.ds(0, rows_own), :], c_sem.at[1])
    own_copy.start()
    own_copy.wait()

    def n_part(k, h):
        if h is None:
            return n2.at[pl.ds(k * rows_own, rows_own), :]
        return n2.at[pl.ds(k * rows_own + h * half, half), :]

    n_rows = links.spread(n_part)
    next(n_rows)
    cot_copy.start()
    for c in range(2, chunks):
        x_start(c)
    for d in x_copies(1, True):
        d.wait()
    for d in x_landed(1):
        d.wait_recv()
    hop_start(1, 1)
    next(n_rows)

    def ag_round(r, top):
        for k in range(shards - 1, 0, -1):
            if k > top:
                continue
            c = r - k + 1

            @pl.when((c >= 1) & (c < chunks))
            def _(c=c, k=k):
                if k == 1:
                    for d in x_copies(c, True):
                        d.wait()
                    for d in x_landed(c):
                        d.wait_recv()
                else:
                    hop_wait(c, k - 1)
                hop_start(c, k)

    for r in range(2, shards - 1):
        ag_round(jnp.int32(r), shards - 1)
    drain(n_rows)
    cot_copy.wait()
    for d in pre_copies:
        d.wait()

    def block_of(i):
        down = shards - 1 - i
        down = down - jnp.where(down <= z, 1, 0)
        up = i + jnp.where(i >= z, 1, 0)
        return jnp.where(i == shards - 1, z, jnp.where(2 * z < shards, down, up))

    def g_copy(c, d, slot):
        return pltpu.make_async_copy(gt.at[slot], g_hbm.at[c, d], g_sem.at[slot])

    def rs_send_copy(src, c, way, d, wait=False):
        where = here_too if wait else above() if way == 0 else below()
        return remote(src, r_hbm.at[c, way, d], rs_send.at[c, way, d], rs_recv.at[c, way, d], where)

    combos = [(way, k) for k in range(2, shards) for way in (0, 1)]

    def target(way, k):
        return z + shards - k if way == 0 else z - (shards - k)

    def sends(way, k):
        if way == 0:
            return z < k
        return z >= shards - k

    def starts(way):
        return z == 0 if way == 0 else z == shards - 1

    def runs(way):
        return z != 0 if way == 0 else z != shards - 1

    def rs_step(s):
        for way in (0, 1):
            for k in range(1, shards):
                c = s - (k - 1)

                @pl.when((c >= 0) & (c < chunks) & starts(way))
                def _(c=c, way=way, k=k):
                    d = target(way, k)
                    rs_send_copy(g_hbm.at[c, d], c, way, d).start()

        for i, (way, k) in enumerate(combos):
            c = s - (k - 1)

            @pl.when((c >= 0) & (c < chunks) & sends(way, k) & runs(way))
            def _(c=c, way=way, k=k, i=i):
                d = target(way, k)

                @pl.when(c >= 1)
                def _():
                    rs_send_copy(st.at[2 * i], c - 1, way, d).wait_send()

                rs_send_copy(st.at[2 * i], c, way, d, True).wait_recv()
                pltpu.make_async_copy(g_hbm.at[c, d], st.at[2 * i], s_sem.at[2 * i]).start()
                pltpu.make_async_copy(r_hbm.at[c, way, d], st.at[2 * i + 1], s_sem.at[2 * i + 1]).start()

        last = 2 * len(combos)
        c_fin = s - (shards - 1)

        @pl.when((c_fin >= 0) & (c_fin < chunks))
        def _():
            pltpu.make_async_copy(g_hbm.at[c_fin, z], st.at[last], s_sem.at[last]).start()
            for way in (0, 1):
                slot = last + 1 + way

                @pl.when(runs(way))
                def _(way=way, slot=slot):
                    rs_send_copy(st.at[slot], c_fin, way, z, True).wait_recv()
                    pltpu.make_async_copy(r_hbm.at[c_fin, way, z], st.at[slot], s_sem.at[slot]).start()

                @pl.when(starts(way))
                def _(slot=slot):
                    st[slot] = jnp.zeros(st.shape[1:], BF)

        for i, (way, k) in enumerate(combos):
            c = s - (k - 1)

            @pl.when((c >= 0) & (c < chunks) & sends(way, k) & runs(way))
            def _(c=c, way=way, k=k, i=i):
                d = target(way, k)
                pltpu.make_async_copy(g_hbm.at[c, d], st.at[2 * i], s_sem.at[2 * i]).wait()
                pltpu.make_async_copy(r_hbm.at[c, way, d], st.at[2 * i + 1], s_sem.at[2 * i + 1]).wait()
                st[2 * i] = (st[2 * i].astype(F32) + st[2 * i + 1].astype(F32)).astype(BF)
                rs_send_copy(st.at[2 * i], c, way, d).start()

        @pl.when((c_fin >= 0) & (c_fin < chunks))
        def _():
            pltpu.make_async_copy(g_hbm.at[c_fin, z], st.at[last], s_sem.at[last]).wait()
            for way in (0, 1):
                slot = last + 1 + way

                @pl.when(runs(way))
                def _(way=way, slot=slot):
                    pltpu.make_async_copy(r_hbm.at[c_fin, way, z], st.at[slot], s_sem.at[slot]).wait()

            @pl.when(c_fin >= 1)
            def _():
                pltpu.make_async_copy(fin, mine_out.at[c_fin - 1], c_sem.at[2]).wait()
                fin_copy(c_fin - 1).wait_send()

            total = st[last].astype(F32) + st[last + 1].astype(F32) + st[last + 2].astype(F32)
            low, high = total[:, :d_own], total[:, d_own:]
            fin[...] = jnp.where(x == 0, low, high)
            away[...] = jnp.where(x == 0, high, low).astype(BF)
            pltpu.make_async_copy(fin, mine_out.at[c_fin], c_sem.at[2]).start()
            fin_copy(c_fin).start()

    def fin_copy(c):
        return remote(away, got_out.at[c], fx_send.at[c], fx_recv.at[c], (z, 1 - x, t))

    tile = 512

    def phase_one(c):
        def body(r, carry):
            at = pl.ds(pl.multiple_of(r * tile, tile), tile)
            gu = mm(n2[at, :], wgu_v[c])
            dh = mm(cot[at, :], wd_v[pl.ds(pl.multiple_of(c * fc, fc), fc), :], NT)
            gate, up = gu[:, :fc], gu[:, fc:]
            sig = 1.0 / (1.0 + jnp.exp(-gate))
            act = gate * sig
            h = (act * up).astype(BF)
            dg = (dh * up * sig * (1.0 + gate * (1.0 - sig))).astype(BF)
            du = (dh * act).astype(BF)
            hid[c, at, :] = h
            dgu[c, at, 0:fc] = dg
            dgu[c, at, fc : 2 * fc] = du
            left_t[0:fc, at] = h.T
            left_t[fc : 2 * fc, at] = dg.T
            left_t[2 * fc : 3 * fc, at] = du.T
            return carry

        lax.fori_loop(0, rows // tile, body, 0)

    def phase_two(c):
        def body(i, carry):
            d = block_of(i)
            slot = i % 2
            at = pl.ds(pl.multiple_of(d * dz, dz), dz)

            @pl.when(i >= 2)
            def _():
                g_copy(c, block_of(i - 2), slot).wait()

            gt[slot, 0:fc, :] = mm(left_t[0:fc, :], cot[:, at]).astype(BF)
            gt[slot, fc : 3 * fc, :] = mm(left_t[fc : 3 * fc, :], n2[:, at]).astype(BF)
            g_copy(c, d, slot).start()
            return carry

        lax.fori_loop(0, shards, body, 0)
        for i in (shards - 2, shards - 1):
            g_copy(c, block_of(jnp.int32(i)), i % 2).wait()

    ot = 256
    units = rows // ot

    def tail_unit(u):
        at = pl.ds(pl.multiple_of((u % units) * ot, ot), ot)
        slot = u % 2

        @pl.when(u >= 2)
        def _():
            pltpu.make_async_copy(ost.at[slot], dn_out.at[at, :], o_sem.at[slot]).wait()

        @pl.when(u < units)
        def _():
            for n in range(width // 512):
                cols = slice(n * 512, (n + 1) * 512)
                acc = jnp.zeros((ot, 512), F32)
                for c in range(chunks):
                    acc = acc + mm(dgu[c, at, :], wgu_v[c, cols, :], NT)
                ost[slot, :, cols] = acc.astype(BF)
            pltpu.make_async_copy(ost.at[slot], dn_out.at[at, :], o_sem.at[slot]).start()

        @pl.when(u >= units)
        def _():
            for n in range(width // 512):
                cols = slice(n * 512, (n + 1) * 512)
                acc = jnp.zeros((ot, 512), F32)
                for c in range(chunks):
                    acc = acc + mm(hid[c, at, :], wd_v[c * fc : (c + 1) * fc, cols])
                ost[slot, :, cols] = acc.astype(BF)
            pltpu.make_async_copy(ost.at[slot], out_out.at[at, :], o_sem.at[slot]).start()

    tail_slots = shards - 1
    per_slot = -(-2 * units // tail_slots)

    def slot_body(s, carry):
        @pl.when(s < chunks)
        def _():
            @pl.when(s >= 1)
            def _():
                hop_wait(s, shards - 1)

            phase_one(s)
            ag_round(s + shards - 1, shards - 1)
            phase_two(s)

        @pl.when(s >= chunks)
        def _():
            first_u = (s - chunks) * per_slot
            last_u = jnp.minimum(first_u + per_slot, 2 * units)

            def body(u, carry):
                tail_unit(u)
                return carry

            lax.fori_loop(first_u, last_u, body, 0)

        rs_step(s)
        return carry

    lax.fori_loop(0, chunks + tail_slots, slot_body, 0)

    for u in (2 * units - 2, 2 * units - 1):
        at = pl.ds((u % units) * ot, ot)
        pltpu.make_async_copy(ost.at[u % 2], out_out.at[at, :], o_sem.at[u % 2]).wait()
    links.all_sent()
    for c in range(1, chunks):
        for d in x_copies(c, False):
            d.wait_send()
        for k in range(1, shards):
            hop_sent(c, k)
    for way in (0, 1):
        for k in range(1, shards):

            @pl.when(starts(way))
            def _(way=way, k=k):
                d = target(way, k)
                for c in range(chunks):
                    rs_send_copy(g_hbm.at[c, d], c, way, d).wait_send()

    for i, (way, k) in enumerate(combos):

        @pl.when(sends(way, k) & runs(way))
        def _(way=way, k=k, i=i):
            rs_send_copy(st.at[2 * i], chunks - 1, way, target(way, k)).wait_send()

    pltpu.make_async_copy(fin, mine_out.at[chunks - 1], c_sem.at[2]).wait()
    fin_copy(chunks - 1).wait_send()
    for c in range(chunks):
        fin_copy(c).wait_recv()


def mlp_call(shards, ctx, tensor, n_own, cot, wg, wu, wd, gu_pre, d_pre):
    rows_own, width = n_own.shape
    group = ctx * tensor
    rows = rows_own * group
    d_own = wg.shape[0]
    ff = wg.shape[1] // ctx
    fc = 256
    chunks = ff // fc
    dz = ctx * d_own
    any_spec = pl.BlockSpec(memory_space=pl.ANY)
    bits_y, bits_x = level_bits(ctx, tensor)
    halves = 2 ** (len(bits_y) + len(bits_x)) - 1
    moves = 2 * halves + halves + 1
    stage = 4 * (shards - 2) + 3
    dims = (shards, ctx, tensor, chunks, fc, rows_own, d_own)
    dma = pltpu.SemaphoreType.DMA
    return pl.pallas_call(
        functools.partial(mlp_kernel, dims),
        in_specs=[any_spec] * 7,
        out_specs=[any_spec] * 6,
        out_shape=[
            jax.ShapeDtypeStruct((rows, width), BF),
            jax.ShapeDtypeStruct((rows, width), BF),
            jax.ShapeDtypeStruct((chunks, 3 * fc, d_own), F32),
            jax.ShapeDtypeStruct((chunks, 3 * fc, d_own), BF),
            jax.ShapeDtypeStruct((chunks, shards, 3 * fc, dz), BF),
            jax.ShapeDtypeStruct((chunks, 2, shards, 3 * fc, dz), BF),
        ],
        scratch_shapes=[
            pltpu.VMEM((rows, width), BF),
            pltpu.VMEM((rows, width), BF),
            pltpu.VMEM((chunks, width, 2 * fc), BF),
            pltpu.VMEM((ff, width), BF),
            pltpu.VMEM((chunks, rows, fc), BF),
            pltpu.VMEM((chunks, rows, 2 * fc), BF),
            pltpu.VMEM((3 * fc, rows), BF),
            pltpu.VMEM((2, 3 * fc, dz), BF),
            pltpu.VMEM((stage, 3 * fc, dz), BF),
            pltpu.VMEM((2, 256, width), BF),
            pltpu.VMEM((3 * fc, d_own), F32),
            pltpu.VMEM((3 * fc, d_own), BF),
            dma((moves,)),
            dma((moves,)),
            dma((chunks, 3)),
            dma((chunks, 3)),
            dma((chunks, 3)),
            dma((chunks, 2, shards - 1, 2)),
            dma((chunks, 2, shards - 1, 2)),
            dma((2,)),
            dma((stage,)),
            dma((chunks, 2, shards)),
            dma((chunks, 2, shards)),
            dma((chunks,)),
            dma((chunks,)),
            dma((2,)),
            dma((3,)),
        ],
        compiler_params=pltpu.CompilerParams(
            collective_id=1, has_side_effects=True, vmem_limit_bytes=63 * 1024 * 1024
        ),
        cost_estimate=pl.CostEstimate(
            flops=18 * rows * width * ff, bytes_accessed=100 * 1024 * 1024, transcendentals=rows * ff
        ),
        name="feed_forward",
    )(n_own, cot, wg, wu, wd, gu_pre, d_pre)


def per_device(
    shards, ctx, tensor, tokens, cotangent, seq_len, block_slot, attn_gain, w_query, w_key, w_value, w_out, mlp_gain, w_gate, w_up, w_down
):
    group = ctx * tensor
    my_x = lax.axis_index("ctx")
    my_t = lax.axis_index("tensor")
    my_z = lax.axis_index("shard")
    me = my_x * tensor + my_t
    width = tokens.shape[1]
    own_rows = tokens.shape[0] // tensor
    level_rows = own_rows * group
    slots_each = own_rows // BLK
    d_own = w_query.shape[0]
    cols = w_query.shape[1] // ctx
    ff = w_gate.shape[1] // ctx
    rel = jnp.arange(group, dtype=jnp.int32)
    swap_x = [(i, i ^ 1) for i in range(ctx)]

    slot = block_slot[0]
    place = ((slot // slots_each) ^ me) * slots_each + slot % slots_each
    order = jnp.arange(slot.shape[0], dtype=jnp.int32)
    at = jnp.sum(jnp.where(place[:, None] == order[None, :], order[:, None], 0), axis=0).astype(jnp.int32)
    slots = jnp.concatenate([place, seq_len]).astype(jnp.int32)

    def x_halves(array, axis):
        size = array.shape[axis] // ctx
        mine = lax.dynamic_slice_in_dim(array, my_x * size, size, axis=axis)
        other = lax.dynamic_slice_in_dim(array, (1 - my_x) * size, size, axis=axis)
        return mine, other

    def x_join(mine, got, axis):
        return jnp.where(
            my_x == 0, jnp.concatenate([mine, got], axis=axis), jnp.concatenate([got, mine], axis=axis)
        )

    angle_at = jnp.arange(level_rows, dtype=F32)
    lane = jnp.arange(128)
    freqs = THETA ** (-(lane % (HDIM // 2)).astype(F32) / (HDIM // 2))
    angles = angle_at[:, None] * freqs[None, :]
    cos = jnp.cos(angles)
    sin = jnp.sin(angles) * jnp.where(lane % HDIM < HDIM // 2, -1.0, 1.0)
    at_pos = (at[:, None] * BLK + jnp.arange(BLK)[None, :]).reshape(-1).astype(F32)
    angles = at_pos[:, None] * freqs[None, :]
    cos_rel = jnp.cos(angles)
    sin_rel = jnp.sin(angles) * jnp.where(lane % HDIM < HDIM // 2, -1.0, 1.0)
    gains = jnp.concatenate([jnp.stack([attn_gain, mlp_gain], axis=0).astype(F32), jnp.zeros((6, d_own), F32)], axis=0)
    n_one, w_qkv, w_o, cot, gu_pre, d_pre, n_two_own, hidden_res, gains, qs, ks, vs, os, stats, o_slot = first_call(
        shards, ctx, tensor, place.astype(jnp.int32), at, seq_len, tokens, cotangent, gains,
        w_query, w_key, w_value, w_out, w_gate, w_up, w_down, cos_rel, sin_rel,
    )
    gain_one, gain_two = gains[0:1], gains[1:2]

    def own_block(array):
        return lax.dynamic_slice_in_dim(array, my_t * own_rows, own_rows)

    x_own = own_block(tokens).astype(F32)
    cot_own = own_block(cotangent)
    scale_two = lax.rsqrt(jnp.mean(hidden_res * hidden_res, axis=-1, keepdims=True) + EPS)
    normed_two = hidden_res * scale_two
    dn_part, out_part, ff_mine, ff_got, _, _ = mlp_call(
        shards, ctx, tensor, n_two_own, cot, w_gate, w_up, w_down, gu_pre, d_pre
    )

    def row_blocks(array):
        return [array[k * own_rows : (k + 1) * own_rows] for k in range(group)]

    d_n_two = level_sum(row_blocks(dn_part), ctx, tensor)
    out_own = hidden_res + level_sum(row_blocks(out_part), ctx, tensor)

    def tensor_rows(own):
        have = [(0, own)]
        bit = tensor // 2
        while bit >= 1:
            sent = jnp.concatenate([v for _, v in have], axis=0) if len(have) > 1 else have[0][1]
            got = swap(sent, group, bit)
            have = have + [(k | bit, got[i * own_rows : (i + 1) * own_rows]) for i, (k, _) in enumerate(have)]
            bit //= 2
        have = [v for _, v in sorted(have, key=lambda e: e[0])]
        ordered = jnp.take(jnp.stack(have, axis=0), my_t ^ jnp.arange(tensor), axis=0)
        return ordered.reshape(tensor * own_rows, width)

    result = tensor_rows(out_own.astype(BF))

    cot_f = cot_own.astype(F32)
    scaled = d_n_two * gain_two
    inner = jnp.mean(scaled * normed_two, axis=-1, keepdims=True)
    d_h = cot_f + scale_two * (scaled - normed_two * inner)
    gain_two_part = jnp.sum(d_n_two * normed_two, axis=0)
    d_h_low = d_h.astype(BF)
    d_h_parts = jnp.transpose(d_h_low.reshape(own_rows, shards, ctx, d_own), (2, 0, 1, 3)).reshape(ctx, own_rows, shards * d_own)
    d_attn = sum(mm(d_h_parts[i], w_o[i], NT) for i in range(ctx)).astype(BF)
    blocks = jnp.transpose(d_attn.reshape(own_rows, group, cols), (1, 0, 2))
    owner_rel = rel ^ me
    col_of = (owner_rel % tensor) * ctx + owner_rel // tensor
    blocks = jnp.take(blocks, col_of, axis=0)
    go = jnp.concatenate(level_exchange([blocks[k] for k in range(group)], group), axis=0)
    d_qkv = attend_back_call(slots, qs, ks, vs, os, stats, go, cos, sin)

    d_h_all = jnp.concatenate(level_gather(d_h_low, ctx, tensor), axis=0)
    grad_wo = mm(d_h_all, o_slot, TN).astype(BF)
    grad_wqkv = mm(n_one, d_qkv, TN).astype(BF)
    d_n_one = level_sum(row_blocks(mm(d_qkv, w_qkv, NT).astype(BF)), ctx, tensor)
    x_scale = lax.rsqrt(jnp.mean(x_own * x_own, axis=-1, keepdims=True) + EPS)
    x_normed = x_own * x_scale
    scaled = d_n_one * gain_one
    inner = jnp.mean(scaled * x_normed, axis=-1, keepdims=True)
    d_x = d_h + x_scale * (scaled - x_normed * inner)
    gain_one_part = jnp.sum(d_n_one * x_normed, axis=0)
    grad_x = tensor_rows(d_x.astype(BF))

    chunks = ff_mine.shape[0]
    fc = ff // chunks
    mine = ff_mine.reshape(chunks, 3, fc, d_own)
    got = ff_got.reshape(chunks, 3, fc, d_own).astype(F32)

    def spread(i):
        return x_join(mine[:, i].reshape(ff, d_own), got[:, i].reshape(ff, d_own), 0)

    grad_down = spread(0)
    grad_gate = spread(1).T
    grad_up = spread(2).T

    def attn_sums(array):
        total = chain_sum(array.reshape(shards, ctx * d_own, array.shape[1]), shards)
        mine, other = x_halves(total, 0)
        got = lax.ppermute(other.astype(BF), "ctx", swap_x).astype(F32)
        return mine, got

    mine, got = attn_sums(grad_wo)
    grad_out = x_join(mine, got, 1).T
    mine, got = attn_sums(grad_wqkv)
    grad_q = x_join(mine[:, :cols], got[:, :cols], 1)
    grad_k = x_join(mine[:, cols : 2 * cols], got[:, cols : 2 * cols], 1)
    grad_v = x_join(mine[:, 2 * cols :], got[:, 2 * cols :], 1)

    def gain_sum(part):
        total = lax.psum(part, ("shard", "ctx", "tensor"))
        return lax.dynamic_slice_in_dim(total, (my_z * ctx + my_x) * d_own, d_own)

    grad_gain_two = gain_sum(gain_two_part)
    grad_gain_one = gain_sum(gain_one_part)
    return (
        result,
        grad_x,
        grad_gain_one,
        grad_q,
        grad_k,
        grad_v,
        grad_out,
        grad_gain_two,
        grad_gate,
        grad_up,
        grad_down,
    )


def solution(mesh):
    rows = P(("shard", "ctx"), None)
    gain = P(("shard", "ctx"))
    into = P(("shard", "ctx"), "tensor")
    back = P("tensor", ("shard", "ctx"))
    sizes = mesh.shape
    return jax.shard_map(
        functools.partial(per_device, sizes["shard"], sizes["ctx"], sizes["tensor"]),
        mesh=mesh,
        in_specs=(rows, rows, P("shard"), P("shard", None), gain, into, into, into, back, gain, into, into, back),
        out_specs=(rows, rows, gain, into, into, into, back, gain, into, into, back),
        check_vma=False,
    )
```

```python
import functools

import jax
import jax.numpy as jnp
from jax import lax
from jax.experimental import pallas as pl
from jax.experimental.pallas import tpu as pltpu
from jax.sharding import PartitionSpec as P

HDIM = 64
BLK = 128
EPS = 1e-05
THETA = 130000.0
NEG = -1e30
LEVEL = ("ctx", "tensor")
BF = jnp.bfloat16
F32 = jnp.float32
QT = 512

NT = (((1,), (1,)), ((), ()))
TN = (((0,), (0,)), ((), ()))


def mm(left, right, dims=None):
    if dims is None:
        return jnp.dot(left, right, preferred_element_type=F32)
    return lax.dot_general(left, right, dims, preferred_element_type=F32)


def level_bits(ctx, tensor):
    bits_y = []
    bit = 2
    while bit < tensor:
        bits_y.append(bit)
        bit *= 2
    bits_x = []
    bit = tensor
    while bit < ctx * tensor:
        bits_x.append(bit)
        bit *= 2
    return bits_y, bits_x


def plus(a, b):
    return (a.astype(F32) + b.astype(F32)).astype(BF)


def turn(u, cos, sin):
    lane = lax.broadcasted_iota(jnp.int32, u.shape, 1)
    width = u.shape[1]
    ahead = pltpu.roll(u, width - HDIM // 2, axis=1)
    behind = pltpu.roll(u, HDIM // 2, axis=1)
    other = jnp.where(lane % HDIM < HDIM // 2, ahead, behind)
    return u * cos + other * sin


def wide(table, cols):
    reps = cols // table.shape[1]
    return jnp.concatenate([table] * reps, axis=1) if reps > 1 else table


def flip(index, bit):
    return index + bit - 2 * bit * ((index // bit) % 2)


class Place:
    def __init__(self, shards, ctx, tensor):
        self.shards, self.ctx, self.tensor = shards, ctx, tensor
        self.group = ctx * tensor
        self.z = lax.axis_index("shard")
        self.x = lax.axis_index("ctx")
        self.t = lax.axis_index("tensor")
        self.bits_y, self.bits_x = level_bits(ctx, tensor)

    def peer(self, offset):
        t, x = self.t, self.x
        bit = 1
        while bit < self.group:
            if offset & bit:
                if bit < self.tensor:
                    t = flip(t, bit)
                else:
                    x = 1 - x
            bit *= 2
        return x, t

    def peer_id(self, offset):
        x, t = self.peer(offset)
        return (self.z, x, t)

    def above(self):
        return (self.z + 1, self.x, self.t)

    def below(self):
        return (self.z - 1, self.x, self.t)

    def meet(self, offsets, chain=True):
        barrier = pltpu.get_barrier_semaphore()
        z, shards = self.z, self.shards
        for k in offsets:
            pl.semaphore_signal(barrier, inc=1, device_id=self.peer_id(k), device_id_type=pl.DeviceIdType.MESH)
        peers = len(offsets)
        if chain:

            @pl.when(z < shards - 1)
            def _():
                pl.semaphore_signal(barrier, inc=1, device_id=self.above(), device_id_type=pl.DeviceIdType.MESH)

            @pl.when(z > 0)
            def _():
                pl.semaphore_signal(barrier, inc=1, device_id=self.below(), device_id_type=pl.DeviceIdType.MESH)

            peers = peers + (z + shards - 1) // shards + (2 * shards - 2 - z) // shards
        pl.semaphore_wait(barrier, peers)


class Move:
    def __init__(self, out, due, goes, comes):
        self.out, self.due, self.goes, self.comes = out, due, goes, comes

    def _run(self, cond, fn):
        if cond is None:
            fn()
        else:
            pl.when(cond)(fn)

    def start(self):
        self._run(self.goes, self.out.start)

    def come(self):
        self._run(self.comes, self.due.wait_recv)

    def sent(self):
        self._run(self.goes, self.out.wait_send)


class Links:
    def __init__(self, place, send_sems, recv_sems):
        self.place, self.send_sems, self.recv_sems = place, send_sems, recv_sems
        self.moves = []

    def send(self, src, dst, where, land=None, goes=None, comes=None, start=True):
        i = len(self.moves)
        land = dst if land is None else land
        safe = self.place.peer_id(1)

        def copy(a, b, w):
            return pltpu.make_async_remote_copy(
                src_ref=a,
                dst_ref=b,
                send_sem=self.send_sems.at[i],
                recv_sem=self.recv_sems.at[i],
                device_id=w,
                device_id_type=pl.DeviceIdType.MESH,
            )

        move = Move(copy(src, dst, where), copy(land, land, safe), goes, comes)
        self.moves.append(move)
        if start:
            move.start()
        return move

    def all_sent(self):
        for m in self.moves:
            m.sent()


    def chain(self, parts):
        p = self.place
        z, shards = p.z, p.shards
        due = []
        for k in range(1, shards):
            for m in due:
                m.come()
            due = []
            up = zip(parts(z - (k - 1)), parts(z - k))
            for src, land in up:
                due.append(self.send(src, src, p.above(), land, (z >= k - 1) & (z < shards - 1), z >= k))
            down = zip(parts(z + (k - 1)), parts(z + k))
            for src, land in down:
                due.append(
                    self.send(src, src, p.below(), land, (z + k - 1 <= shards - 1) & (z > 0), z + k <= shards - 1)
                )
            yield
        for m in due:
            m.come()

    def spread(self, part, absolute=False):
        p = self.place

        def put(k, bit, h):
            return self.send(part(k, h), part(k if absolute else k | bit, h), p.peer_id(bit), part(k | bit, h))

        cores = [put(0, 1, None)]
        have = [[0], [0]]
        found = {}
        orders = [p.bits_x + p.bits_y, p.bits_y + p.bits_x]
        for stage in range(len(orders[0])):
            step = []
            for h in (0, 1):
                bit = orders[h][stage]
                step += [(k | bit, put(k, bit, h)) for k in have[h]]
                have[h] = have[h] + [k | bit for k in have[h]]
            yield
            for k, m in step:
                m.come()
                found[k] = found.get(k, 0) + 1
                if found[k] == 2:
                    cores.append(put(k, 1, None))
        yield
        for m in cores:
            m.come()

    def rows(self, source, keep, own_rows, log):
        p = self.place

        def slot(k):
            return keep.at[pl.ds(k * own_rows, own_rows), :]

        mine = source.at[pl.ds(pl.multiple_of(p.t * own_rows, own_rows), own_rows), :]
        first = self.send(mine, slot(p.tensor), p.peer_id(p.tensor))
        log.append(first)
        yield
        first.come()
        far = [p.tensor]
        for bit in p.bits_y:
            step = [self.send(slot(k), slot(k | bit), p.peer_id(bit)) for k in far]
            log += step
            yield
            for m in step:
                m.come()
            far = far + [k | bit for k in far]
        last = [self.send(slot(k), slot(k | 1), p.peer_id(1)) for k in far]
        log += last
        yield
        for m in last:
            m.come()


def drain(*gens):
    for g in gens:
        for _ in g:
            pass


def first_kernel(
    dims, place_s, at_s, live_s, tokens, cotangent, gains_in, wq, wk, wv, w_out, wg, wu, wd, cos_ref, sin_ref,
    n_one_out, w_qkv_out, w_o_out, cot_out, gu_out, d_out, n_own_out, h_out, gains, qs, ks, vs, os, stats, o_rel,
    n_one, w_qkv, w_o, qkv_rel, attn_rows, h_own, n_own, x_keep,
    send_sems, recv_sems, own_sems,
):
    shards, ctx, tensor, fc, own_rows, d_own = dims
    p = Place(shards, ctx, tensor)
    z, x, t = p.z, p.x, p.t
    group = p.group
    rows, width = n_one.shape
    cols = qs.shape[1]
    heads = cols // HDIM
    ff = wg.shape[1] // ctx
    dz = ctx * d_own
    links = Links(p, send_sems, recv_sems)
    own_count = [0]

    def own(src, dst):
        i = own_count[0]
        own_count[0] += 1
        c = pltpu.make_async_copy(src, dst, own_sems.at[i])
        c.start()
        return c

    p.meet(list(range(1, group)))

    def d_at(xx):
        return pl.ds(pl.multiple_of((z * ctx + xx) * d_own, d_own), d_own)

    def z_at(b):
        return pl.ds(pl.multiple_of(b * dz, dz), dz)

    def part_cols(xx, size):
        return pl.ds(pl.multiple_of(xx * size, size), size)

    across = p.peer_id(tensor)

    wo_rows = w_out.shape[0]

    def o_at(tt, xx, zz):
        return w_o.at[xx, pl.ds(pl.multiple_of(tt * wo_rows, wo_rows), wo_rows), pl.ds(pl.multiple_of(zz * d_own, d_own), d_own)]

    own_o = own(w_out, o_at(t, x, z))
    own_gain = own(gains_in, gains.at[:, d_at(x)])
    own_w = [own(w.at[:, part_cols(x, cols)], w_qkv.at[d_at(x), i * cols : (i + 1) * cols]) for i, w in enumerate((wq, wk, wv))]
    own_gain.wait()
    gain_x = links.send(gains.at[:, d_at(x)], gains.at[:, d_at(x)], across, gains.at[:, d_at(1 - x)])
    qkv_x = [
        links.send(
            w.at[:, part_cols(1 - x, cols)],
            w_qkv.at[d_at(x), i * cols : (i + 1) * cols],
            across,
            w_qkv.at[d_at(1 - x), i * cols : (i + 1) * cols],
        )
        for i, w in enumerate((wq, wk, wv))
    ]
    tok_log = []
    tok_rows = links.rows(tokens, n_one, own_rows, tok_log)
    next(tok_rows)
    own_tok = []
    for k in range(tensor):
        _, tt = p.peer(k)
        src = tokens.at[pl.ds(pl.multiple_of(tt * own_rows, own_rows), own_rows), :]
        own_tok.append(own(src, n_one.at[pl.ds(k * own_rows, own_rows), :]))
    own_o.wait()
    o_chain = links.chain(lambda b: [o_at(t, x, b)])
    next(o_chain)
    gain_x.come()
    gain_chain = links.chain(lambda b: [gains.at[:, z_at(b)]])
    next(gain_chain)
    next(o_chain, None)
    for c in own_w:
        c.wait()
    for m in qkv_x:
        m.come()
    next(gain_chain, None)
    qkv_chain = links.chain(lambda b: [w_qkv.at[z_at(b), :]])
    next(qkv_chain)

    gu_pairs = [(wg, 0), (wu, 1)]

    def gu_place(xx, i):
        return gu_out.at[d_at(xx), i * fc : (i + 1) * fc]

    ff_own = [own(w.at[:, pl.ds(pl.multiple_of(x * ff, fc), fc)], gu_place(x, i)) for w, i in gu_pairs]
    ff_own.append(own(wd.at[pl.ds(pl.multiple_of(x * ff, fc), fc), :], d_out.at[:, d_at(x)]))
    ff_x = [
        links.send(w.at[:, pl.ds(pl.multiple_of((1 - x) * ff, fc), fc)], gu_place(x, i), across, gu_place(1 - x, i))
        for w, i in gu_pairs
    ]
    ff_x.append(
        links.send(wd.at[pl.ds(pl.multiple_of((1 - x) * ff, fc), fc), :], d_out.at[:, d_at(x)], across, d_out.at[:, d_at(1 - x)])
    )
    drain(gain_chain)
    drain(o_chain)
    for c in own_tok:
        c.wait()
    x_keep[...] = n_one[0:own_rows, :]
    next(tok_rows, None)

    def o_part(k, h):
        xx, tt = p.peer(k)
        size = wo_rows if h is None else wo_rows // 2
        start = tt * wo_rows + (0 if h is None else h * size)
        return w_o.at[xx, pl.ds(pl.multiple_of(start, size), size), :]

    o_spread = links.spread(o_part, absolute=True)
    next(o_spread)

    def norm(r, carry):
        at = pl.ds(pl.multiple_of(r * own_rows, own_rows), own_rows)
        v = n_one[at, :].astype(F32)
        scale = lax.rsqrt(jnp.mean(v * v, axis=-1, keepdims=True) + EPS)
        n_one[at, :] = (v * scale * gains[0:1, :]).astype(BF)
        return carry

    next(qkv_chain, None)
    lax.fori_loop(0, tensor, norm, 0)
    for c in ff_own:
        c.wait()
    for m in ff_x:
        m.come()
    next(tok_rows, None)
    next(qkv_chain, None)
    ff_chain = links.chain(lambda b: [gu_out.at[z_at(b), :], d_out.at[:, z_at(b)]])
    next(ff_chain)
    drain(tok_rows)
    for m in tok_log:
        m.sent()
    lax.fori_loop(tensor, group, norm, 0)
    out_n = own(n_one, n_one_out)
    next(o_spread, None)
    drain(qkv_chain)
    next(ff_chain, None)
    out_w = own(w_qkv, w_qkv_out)

    def project(r, carry):
        at = pl.ds(pl.multiple_of(r * own_rows, own_rows), own_rows)
        lin = mm(n_one[at, :], w_qkv[...])
        per = own_rows // BLK
        for i in range(per):
            where = pl.ds(pl.multiple_of(r * own_rows + i * BLK, BLK), BLK)
            cos, sin = wide(cos_ref[where, :], cols), wide(sin_ref[where, :], cols)
            part = lin[i * BLK : (i + 1) * BLK, :]
            dst = pl.ds(pl.multiple_of(r * own_rows + i * BLK, BLK), BLK)
            qkv_rel[dst, 0:cols] = turn(part[:, 0:cols], cos, sin).astype(BF)
            qkv_rel[dst, cols : 2 * cols] = turn(part[:, cols : 2 * cols], cos, sin).astype(BF)
            qkv_rel[dst, 2 * cols : 3 * cols] = part[:, 2 * cols : 3 * cols].astype(BF)
        return carry

    lax.fori_loop(0, group, project, 0)
    next(o_spread, None)

    def fill(b, carry):
        dst = pl.ds(pl.multiple_of(b * BLK, BLK), BLK)
        found = picked(qkv_rel, place_s[b])
        qs[dst, :] = found[:, 0:cols]
        ks[dst, :] = found[:, cols : 2 * cols]
        vs[dst, :] = found[:, 2 * cols : 3 * cols]
        return carry

    lax.fori_loop(0, rows // BLK, fill, 0)
    cot_rows = links.rows(cotangent, cot_out, own_rows, [])
    next(cot_rows)
    own_cot = []
    for k in range(tensor):
        _, tt = p.peer(k)
        src = cotangent.at[pl.ds(pl.multiple_of(tt * own_rows, own_rows), own_rows), :]
        own_cot.append(own(src, cot_out.at[pl.ds(k * own_rows, own_rows), :]))
    live = live_s[0]
    for tile in range(rows // QT):
        attend_tile(tile, live, qs, ks, vs, os, stats)
        next(ff_chain, None)
        next(o_spread, None)
        next(cot_rows, None)

    def back_to_rows(j, carry):
        dst = pl.ds(pl.multiple_of(j * BLK, BLK), BLK)
        o_rel[dst, :] = picked(os, at_s[j])
        return carry

    lax.fori_loop(0, rows // BLK, back_to_rows, 0)

    def head_at(k):
        xx, tt = p.peer(k)
        return attn_rows.at[:, pl.ds(pl.multiple_of((tt * ctx + xx) * cols, cols), cols)]

    swaps = [
        links.send(o_rel.at[pl.ds(k * own_rows, own_rows), :], head_at(0), p.peer_id(k), head_at(k)) for k in range(1, group)
    ]
    own_heads = own(o_rel.at[pl.ds(0, own_rows), :], head_at(0))
    drain(o_spread)
    out_o = own(w_o, w_o_out)
    own_heads.wait()
    for m in swaps:
        m.come()
    for xx in range(ctx):
        span = shards * d_own
        mixed = mm(attn_rows[...], w_o[xx])
        for zz in range(shards):
            at = slice((zz * ctx + xx) * d_own, (zz * ctx + xx + 1) * d_own)
            h_own[:, at] = x_keep[:, at].astype(F32) + mixed[:, zz * d_own : (zz + 1) * d_own]
    h = h_own[...]
    scale = lax.rsqrt(jnp.mean(h * h, axis=-1, keepdims=True) + EPS)
    n_own[...] = (h * scale * gains[1:2, :]).astype(BF)
    out_h = own(h_own, h_out)
    out_own = own(n_own, n_own_out)
    drain(ff_chain)
    drain(cot_rows)
    for c in own_cot:
        c.wait()
    for m in links.moves:
        if m not in tok_log:
            m.sent()
    for c in (out_n, out_w, out_o, out_h, out_own):
        c.wait()


def picked(ref, block):
    found = ref[0:BLK, :]
    for j in range(1, ref.shape[0] // BLK):
        found = jnp.where(block == j, ref[j * BLK : (j + 1) * BLK, :], found)
    return found


def attend_tile(t, live, qs, ks, vs, os, stats):
    rows, cols = qs.shape
    heads = cols // HDIM
    ext = (t + 1) * QT
    lane = lax.broadcasted_iota(jnp.int32, (QT, cols), 1) // HDIM
    qpos = lax.broadcasted_iota(jnp.int32, (QT, QT), 0)
    kpos = lax.broadcasted_iota(jnp.int32, (QT, QT), 1)
    diag = jnp.where(kpos <= qpos, 0.0, NEG)
    dead = jnp.where(lax.broadcasted_iota(jnp.int32, (1, ext), 1) < live, 0.0, NEG)

    def head(h, acc):
        q = jnp.where(lane == h, qs[t * QT : ext, :] * BF(0.125), BF(0))
        s = mm(q, ks[0:ext, :], NT) + dead
        last = s[:, t * QT :] + diag
        s = jnp.concatenate([s[:, : t * QT], last], axis=1) if t else last
        top = jnp.max(s, axis=1, keepdims=True)
        e = jnp.exp(s - top)
        total = jnp.sum(e, axis=1, keepdims=True)
        mixed = mm(e.astype(BF), vs[0:ext, :]) / total
        note = jnp.broadcast_to(top + jnp.log(total), (QT, 128))
        stats[pl.ds(h, 1), t * QT : ext] = jnp.transpose(note)[0:1, :]
        return jnp.where(lane == h, mixed, acc)

    acc = lax.fori_loop(0, heads, head, jnp.zeros((QT, cols), F32))
    os[t * QT : ext, :] = acc.astype(BF)


def first_call(shards, ctx, tensor, place, at, live, tokens, cotangent, gains, wq, wk, wv, w_out, wg, wu, wd, cos, sin):
    width = tokens.shape[1]
    own_rows = tokens.shape[0] // tensor
    group = ctx * tensor
    rows = own_rows * group
    d_own = wq.shape[0]
    cols = wq.shape[1] // ctx
    fc = 256
    dims = (shards, ctx, tensor, fc, own_rows, d_own)
    any_spec = pl.BlockSpec(memory_space=pl.ANY)
    smem = pl.BlockSpec(memory_space=pltpu.SMEM)
    vmem = pl.BlockSpec(memory_space=pltpu.VMEM)
    piece = jax.ShapeDtypeStruct((rows, cols), BF)
    moves = 400
    dma = pltpu.SemaphoreType.DMA
    return pl.pallas_call(
        functools.partial(first_kernel, dims),
        in_specs=[smem] * 3 + [any_spec] * 10 + [vmem] * 2,
        out_specs=[any_spec] * 8 + [vmem] * 7,
        out_shape=[
            jax.ShapeDtypeStruct((rows, width), BF),
            jax.ShapeDtypeStruct((width, 3 * cols), BF),
            jax.ShapeDtypeStruct((ctx, width, shards * d_own), BF),
            jax.ShapeDtypeStruct((rows, width), BF),
            jax.ShapeDtypeStruct((width, 2 * fc), BF),
            jax.ShapeDtypeStruct((fc, width), BF),
            jax.ShapeDtypeStruct((own_rows, width), BF),
            jax.ShapeDtypeStruct((own_rows, width), F32),
            jax.ShapeDtypeStruct((8, width), F32),
            piece,
            piece,
            piece,
            piece,
            jax.ShapeDtypeStruct((8, rows), F32),
            piece,
        ],
        scratch_shapes=[
            pltpu.VMEM((rows, width), BF),
            pltpu.VMEM((width, 3 * cols), BF),
            pltpu.VMEM((ctx, width, shards * d_own), BF),
            pltpu.VMEM((rows, 3 * cols), BF),
            pltpu.VMEM((own_rows, width), BF),
            pltpu.VMEM((own_rows, width), F32),
            pltpu.VMEM((own_rows, width), BF),
            pltpu.VMEM((own_rows, width), BF),
            dma((moves,)),
            dma((moves,)),
            dma((40,)),
        ],
        compiler_params=pltpu.CompilerParams(
            collective_id=0, has_side_effects=True, vmem_limit_bytes=62 * 1024 * 1024
        ),
        cost_estimate=pl.CostEstimate(
            flops=2 * rows * width * cols * 4, bytes_accessed=64 * 1024 * 1024, transcendentals=rows * rows * cols // HDIM
        ),
        name="first",
    )(place, at, live, tokens, cotangent, gains, wq, wk, wv, w_out, wg, wu, wd, cos, sin)


def mlp_kernel(
    dims, n_own, cot_in, wg, wu, wd, gu_pre, d_pre,
    dn_out, out_out, mine_out, got_out, g_hbm, r_hbm,
    n2, cot, wgu_v, wd_v, hid, dgu, left_t, gt, st, ost, fin, away,
    lev_send, lev_recv, x_own, x_send, x_recv, a_send, a_recv, g_sem, s_sem, rs_send, rs_recv, fx_send, fx_recv, o_sem, c_sem,
):
    shards, ctx, tensor, chunks, fc, rows_own, d_own = dims
    group = ctx * tensor
    rows, width = n2.shape
    dz = ctx * d_own
    ff = chunks * fc
    z = lax.axis_index("shard")
    x = lax.axis_index("ctx")
    t = lax.axis_index("tensor")
    bits_y, bits_x = level_bits(ctx, tensor)

    p = Place(shards, ctx, tensor)
    above, below = p.above, p.below
    p.meet([1] + bits_y + bits_x)

    here_too = (z, x, flip(t, 1))

    def remote(src, dst, send, recv, where):
        return pltpu.make_async_remote_copy(
            src_ref=src, dst_ref=dst, send_sem=send, recv_sem=recv, device_id=where, device_id_type=pl.DeviceIdType.MESH
        )

    def x_copies(c, own):
        half = x if own else 1 - x
        low_c = pl.multiple_of(half * ff + c * fc, fc)
        d_at = pl.ds(pl.multiple_of((z * ctx + x) * d_own, d_own), d_own)
        pairs = [
            (wg.at[:, pl.ds(low_c, fc)], wgu_v.at[c, d_at, pl.ds(0, fc)]),
            (wu.at[:, pl.ds(low_c, fc)], wgu_v.at[c, d_at, pl.ds(fc, fc)]),
            (wd.at[pl.ds(low_c, fc), :], wd_v.at[pl.ds(pl.multiple_of(c * fc, fc), fc), d_at]),
        ]
        if own:
            return [pltpu.make_async_copy(a, b, x_own.at[c, i]) for i, (a, b) in enumerate(pairs)]
        return [remote(a, b, x_send.at[c, i], x_recv.at[c, i], (z, 1 - x, t)) for i, (a, b) in enumerate(pairs)]

    def x_landed(c):
        d_at = pl.ds(pl.multiple_of((z * ctx + 1 - x) * d_own, d_own), d_own)
        lands = [
            wgu_v.at[c, d_at, pl.ds(0, fc)],
            wgu_v.at[c, d_at, pl.ds(fc, fc)],
            wd_v.at[pl.ds(pl.multiple_of(c * fc, fc), fc), d_at],
        ]
        return [remote(a, a, x_send.at[c, i], x_recv.at[c, i], here_too) for i, a in enumerate(lands)]

    def hop(c, way, k, b, wait=False):
        at = pl.ds(pl.multiple_of(b * dz, dz), dz)
        parts = [wgu_v.at[c, at, :], wd_v.at[pl.ds(pl.multiple_of(c * fc, fc), fc), at]]
        where = here_too if wait else above() if way == 0 else below()
        return [remote(p, p, a_send.at[c, way, k, i], a_recv.at[c, way, k, i], where) for i, p in enumerate(parts)]

    def hop_start(c, k):
        @pl.when((z >= k - 1) & (z < shards - 1))
        def _():
            for d in hop(c, 0, k - 1, z - (k - 1)):
                d.start()

        @pl.when((z + k - 1 <= shards - 1) & (z > 0))
        def _():
            for d in hop(c, 1, k - 1, z + (k - 1)):
                d.start()

    def hop_sent(c, k):
        @pl.when((z >= k - 1) & (z < shards - 1))
        def _():
            for d in hop(c, 0, k - 1, z - (k - 1)):
                d.wait_send()

        @pl.when((z + k - 1 <= shards - 1) & (z > 0))
        def _():
            for d in hop(c, 1, k - 1, z + (k - 1)):
                d.wait_send()

    def hop_wait(c, k):
        @pl.when(z >= k)
        def _():
            for d in hop(c, 0, k - 1, z - k, True):
                d.wait_recv()

        @pl.when(z + k <= shards - 1)
        def _():
            for d in hop(c, 1, k - 1, z + k, True):
                d.wait_recv()

    def x_start(c):
        for d in x_copies(c, False):
            d.start()
        for d in x_copies(c, True):
            d.start()

    x_start(1)
    pre_copies = [
        pltpu.make_async_copy(gu_pre, wgu_v.at[0], x_own.at[0, 0]),
        pltpu.make_async_copy(d_pre, wd_v.at[pl.ds(0, fc), :], x_own.at[0, 1]),
    ]
    for d in pre_copies:
        d.start()

    half = rows_own // 2
    links = Links(p, lev_send, lev_recv)
    cot_copy = pltpu.make_async_copy(cot_in, cot, c_sem.at[0])
    own_copy = pltpu.make_async_copy(n_own, n2.at[pl.ds(0, rows_own), :], c_sem.at[1])
    own_copy.start()
    own_copy.wait()

    def n_part(k, h):
        if h is None:
            return n2.at[pl.ds(k * rows_own, rows_own), :]
        return n2.at[pl.ds(k * rows_own + h * half, half), :]

    n_rows = links.spread(n_part)
    next(n_rows)
    cot_copy.start()
    for c in range(2, chunks):
        x_start(c)
    for d in x_copies(1, True):
        d.wait()
    for d in x_landed(1):
        d.wait_recv()
    hop_start(1, 1)
    next(n_rows)

    def ag_round(r, top):
        for k in range(shards - 1, 0, -1):
            if k > top:
                continue
            c = r - k + 1

            @pl.when((c >= 1) & (c < chunks))
            def _(c=c, k=k):
                if k == 1:
                    for d in x_copies(c, True):
                        d.wait()
                    for d in x_landed(c):
                        d.wait_recv()
                else:
                    hop_wait(c, k - 1)
                hop_start(c, k)

    for r in range(2, shards - 1):
        ag_round(jnp.int32(r), shards - 1)
    drain(n_rows)
    cot_copy.wait()
    for d in pre_copies:
        d.wait()

    def block_of(i):
        down = shards - 1 - i
        down = down - jnp.where(down <= z, 1, 0)
        up = i + jnp.where(i >= z, 1, 0)
        return jnp.where(i == shards - 1, z, jnp.where(2 * z < shards, down, up))

    def g_copy(c, d, slot):
        return pltpu.make_async_copy(gt.at[slot], g_hbm.at[c, d], g_sem.at[slot])

    def rs_send_copy(src, c, way, d, wait=False):
        where = here_too if wait else above() if way == 0 else below()
        return remote(src, r_hbm.at[c, way, d], rs_send.at[c, way, d], rs_recv.at[c, way, d], where)

    combos = [(way, k) for k in range(2, shards) for way in (0, 1)]

    def target(way, k):
        return z + shards - k if way == 0 else z - (shards - k)

    def sends(way, k):
        if way == 0:
            return z < k
        return z >= shards - k

    def starts(way):
        return z == 0 if way == 0 else z == shards - 1

    def runs(way):
        return z != 0 if way == 0 else z != shards - 1

    def rs_step(s):
        for way in (0, 1):
            for k in range(1, shards):
                c = s - (k - 1)

                @pl.when((c >= 0) & (c < chunks) & starts(way))
                def _(c=c, way=way, k=k):
                    d = target(way, k)
                    rs_send_copy(g_hbm.at[c, d], c, way, d).start()

        for i, (way, k) in enumerate(combos):
            c = s - (k - 1)

            @pl.when((c >= 0) & (c < chunks) & sends(way, k) & runs(way))
            def _(c=c, way=way, k=k, i=i):
                d = target(way, k)

                @pl.when(c >= 1)
                def _():
                    rs_send_copy(st.at[2 * i], c - 1, way, d).wait_send()

                rs_send_copy(st.at[2 * i], c, way, d, True).wait_recv()
                pltpu.make_async_copy(g_hbm.at[c, d], st.at[2 * i], s_sem.at[2 * i]).start()
                pltpu.make_async_copy(r_hbm.at[c, way, d], st.at[2 * i + 1], s_sem.at[2 * i + 1]).start()

        last = 2 * len(combos)
        c_fin = s - (shards - 1)

        @pl.when((c_fin >= 0) & (c_fin < chunks))
        def _():
            pltpu.make_async_copy(g_hbm.at[c_fin, z], st.at[last], s_sem.at[last]).start()
            for way in (0, 1):
                slot = last + 1 + way

                @pl.when(runs(way))
                def _(way=way, slot=slot):
                    rs_send_copy(st.at[slot], c_fin, way, z, True).wait_recv()
                    pltpu.make_async_copy(r_hbm.at[c_fin, way, z], st.at[slot], s_sem.at[slot]).start()

                @pl.when(starts(way))
                def _(slot=slot):
                    st[slot] = jnp.zeros(st.shape[1:], BF)

        for i, (way, k) in enumerate(combos):
            c = s - (k - 1)

            @pl.when((c >= 0) & (c < chunks) & sends(way, k) & runs(way))
            def _(c=c, way=way, k=k, i=i):
                d = target(way, k)
                pltpu.make_async_copy(g_hbm.at[c, d], st.at[2 * i], s_sem.at[2 * i]).wait()
                pltpu.make_async_copy(r_hbm.at[c, way, d], st.at[2 * i + 1], s_sem.at[2 * i + 1]).wait()
                st[2 * i] = (st[2 * i].astype(F32) + st[2 * i + 1].astype(F32)).astype(BF)
                rs_send_copy(st.at[2 * i], c, way, d).start()

        @pl.when((c_fin >= 0) & (c_fin < chunks))
        def _():
            pltpu.make_async_copy(g_hbm.at[c_fin, z], st.at[last], s_sem.at[last]).wait()
            for way in (0, 1):
                slot = last + 1 + way

                @pl.when(runs(way))
                def _(way=way, slot=slot):
                    pltpu.make_async_copy(r_hbm.at[c_fin, way, z], st.at[slot], s_sem.at[slot]).wait()

            @pl.when(c_fin >= 1)
            def _():
                pltpu.make_async_copy(fin, mine_out.at[c_fin - 1], c_sem.at[2]).wait()
                fin_copy(c_fin - 1).wait_send()

            total = st[last].astype(F32) + st[last + 1].astype(F32) + st[last + 2].astype(F32)
            low, high = total[:, :d_own], total[:, d_own:]
            fin[...] = jnp.where(x == 0, low, high)
            away[...] = jnp.where(x == 0, high, low).astype(BF)
            pltpu.make_async_copy(fin, mine_out.at[c_fin], c_sem.at[2]).start()
            fin_copy(c_fin).start()

    def fin_copy(c):
        return remote(away, got_out.at[c], fx_send.at[c], fx_recv.at[c], (z, 1 - x, t))

    tile = 512

    def phase_one(c):
        def body(r, carry):
            at = pl.ds(pl.multiple_of(r * tile, tile), tile)
            gu = mm(n2[at, :], wgu_v[c])
            dh = mm(cot[at, :], wd_v[pl.ds(pl.multiple_of(c * fc, fc), fc), :], NT)
            gate, up = gu[:, :fc], gu[:, fc:]
            sig = 1.0 / (1.0 + jnp.exp(-gate))
            act = gate * sig
            h = (act * up).astype(BF)
            dg = (dh * up * sig * (1.0 + gate * (1.0 - sig))).astype(BF)
            du = (dh * act).astype(BF)
            hid[c, at, :] = h
            dgu[c, at, 0:fc] = dg
            dgu[c, at, fc : 2 * fc] = du
            left_t[0:fc, at] = h.T
            left_t[fc : 2 * fc, at] = dg.T
            left_t[2 * fc : 3 * fc, at] = du.T
            return carry

        lax.fori_loop(0, rows // tile, body, 0)

    def phase_two(c):
        def body(i, carry):
            d = block_of(i)
            slot = i % 2
            at = pl.ds(pl.multiple_of(d * dz, dz), dz)

            @pl.when(i >= 2)
            def _():
                g_copy(c, block_of(i - 2), slot).wait()

            gt[slot, 0:fc, :] = mm(left_t[0:fc, :], cot[:, at]).astype(BF)
            gt[slot, fc : 3 * fc, :] = mm(left_t[fc : 3 * fc, :], n2[:, at]).astype(BF)
            g_copy(c, d, slot).start()
            return carry

        lax.fori_loop(0, shards, body, 0)
        for i in (shards - 2, shards - 1):
            g_copy(c, block_of(jnp.int32(i)), i % 2).wait()

    ot = 256
    units = rows // ot

    def tail_unit(u):
        at = pl.ds(pl.multiple_of((u % units) * ot, ot), ot)
        slot = u % 2

        @pl.when(u >= 2)
        def _():
            pltpu.make_async_copy(ost.at[slot], dn_out.at[at, :], o_sem.at[slot]).wait()

        @pl.when(u < units)
        def _():
            for n in range(width // 512):
                cols = slice(n * 512, (n + 1) * 512)
                acc = jnp.zeros((ot, 512), F32)
                for c in range(chunks):
                    acc = acc + mm(dgu[c, at, :], wgu_v[c, cols, :], NT)
                ost[slot, :, cols] = acc.astype(BF)
            pltpu.make_async_copy(ost.at[slot], dn_out.at[at, :], o_sem.at[slot]).start()

        @pl.when(u >= units)
        def _():
            for n in range(width // 512):
                cols = slice(n * 512, (n + 1) * 512)
                acc = jnp.zeros((ot, 512), F32)
                for c in range(chunks):
                    acc = acc + mm(hid[c, at, :], wd_v[c * fc : (c + 1) * fc, cols])
                ost[slot, :, cols] = acc.astype(BF)
            pltpu.make_async_copy(ost.at[slot], out_out.at[at, :], o_sem.at[slot]).start()

    tail_slots = shards - 1
    per_slot = -(-2 * units // tail_slots)

    def slot_body(s, carry):
        @pl.when(s < chunks)
        def _():
            @pl.when(s >= 1)
            def _():
                hop_wait(s, shards - 1)

            phase_one(s)
            ag_round(s + shards - 1, shards - 1)
            phase_two(s)

        @pl.when(s >= chunks)
        def _():
            first_u = (s - chunks) * per_slot
            last_u = jnp.minimum(first_u + per_slot, 2 * units)

            def body(u, carry):
                tail_unit(u)
                return carry

            lax.fori_loop(first_u, last_u, body, 0)

        rs_step(s)
        return carry

    lax.fori_loop(0, chunks + tail_slots, slot_body, 0)

    for u in (2 * units - 2, 2 * units - 1):
        at = pl.ds((u % units) * ot, ot)
        pltpu.make_async_copy(ost.at[u % 2], out_out.at[at, :], o_sem.at[u % 2]).wait()
    links.all_sent()
    for c in range(1, chunks):
        for d in x_copies(c, False):
            d.wait_send()
        for k in range(1, shards):
            hop_sent(c, k)
    for way in (0, 1):
        for k in range(1, shards):

            @pl.when(starts(way))
            def _(way=way, k=k):
                d = target(way, k)
                for c in range(chunks):
                    rs_send_copy(g_hbm.at[c, d], c, way, d).wait_send()

    for i, (way, k) in enumerate(combos):

        @pl.when(sends(way, k) & runs(way))
        def _(way=way, k=k, i=i):
            rs_send_copy(st.at[2 * i], chunks - 1, way, target(way, k)).wait_send()

    pltpu.make_async_copy(fin, mine_out.at[chunks - 1], c_sem.at[2]).wait()
    fin_copy(chunks - 1).wait_send()
    for c in range(chunks):
        fin_copy(c).wait_recv()


def mlp_call(shards, ctx, tensor, n_own, cot, wg, wu, wd, gu_pre, d_pre):
    rows_own, width = n_own.shape
    group = ctx * tensor
    rows = rows_own * group
    d_own = wg.shape[0]
    ff = wg.shape[1] // ctx
    fc = 256
    chunks = ff // fc
    dz = ctx * d_own
    any_spec = pl.BlockSpec(memory_space=pl.ANY)
    bits_y, bits_x = level_bits(ctx, tensor)
    halves = 2 ** (len(bits_y) + len(bits_x)) - 1
    moves = 2 * halves + halves + 1
    stage = 4 * (shards - 2) + 3
    dims = (shards, ctx, tensor, chunks, fc, rows_own, d_own)
    dma = pltpu.SemaphoreType.DMA
    return pl.pallas_call(
        functools.partial(mlp_kernel, dims),
        in_specs=[any_spec] * 7,
        out_specs=[any_spec] * 6,
        out_shape=[
            jax.ShapeDtypeStruct((rows, width), BF),
            jax.ShapeDtypeStruct((rows, width), BF),
            jax.ShapeDtypeStruct((chunks, 3 * fc, d_own), F32),
            jax.ShapeDtypeStruct((chunks, 3 * fc, d_own), BF),
            jax.ShapeDtypeStruct((chunks, shards, 3 * fc, dz), BF),
            jax.ShapeDtypeStruct((chunks, 2, shards, 3 * fc, dz), BF),
        ],
        scratch_shapes=[
            pltpu.VMEM((rows, width), BF),
            pltpu.VMEM((rows, width), BF),
            pltpu.VMEM((chunks, width, 2 * fc), BF),
            pltpu.VMEM((ff, width), BF),
            pltpu.VMEM((chunks, rows, fc), BF),
            pltpu.VMEM((chunks, rows, 2 * fc), BF),
            pltpu.VMEM((3 * fc, rows), BF),
            pltpu.VMEM((2, 3 * fc, dz), BF),
            pltpu.VMEM((stage, 3 * fc, dz), BF),
            pltpu.VMEM((2, 256, width), BF),
            pltpu.VMEM((3 * fc, d_own), F32),
            pltpu.VMEM((3 * fc, d_own), BF),
            dma((moves,)),
            dma((moves,)),
            dma((chunks, 3)),
            dma((chunks, 3)),
            dma((chunks, 3)),
            dma((chunks, 2, shards - 1, 2)),
            dma((chunks, 2, shards - 1, 2)),
            dma((2,)),
            dma((stage,)),
            dma((chunks, 2, shards)),
            dma((chunks, 2, shards)),
            dma((chunks,)),
            dma((chunks,)),
            dma((2,)),
            dma((3,)),
        ],
        compiler_params=pltpu.CompilerParams(
            collective_id=1, has_side_effects=True, vmem_limit_bytes=63 * 1024 * 1024
        ),
        cost_estimate=pl.CostEstimate(
            flops=18 * rows * width * ff, bytes_accessed=100 * 1024 * 1024, transcendentals=rows * ff
        ),
        name="feed_forward",
    )(n_own, cot, wg, wu, wd, gu_pre, d_pre)


def last_kernel(
    dims, place_s, at_s, live_s, dn_part, out_part, h_in, cot_in, tokens, gains_in, n_one, w_qkv_in, w_o_in, o_rel_in,
    qs, ks, vs, os, stats, cos_ref, sin_ref,
    result, grad_x, mine_o, got_o, mine_w, got_w, gain_out, dh_all, dh_keep, o_land, o_parts,
    big, w_qkv, chip, c_land, parts_land, stage_own, tile_h, tile_c, gains, dh_low, d_attn, go_rel, go, delta, dq,
    d_seq, d_rel, left_o, left_w, g_o, r_o, g_w, r_w, away_o, away_w, g_sum, g_land, g_chain, half_sum,
    send_sems, recv_sems, own_sems,
):
    shards, ctx, tensor, own_rows, d_own = dims
    p = Place(shards, ctx, tensor)
    z, x, t = p.z, p.x, p.t
    group = p.group
    rows, cols = qs.shape
    width = dh_low.shape[1]
    heads = cols // HDIM
    dz = ctx * d_own
    half = own_rows // 2
    links = Links(p, send_sems, recv_sems)
    count = [0]

    def own(src, dst):
        i = count[0]
        count[0] += 1
        c = pltpu.make_async_copy(src, dst, own_sems.at[i])
        c.start()
        return c

    p.meet(list(range(1, group)))

    def block(k):
        return pl.ds(k * own_rows, own_rows)

    def mine(k=0):
        _, tt = p.peer(k)
        return pl.ds(pl.multiple_of(tt * own_rows, own_rows), own_rows)

    orders = [p.bits_x + p.bits_y, p.bits_y + p.bits_x]

    def halves(land, in_hbm=False):
        have = [list(range(0, group, 2)), list(range(0, group, 2))]
        spot = 0
        for stage in range(len(orders[0])):
            step = []
            for h in (0, 1):
                bit = orders[h][stage]
                leave = [k for k in have[h] if k & bit]
                for i, k in enumerate(leave):
                    at = pl.ds(h * half, half)
                    dst = land.at[h, spot + i]
                    step.append((h, k, bit, spot + i, links.send(chip.at[k // 2, at, :], dst, p.peer_id(bit))))
                have[h] = [k for k in have[h] if not k & bit]
            spot += len(leave)
            yield
            for h, k, bit, i, m in step:
                m.come()
                at = pl.ds(h * half, half)
                keep = (k ^ bit) // 2
                if in_hbm:
                    own(land.at[h, i], stage_own.at[pl.ds(0, half), :]).wait()
                    came = stage_own[0:half, :].astype(F32)
                else:
                    came = land[h, i].astype(F32)
                total = chip[keep, at, :].astype(F32) + came
                if stage == len(orders[0]) - 1:
                    half_sum[at, :] = total
                else:
                    chip[keep, at, :] = total.astype(BF)
            for h, k, bit, i, m in step:
                m.sent()
                done_moves.append(m)

    done_moves = []

    odd = list(range(1, group, 2))
    core = [links.send(dn_part.at[block(k), :], c_land.at[k // 2], p.peer_id(1)) for k in odd]
    even = [own(dn_part.at[block(k - 1), :], chip.at[k // 2]) for k in odd]
    load_gain = own(gains_in, gains)
    load_o = own(w_o_in, big)
    load_w = own(w_qkv_in, w_qkv)
    core_out = [links.send(out_part.at[block(k), :], o_land.at[k // 2], p.peer_id(1), start=False) for k in odd]
    for i in range(group // 2):
        even[i].wait()
        core[i].come()
        chip[i] = plus(chip[i], c_land[i])
    sums = halves(parts_land)
    next(sums)
    for m in core_out:
        m.start()
    load_gain.wait()
    for _ in sums:
        pass

    per = tile_h.shape[0]
    for r in range(own_rows // per):
        at = pl.ds(r * per, per)
        a, b = own(h_in.at[at, :], tile_h), own(cot_in.at[at, :], tile_c)
        a.wait()
        b.wait()
        h = tile_h[...]
        dn = half_sum[at, :]
        scale = lax.rsqrt(jnp.mean(h * h, axis=-1, keepdims=True) + EPS)
        normed = h * scale
        scaled = dn * gains[1:2, :]
        inner = jnp.mean(scaled * normed, axis=-1, keepdims=True)
        d_h = tile_c[...].astype(F32) + scale * (scaled - normed * inner)
        part = jnp.sum(dn * normed, axis=0, keepdims=True)
        g_sum[0, 0:1, :] = part if r == 0 else g_sum[0, 0:1, :] + part
        dh_low[at, :] = d_h.astype(BF)
        tile_h[...] = d_h
        own(tile_h, dh_keep.at[at, :]).wait()
    own(dh_low, dh_all.at[block(0), :]).wait()

    def dh_part(k, h):
        if h is None:
            return dh_all.at[block(k), :]
        return dh_all.at[pl.ds(k * own_rows + h * half, half), :]

    load_o.wait()
    wo_rows = width // tensor
    for tt in range(tensor):
        acc = jnp.zeros((own_rows, wo_rows), F32)
        for xx in range(ctx):
            left = jnp.concatenate(
                [dh_low[:, (zz * ctx + xx) * d_own : (zz * ctx + xx + 1) * d_own] for zz in range(shards)], axis=1
            )
            acc = acc + mm(left, big[xx * width + tt * wo_rows : xx * width + (tt + 1) * wo_rows, :], NT)
        d_attn[:, tt * wo_rows : (tt + 1) * wo_rows] = acc.astype(BF)

    def heads_of(k):
        xx, tt = p.peer(k)
        return d_attn.at[:, pl.ds(pl.multiple_of((tt * ctx + xx) * cols, cols), cols)]

    swaps = [links.send(heads_of(k), go_rel.at[block(k), :], p.peer_id(k)) for k in range(1, group)]
    own_heads = own(heads_of(0), go_rel.at[block(0), :])
    dh_rows = links.spread(dh_part)
    next(dh_rows)
    load_n = []
    per_n = shards // ctx
    for d in range(shards):
        load_n.append(
            own(
                n_one.at[:, d * dz : (d + 1) * dz],
                big.at[(d // per_n) * rows : (d // per_n + 1) * rows, (d % per_n) * dz : (d % per_n + 1) * dz],
            )
        )
    load_left = own(o_rel_in, d_rel.at[:, 0:cols])

    def output():
        for i in range(group // 2):
            even_copy = own(out_part.at[block(2 * i), :], chip.at[i])
            core_out[i].come()
            land_copy = own(o_land.at[i], stage_own)
            even_copy.wait()
            land_copy.wait()
            chip[i] = plus(chip[i], stage_own[...])
        steps = halves(o_parts, True)
        for _ in steps:
            yield
        for r in range(own_rows // per):
            at = pl.ds(r * per, per)
            own(h_in.at[at, :], tile_h).wait()
            stage_own[at, :] = (tile_h[...] + half_sum[at, :]).astype(BF)
        own(stage_own, result.at[mine(), :]).wait()
        yield from everywhere(result)

    def everywhere(ref):
        def put(k, bit):
            return links.send(ref.at[mine(k), :], ref.at[mine(k), :], p.peer_id(bit), ref.at[mine(k | bit), :])

        cores = [put(0, 1)]
        have = [0]
        for bit in p.bits_y:
            step = [put(k, bit) for k in have]
            yield
            for m in step:
                m.come()
            new = [k | bit for k in have]
            cores += [put(k, 1) for k in new]
            have = have + new
        yield
        for m in cores:
            m.come()

    own_heads.wait()
    for m in swaps:
        m.come()

    def fill(b, carry):
        go[pl.ds(pl.multiple_of(b * BLK, BLK), BLK), :] = picked(go_rel, place_s[b])
        return carry

    lax.fori_loop(0, rows // BLK, fill, 0)
    load_left.wait()
    for k in range(group):
        left_o[:, k * own_rows : (k + 1) * own_rows] = d_rel[k * own_rows : (k + 1) * own_rows, 0:cols].T
    head_row = lax.broadcasted_iota(jnp.int32, (8, cols), 0)
    head_col = lax.broadcasted_iota(jnp.int32, (8, cols), 1) // HDIM
    pick = jnp.where(head_row == head_col, 1.0, 0.0)
    for i in range(rows // QT):
        part = slice(i * QT, (i + 1) * QT)
        both = go[part, :].astype(F32) * os[part, :].astype(F32)
        delta[:, part] = lax.dot_general(pick, both, NT, precision=lax.Precision.HIGHEST, preferred_element_type=F32)
    dq[...] = jnp.zeros_like(dq)
    live = live_s[0]
    tiles = rows // QT

    def store(i, column, value, turned):
        at = slice(i * QT, (i + 1) * QT)
        if turned:
            value = turn(value, wide(cos_ref[at, :], cols), -wide(sin_ref[at, :], cols))
        d_seq[at, column * cols : (column + 1) * cols] = value.astype(BF)

    out_steps = output()

    def grads_o():
        steps = sums_along(g_o, r_o, dq.at[pl.ds(0, cols), :], away_o, got_o, mine_o)
        dh_block = d_rel.at[:, pl.ds(0, dz)]
        for i in range(shards):
            d = far_first(i)
            own(dh_all.at[:, pl.ds(pl.multiple_of(d * dz, dz), dz)], dh_block).wait()
            g_o[d] = mm(left_o[...], d_rel[:, 0:dz]).astype(BF)
            if i < shards - 2:
                next(steps)
                yield
        for _ in steps:
            yield

    def far_first(i):
        down = shards - 1 - i
        down = down - jnp.where(down <= z, 1, 0)
        up = i + jnp.where(i >= z, 1, 0)
        return z if i == shards - 1 else jnp.where(2 * z < shards, down, up)

    def sums_along(g, r, fin, away, got_ref, mine_ref):
        before = [None, None]
        for k in range(1, shards):
            now = []
            for way in (0, 1):
                d = z + shards - k if way == 0 else z - (shards - k)
                came = z + shards - (k + 1) if way == 0 else z - (shards - (k + 1))
                goes = z < k if way == 0 else z >= shards - k
                comes = (z >= 1) & (z <= k) if way == 0 else (z <= shards - 2) & (z >= shards - 1 - k)
                if k > 1:
                    before[way].come()
                    mid = (z >= 1) & (z < k) if way == 0 else (z <= shards - 2) & (z >= shards - k)

                    @pl.when(mid)
                    def _(d=d):
                        g[d] = plus(g[d], r[d])

                last = way == 1 and k == shards - 1
                dst = r.at[shards] if last else r.at[d]
                land = r.at[shards] if last else r.at[came]
                now.append(links.send(g.at[d], dst, p.above() if way == 0 else p.below(), land, goes, comes))
            before = now
            yield
        for m in before:
            m.come()

        def half_of(xx):
            at = pl.ds(pl.multiple_of(xx * d_own, d_own), d_own)
            fin[...] = g[z, :, at].astype(F32)

            @pl.when(z > 0)
            def _():
                fin[...] += r[z, :, at].astype(F32)

            @pl.when(z < shards - 1)
            def _():
                fin[...] += r[shards, :, at].astype(F32)

        half_of(1 - x)
        away[...] = fin[...].astype(BF)
        across = links.send(away, got_ref, p.peer_id(tensor))
        half_of(x)
        keep = own(fin, mine_ref)
        yield
        across.come()
        keep.wait()

    o_steps = None
    next(out_steps)
    for i in range(tiles):
        begin = i * QT

        def head(h, carry):
            dk, dv = carry
            kt = ks[begin : begin + QT, :]
            lane = lax.broadcasted_iota(jnp.int32, (QT, cols), 1) // HDIM
            km = jnp.where(lane == h, kt * BF(0.125), BF(0))
            dead = jnp.where(lax.broadcasted_iota(jnp.int32, (QT, 1), 0) + begin < live, 0.0, NEG)
            for j in range(i, tiles):
                at = slice(j * QT, (j + 1) * QT)
                qm = jnp.where(lane == h, qs[at, :] * BF(0.125), BF(0))
                gm = jnp.where(lane == h, go[at, :], BF(0))
                s = mm(kt, qm, NT) + dead
                if j == i:
                    kpos = lax.broadcasted_iota(jnp.int32, (QT, QT), 0)
                    qpos = lax.broadcasted_iota(jnp.int32, (QT, QT), 1)
                    s = s + jnp.where(kpos <= qpos, 0.0, NEG)
                e = jnp.exp(s - stats[pl.ds(h, 1), at])
                dp = mm(vs[begin : begin + QT, :], gm, NT)
                ds = (e * (dp - delta[pl.ds(h, 1), at])).astype(BF)
                dq[at, :] += mm(ds, km, TN)
                dk = dk + mm(ds, qm)
                dv = dv + mm(e.astype(BF), gm)
            return dk, dv

        zero = jnp.zeros((QT, cols), F32)
        dk, dv = lax.fori_loop(0, heads, head, (zero, zero))
        store(i, 1, dk, True)
        store(i, 2, dv, False)
        store(i, 0, dq[begin : begin + QT, :], True)
        next(out_steps, None)
        if i == 0:
            next(dh_rows, None)
        elif i == 1:
            drain(dh_rows)
            o_steps = grads_o()
            next(o_steps, None)
        else:
            next(o_steps, None)

    def back_to_rows(j, carry):
        dst = pl.ds(pl.multiple_of(j * BLK, BLK), BLK)
        d_rel[dst, :] = picked(d_seq, at_s[j])
        return carry

    lax.fori_loop(0, rows // BLK, back_to_rows, 0)
    drain(out_steps)
    load_w.wait()

    def d_n_one(k):
        return mm(d_rel[k * own_rows : (k + 1) * own_rows, :], w_qkv[...], NT).astype(BF)

    core = []
    for i, k in enumerate(odd):
        chip[i] = d_n_one(k)
        core.append(links.send(chip.at[i], c_land.at[i], p.peer_id(1)))
    next(o_steps, None)
    for k in range(group):
        left_w[:, k * own_rows : (k + 1) * own_rows] = d_rel[k * own_rows : (k + 1) * own_rows, :].T
    for c in load_n:
        c.wait()

    def n_block(d):
        row = pl.ds(pl.multiple_of((d // per_n) * rows, rows), rows)
        return big[row, pl.ds(pl.multiple_of((d % per_n) * dz, dz), dz)]

    w_steps = sums_along(g_w, r_w, dq.at[pl.ds(cols, 3 * cols), :], away_w, got_w, mine_w)

    def grad_w(i):
        d = far_first(i)
        g_w[d] = mm(left_w[...], n_block(d)).astype(BF)

    grad_w(0)
    next(w_steps)
    grad_w(1)
    for i in range(group // 2):
        core[i].sent()
        done_moves.append(core[i])
        core[i].come()
        chip[i] = plus(d_n_one(2 * i), c_land[i])
    sums = halves(parts_land)
    next(sums)
    next(w_steps, None)
    for i in range(2, shards):
        grad_w(i)
        if i < shards - 1:
            next(w_steps, None)
    next(o_steps, None)
    for _ in sums:
        pass
    for r in range(own_rows // per):
        at = pl.ds(r * per, per)
        src = pl.ds(pl.multiple_of(t * own_rows + r * per, per), per)
        a, b = own(dh_keep.at[at, :], tile_h), own(tokens.at[src, :], tile_c)
        a.wait()
        b.wait()
        v = tile_c[...].astype(F32)
        dn = half_sum[at, :]
        scale = lax.rsqrt(jnp.mean(v * v, axis=-1, keepdims=True) + EPS)
        normed = v * scale
        scaled = dn * gains[0:1, :]
        inner = jnp.mean(scaled * normed, axis=-1, keepdims=True)
        stage_own[at, :] = (tile_h[...] + scale * (scaled - normed * inner)).astype(BF)
        part = jnp.sum(dn * normed, axis=0, keepdims=True)
        g_sum[0, 1:2, :] = part if r == 0 else g_sum[0, 1:2, :] + part
    g_sum[0, 2:8, :] = jnp.zeros((6, width), F32)
    own(stage_own, grad_x.at[mine(), :]).wait()
    x_steps = everywhere(grad_x)
    next(x_steps)
    bit, i = 1, 0
    while bit < group:
        m = links.send(g_sum.at[i], g_land.at[i], p.peer_id(bit))
        m.come()
        g_sum[i + 1] = g_sum[i] + g_land[i]
        bit, i = bit * 2, i + 1
    own(g_sum.at[i], g_chain.at[z]).wait()
    g_steps = links.chain(lambda b: [g_chain.at[b]])
    next(g_steps)
    next(w_steps, None)
    next(x_steps, None)
    drain(g_steps)
    total = g_chain[0]
    for b in range(1, shards):
        total = total + g_chain[b]
    g_land[0] = total
    own(g_land.at[0, :, pl.ds(pl.multiple_of((z * ctx + x) * d_own, d_own), d_own)], gain_out).wait()
    drain(o_steps, x_steps, w_steps)
    for m in links.moves:
        if m not in done_moves:
            m.sent()


def last_call(
    shards, ctx, tensor, place, at, live, dn_part, out_part, hidden, cot, tokens, gains, n_one, w_qkv, w_o, o_rel,
    qs, ks, vs, os, stats, cos, sin,
):
    rows, cols = qs.shape
    width = hidden.shape[1]
    own_rows = hidden.shape[0]
    group = ctx * tensor
    d_own = width // (shards * ctx)
    dz = ctx * d_own
    dims = (shards, ctx, tensor, own_rows, d_own)
    any_spec = pl.BlockSpec(memory_space=pl.ANY)
    smem = pl.BlockSpec(memory_space=pltpu.SMEM)
    vmem = pl.BlockSpec(memory_space=pltpu.VMEM)
    dma = pltpu.SemaphoreType.DMA
    half = own_rows // 2
    per = min(64, own_rows)
    bits = group.bit_length() - 1

    def out(shape, kind=BF):
        return jax.ShapeDtypeStruct(shape, kind)

    parts = (2, group // 2 - 1, half, width)
    return pl.pallas_call(
        functools.partial(last_kernel, dims),
        in_specs=[smem] * 3 + [any_spec] * 10 + [vmem] * 7,
        out_specs=[any_spec] * 11,
        out_shape=[
            out((tensor * own_rows, width)),
            out((tensor * own_rows, width)),
            out((cols, d_own), F32),
            out((cols, d_own)),
            out((3 * cols, d_own), F32),
            out((3 * cols, d_own)),
            out((8, d_own), F32),
            out((rows, width)),
            out((own_rows, width), F32),
            out((group // 2, own_rows, width)),
            out(parts),
        ],
        scratch_shapes=[
            pltpu.VMEM((ctx * width, shards * d_own), BF),
            pltpu.VMEM((width, 3 * cols), BF),
            pltpu.VMEM((group // 2, own_rows, width), BF),
            pltpu.VMEM((group // 2, own_rows, width), BF),
            pltpu.VMEM(parts, BF),
            pltpu.VMEM((own_rows, width), BF),
            pltpu.VMEM((per, width), F32),
            pltpu.VMEM((per, width), BF),
            pltpu.VMEM((8, width), F32),
            pltpu.VMEM((own_rows, width), BF),
            pltpu.VMEM((own_rows, width), BF),
            pltpu.VMEM((rows, cols), BF),
            pltpu.VMEM((rows, cols), BF),
            pltpu.VMEM((8, rows), F32),
            pltpu.VMEM((rows, cols), F32),
            pltpu.VMEM((rows, 3 * cols), BF),
            pltpu.VMEM((rows, 3 * cols), BF),
            pltpu.VMEM((cols, rows), BF),
            pltpu.VMEM((3 * cols, rows), BF),
            pltpu.VMEM((shards, cols, dz), BF),
            pltpu.VMEM((shards + 1, cols, dz), BF),
            pltpu.VMEM((shards, 3 * cols, dz), BF),
            pltpu.VMEM((shards + 1, 3 * cols, dz), BF),
            pltpu.VMEM((cols, d_own), BF),
            pltpu.VMEM((3 * cols, d_own), BF),
            pltpu.VMEM((bits + 1, 8, width), F32),
            pltpu.VMEM((bits, 8, width), F32),
            pltpu.VMEM((shards, 8, width), F32),
            pltpu.VMEM((own_rows, width), F32),
            dma((300,)),
            dma((300,)),
            dma((100,)),
        ],
        compiler_params=pltpu.CompilerParams(
            collective_id=2, has_side_effects=True, vmem_limit_bytes=63 * 1024 * 1024
        ),
        cost_estimate=pl.CostEstimate(
            flops=2 * rows * width * cols * 8, bytes_accessed=64 * 1024 * 1024, transcendentals=rows * rows * cols // HDIM
        ),
        name="last",
    )(place, at, live, dn_part, out_part, hidden, cot, tokens, gains, n_one, w_qkv, w_o, o_rel, qs, ks, vs, os, stats, cos, sin)


def per_device(
    shards, ctx, tensor, tokens, cotangent, seq_len, block_slot, attn_gain, w_query, w_key, w_value, w_out, mlp_gain, w_gate, w_up, w_down
):
    group = ctx * tensor
    my_x = lax.axis_index("ctx")
    my_t = lax.axis_index("tensor")
    me = my_x * tensor + my_t
    width = tokens.shape[1]
    own_rows = tokens.shape[0] // tensor
    level_rows = own_rows * group
    slots_each = own_rows // BLK
    d_own = w_query.shape[0]
    cols = w_query.shape[1] // ctx
    ff = w_gate.shape[1] // ctx
    slot = block_slot[0]
    place = ((slot // slots_each) ^ me) * slots_each + slot % slots_each
    order = jnp.arange(slot.shape[0], dtype=jnp.int32)
    at = jnp.sum(jnp.where(place[:, None] == order[None, :], order[:, None], 0), axis=0).astype(jnp.int32)

    def x_join(mine, got, axis):
        return jnp.where(
            my_x == 0, jnp.concatenate([mine, got], axis=axis), jnp.concatenate([got, mine], axis=axis)
        )

    angle_at = jnp.arange(level_rows, dtype=F32)
    lane = jnp.arange(128)
    freqs = THETA ** (-(lane % (HDIM // 2)).astype(F32) / (HDIM // 2))
    angles = angle_at[:, None] * freqs[None, :]
    cos = jnp.cos(angles)
    sin = jnp.sin(angles) * jnp.where(lane % HDIM < HDIM // 2, -1.0, 1.0)
    at_pos = (at[:, None] * BLK + jnp.arange(BLK)[None, :]).reshape(-1).astype(F32)
    angles = at_pos[:, None] * freqs[None, :]
    cos_rel = jnp.cos(angles)
    sin_rel = jnp.sin(angles) * jnp.where(lane % HDIM < HDIM // 2, -1.0, 1.0)
    gains = jnp.concatenate([jnp.stack([attn_gain, mlp_gain], axis=0).astype(F32), jnp.zeros((6, d_own), F32)], axis=0)
    n_one, w_qkv, w_o, cot, gu_pre, d_pre, n_two_own, hidden_res, gains, qs, ks, vs, os, stats, o_slot = first_call(
        shards, ctx, tensor, place.astype(jnp.int32), at, seq_len, tokens, cotangent, gains,
        w_query, w_key, w_value, w_out, w_gate, w_up, w_down, cos_rel, sin_rel,
    )
    dn_part, out_part, ff_mine, ff_got, _, _ = mlp_call(
        shards, ctx, tensor, n_two_own, cot, w_gate, w_up, w_down, gu_pre, d_pre
    )

    result, grad_x, mine_o, got_o, mine_w, got_w, gain_sums, _, _, _, _ = last_call(
        shards, ctx, tensor, place.astype(jnp.int32), at, seq_len, dn_part, out_part, hidden_res, cot, tokens, gains,
        n_one, w_qkv, w_o.reshape(ctx * width, shards * d_own), o_slot, qs, ks, vs, os, stats, cos, sin,
    )
    chunks = ff_mine.shape[0]
    fc = ff // chunks
    mine = ff_mine.reshape(chunks, 3, fc, d_own)
    got = ff_got.reshape(chunks, 3, fc, d_own).astype(F32)

    def spread(i):
        return x_join(mine[:, i].reshape(ff, d_own), got[:, i].reshape(ff, d_own), 0)

    grad_down = spread(0)
    grad_gate = spread(1).T
    grad_up = spread(2).T

    grad_out = x_join(mine_o, got_o.astype(F32), 0)
    mine = mine_w.reshape(3, cols, d_own)
    got = got_w.reshape(3, cols, d_own).astype(F32)
    grad_q, grad_k, grad_v = (x_join(mine[i], got[i], 0).T for i in range(3))
    grad_gain_two, grad_gain_one = gain_sums[0], gain_sums[1]
    return (
        result,
        grad_x,
        grad_gain_one,
        grad_q,
        grad_k,
        grad_v,
        grad_out,
        grad_gain_two,
        grad_gate,
        grad_up,
        grad_down,
    )


def solution(mesh):
    rows = P(("shard", "ctx"), None)
    gain = P(("shard", "ctx"))
    into = P(("shard", "ctx"), "tensor")
    back = P("tensor", ("shard", "ctx"))
    sizes = mesh.shape
    return jax.shard_map(
        functools.partial(per_device, sizes["shard"], sizes["ctx"], sizes["tensor"]),
        mesh=mesh,
        in_specs=(rows, rows, P("shard"), P("shard", None), gain, into, into, into, back, gain, into, into, back),
        out_specs=(rows, rows, gain, into, into, into, back, gain, into, into, back),
        check_vma=False,
    )
```

```python
import functools

import jax
import jax.numpy as jnp
from jax import lax
from jax.experimental import pallas as pl
from jax.experimental.pallas import tpu as pltpu
from jax.sharding import PartitionSpec as P

HDIM = 64
BLK = 128
EPS = 1e-05
THETA = 130000.0
NEG = -1e30
LEVEL = ("ctx", "tensor")
BF = jnp.bfloat16
F32 = jnp.float32
QT = 512
PRE = 2

NT = (((1,), (1,)), ((), ()))
TN = (((0,), (0,)), ((), ()))


def mm(left, right, dims=None):
    if dims is None:
        return jnp.dot(left, right, preferred_element_type=F32)
    return lax.dot_general(left, right, dims, preferred_element_type=F32)


def level_bits(ctx, tensor):
    bits_y = []
    bit = 2
    while bit < tensor:
        bits_y.append(bit)
        bit *= 2
    bits_x = []
    bit = tensor
    while bit < ctx * tensor:
        bits_x.append(bit)
        bit *= 2
    return bits_y, bits_x


def plus(a, b):
    return (a.astype(F32) + b.astype(F32)).astype(BF)


def turn(u, cos, sin):
    lane = lax.broadcasted_iota(jnp.int32, u.shape, 1)
    width = u.shape[1]
    ahead = pltpu.roll(u, width - HDIM // 2, axis=1)
    behind = pltpu.roll(u, HDIM // 2, axis=1)
    other = jnp.where(lane % HDIM < HDIM // 2, ahead, behind)
    return u * cos + other * sin


def wide(table, cols):
    reps = cols // table.shape[1]
    return jnp.concatenate([table] * reps, axis=1) if reps > 1 else table


def flip(index, bit):
    return index + bit - 2 * bit * ((index // bit) % 2)


class Place:
    def __init__(self, shards, ctx, tensor):
        self.shards, self.ctx, self.tensor = shards, ctx, tensor
        self.group = ctx * tensor
        self.z = lax.axis_index("shard")
        self.x = lax.axis_index("ctx")
        self.t = lax.axis_index("tensor")
        self.bits_y, self.bits_x = level_bits(ctx, tensor)

    def peer(self, offset):
        t, x = self.t, self.x
        bit = 1
        while bit < self.group:
            if offset & bit:
                if bit < self.tensor:
                    t = flip(t, bit)
                else:
                    x = 1 - x
            bit *= 2
        return x, t

    def peer_id(self, offset):
        x, t = self.peer(offset)
        return (self.z, x, t)

    def above(self):
        return (self.z + 1, self.x, self.t)

    def below(self):
        return (self.z - 1, self.x, self.t)

    def meet(self, offsets, chain=True):
        barrier = pltpu.get_barrier_semaphore()
        z, shards = self.z, self.shards
        for k in offsets:
            pl.semaphore_signal(barrier, inc=1, device_id=self.peer_id(k), device_id_type=pl.DeviceIdType.MESH)
        peers = len(offsets)
        if chain:

            @pl.when(z < shards - 1)
            def _():
                pl.semaphore_signal(barrier, inc=1, device_id=self.above(), device_id_type=pl.DeviceIdType.MESH)

            @pl.when(z > 0)
            def _():
                pl.semaphore_signal(barrier, inc=1, device_id=self.below(), device_id_type=pl.DeviceIdType.MESH)

            peers = peers + (z + shards - 1) // shards + (2 * shards - 2 - z) // shards
        pl.semaphore_wait(barrier, peers)


class Move:
    def __init__(self, out, due, goes, comes, place=None):
        self.out, self.due, self.goes, self.comes, self.place = out, due, goes, comes, place

    def _run(self, cond, fn):
        if cond is None:
            fn()
        else:
            pl.when(cond)(fn)

    def start(self):
        self._run(self.goes, self.out.start)

    def come(self):
        self._run(self.comes, self.due.wait_recv)

    def sent(self):
        self._run(self.goes, self.out.wait_send)


class Links:
    def __init__(self, place, send_sems, recv_sems):
        self.place, self.send_sems, self.recv_sems = place, send_sems, recv_sems
        self.moves = []

    def send(self, src, dst, where, land=None, goes=None, comes=None, start=True):
        i = len(self.moves)
        land = dst if land is None else land
        safe = self.place.peer_id(1)

        def copy(a, b, w):
            return pltpu.make_async_remote_copy(
                src_ref=a,
                dst_ref=b,
                send_sem=self.send_sems.at[i],
                recv_sem=self.recv_sems.at[i],
                device_id=w,
                device_id_type=pl.DeviceIdType.MESH,
            )

        move = Move(copy(src, dst, where), copy(land, land, safe), goes, comes, i)
        self.moves.append(move)
        if start:
            move.start()
        return move

    def all_sent(self):
        for m in self.moves:
            m.sent()


    def chain(self, parts):
        p = self.place
        z, shards = p.z, p.shards
        due = []
        for k in range(1, shards):
            for m in due:
                m.come()
            due = []
            up = zip(parts(z - (k - 1)), parts(z - k))
            for src, land in up:
                due.append(self.send(src, src, p.above(), land, (z >= k - 1) & (z < shards - 1), z >= k))
            down = zip(parts(z + (k - 1)), parts(z + k))
            for src, land in down:
                due.append(
                    self.send(src, src, p.below(), land, (z + k - 1 <= shards - 1) & (z > 0), z + k <= shards - 1)
                )
            yield
        for m in due:
            m.come()

    def spread(self, part, absolute=False):
        p = self.place

        def put(k, bit, h):
            return self.send(part(k, h), part(k if absolute else k | bit, h), p.peer_id(bit), part(k | bit, h))

        cores = [put(0, 1, None)]
        have = [[0], [0]]
        found = {}
        orders = [p.bits_x + p.bits_y, p.bits_y + p.bits_x]
        for stage in range(len(orders[0])):
            step = []
            for h in (0, 1):
                bit = orders[h][stage]
                step += [(k | bit, put(k, bit, h)) for k in have[h]]
                have[h] = have[h] + [k | bit for k in have[h]]
            yield
            for k, m in step:
                m.come()
                found[k] = found.get(k, 0) + 1
                if found[k] == 2:
                    cores.append(put(k, 1, None))
        yield
        for m in cores:
            m.come()

    def rows(self, source, keep, own_rows, log):
        p = self.place

        def slot(k):
            return keep.at[pl.ds(k * own_rows, own_rows), :]

        mine = source.at[pl.ds(pl.multiple_of(p.t * own_rows, own_rows), own_rows), :]
        first = self.send(mine, slot(p.tensor), p.peer_id(p.tensor))
        log.append(first)
        yield
        first.come()
        far = [p.tensor]
        for bit in p.bits_y:
            step = [self.send(slot(k), slot(k | bit), p.peer_id(bit)) for k in far]
            log += step
            yield
            for m in step:
                m.come()
            far = far + [k | bit for k in far]
        last = [self.send(slot(k), slot(k | 1), p.peer_id(1)) for k in far]
        log += last
        yield
        for m in last:
            m.come()


def drain(*gens):
    for g in gens:
        for _ in g:
            pass


def first_kernel(
    dims, place_s, at_s, live_s, tokens, cotangent, gains_in, wq, wk, wv, w_out, wg, wu, wd, cos_ref, sin_ref,
    n_one_out, w_qkv_out, w_o_out, cot_out, gu_out, d_out, n_own_out, h_out, gains, qs, ks, vs, os, stats, o_rel,
    n_one, w_qkv, w_o, qkv_rel, attn_rows, h_own, n_own, x_keep, gu_v, d_v,
    send_sems, recv_sems, own_sems,
):
    shards, ctx, tensor, fc, own_rows, d_own = dims
    p = Place(shards, ctx, tensor)
    z, x, t = p.z, p.x, p.t
    group = p.group
    rows, width = n_one.shape
    cols = qs.shape[1]
    heads = cols // HDIM
    ff = wg.shape[1] // ctx
    dz = ctx * d_own
    links = Links(p, send_sems, recv_sems)
    own_count = [0]

    def own(src, dst):
        i = own_count[0]
        own_count[0] += 1
        c = pltpu.make_async_copy(src, dst, own_sems.at[i])
        c.start()
        return c

    p.meet(list(range(1, group)))

    def d_at(xx):
        return pl.ds(pl.multiple_of((z * ctx + xx) * d_own, d_own), d_own)

    def z_at(b):
        return pl.ds(pl.multiple_of(b * dz, dz), dz)

    def part_cols(xx, size):
        return pl.ds(pl.multiple_of(xx * size, size), size)

    across = p.peer_id(tensor)

    wo_rows = w_out.shape[0]

    def o_at(tt, xx, zz):
        return w_o.at[xx, pl.ds(pl.multiple_of(tt * wo_rows, wo_rows), wo_rows), pl.ds(pl.multiple_of(zz * d_own, d_own), d_own)]

    own_o = own(w_out, o_at(t, x, z))
    own_gain = own(gains_in, gains.at[:, d_at(x)])
    own_w = [own(w.at[:, part_cols(x, cols)], w_qkv.at[d_at(x), i * cols : (i + 1) * cols]) for i, w in enumerate((wq, wk, wv))]
    own_gain.wait()
    gain_x = links.send(gains.at[:, d_at(x)], gains.at[:, d_at(x)], across, gains.at[:, d_at(1 - x)])
    qkv_x = [
        links.send(
            w.at[:, part_cols(1 - x, cols)],
            w_qkv.at[d_at(x), i * cols : (i + 1) * cols],
            across,
            w_qkv.at[d_at(1 - x), i * cols : (i + 1) * cols],
        )
        for i, w in enumerate((wq, wk, wv))
    ]
    tok_log = []
    tok_rows = links.rows(tokens, n_one, own_rows, tok_log)
    next(tok_rows)
    own_tok = []
    for k in range(tensor):
        _, tt = p.peer(k)
        src = tokens.at[pl.ds(pl.multiple_of(tt * own_rows, own_rows), own_rows), :]
        own_tok.append(own(src, n_one.at[pl.ds(k * own_rows, own_rows), :]))
    own_o.wait()
    o_chain = links.chain(lambda b: [o_at(t, x, b)])
    next(o_chain)
    gain_x.come()
    gain_chain = links.chain(lambda b: [gains.at[:, z_at(b)]])
    next(gain_chain)
    next(o_chain, None)
    for c in own_w:
        c.wait()
    for m in qkv_x:
        m.come()
    next(gain_chain, None)
    qkv_chain = links.chain(lambda b: [w_qkv.at[z_at(b), :]])
    next(qkv_chain)

    gu_pairs = [(wg, 0), (wu, 1)]

    def gu_place(c, xx, i):
        return gu_v.at[c, d_at(xx), i * fc : (i + 1) * fc]

    def ff_begin(c):
        at = [pl.ds(pl.multiple_of(xx * ff + c * fc, fc), fc) for xx in (x, 1 - x)]
        d_rows = slice(c * fc, (c + 1) * fc)
        mine = [own(w.at[:, at[0]], gu_place(c, x, i)) for w, i in gu_pairs]
        mine.append(own(wd.at[at[0], :], d_v.at[d_rows, d_at(x)]))
        came = [links.send(w.at[:, at[1]], gu_place(c, x, i), across, gu_place(c, 1 - x, i)) for w, i in gu_pairs]
        came.append(links.send(wd.at[at[1], :], d_v.at[d_rows, d_at(x)], across, d_v.at[d_rows, d_at(1 - x)]))
        return mine, came

    def ff_moves():
        running = []
        for c in range(PRE + shards):
            if c < PRE:
                mine, came = begun[c]
                for m in mine:
                    m.wait()
                for m in came:
                    m.come()
                running.append(links.chain(lambda b, c=c: [gu_v.at[c, z_at(b), :], d_v.at[c * fc : (c + 1) * fc, z_at(b)]]))
            for g in running:
                next(g, None)
            yield

    begun = [ff_begin(0)]
    drain(gain_chain)
    drain(o_chain)
    for c in own_tok:
        c.wait()
    x_keep[...] = n_one[0:own_rows, :]
    next(tok_rows, None)

    def o_part(k, h):
        xx, tt = p.peer(k)
        size = wo_rows if h is None else wo_rows // 2
        start = tt * wo_rows + (0 if h is None else h * size)
        return w_o.at[xx, pl.ds(pl.multiple_of(start, size), size), :]

    o_spread = links.spread(o_part, absolute=True)
    next(o_spread)

    def norm(r, carry):
        at = pl.ds(pl.multiple_of(r * own_rows, own_rows), own_rows)
        v = n_one[at, :].astype(F32)
        scale = lax.rsqrt(jnp.mean(v * v, axis=-1, keepdims=True) + EPS)
        n_one[at, :] = (v * scale * gains[0:1, :]).astype(BF)
        return carry

    next(qkv_chain, None)
    lax.fori_loop(0, tensor, norm, 0)
    next(tok_rows, None)
    next(qkv_chain, None)
    for c in range(1, PRE):
        begun.append(ff_begin(c))
    ff_chain = ff_moves()
    next(ff_chain)
    drain(tok_rows)
    for m in tok_log:
        m.sent()
    lax.fori_loop(tensor, group, norm, 0)
    out_n = own(n_one, n_one_out)
    next(o_spread, None)
    drain(qkv_chain)
    next(ff_chain, None)
    out_w = own(w_qkv, w_qkv_out)

    def project(r, carry):
        at = pl.ds(pl.multiple_of(r * own_rows, own_rows), own_rows)
        lin = mm(n_one[at, :], w_qkv[...])
        per = own_rows // BLK
        for i in range(per):
            where = pl.ds(pl.multiple_of(r * own_rows + i * BLK, BLK), BLK)
            cos, sin = wide(cos_ref[where, :], cols), wide(sin_ref[where, :], cols)
            part = lin[i * BLK : (i + 1) * BLK, :]
            dst = pl.ds(pl.multiple_of(r * own_rows + i * BLK, BLK), BLK)
            qkv_rel[dst, 0:cols] = turn(part[:, 0:cols], cos, sin).astype(BF)
            qkv_rel[dst, cols : 2 * cols] = turn(part[:, cols : 2 * cols], cos, sin).astype(BF)
            qkv_rel[dst, 2 * cols : 3 * cols] = part[:, 2 * cols : 3 * cols].astype(BF)
        return carry

    lax.fori_loop(0, group, project, 0)
    next(o_spread, None)

    def fill(b, carry):
        dst = pl.ds(pl.multiple_of(b * BLK, BLK), BLK)
        found = picked(qkv_rel, place_s[b])
        qs[dst, :] = found[:, 0:cols]
        ks[dst, :] = found[:, cols : 2 * cols]
        vs[dst, :] = found[:, 2 * cols : 3 * cols]
        return carry

    lax.fori_loop(0, rows // BLK, fill, 0)
    cot_rows = links.rows(cotangent, cot_out, own_rows, [])
    next(cot_rows)
    live = live_s[0]
    for tile in range(rows // QT):
        attend_tile(tile, live, qs, ks, vs, os, stats)
        next(ff_chain, None)
        next(o_spread, None)
        next(cot_rows, None)

    def back_to_rows(j, carry):
        dst = pl.ds(pl.multiple_of(j * BLK, BLK), BLK)
        o_rel[dst, :] = picked(os, at_s[j])
        return carry

    lax.fori_loop(0, rows // BLK, back_to_rows, 0)

    def head_at(k):
        xx, tt = p.peer(k)
        return attn_rows.at[:, pl.ds(pl.multiple_of((tt * ctx + xx) * cols, cols), cols)]

    swaps = [
        links.send(o_rel.at[pl.ds(k * own_rows, own_rows), :], head_at(0), p.peer_id(k), head_at(k)) for k in range(1, group)
    ]
    own_heads = own(o_rel.at[pl.ds(0, own_rows), :], head_at(0))
    drain(o_spread)
    out_o = own(w_o, w_o_out)
    own_heads.wait()
    for m in swaps:
        m.come()
    for xx in range(ctx):
        span = shards * d_own
        mixed = mm(attn_rows[...], w_o[xx])
        for zz in range(shards):
            at = slice((zz * ctx + xx) * d_own, (zz * ctx + xx + 1) * d_own)
            h_own[:, at] = x_keep[:, at].astype(F32) + mixed[:, zz * d_own : (zz + 1) * d_own]
    h = h_own[...]
    scale = lax.rsqrt(jnp.mean(h * h, axis=-1, keepdims=True) + EPS)
    n_own[...] = (h * scale * gains[1:2, :]).astype(BF)
    out_h = own(h_own, h_out)
    out_own = own(n_own, n_own_out)
    drain(ff_chain)
    out_gu = own(gu_v, gu_out)
    out_d = own(d_v, d_out)
    drain(cot_rows)
    for m in links.moves:
        if m not in tok_log:
            m.sent()
    for c in (out_n, out_w, out_o, out_h, out_own, out_gu, out_d):
        c.wait()


def picked(ref, block):
    found = ref[0:BLK, :]
    for j in range(1, ref.shape[0] // BLK):
        found = jnp.where(block == j, ref[j * BLK : (j + 1) * BLK, :], found)
    return found


def attend_tile(t, live, qs, ks, vs, os, stats):
    rows, cols = qs.shape
    heads = cols // HDIM
    ext = (t + 1) * QT
    lane = lax.broadcasted_iota(jnp.int32, (QT, cols), 1) // HDIM
    qpos = lax.broadcasted_iota(jnp.int32, (QT, QT), 0)
    kpos = lax.broadcasted_iota(jnp.int32, (QT, QT), 1)
    diag = jnp.where(kpos <= qpos, 0.0, NEG)
    dead = jnp.where(lax.broadcasted_iota(jnp.int32, (1, ext), 1) < live, 0.0, NEG)

    def head(h, acc):
        q = jnp.where(lane == h, qs[t * QT : ext, :] * BF(0.125), BF(0))
        s = mm(q, ks[0:ext, :], NT) + dead
        last = s[:, t * QT :] + diag
        s = jnp.concatenate([s[:, : t * QT], last], axis=1) if t else last
        top = jnp.max(s, axis=1, keepdims=True)
        e = jnp.exp(s - top)
        total = jnp.sum(e, axis=1, keepdims=True)
        mixed = mm(e.astype(BF), vs[0:ext, :]) / total
        note = jnp.broadcast_to(top + jnp.log(total), (QT, 128))
        stats[pl.ds(h, 1), t * QT : ext] = jnp.transpose(note)[0:1, :]
        return jnp.where(lane == h, mixed, acc)

    acc = lax.fori_loop(0, heads, head, jnp.zeros((QT, cols), F32))
    os[t * QT : ext, :] = acc.astype(BF)


def first_call(shards, ctx, tensor, place, at, live, tokens, cotangent, gains, wq, wk, wv, w_out, wg, wu, wd, cos, sin):
    width = tokens.shape[1]
    own_rows = tokens.shape[0] // tensor
    group = ctx * tensor
    rows = own_rows * group
    d_own = wq.shape[0]
    cols = wq.shape[1] // ctx
    fc = cols
    dims = (shards, ctx, tensor, fc, own_rows, d_own)
    any_spec = pl.BlockSpec(memory_space=pl.ANY)
    smem = pl.BlockSpec(memory_space=pltpu.SMEM)
    vmem = pl.BlockSpec(memory_space=pltpu.VMEM)
    piece = jax.ShapeDtypeStruct((rows, cols), BF)
    moves = 400
    dma = pltpu.SemaphoreType.DMA
    return pl.pallas_call(
        functools.partial(first_kernel, dims),
        in_specs=[smem] * 3 + [any_spec] * 10 + [vmem] * 2,
        out_specs=[any_spec] * 8 + [vmem] * 7,
        out_shape=[
            jax.ShapeDtypeStruct((rows, width), BF),
            jax.ShapeDtypeStruct((width, 3 * cols), BF),
            jax.ShapeDtypeStruct((ctx, width, shards * d_own), BF),
            jax.ShapeDtypeStruct((rows, width), BF),
            jax.ShapeDtypeStruct((PRE, width, 2 * fc), BF),
            jax.ShapeDtypeStruct((PRE * fc, width), BF),
            jax.ShapeDtypeStruct((own_rows, width), BF),
            jax.ShapeDtypeStruct((own_rows, width), F32),
            jax.ShapeDtypeStruct((8, width), F32),
            piece,
            piece,
            piece,
            piece,
            jax.ShapeDtypeStruct((8, rows), F32),
            piece,
        ],
        scratch_shapes=[
            pltpu.VMEM((rows, width), BF),
            pltpu.VMEM((width, 3 * cols), BF),
            pltpu.VMEM((ctx, width, shards * d_own), BF),
            pltpu.VMEM((rows, 3 * cols), BF),
            pltpu.VMEM((own_rows, width), BF),
            pltpu.VMEM((own_rows, width), F32),
            pltpu.VMEM((own_rows, width), BF),
            pltpu.VMEM((own_rows, width), BF),
            pltpu.VMEM((PRE, width, 2 * fc), BF),
            pltpu.VMEM((PRE * fc, width), BF),
            dma((moves,)),
            dma((moves,)),
            dma((40,)),
        ],
        compiler_params=pltpu.CompilerParams(
            collective_id=0, has_side_effects=True, vmem_limit_bytes=62 * 1024 * 1024
        ),
        cost_estimate=pl.CostEstimate(
            flops=2 * rows * width * cols * 4, bytes_accessed=64 * 1024 * 1024, transcendentals=rows * rows * cols // HDIM
        ),
        name="first",
    )(place, at, live, tokens, cotangent, gains, wq, wk, wv, w_out, wg, wu, wd, cos, sin)


def mlp_kernel(
    dims, n_own, cot_far, cotangent, wg, wu, wd, gu_pre, d_pre,
    dn_out, out_out, mine_out, got_out, g_hbm, r_hbm,
    n2, cot, wgu_v, wd_v, hid, dgu, left_t, gt, st, ost, fin, away,
    lev_send, lev_recv, x_own, x_send, x_recv, a_send, a_recv, g_sem, s_sem, rs_send, rs_recv, fx_send, fx_recv, o_sem, c_sem,
):
    shards, ctx, tensor, chunks, kept, fc, rows_own, d_own = dims
    rows, width = n2.shape
    dz = ctx * d_own
    ff = chunks * fc
    z = lax.axis_index("shard")
    x = lax.axis_index("ctx")
    t = lax.axis_index("tensor")
    bits_y, bits_x = level_bits(ctx, tensor)

    p = Place(shards, ctx, tensor)
    above, below = p.above, p.below
    p.meet([1] + bits_y + bits_x)

    here_too = (z, x, flip(t, 1))

    def remote(src, dst, send, recv, where):
        return pltpu.make_async_remote_copy(
            src_ref=src, dst_ref=dst, send_sem=send, recv_sem=recv, device_id=where, device_id_type=pl.DeviceIdType.MESH
        )

    def x_copies(c, own):
        half = x if own else 1 - x
        low_c = pl.multiple_of(half * ff + c * fc, fc)
        d_at = pl.ds(pl.multiple_of((z * ctx + x) * d_own, d_own), d_own)
        pairs = [
            (wg.at[:, pl.ds(low_c, fc)], wgu_v.at[c, d_at, pl.ds(0, fc)]),
            (wu.at[:, pl.ds(low_c, fc)], wgu_v.at[c, d_at, pl.ds(fc, fc)]),
            (wd.at[pl.ds(low_c, fc), :], wd_v.at[pl.ds(pl.multiple_of(c * fc, fc), fc), d_at]),
        ]
        if own:
            return [pltpu.make_async_copy(a, b, x_own.at[c, i]) for i, (a, b) in enumerate(pairs)]
        return [remote(a, b, x_send.at[c, i], x_recv.at[c, i], (z, 1 - x, t)) for i, (a, b) in enumerate(pairs)]

    def x_landed(c):
        d_at = pl.ds(pl.multiple_of((z * ctx + 1 - x) * d_own, d_own), d_own)
        lands = [
            wgu_v.at[c, d_at, pl.ds(0, fc)],
            wgu_v.at[c, d_at, pl.ds(fc, fc)],
            wd_v.at[pl.ds(pl.multiple_of(c * fc, fc), fc), d_at],
        ]
        return [remote(a, a, x_send.at[c, i], x_recv.at[c, i], here_too) for i, a in enumerate(lands)]

    def hop(c, way, k, b, wait=False):
        at = pl.ds(pl.multiple_of(b * dz, dz), dz)
        parts = [wgu_v.at[c, at, :], wd_v.at[pl.ds(pl.multiple_of(c * fc, fc), fc), at]]
        where = here_too if wait else above() if way == 0 else below()
        return [remote(p, p, a_send.at[c, way, k, i], a_recv.at[c, way, k, i], where) for i, p in enumerate(parts)]

    def hop_start(c, k):
        @pl.when((z >= k - 1) & (z < shards - 1))
        def _():
            for d in hop(c, 0, k - 1, z - (k - 1)):
                d.start()

        @pl.when((z + k - 1 <= shards - 1) & (z > 0))
        def _():
            for d in hop(c, 1, k - 1, z + (k - 1)):
                d.start()

    def hop_sent(c, k):
        @pl.when((z >= k - 1) & (z < shards - 1))
        def _():
            for d in hop(c, 0, k - 1, z - (k - 1)):
                d.wait_send()

        @pl.when((z + k - 1 <= shards - 1) & (z > 0))
        def _():
            for d in hop(c, 1, k - 1, z + (k - 1)):
                d.wait_send()

    def hop_wait(c, k):
        @pl.when(z >= k)
        def _():
            for d in hop(c, 0, k - 1, z - k, True):
                d.wait_recv()

        @pl.when(z + k <= shards - 1)
        def _():
            for d in hop(c, 1, k - 1, z + k, True):
                d.wait_recv()

    def x_start(c):
        for d in x_copies(c, False):
            d.start()
        for d in x_copies(c, True):
            d.start()

    if chunks > PRE:
        x_start(PRE)
    pre_copies = [
        pltpu.make_async_copy(gu_pre, wgu_v.at[pl.ds(0, PRE)], x_own.at[0, 0]),
        pltpu.make_async_copy(d_pre, wd_v.at[pl.ds(0, PRE * fc), :], x_own.at[0, 1]),
    ]
    for d in pre_copies:
        d.start()

    half = rows_own // 2
    links = Links(p, lev_send, lev_recv)
    near = tensor * rows_own
    cot_copies = [pltpu.make_async_copy(cot_far.at[pl.ds(near, near), :], cot.at[pl.ds(near, near), :], c_sem.at[0])]
    for k in range(tensor):
        _, tt = p.peer(k)
        src = cotangent.at[pl.ds(pl.multiple_of(tt * rows_own, rows_own), rows_own), :]
        cot_copies.append(pltpu.make_async_copy(src, cot.at[pl.ds(k * rows_own, rows_own), :], c_sem.at[3 + k]))
    own_copy = pltpu.make_async_copy(n_own, n2.at[pl.ds(0, rows_own), :], c_sem.at[1])
    own_copy.start()
    own_copy.wait()

    def n_part(k, h):
        if h is None:
            return n2.at[pl.ds(k * rows_own, rows_own), :]
        return n2.at[pl.ds(k * rows_own + h * half, half), :]

    n_rows = links.spread(n_part)
    next(n_rows)
    for d in cot_copies:
        d.start()
    for c in range(PRE + 1, chunks):
        x_start(c)
    if chunks > PRE:
        for d in x_copies(PRE, True):
            d.wait()
        for d in x_landed(PRE):
            d.wait_recv()
        hop_start(PRE, 1)
    next(n_rows)

    def ag_round(r, top):
        for k in range(shards - 1, 0, -1):
            if k > top:
                continue
            c = r - k + 1

            @pl.when((c >= PRE) & (c < chunks))
            def _(c=c, k=k):
                if k == 1:
                    for d in x_copies(c, True):
                        d.wait()
                    for d in x_landed(c):
                        d.wait_recv()
                else:
                    hop_wait(c, k - 1)
                hop_start(c, k)

    for r in range(PRE + 1, shards):
        ag_round(jnp.int32(r), shards - 1)
    drain(n_rows)
    for d in cot_copies:
        d.wait()
    for d in pre_copies:
        d.wait()

    def block_of(i):
        down = shards - 1 - i
        down = down - jnp.where(down <= z, 1, 0)
        up = i + jnp.where(i >= z, 1, 0)
        return jnp.where(i == shards - 1, z, jnp.where(2 * z < shards, down, up))

    def g_copy(c, d, slot):
        return pltpu.make_async_copy(gt.at[slot], g_hbm.at[c, d], g_sem.at[slot])

    def rs_send_copy(src, c, way, d, wait=False):
        where = here_too if wait else above() if way == 0 else below()
        return remote(src, r_hbm.at[c, way, d], rs_send.at[c, way, d], rs_recv.at[c, way, d], where)

    combos = [(way, k) for k in range(2, shards) for way in (0, 1)]

    def target(way, k):
        return z + shards - k if way == 0 else z - (shards - k)

    def sends(way, k):
        if way == 0:
            return z < k
        return z >= shards - k

    def starts(way):
        return z == 0 if way == 0 else z == shards - 1

    def runs(way):
        return z != 0 if way == 0 else z != shards - 1

    def at_slot(first):
        return first // 2, (first >= 0) & (first % 2 == 0) & (first // 2 < kept)

    def rs_step(s):
        for way in (0, 1):
            for k in range(1, shards):
                c, due = at_slot(s - (k - 1))

                @pl.when(due & starts(way))
                def _(c=c, way=way, k=k):
                    d = target(way, k)
                    rs_send_copy(g_hbm.at[c, d], c, way, d).start()

        for i, (way, k) in enumerate(combos):
            c, due = at_slot(s - (k - 1))

            @pl.when(due & sends(way, k) & runs(way))
            def _(c=c, way=way, k=k, i=i):
                d = target(way, k)

                @pl.when(c >= 1)
                def _():
                    rs_send_copy(st.at[2 * i], c - 1, way, d).wait_send()

                rs_send_copy(st.at[2 * i], c, way, d, True).wait_recv()
                pltpu.make_async_copy(g_hbm.at[c, d], st.at[2 * i], s_sem.at[2 * i]).start()
                pltpu.make_async_copy(r_hbm.at[c, way, d], st.at[2 * i + 1], s_sem.at[2 * i + 1]).start()

        last = 2 * len(combos)
        c_fin, due_fin = at_slot(s - (shards - 1))

        @pl.when(due_fin)
        def _():
            pltpu.make_async_copy(g_hbm.at[c_fin, z], st.at[last], s_sem.at[last]).start()
            for way in (0, 1):
                slot = last + 1 + way

                @pl.when(runs(way))
                def _(way=way, slot=slot):
                    rs_send_copy(st.at[slot], c_fin, way, z, True).wait_recv()
                    pltpu.make_async_copy(r_hbm.at[c_fin, way, z], st.at[slot], s_sem.at[slot]).start()

                @pl.when(starts(way))
                def _(slot=slot):
                    st[slot] = jnp.zeros(st.shape[1:], BF)

        for i, (way, k) in enumerate(combos):
            c, due = at_slot(s - (k - 1))

            @pl.when(due & sends(way, k) & runs(way))
            def _(c=c, way=way, k=k, i=i):
                d = target(way, k)
                pltpu.make_async_copy(g_hbm.at[c, d], st.at[2 * i], s_sem.at[2 * i]).wait()
                pltpu.make_async_copy(r_hbm.at[c, way, d], st.at[2 * i + 1], s_sem.at[2 * i + 1]).wait()
                st[2 * i] = (st[2 * i].astype(F32) + st[2 * i + 1].astype(F32)).astype(BF)
                rs_send_copy(st.at[2 * i], c, way, d).start()

        @pl.when(due_fin)
        def _():
            pltpu.make_async_copy(g_hbm.at[c_fin, z], st.at[last], s_sem.at[last]).wait()
            for way in (0, 1):
                slot = last + 1 + way

                @pl.when(runs(way))
                def _(way=way, slot=slot):
                    pltpu.make_async_copy(r_hbm.at[c_fin, way, z], st.at[slot], s_sem.at[slot]).wait()

            @pl.when(c_fin >= 1)
            def _():
                pltpu.make_async_copy(fin, mine_out.at[c_fin - 1], c_sem.at[2]).wait()
                fin_copy(c_fin - 1).wait_send()

            total = st[last].astype(F32) + st[last + 1].astype(F32) + st[last + 2].astype(F32)
            low, high = total[:, :d_own], total[:, d_own:]
            fin[...] = jnp.where(x == 0, low, high)
            away[...] = jnp.where(x == 0, high, low).astype(BF)
            pltpu.make_async_copy(fin, mine_out.at[c_fin], c_sem.at[2]).start()
            fin_copy(c_fin).start()

    def fin_copy(c):
        return remote(away, got_out.at[c], fx_send.at[c], fx_recv.at[c], (z, 1 - x, t))

    tile = 512

    def phase_one(c):
        def body(r, carry):
            at = pl.ds(pl.multiple_of(r * tile, tile), tile)
            gu = mm(n2[at, :], wgu_v[c])
            dh = mm(cot[at, :], wd_v[pl.ds(pl.multiple_of(c * fc, fc), fc), :], NT)
            gate, up = gu[:, :fc], gu[:, fc:]
            sig = 1.0 / (1.0 + jnp.exp(-gate))
            act = gate * sig
            h = (act * up).astype(BF)
            dg = (dh * up * sig * (1.0 + gate * (1.0 - sig))).astype(BF)
            du = (dh * act).astype(BF)
            hid[c, at, :] = h
            dgu[c, at, 0:fc] = dg
            dgu[c, at, fc : 2 * fc] = du
            left_t[0:fc, at] = h.T
            left_t[fc : 2 * fc, at] = dg.T
            left_t[2 * fc : 3 * fc, at] = du.T
            return carry

        lax.fori_loop(0, rows // tile, body, 0)

    def phase_two(c):
        def body(i, carry):
            d = block_of(i)
            slot = i % 2
            at = pl.ds(pl.multiple_of(d * dz, dz), dz)

            @pl.when(i >= 2)
            def _():
                g_copy(c, block_of(i - 2), slot).wait()

            gt[slot, 0:fc, :] = mm(left_t[0:fc, :], cot[:, at]).astype(BF)
            gt[slot, fc : 3 * fc, :] = mm(left_t[fc : 3 * fc, :], n2[:, at]).astype(BF)
            g_copy(c, d, slot).start()
            return carry

        lax.fori_loop(0, shards, body, 0)
        for i in (shards - 2, shards - 1):
            g_copy(c, block_of(jnp.int32(i)), i % 2).wait()

    ot = 256
    units = rows // ot

    def tail_unit(u):
        at = pl.ds(pl.multiple_of((u % units) * ot, ot), ot)
        slot = u % 2

        @pl.when(u >= 2)
        def _():
            pltpu.make_async_copy(ost.at[slot], dn_out.at[at, :], o_sem.at[slot]).wait()

        @pl.when(u < units)
        def _():
            for n in range(width // 512):
                cols = slice(n * 512, (n + 1) * 512)
                acc = jnp.zeros((ot, 512), F32)
                for c in range(chunks):
                    acc = acc + mm(dgu[c, at, :], wgu_v[c, cols, :], NT)
                ost[slot, :, cols] = acc.astype(BF)
            pltpu.make_async_copy(ost.at[slot], dn_out.at[at, :], o_sem.at[slot]).start()

        @pl.when(u >= units)
        def _():
            for n in range(width // 512):
                cols = slice(n * 512, (n + 1) * 512)
                acc = jnp.zeros((ot, 512), F32)
                for c in range(chunks):
                    acc = acc + mm(hid[c, at, :], wd_v[c * fc : (c + 1) * fc, cols])
                ost[slot, :, cols] = acc.astype(BF)
            pltpu.make_async_copy(ost.at[slot], out_out.at[at, :], o_sem.at[slot]).start()

    tail_slots = 2 * (kept - 1) + shards - chunks if 2 * (kept - 1) + shards > chunks else 1
    per_slot = -(-2 * units // tail_slots)

    def slot_body(s, carry):
        @pl.when(s < chunks)
        def _():
            @pl.when(s >= PRE)
            def _():
                hop_wait(s, shards - 1)

            phase_one(s)
            ag_round(s + shards, shards - 1)
            phase_two(s)

        @pl.when(s >= chunks)
        def _():
            first_u = (s - chunks) * per_slot
            last_u = jnp.minimum(first_u + per_slot, 2 * units)

            def body(u, carry):
                tail_unit(u)
                return carry

            lax.fori_loop(first_u, last_u, body, 0)

        rs_step(s)
        return carry

    lax.fori_loop(0, chunks + tail_slots, slot_body, 0)

    for u in (2 * units - 2, 2 * units - 1):
        at = pl.ds((u % units) * ot, ot)
        pltpu.make_async_copy(ost.at[u % 2], out_out.at[at, :], o_sem.at[u % 2]).wait()
    links.all_sent()
    for c in range(PRE, chunks):
        for d in x_copies(c, False):
            d.wait_send()
        for k in range(1, shards):
            hop_sent(c, k)
    for way in (0, 1):
        for k in range(1, shards):

            @pl.when(starts(way))
            def _(way=way, k=k):
                d = target(way, k)
                for c in range(kept):
                    rs_send_copy(g_hbm.at[c, d], c, way, d).wait_send()

    for i, (way, k) in enumerate(combos):

        @pl.when(sends(way, k) & runs(way))
        def _(way=way, k=k, i=i):
            rs_send_copy(st.at[2 * i], kept - 1, way, target(way, k)).wait_send()

    pltpu.make_async_copy(fin, mine_out.at[kept - 1], c_sem.at[2]).wait()
    fin_copy(kept - 1).wait_send()
    for c in range(kept):
        fin_copy(c).wait_recv()


def mlp_call(shards, ctx, tensor, n_own, cot, cotangent, wg, wu, wd, gu_pre, d_pre):
    rows_own, width = n_own.shape
    group = ctx * tensor
    rows = rows_own * group
    d_own = wg.shape[0]
    ff = wg.shape[1] // ctx
    fc = gu_pre.shape[2] // 2
    chunks = ff // fc
    dz = ctx * d_own
    any_spec = pl.BlockSpec(memory_space=pl.ANY)
    bits_y, bits_x = level_bits(ctx, tensor)
    halves = 2 ** (len(bits_y) + len(bits_x)) - 1
    moves = 2 * halves + halves + 1
    stage = 4 * (shards - 2) + 3
    kept = chunks - chunks // 2
    dims = (shards, ctx, tensor, chunks, kept, fc, rows_own, d_own)
    dma = pltpu.SemaphoreType.DMA
    return pl.pallas_call(
        functools.partial(mlp_kernel, dims),
        in_specs=[any_spec] * 8,
        out_specs=[any_spec] * 6,
        out_shape=[
            jax.ShapeDtypeStruct((rows, width), BF),
            jax.ShapeDtypeStruct((rows, width), BF),
            jax.ShapeDtypeStruct((kept, 3 * fc, d_own), F32),
            jax.ShapeDtypeStruct((kept, 3 * fc, d_own), BF),
            jax.ShapeDtypeStruct((chunks, shards, 3 * fc, dz), BF),
            jax.ShapeDtypeStruct((kept, 2, shards, 3 * fc, dz), BF),
        ],
        scratch_shapes=[
            pltpu.VMEM((rows, width), BF),
            pltpu.VMEM((rows, width), BF),
            pltpu.VMEM((chunks, width, 2 * fc), BF),
            pltpu.VMEM((ff, width), BF),
            pltpu.VMEM((chunks, rows, fc), BF),
            pltpu.VMEM((chunks, rows, 2 * fc), BF),
            pltpu.VMEM((3 * fc, rows), BF),
            pltpu.VMEM((2, 3 * fc, dz), BF),
            pltpu.VMEM((stage, 3 * fc, dz), BF),
            pltpu.VMEM((2, 256, width), BF),
            pltpu.VMEM((3 * fc, d_own), F32),
            pltpu.VMEM((3 * fc, d_own), BF),
            dma((moves,)),
            dma((moves,)),
            dma((chunks, 3)),
            dma((chunks, 3)),
            dma((chunks, 3)),
            dma((chunks, 2, shards - 1, 2)),
            dma((chunks, 2, shards - 1, 2)),
            dma((2,)),
            dma((stage,)),
            dma((chunks, 2, shards)),
            dma((chunks, 2, shards)),
            dma((chunks,)),
            dma((chunks,)),
            dma((2,)),
            dma((3 + tensor,)),
        ],
        compiler_params=pltpu.CompilerParams(
            collective_id=1, has_side_effects=True, vmem_limit_bytes=63 * 1024 * 1024
        ),
        cost_estimate=pl.CostEstimate(
            flops=18 * rows * width * ff, bytes_accessed=100 * 1024 * 1024, transcendentals=rows * ff
        ),
        name="feed_forward",
    )(n_own, cot, cotangent, wg, wu, wd, gu_pre, d_pre)


def last_kernel(
    dims, place_s, at_s, live_s, g_late, dn_part, out_part, h_in, cot_in, tokens, gains_in, n_one, w_qkv_in, w_o_in, o_rel_in,
    os_in, qs, ks, vs, stats, cos_ref, sin_ref,
    result, grad_x, mine_o, got_o, mine_w, got_w, gain_out, mine_late, got_late, dh_all, dh_keep, o_land, o_parts, r_late,
    big, w_qkv, chip, c_land, parts_land, stage_own, tile_h, gains, dh_low, go_rel, go, delta, dq,
    d_rel, left_o, left_w, g_o, r_o, g_w, r_w, away_o, g_sum, g_land, g_chain, half_sum, fin_late, away_late,
    send_sems, recv_sems, own_sems,
):
    shards, ctx, tensor, own_rows, d_own, kept = dims
    p = Place(shards, ctx, tensor)
    z, x, t = p.z, p.x, p.t
    group = p.group
    rows, cols = qs.shape
    width = dh_low.shape[1]
    heads = cols // HDIM
    dz = ctx * d_own
    half = own_rows // 2
    d_seq = big.at[pl.ds(0, rows), pl.ds(0, 3 * cols)]
    links = Links(p, send_sems, recv_sems)
    count = [0]

    def own(src, dst):
        i = count[0]
        count[0] += 1
        c = pltpu.make_async_copy(src, dst, own_sems.at[i])
        c.start()
        return c

    p.meet(list(range(1, group)))

    def block(k):
        return pl.ds(k * own_rows, own_rows)

    def mine(k=0):
        _, tt = p.peer(k)
        return pl.ds(pl.multiple_of(tt * own_rows, own_rows), own_rows)

    orders = [p.bits_x + p.bits_y, p.bits_y + p.bits_x]

    def halves(land, in_hbm=False):
        have = [list(range(0, group, 2)), list(range(0, group, 2))]
        spot = 0
        for stage in range(len(orders[0])):
            step = []
            for h in (0, 1):
                bit = orders[h][stage]
                leave = [k for k in have[h] if k & bit]
                for i, k in enumerate(leave):
                    at = pl.ds(h * half, half)
                    dst = land.at[h, spot + i]
                    step.append((h, k, bit, spot + i, links.send(chip.at[k // 2, at, :], dst, p.peer_id(bit))))
                have[h] = [k for k in have[h] if not k & bit]
            spot += len(leave)
            yield
            for h, k, bit, i, m in step:
                m.come()
                at = pl.ds(h * half, half)
                keep = (k ^ bit) // 2
                if in_hbm:
                    own(land.at[h, i], stage_own.at[pl.ds(0, half), :]).wait()
                    came = stage_own[0:half, :].astype(F32)
                else:
                    came = land[h, i].astype(F32)
                total = chip[keep, at, :].astype(F32) + came
                if stage == len(orders[0]) - 1:
                    half_sum[at, :] = total
                else:
                    chip[keep, at, :] = total.astype(BF)
            for h, k, bit, i, m in step:
                m.sent()
                done_moves.append(m)

    done_moves = []

    late = r_late.shape[0]
    late_moves = {}

    def late_wait(copies, conds):
        for c, cond in zip(copies, conds):
            pl.when(cond)(c.wait)

    def tile_copy(src, slot, sem):
        return pltpu.make_async_copy(src, g_w.at[slot], own_sems.at[sem])

    for c in range(late):
        for k in range(1, shards):
            for way in (0, 1):
                d = z + shards - k if way == 0 else z - (shards - k)
                came = z + shards - (k + 1) if way == 0 else z - (shards - (k + 1))
                last = way == 1 and k == shards - 1
                dst = r_late.at[c, shards] if last else r_late.at[c, d]
                land = r_late.at[c, shards] if last else r_late.at[c, came]
                end = z == 0 if way == 0 else z == shards - 1
                mid = (z >= 1) & (z < k) if way == 0 else (z <= shards - 2) & (z >= shards - k)
                comes = (z >= 1) & (z <= k) if way == 0 else (z <= shards - 2) & (z >= shards - 1 - k)
                where = p.above() if way == 0 else p.below()
                src = g_late.at[kept + c, d]
                move = links.send(src, dst, where, land, end, comes)
                pair = g_w.at[2 * way]
                add = Move(
                    pltpu.make_async_remote_copy(
                        src_ref=pair,
                        dst_ref=dst,
                        send_sem=links.send_sems.at[move.place],
                        recv_sem=links.recv_sems.at[move.place],
                        device_id=where,
                        device_id_type=pl.DeviceIdType.MESH,
                    ),
                    move.due,
                    mid,
                    comes,
                )
                late_moves[c, k, way] = (move, add, d, mid)

    def late_sums():
        sent = []
        sem = late_sem
        for c in range(late):
            for k in range(2, shards):
                copies = []
                for m in sent:
                    m.sent()
                sent = []
                for way in (0, 1):
                    late_moves[c, k - 1, way][0].come()
                    _, add, d, mid = late_moves[c, k, way]
                    pair = [
                        tile_copy(g_late.at[kept + c, d], 2 * way, sem),
                        tile_copy(r_late.at[c, d], 2 * way + 1, sem + 1),
                    ]
                    sem += 2
                    for cp in pair:
                        pl.when(mid)(cp.start)
                    copies.append((way, add, mid, pair))
                for way, add, mid, pair in copies:

                    @pl.when(mid)
                    def _(way=way, pair=pair):
                        for cp in pair:
                            cp.wait()
                        g_w[2 * way] = plus(g_w[2 * way], g_w[2 * way + 1])

                    add.start()
                    sent.append(add)
                yield
            for m in sent:
                m.sent()
            sent = []
            for way in (0, 1):
                late_moves[c, shards - 1, way][0].come()
            has_low, has_high = z > 0, z < shards - 1
            loads = [
                (tile_copy(g_late.at[kept + c, z], 0, sem), None),
                (tile_copy(r_late.at[c, z], 1, sem + 1), has_low),
                (tile_copy(r_late.at[c, shards], 2, sem + 2), has_high),
            ]
            sem += 3
            for cp, cond in loads:
                cp.start() if cond is None else pl.when(cond)(cp.start)
            for cp, cond in loads:
                cp.wait() if cond is None else pl.when(cond)(cp.wait)

            fin = fin_late.at[pl.ds(0, 3 * cols), :]

            def half_of(xx):
                at = pl.ds(pl.multiple_of(xx * d_own, d_own), d_own)
                fin[...] = g_w[0, :, at].astype(F32)

                @pl.when(has_low)
                def _():
                    fin[...] += g_w[1, :, at].astype(F32)

                @pl.when(has_high)
                def _():
                    fin[...] += g_w[2, :, at].astype(F32)

            half_of(1 - x)
            if c > 0:
                across_late[-1].sent()
                done_moves.append(across_late[-1])
            away_late[...] = fin[...].astype(BF)
            across_late.append(links.send(away_late, got_late.at[c], p.peer_id(tensor)))
            half_of(x)
            keep = tile_out(c, sem)
            sem += 1
            keep.start()
            keep.wait()
            yield

    def tile_out(c, sem):
        return pltpu.make_async_copy(fin_late.at[pl.ds(0, 3 * cols), :], mine_late.at[c], own_sems.at[sem])

    across_late = []
    late_sem = 120
    late_steps = late_sums()

    odd = list(range(1, group, 2))
    core = [links.send(dn_part.at[block(k), :], c_land.at[k // 2], p.peer_id(1)) for k in odd]
    even = [own(dn_part.at[block(k - 1), :], chip.at[k // 2]) for k in odd]
    load_gain = own(gains_in, gains)
    load_h = [
        own(h_in.at[:, j * cols : (j + 1) * cols], dq.at[j * own_rows : (j + 1) * own_rows, :]) for j in range(width // cols)
    ]
    load_cot = own(cot_in.at[mine(), :], stage_own)
    load_o = own(w_o_in, big)
    load_w = own(w_qkv_in, w_qkv)
    core_out = [links.send(out_part.at[block(k), :], o_land.at[k // 2], p.peer_id(1), start=False) for k in odd]
    for i in range(group // 2):
        even[i].wait()
        core[i].come()
        chip[i] = plus(chip[i], c_land[i])
    sums = halves(parts_land)
    next(sums)
    next(late_steps, None)
    for m in core_out:
        m.start()
    load_gain.wait()
    for _ in sums:
        pass

    per = tile_h.shape[1]
    spans = [(slice(j * own_rows, (j + 1) * own_rows), slice(j * cols, (j + 1) * cols)) for j in range(width // cols)]

    def spread_out(r):
        return jnp.concatenate([dq[j * own_rows + r * per : j * own_rows + (r + 1) * per, :] for j in range(len(spans))], axis=1)

    for c in load_h:
        c.wait()
    load_cot.wait()
    for r in range(own_rows // per):
        at = pl.ds(r * per, per)
        h = spread_out(r)
        dn = half_sum[at, :]
        scale = lax.rsqrt(jnp.mean(h * h, axis=-1, keepdims=True) + EPS)
        normed = h * scale
        scaled = dn * gains[1:2, :]
        inner = jnp.mean(scaled * normed, axis=-1, keepdims=True)
        d_h = stage_own[at, :].astype(F32) + scale * (scaled - normed * inner)
        part = jnp.sum(dn * normed, axis=0, keepdims=True)
        g_sum[0, 0:1, :] = part if r == 0 else g_sum[0, 0:1, :] + part
        dh_low[at, :] = d_h.astype(BF)
        for j, (_, c) in enumerate(spans):
            dq[j * own_rows + r * per : j * own_rows + (r + 1) * per, :] = d_h[:, c]
    keep_dh = [own(dq.at[a, :], dh_keep.at[:, c]) for a, c in spans]
    own(dh_low, dh_all.at[block(0), :]).wait()
    next(late_steps, None)

    def dh_part(k, h):
        if h is None:
            return dh_all.at[block(k), :]
        return dh_all.at[pl.ds(k * own_rows + h * half, half), :]

    load_o.wait()
    wo_rows = width // tensor
    for tt in range(tensor):
        acc = jnp.zeros((own_rows, wo_rows), F32)
        for xx in range(ctx):
            left = jnp.concatenate(
                [dh_low[:, (zz * ctx + xx) * d_own : (zz * ctx + xx + 1) * d_own] for zz in range(shards)], axis=1
            )
            acc = acc + mm(left, big[xx * width + tt * wo_rows : xx * width + (tt + 1) * wo_rows, :], NT)
        stage_own[:, tt * wo_rows : (tt + 1) * wo_rows] = acc.astype(BF)

    def heads_of(k):
        xx, tt = p.peer(k)
        return stage_own.at[:, pl.ds(pl.multiple_of((tt * ctx + xx) * cols, cols), cols)]

    swaps = [links.send(heads_of(k), go_rel.at[block(k), :], p.peer_id(k)) for k in range(1, group)]
    own_heads = own(heads_of(0), go_rel.at[block(0), :])
    dh_rows = links.spread(dh_part)
    next(dh_rows)
    load_left = own(o_rel_in, d_rel.at[:, 0:cols])
    load_tok = own(tokens.at[mine(), :], dh_low)

    def output():
        for i in range(group // 2):
            even_copy = own(out_part.at[block(2 * i), :], chip.at[i])
            core_out[i].come()
            land_copy = own(o_land.at[i], stage_own)
            even_copy.wait()
            land_copy.wait()
            chip[i] = plus(chip[i], stage_own[...])
        steps = halves(o_parts, True)
        for _ in steps:
            yield
        loads = [own(h_in.at[pl.ds(r * per, per), :], tile_h.at[r]) for r in range(2)]
        for r in range(own_rows // per):
            at = pl.ds(r * per, per)
            loads[r].wait()
            stage_own[at, :] = (tile_h[r % 2] + half_sum[at, :]).astype(BF)
            if r + 2 < own_rows // per:
                loads.append(own(h_in.at[pl.ds((r + 2) * per, per), :], tile_h.at[r % 2]))
        own(stage_own, result.at[mine(), :]).wait()
        yield from everywhere(result)

    def everywhere(ref):
        def put(k, bit):
            return links.send(ref.at[mine(k), :], ref.at[mine(k), :], p.peer_id(bit), ref.at[mine(k | bit), :])

        cores = [put(0, 1)]
        have = [0]
        for bit in p.bits_y:
            step = [put(k, bit) for k in have]
            yield
            for m in step:
                m.come()
            new = [k | bit for k in have]
            cores += [put(k, 1) for k in new]
            have = have + new
        yield
        for m in cores:
            m.come()

    next(late_steps, None)
    own_heads.wait()
    for m in swaps:
        m.come()
    for m in swaps:
        m.sent()
        done_moves.append(m)

    def fill(b, carry):
        go[pl.ds(pl.multiple_of(b * BLK, BLK), BLK), :] = picked(go_rel, place_s[b])
        return carry

    lax.fori_loop(0, rows // BLK, fill, 0)
    load_os = own(os_in, go_rel)
    load_left.wait()
    for k in range(group):
        left_o[:, k * own_rows : (k + 1) * own_rows] = d_rel[k * own_rows : (k + 1) * own_rows, 0:cols].T
    load_os.wait()
    head_row = lax.broadcasted_iota(jnp.int32, (8, cols), 0)
    head_col = lax.broadcasted_iota(jnp.int32, (8, cols), 1) // HDIM
    pick = jnp.where(head_row == head_col, 1.0, 0.0)
    for i in range(rows // QT):
        part = slice(i * QT, (i + 1) * QT)
        both = go[part, :].astype(F32) * go_rel[part, :].astype(F32)
        delta[:, part] = lax.dot_general(pick, both, NT, precision=lax.Precision.HIGHEST, preferred_element_type=F32)
    for c in keep_dh:
        c.wait()
    dq[...] = jnp.zeros_like(dq)
    live = live_s[0]
    tiles = rows // QT

    def store(i, column, value, turned):
        at = slice(i * QT, (i + 1) * QT)
        if turned:
            value = turn(value, wide(cos_ref[at, :], cols), -wide(sin_ref[at, :], cols))
        d_seq[at, column * cols : (column + 1) * cols] = value.astype(BF)

    out_steps = output()

    def grads_o():
        steps = sums_along(g_o, r_o, fin_late.at[pl.ds(0, cols), :], away_o, got_o, mine_o)
        dh_block = d_rel.at[:, pl.ds(0, dz)]
        for i in range(shards):
            d = far_first(i)
            own(dh_all.at[:, pl.ds(pl.multiple_of(d * dz, dz), dz)], dh_block).wait()
            g_o[d] = mm(left_o[...], d_rel[:, 0:dz]).astype(BF)
            if i < shards - 2:
                next(steps)
                yield
        for _ in steps:
            yield

    def far_first(i):
        down = shards - 1 - i
        down = down - jnp.where(down <= z, 1, 0)
        up = i + jnp.where(i >= z, 1, 0)
        return z if i == shards - 1 else jnp.where(2 * z < shards, down, up)

    def sums_along(g, r, fin, away, got_ref, mine_ref):
        before = [None, None]
        for k in range(1, shards):
            now = []
            for way in (0, 1):
                d = z + shards - k if way == 0 else z - (shards - k)
                came = z + shards - (k + 1) if way == 0 else z - (shards - (k + 1))
                goes = z < k if way == 0 else z >= shards - k
                comes = (z >= 1) & (z <= k) if way == 0 else (z <= shards - 2) & (z >= shards - 1 - k)
                if k > 1:
                    before[way].come()
                    mid = (z >= 1) & (z < k) if way == 0 else (z <= shards - 2) & (z >= shards - k)

                    @pl.when(mid)
                    def _(d=d):
                        g[d] = plus(g[d], r[d])

                last = way == 1 and k == shards - 1
                dst = r.at[shards] if last else r.at[d]
                land = r.at[shards] if last else r.at[came]
                now.append(links.send(g.at[d], dst, p.above() if way == 0 else p.below(), land, goes, comes))
            before = now
            yield
        for m in before:
            m.come()

        def half_of(xx):
            at = pl.ds(pl.multiple_of(xx * d_own, d_own), d_own)
            fin[...] = g[z, :, at].astype(F32)

            @pl.when(z > 0)
            def _():
                fin[...] += r[z, :, at].astype(F32)

            @pl.when(z < shards - 1)
            def _():
                fin[...] += r[shards, :, at].astype(F32)

        half_of(1 - x)
        away[...] = fin[...].astype(BF)
        across = links.send(away, got_ref, p.peer_id(tensor))
        half_of(x)
        keep = own(fin, mine_ref)
        yield
        across.come()
        keep.wait()

    o_steps = None
    next(out_steps)
    for i in range(tiles):
        begin = i * QT

        def head(h, carry):
            dk, dv = carry
            kt = ks[begin : begin + QT, :]
            lane = lax.broadcasted_iota(jnp.int32, (QT, cols), 1) // HDIM
            km = jnp.where(lane == h, kt * BF(0.125), BF(0))
            dead = jnp.where(lax.broadcasted_iota(jnp.int32, (QT, 1), 0) + begin < live, 0.0, NEG)
            for j in range(i, tiles):
                at = slice(j * QT, (j + 1) * QT)
                qm = jnp.where(lane == h, qs[at, :] * BF(0.125), BF(0))
                gm = jnp.where(lane == h, go[at, :], BF(0))
                s = mm(kt, qm, NT) + dead
                if j == i:
                    kpos = lax.broadcasted_iota(jnp.int32, (QT, QT), 0)
                    qpos = lax.broadcasted_iota(jnp.int32, (QT, QT), 1)
                    s = s + jnp.where(kpos <= qpos, 0.0, NEG)
                e = jnp.exp(s - stats[pl.ds(h, 1), at])
                dp = mm(vs[begin : begin + QT, :], gm, NT)
                ds = (e * (dp - delta[pl.ds(h, 1), at])).astype(BF)
                dq[at, :] += mm(ds, km, TN)
                dk = dk + mm(ds, qm)
                dv = dv + mm(e.astype(BF), gm)
            return dk, dv

        zero = jnp.zeros((QT, cols), F32)
        dk, dv = lax.fori_loop(0, heads, head, (zero, zero))
        store(i, 1, dk, True)
        store(i, 2, dv, False)
        store(i, 0, dq[begin : begin + QT, :], True)
        next(late_steps, None)
        next(out_steps, None)
        if i == 0:
            next(dh_rows, None)
        elif i == 1:
            drain(dh_rows)
            o_steps = grads_o()
            next(o_steps, None)
        else:
            next(o_steps, None)

    def back_to_rows(j, carry):
        dst = pl.ds(pl.multiple_of(j * BLK, BLK), BLK)
        d_rel[dst, :] = picked(d_seq, at_s[j])
        return carry

    lax.fori_loop(0, rows // BLK, back_to_rows, 0)
    drain(late_steps)
    for m in across_late:
        m.come()
    across_late[-1].sent()
    done_moves.append(across_late[-1])
    drain(out_steps)
    load_w.wait()

    def d_n_one(k, c):
        return mm(d_rel[k * own_rows : (k + 1) * own_rows, :], w_qkv[c, :], NT)

    quarters = [slice(c, c + width // 4) for c in range(0, width, width // 4)]

    load_n = []
    per_n = shards // ctx
    for d in range(shards):
        load_n.append(
            own(
                n_one.at[:, d * dz : (d + 1) * dz],
                big.at[(d // per_n) * rows : (d // per_n + 1) * rows, (d % per_n) * dz : (d % per_n + 1) * dz],
            )
        )
    load_dh = [own(dh_keep.at[:, c], dq.at[a, :]) for a, c in spans]
    core = []
    for i, k in enumerate(odd):
        for c in quarters:
            chip[i, :, c] = d_n_one(k, c).astype(BF)
        core.append(links.send(chip.at[i], c_land.at[i], p.peer_id(1)))
    next(o_steps, None)
    for k in range(group):
        left_w[:, k * own_rows : (k + 1) * own_rows] = d_rel[k * own_rows : (k + 1) * own_rows, :].T
    for c in load_n:
        c.wait()

    def n_block(d):
        row = pl.ds(pl.multiple_of((d // per_n) * rows, rows), rows)
        return big[row, pl.ds(pl.multiple_of((d % per_n) * dz, dz), dz)]

    w_steps = sums_along(g_w, r_w, fin_late.at[pl.ds(0, 3 * cols), :], away_late, got_w, mine_w)

    def grad_w(i):
        d = far_first(i)
        for i in range(3):
            at = slice(i * cols, (i + 1) * cols)
            g_w[d, at, :] = mm(left_w[at, :], n_block(d)).astype(BF)

    grad_w(0)
    next(w_steps)
    grad_w(1)
    for i in range(group // 2):
        core[i].sent()
        done_moves.append(core[i])
        core[i].come()
        for c in quarters:
            chip[i, :, c] = (d_n_one(2 * i, c) + c_land[i, :, c].astype(F32)).astype(BF)
    sums = halves(parts_land)
    next(sums)
    next(w_steps, None)
    for i in range(2, shards):
        grad_w(i)
        if i < shards - 1:
            next(w_steps, None)
    next(o_steps, None)
    for _ in sums:
        pass
    for c in load_dh:
        c.wait()
    load_tok.wait()
    for r in range(own_rows // per):
        at = pl.ds(r * per, per)
        v = dh_low[at, :].astype(F32)
        dn = half_sum[at, :]
        scale = lax.rsqrt(jnp.mean(v * v, axis=-1, keepdims=True) + EPS)
        normed = v * scale
        scaled = dn * gains[0:1, :]
        inner = jnp.mean(scaled * normed, axis=-1, keepdims=True)
        stage_own[at, :] = (spread_out(r) + scale * (scaled - normed * inner)).astype(BF)
        part = jnp.sum(dn * normed, axis=0, keepdims=True)
        g_sum[0, 1:2, :] = part if r == 0 else g_sum[0, 1:2, :] + part
    g_sum[0, 2:8, :] = jnp.zeros((6, width), F32)
    own(stage_own, grad_x.at[mine(), :]).wait()
    x_steps = everywhere(grad_x)
    next(x_steps)
    bit, i = 1, 0
    while bit < group:
        m = links.send(g_sum.at[i], g_land.at[i], p.peer_id(bit))
        m.come()
        g_sum[i + 1] = g_sum[i] + g_land[i]
        bit, i = bit * 2, i + 1
    own(g_sum.at[i], g_chain.at[z]).wait()
    g_steps = links.chain(lambda b: [g_chain.at[b]])
    next(g_steps)
    next(w_steps, None)
    next(x_steps, None)
    drain(g_steps)
    total = g_chain[0]
    for b in range(1, shards):
        total = total + g_chain[b]
    g_land[0] = total
    own(g_land.at[0, :, pl.ds(pl.multiple_of((z * ctx + x) * d_own, d_own), d_own)], gain_out).wait()
    drain(o_steps, x_steps, w_steps)
    for m in links.moves:
        if m not in done_moves:
            m.sent()


def last_call(
    shards, ctx, tensor, place, at, live, g_late, dn_part, out_part, hidden, cot, tokens, gains, n_one, w_qkv, w_o, o_rel,
    os, qs, ks, vs, stats, cos, sin,
):
    rows, cols = qs.shape
    width = hidden.shape[1]
    own_rows = hidden.shape[0]
    group = ctx * tensor
    d_own = width // (shards * ctx)
    dz = ctx * d_own
    chunks = g_late.shape[0]
    late = chunks // 2
    dims = (shards, ctx, tensor, own_rows, d_own, chunks - late)
    any_spec = pl.BlockSpec(memory_space=pl.ANY)
    smem = pl.BlockSpec(memory_space=pltpu.SMEM)
    vmem = pl.BlockSpec(memory_space=pltpu.VMEM)
    dma = pltpu.SemaphoreType.DMA
    half = own_rows // 2
    per = min(32, own_rows)
    bits = group.bit_length() - 1

    def out(shape, kind=BF):
        return jax.ShapeDtypeStruct(shape, kind)

    parts = (2, group // 2 - 1, half, width)
    return pl.pallas_call(
        functools.partial(last_kernel, dims),
        in_specs=[smem] * 3 + [any_spec] * 12 + [vmem] * 6,
        out_specs=[any_spec] * 14,
        out_shape=[
            out((tensor * own_rows, width)),
            out((tensor * own_rows, width)),
            out((cols, d_own), F32),
            out((cols, d_own)),
            out((3 * cols, d_own), F32),
            out((3 * cols, d_own)),
            out((8, d_own), F32),
            out((late, 3 * cols, d_own), F32),
            out((late, 3 * cols, d_own)),
            out((rows, width)),
            out((own_rows, width), F32),
            out((group // 2, own_rows, width)),
            out(parts),
            out((late, shards + 1, 3 * cols, dz)),
        ],
        scratch_shapes=[
            pltpu.VMEM((ctx * width, shards * d_own), BF),
            pltpu.VMEM((width, 3 * cols), BF),
            pltpu.VMEM((group // 2, own_rows, width), BF),
            pltpu.VMEM((group // 2, own_rows, width), BF),
            pltpu.VMEM(parts, BF),
            pltpu.VMEM((own_rows, width), BF),
            pltpu.VMEM((2, per, width), F32),
            pltpu.VMEM((8, width), F32),
            pltpu.VMEM((own_rows, width), BF),
            pltpu.VMEM((rows, cols), BF),
            pltpu.VMEM((rows, cols), BF),
            pltpu.VMEM((8, rows), F32),
            pltpu.VMEM((rows, cols), F32),
            pltpu.VMEM((rows, 3 * cols), BF),
            pltpu.VMEM((cols, rows), BF),
            pltpu.VMEM((3 * cols, rows), BF),
            pltpu.VMEM((shards, cols, dz), BF),
            pltpu.VMEM((shards + 1, cols, dz), BF),
            pltpu.VMEM((shards, 3 * cols, dz), BF),
            pltpu.VMEM((shards + 1, 3 * cols, dz), BF),
            pltpu.VMEM((cols, d_own), BF),
            pltpu.VMEM((bits + 1, 8, width), F32),
            pltpu.VMEM((bits, 8, width), F32),
            pltpu.VMEM((shards, 8, width), F32),
            pltpu.VMEM((own_rows, width), F32),
            pltpu.VMEM((3 * cols, d_own), F32),
            pltpu.VMEM((3 * cols, d_own), BF),
            dma((300,)),
            dma((300,)),
            dma((240,)),
        ],
        compiler_params=pltpu.CompilerParams(
            collective_id=2, has_side_effects=True, vmem_limit_bytes=63 * 1024 * 1024
        ),
        cost_estimate=pl.CostEstimate(
            flops=2 * rows * width * cols * 8, bytes_accessed=64 * 1024 * 1024, transcendentals=rows * rows * cols // HDIM
        ),
        name="last",
    )(place, at, live, g_late, dn_part, out_part, hidden, cot, tokens, gains, n_one, w_qkv, w_o, o_rel, os, qs, ks, vs, stats, cos, sin)


def per_device(
    shards, ctx, tensor, tokens, cotangent, seq_len, block_slot, attn_gain, w_query, w_key, w_value, w_out, mlp_gain, w_gate, w_up, w_down
):
    group = ctx * tensor
    my_x = lax.axis_index("ctx")
    my_t = lax.axis_index("tensor")
    me = my_x * tensor + my_t
    width = tokens.shape[1]
    own_rows = tokens.shape[0] // tensor
    level_rows = own_rows * group
    slots_each = own_rows // BLK
    d_own = w_query.shape[0]
    cols = w_query.shape[1] // ctx
    ff = w_gate.shape[1] // ctx
    slot = block_slot[0]
    place = ((slot // slots_each) ^ me) * slots_each + slot % slots_each
    order = jnp.arange(slot.shape[0], dtype=jnp.int32)
    at = jnp.sum(jnp.where(place[:, None] == order[None, :], order[:, None], 0), axis=0).astype(jnp.int32)

    def x_join(mine, got, axis):
        return jnp.where(
            my_x == 0, jnp.concatenate([mine, got], axis=axis), jnp.concatenate([got, mine], axis=axis)
        )

    angle_at = jnp.arange(level_rows, dtype=F32)
    lane = jnp.arange(128)
    freqs = THETA ** (-(lane % (HDIM // 2)).astype(F32) / (HDIM // 2))
    angles = angle_at[:, None] * freqs[None, :]
    cos = jnp.cos(angles)
    sin = jnp.sin(angles) * jnp.where(lane % HDIM < HDIM // 2, -1.0, 1.0)
    at_pos = (at[:, None] * BLK + jnp.arange(BLK)[None, :]).reshape(-1).astype(F32)
    angles = at_pos[:, None] * freqs[None, :]
    cos_rel = jnp.cos(angles)
    sin_rel = jnp.sin(angles) * jnp.where(lane % HDIM < HDIM // 2, -1.0, 1.0)
    gains = jnp.concatenate([jnp.stack([attn_gain, mlp_gain], axis=0).astype(F32), jnp.zeros((6, d_own), F32)], axis=0)
    n_one, w_qkv, w_o, cot, gu_pre, d_pre, n_two_own, hidden_res, gains, qs, ks, vs, os, stats, o_slot = first_call(
        shards, ctx, tensor, place.astype(jnp.int32), at, seq_len, tokens, cotangent, gains,
        w_query, w_key, w_value, w_out, w_gate, w_up, w_down, cos_rel, sin_rel,
    )
    dn_part, out_part, ff_mine, ff_got, g_late, _ = mlp_call(
        shards, ctx, tensor, n_two_own, cot, cotangent, w_gate, w_up, w_down, gu_pre, d_pre
    )

    result, grad_x, mine_o, got_o, mine_w, got_w, gain_sums, late_mine, late_got, *_ = last_call(
        shards, ctx, tensor, place.astype(jnp.int32), at, seq_len, g_late, dn_part, out_part, hidden_res, cotangent, tokens, gains,
        n_one, w_qkv, w_o.reshape(ctx * width, shards * d_own), o_slot, os, qs, ks, vs, stats, cos, sin,
    )
    ff_mine = jnp.concatenate([ff_mine, late_mine], axis=0)
    ff_got = jnp.concatenate([ff_got, late_got], axis=0)
    chunks = ff_mine.shape[0]
    fc = ff // chunks
    mine = ff_mine.reshape(chunks, 3, fc, d_own)
    got = ff_got.reshape(chunks, 3, fc, d_own).astype(F32)

    def spread(i):
        return x_join(mine[:, i].reshape(ff, d_own), got[:, i].reshape(ff, d_own), 0)

    grad_down = spread(0)
    grad_gate = spread(1).T
    grad_up = spread(2).T

    grad_out = x_join(mine_o, got_o.astype(F32), 0)
    mine = mine_w.reshape(3, cols, d_own)
    got = got_w.reshape(3, cols, d_own).astype(F32)
    grad_q, grad_k, grad_v = (x_join(mine[i], got[i], 0).T for i in range(3))
    grad_gain_two, grad_gain_one = gain_sums[0], gain_sums[1]
    return (
        result,
        grad_x,
        grad_gain_one,
        grad_q,
        grad_k,
        grad_v,
        grad_out,
        grad_gain_two,
        grad_gate,
        grad_up,
        grad_down,
    )


def solution(mesh):
    rows = P(("shard", "ctx"), None)
    gain = P(("shard", "ctx"))
    into = P(("shard", "ctx"), "tensor")
    back = P("tensor", ("shard", "ctx"))
    sizes = mesh.shape
    return jax.shard_map(
        functools.partial(per_device, sizes["shard"], sizes["ctx"], sizes["tensor"]),
        mesh=mesh,
        in_specs=(rows, rows, P("shard"), P("shard", None), gain, into, into, into, back, gain, into, into, back),
        out_specs=(rows, rows, gain, into, into, into, back, gain, into, into, back),
        check_vma=False,
    )
```

```python
import functools

import jax
import jax.numpy as jnp
from jax import lax
from jax.experimental import pallas as pl
from jax.experimental.pallas import tpu as pltpu
from jax.sharding import PartitionSpec as P

HDIM = 64
BLK = 128
EPS = 1e-05
THETA = 130000.0
NEG = -1e30
LEVEL = ("ctx", "tensor")
BF = jnp.bfloat16
F32 = jnp.float32
QT = 512
PRE = 2

NT = (((1,), (1,)), ((), ()))
TN = (((0,), (0,)), ((), ()))


def mm(left, right, dims=None):
    if dims is None:
        return jnp.dot(left, right, preferred_element_type=F32)
    return lax.dot_general(left, right, dims, preferred_element_type=F32)


def level_bits(ctx, tensor):
    bits_y = []
    bit = 2
    while bit < tensor:
        bits_y.append(bit)
        bit *= 2
    bits_x = []
    bit = tensor
    while bit < ctx * tensor:
        bits_x.append(bit)
        bit *= 2
    return bits_y, bits_x


def plus(a, b):
    return (a.astype(F32) + b.astype(F32)).astype(BF)


def turn(u, cos, sin):
    lane = lax.broadcasted_iota(jnp.int32, u.shape, 1)
    width = u.shape[1]
    ahead = pltpu.roll(u, width - HDIM // 2, axis=1)
    behind = pltpu.roll(u, HDIM // 2, axis=1)
    other = jnp.where(lane % HDIM < HDIM // 2, ahead, behind)
    return u * cos + other * sin


def wide(table, cols):
    reps = cols // table.shape[1]
    return jnp.concatenate([table] * reps, axis=1) if reps > 1 else table


def flip(index, bit):
    return index + bit - 2 * bit * ((index // bit) % 2)


class Place:
    def __init__(self, shards, ctx, tensor):
        self.shards, self.ctx, self.tensor = shards, ctx, tensor
        self.group = ctx * tensor
        self.z = lax.axis_index("shard")
        self.x = lax.axis_index("ctx")
        self.t = lax.axis_index("tensor")
        self.bits_y, self.bits_x = level_bits(ctx, tensor)

    def peer(self, offset):
        t, x = self.t, self.x
        bit = 1
        while bit < self.group:
            if offset & bit:
                if bit < self.tensor:
                    t = flip(t, bit)
                else:
                    x = 1 - x
            bit *= 2
        return x, t

    def peer_id(self, offset):
        x, t = self.peer(offset)
        return (self.z, x, t)

    def above(self):
        return (self.z + 1, self.x, self.t)

    def below(self):
        return (self.z - 1, self.x, self.t)

    def meet(self, offsets, chain=True):
        barrier = pltpu.get_barrier_semaphore()
        z, shards = self.z, self.shards
        for k in offsets:
            pl.semaphore_signal(barrier, inc=1, device_id=self.peer_id(k), device_id_type=pl.DeviceIdType.MESH)
        peers = len(offsets)
        if chain:

            @pl.when(z < shards - 1)
            def _():
                pl.semaphore_signal(barrier, inc=1, device_id=self.above(), device_id_type=pl.DeviceIdType.MESH)

            @pl.when(z > 0)
            def _():
                pl.semaphore_signal(barrier, inc=1, device_id=self.below(), device_id_type=pl.DeviceIdType.MESH)

            peers = peers + (z + shards - 1) // shards + (2 * shards - 2 - z) // shards
        pl.semaphore_wait(barrier, peers)


class Move:
    def __init__(self, out, due, goes, comes, place=None):
        self.out, self.due, self.goes, self.comes, self.place = out, due, goes, comes, place

    def _run(self, cond, fn):
        if cond is None:
            fn()
        else:
            pl.when(cond)(fn)

    def start(self):
        self._run(self.goes, self.out.start)

    def come(self):
        self._run(self.comes, self.due.wait_recv)

    def sent(self):
        self._run(self.goes, self.out.wait_send)


class Links:
    def __init__(self, place, send_sems, recv_sems):
        self.place, self.send_sems, self.recv_sems = place, send_sems, recv_sems
        self.moves = []

    def send(self, src, dst, where, land=None, goes=None, comes=None, start=True):
        i = len(self.moves)
        land = dst if land is None else land
        safe = self.place.peer_id(1)

        def copy(a, b, w):
            return pltpu.make_async_remote_copy(
                src_ref=a,
                dst_ref=b,
                send_sem=self.send_sems.at[i],
                recv_sem=self.recv_sems.at[i],
                device_id=w,
                device_id_type=pl.DeviceIdType.MESH,
            )

        move = Move(copy(src, dst, where), copy(land, land, safe), goes, comes, i)
        self.moves.append(move)
        if start:
            move.start()
        return move

    def all_sent(self):
        for m in self.moves:
            m.sent()


    def chain(self, parts):
        p = self.place
        z, shards = p.z, p.shards
        due = []
        for k in range(1, shards):
            for m in due:
                m.come()
            due = []
            up = zip(parts(z - (k - 1)), parts(z - k))
            for src, land in up:
                due.append(self.send(src, src, p.above(), land, (z >= k - 1) & (z < shards - 1), z >= k))
            down = zip(parts(z + (k - 1)), parts(z + k))
            for src, land in down:
                due.append(
                    self.send(src, src, p.below(), land, (z + k - 1 <= shards - 1) & (z > 0), z + k <= shards - 1)
                )
            yield
        for m in due:
            m.come()

    def spread(self, part, absolute=False):
        p = self.place

        def put(k, bit, h):
            return self.send(part(k, h), part(k if absolute else k | bit, h), p.peer_id(bit), part(k | bit, h))

        cores = [put(0, 1, None)]
        have = [[0], [0]]
        found = {}
        orders = [p.bits_x + p.bits_y, p.bits_y + p.bits_x]
        for stage in range(len(orders[0])):
            step = []
            for h in (0, 1):
                bit = orders[h][stage]
                step += [(k | bit, put(k, bit, h)) for k in have[h]]
                have[h] = have[h] + [k | bit for k in have[h]]
            yield
            for k, m in step:
                m.come()
                found[k] = found.get(k, 0) + 1
                if found[k] == 2:
                    cores.append(put(k, 1, None))
        yield
        for m in cores:
            m.come()

    def rows(self, source, keep, own_rows, log):
        p = self.place

        def slot(k):
            return keep.at[pl.ds(k * own_rows, own_rows), :]

        mine = source.at[pl.ds(pl.multiple_of(p.t * own_rows, own_rows), own_rows), :]
        first = self.send(mine, slot(p.tensor), p.peer_id(p.tensor))
        log.append(first)
        yield
        first.come()
        far = [p.tensor]
        for bit in p.bits_y:
            step = [self.send(slot(k), slot(k | bit), p.peer_id(bit)) for k in far]
            log += step
            yield
            for m in step:
                m.come()
            far = far + [k | bit for k in far]
        last = [self.send(slot(k), slot(k | 1), p.peer_id(1)) for k in far]
        log += last
        yield
        for m in last:
            m.come()


def drain(*gens):
    for g in gens:
        for _ in g:
            pass


def first_kernel(
    dims, place_s, at_s, live_s, tokens, cotangent, gains_in, wq, wk, wv, w_out, wg, wu, wd, cos_ref, sin_ref,
    n_one_out, w_qkv_out, w_o_out, cot_out, gu_out, d_out, n_all, h_out, gains, qs, ks, vs, os, stats, o_rel,
    n_one, w_qkv, w_o, qkv_rel, attn_rows, h_own, n_own, x_keep, gu_v, d_v,
    send_sems, recv_sems, own_sems,
):
    shards, ctx, tensor, fc, own_rows, d_own = dims
    p = Place(shards, ctx, tensor)
    z, x, t = p.z, p.x, p.t
    group = p.group
    rows, width = n_one.shape
    cols = qs.shape[1]
    heads = cols // HDIM
    ff = wg.shape[1] // ctx
    dz = ctx * d_own
    links = Links(p, send_sems, recv_sems)
    own_count = [0]

    def own(src, dst):
        i = own_count[0]
        own_count[0] += 1
        c = pltpu.make_async_copy(src, dst, own_sems.at[i])
        c.start()
        return c

    p.meet(list(range(1, group)))

    def d_at(xx):
        return pl.ds(pl.multiple_of((z * ctx + xx) * d_own, d_own), d_own)

    def z_at(b):
        return pl.ds(pl.multiple_of(b * dz, dz), dz)

    def part_cols(xx, size):
        return pl.ds(pl.multiple_of(xx * size, size), size)

    across = p.peer_id(tensor)

    wo_rows = w_out.shape[0]

    def o_at(tt, xx, zz):
        return w_o.at[xx, pl.ds(pl.multiple_of(tt * wo_rows, wo_rows), wo_rows), pl.ds(pl.multiple_of(zz * d_own, d_own), d_own)]

    own_o = own(w_out, o_at(t, x, z))
    own_gain = own(gains_in, gains.at[:, d_at(x)])
    own_w = [own(w.at[:, part_cols(x, cols)], w_qkv.at[d_at(x), i * cols : (i + 1) * cols]) for i, w in enumerate((wq, wk, wv))]
    own_gain.wait()
    gain_x = links.send(gains.at[:, d_at(x)], gains.at[:, d_at(x)], across, gains.at[:, d_at(1 - x)])
    qkv_x = [
        links.send(
            w.at[:, part_cols(1 - x, cols)],
            w_qkv.at[d_at(x), i * cols : (i + 1) * cols],
            across,
            w_qkv.at[d_at(1 - x), i * cols : (i + 1) * cols],
        )
        for i, w in enumerate((wq, wk, wv))
    ]
    tok_log = []
    tok_rows = links.rows(tokens, n_one, own_rows, tok_log)
    next(tok_rows)
    own_tok = []
    for k in range(tensor):
        _, tt = p.peer(k)
        src = tokens.at[pl.ds(pl.multiple_of(tt * own_rows, own_rows), own_rows), :]
        own_tok.append(own(src, n_one.at[pl.ds(k * own_rows, own_rows), :]))
    own_o.wait()
    o_chain = links.chain(lambda b: [o_at(t, x, b)])
    next(o_chain)
    gain_x.come()
    gain_chain = links.chain(lambda b: [gains.at[:, z_at(b)]])
    next(gain_chain)
    next(o_chain, None)
    for c in own_w:
        c.wait()
    for m in qkv_x:
        m.come()
    next(gain_chain, None)
    qkv_chain = links.chain(lambda b: [w_qkv.at[z_at(b), :]])
    next(qkv_chain)

    gu_pairs = [(wg, 0), (wu, 1)]

    def gu_place(c, xx, i):
        return gu_v.at[c, d_at(xx), i * fc : (i + 1) * fc]

    def ff_begin(c):
        at = [pl.ds(pl.multiple_of(xx * ff + c * fc, fc), fc) for xx in (x, 1 - x)]
        d_rows = slice(c * fc, (c + 1) * fc)
        mine = [own(w.at[:, at[0]], gu_place(c, x, i)) for w, i in gu_pairs]
        mine.append(own(wd.at[at[0], :], d_v.at[d_rows, d_at(x)]))
        came = [links.send(w.at[:, at[1]], gu_place(c, x, i), across, gu_place(c, 1 - x, i)) for w, i in gu_pairs]
        came.append(links.send(wd.at[at[1], :], d_v.at[d_rows, d_at(x)], across, d_v.at[d_rows, d_at(1 - x)]))
        return mine, came

    def ff_moves():
        running = []
        for c in range(PRE + shards):
            if c < PRE:
                mine, came = begun[c]
                for m in mine:
                    m.wait()
                for m in came:
                    m.come()
                running.append(links.chain(lambda b, c=c: [gu_v.at[c, z_at(b), :], d_v.at[c * fc : (c + 1) * fc, z_at(b)]]))
            for g in running:
                next(g, None)
            yield

    begun = [ff_begin(0)]
    drain(gain_chain)
    drain(o_chain)
    for c in own_tok:
        c.wait()
    x_keep[...] = n_one[0:own_rows, :]
    next(tok_rows, None)

    def o_part(k, h):
        xx, tt = p.peer(k)
        size = wo_rows if h is None else wo_rows // 2
        start = tt * wo_rows + (0 if h is None else h * size)
        return w_o.at[xx, pl.ds(pl.multiple_of(start, size), size), :]

    o_spread = links.spread(o_part, absolute=True)
    next(o_spread)

    def norm(r, carry):
        at = pl.ds(pl.multiple_of(r * own_rows, own_rows), own_rows)
        v = n_one[at, :].astype(F32)
        scale = lax.rsqrt(jnp.mean(v * v, axis=-1, keepdims=True) + EPS)
        n_one[at, :] = (v * scale * gains[0:1, :]).astype(BF)
        return carry

    next(qkv_chain, None)
    lax.fori_loop(0, tensor, norm, 0)
    next(tok_rows, None)
    next(qkv_chain, None)
    for c in range(1, PRE):
        begun.append(ff_begin(c))
    ff_chain = ff_moves()
    next(ff_chain)
    cot_rows = links.rows(cotangent, cot_out, own_rows, [])
    next(cot_rows)
    drain(tok_rows)
    for m in tok_log:
        m.sent()
    lax.fori_loop(tensor, group, norm, 0)
    out_n = own(n_one, n_one_out)
    next(o_spread, None)
    drain(qkv_chain)
    out_w = own(w_qkv, w_qkv_out)

    def project(r, carry):
        at = pl.ds(pl.multiple_of(r * own_rows, own_rows), own_rows)
        lin = mm(n_one[at, :], w_qkv[...])
        per = own_rows // BLK
        for i in range(per):
            where = pl.ds(pl.multiple_of(r * own_rows + i * BLK, BLK), BLK)
            cos, sin = wide(cos_ref[where, :], cols), wide(sin_ref[where, :], cols)
            part = lin[i * BLK : (i + 1) * BLK, :]
            dst = pl.ds(pl.multiple_of(r * own_rows + i * BLK, BLK), BLK)
            qkv_rel[dst, 0:cols] = turn(part[:, 0:cols], cos, sin).astype(BF)
            qkv_rel[dst, cols : 2 * cols] = turn(part[:, cols : 2 * cols], cos, sin).astype(BF)
            qkv_rel[dst, 2 * cols : 3 * cols] = part[:, 2 * cols : 3 * cols].astype(BF)
        return carry

    lax.fori_loop(0, group, project, 0)

    def fill(b, carry):
        dst = pl.ds(pl.multiple_of(b * BLK, BLK), BLK)
        found = picked(qkv_rel, place_s[b])
        qs[dst, :] = found[:, 0:cols]
        ks[dst, :] = found[:, cols : 2 * cols]
        vs[dst, :] = found[:, 2 * cols : 3 * cols]
        return carry

    lax.fori_loop(0, rows // BLK, fill, 0)
    next(ff_chain, None)
    live = live_s[0]
    tiles = rows // QT
    for tile in range(tiles):
        attend_tile(tile, live, qs, ks, vs, os, stats)
        if tile == 1:
            next(cot_rows, None)
        if tile == 2:
            next(o_spread, None)
    next(ff_chain, None)

    def back_to_rows(j, carry):
        dst = pl.ds(pl.multiple_of(j * BLK, BLK), BLK)
        o_rel[dst, :] = picked(os, at_s[j])
        return carry

    lax.fori_loop(0, rows // BLK, back_to_rows, 0)

    def head_at(k):
        xx, tt = p.peer(k)
        return attn_rows.at[:, pl.ds(pl.multiple_of((tt * ctx + xx) * cols, cols), cols)]

    swaps = [
        links.send(o_rel.at[pl.ds(k * own_rows, own_rows), :], head_at(0), p.peer_id(k), head_at(k)) for k in range(1, group)
    ]
    own_heads = own(o_rel.at[pl.ds(0, own_rows), :], head_at(0))
    drain(o_spread)
    out_o = own(w_o, w_o_out)
    next(cot_rows, None)
    own_heads.wait()
    for m in swaps:
        m.come()
    for xx in range(ctx):
        span = shards * d_own
        mixed = mm(attn_rows[...], w_o[xx])
        for zz in range(shards):
            at = slice((zz * ctx + xx) * d_own, (zz * ctx + xx + 1) * d_own)
            h_own[:, at] = x_keep[:, at].astype(F32) + mixed[:, zz * d_own : (zz + 1) * d_own]
    h = h_own[...]
    scale = lax.rsqrt(jnp.mean(h * h, axis=-1, keepdims=True) + EPS)
    n_own[...] = (h * scale * gains[1:2, :]).astype(BF)
    out_h = own(h_own, h_out)
    own(n_own, n_all.at[pl.ds(0, own_rows), :]).wait()

    def n_part(k, h):
        if h is None:
            return n_all.at[pl.ds(k * own_rows, own_rows), :]
        return n_all.at[pl.ds(k * own_rows + h * (own_rows // 2), own_rows // 2), :]

    n_spread = links.spread(n_part)
    next(n_spread)
    next(ff_chain, None)
    next(n_spread, None)
    next(cot_rows, None)
    next(n_spread, None)
    drain(ff_chain)
    out_gu = own(gu_v, gu_out)
    out_d = own(d_v, d_out)
    drain(cot_rows)
    drain(n_spread)
    for m in links.moves:
        if m not in tok_log:
            m.sent()
    for c in (out_n, out_w, out_o, out_h, out_gu, out_d):
        c.wait()


def picked(ref, block):
    found = ref[0:BLK, :]
    for j in range(1, ref.shape[0] // BLK):
        found = jnp.where(block == j, ref[j * BLK : (j + 1) * BLK, :], found)
    return found


def attend_tile(t, live, qs, ks, vs, os, stats):
    rows, cols = qs.shape
    heads = cols // HDIM
    ext = (t + 1) * QT
    lane = lax.broadcasted_iota(jnp.int32, (QT, cols), 1) // HDIM
    qpos = lax.broadcasted_iota(jnp.int32, (QT, QT), 0)
    kpos = lax.broadcasted_iota(jnp.int32, (QT, QT), 1)
    diag = jnp.where(kpos <= qpos, 0.0, NEG)
    dead = jnp.where(lax.broadcasted_iota(jnp.int32, (1, ext), 1) < live, 0.0, NEG)

    def head(h, acc):
        q = jnp.where(lane == h, qs[t * QT : ext, :] * BF(0.125), BF(0))
        s = mm(q, ks[0:ext, :], NT) + dead
        last = s[:, t * QT :] + diag
        s = jnp.concatenate([s[:, : t * QT], last], axis=1) if t else last
        top = jnp.max(s, axis=1, keepdims=True)
        e = jnp.exp(s - top)
        total = jnp.sum(e, axis=1, keepdims=True)
        mixed = mm(e.astype(BF), vs[0:ext, :]) / total
        note = jnp.broadcast_to(top + jnp.log(total), (QT, 128))
        stats[pl.ds(h, 1), t * QT : ext] = jnp.transpose(note)[0:1, :]
        return jnp.where(lane == h, mixed, acc)

    acc = lax.fori_loop(0, heads, head, jnp.zeros((QT, cols), F32))
    os[t * QT : ext, :] = acc.astype(BF)


def first_call(shards, ctx, tensor, place, at, live, tokens, cotangent, gains, wq, wk, wv, w_out, wg, wu, wd, cos, sin):
    width = tokens.shape[1]
    own_rows = tokens.shape[0] // tensor
    group = ctx * tensor
    rows = own_rows * group
    d_own = wq.shape[0]
    cols = wq.shape[1] // ctx
    fc = cols
    dims = (shards, ctx, tensor, fc, own_rows, d_own)
    any_spec = pl.BlockSpec(memory_space=pl.ANY)
    smem = pl.BlockSpec(memory_space=pltpu.SMEM)
    vmem = pl.BlockSpec(memory_space=pltpu.VMEM)
    piece = jax.ShapeDtypeStruct((rows, cols), BF)
    moves = 400
    dma = pltpu.SemaphoreType.DMA
    return pl.pallas_call(
        functools.partial(first_kernel, dims),
        in_specs=[smem] * 3 + [any_spec] * 10 + [vmem] * 2,
        out_specs=[any_spec] * 8 + [vmem] * 7,
        out_shape=[
            jax.ShapeDtypeStruct((rows, width), BF),
            jax.ShapeDtypeStruct((width, 3 * cols), BF),
            jax.ShapeDtypeStruct((ctx, width, shards * d_own), BF),
            jax.ShapeDtypeStruct((rows, width), BF),
            jax.ShapeDtypeStruct((PRE, width, 2 * fc), BF),
            jax.ShapeDtypeStruct((PRE * fc, width), BF),
            jax.ShapeDtypeStruct((rows, width), BF),
            jax.ShapeDtypeStruct((own_rows, width), F32),
            jax.ShapeDtypeStruct((8, width), F32),
            piece,
            piece,
            piece,
            piece,
            jax.ShapeDtypeStruct((8, rows), F32),
            piece,
        ],
        scratch_shapes=[
            pltpu.VMEM((rows, width), BF),
            pltpu.VMEM((width, 3 * cols), BF),
            pltpu.VMEM((ctx, width, shards * d_own), BF),
            pltpu.VMEM((rows, 3 * cols), BF),
            pltpu.VMEM((own_rows, width), BF),
            pltpu.VMEM((own_rows, width), F32),
            pltpu.VMEM((own_rows, width), BF),
            pltpu.VMEM((own_rows, width), BF),
            pltpu.VMEM((PRE, width, 2 * fc), BF),
            pltpu.VMEM((PRE * fc, width), BF),
            dma((moves,)),
            dma((moves,)),
            dma((40,)),
        ],
        compiler_params=pltpu.CompilerParams(
            collective_id=0, has_side_effects=True, vmem_limit_bytes=62 * 1024 * 1024
        ),
        cost_estimate=pl.CostEstimate(
            flops=2 * rows * width * cols * 4, bytes_accessed=64 * 1024 * 1024, transcendentals=rows * rows * cols // HDIM
        ),
        name="first",
    )(place, at, live, tokens, cotangent, gains, wq, wk, wv, w_out, wg, wu, wd, cos, sin)


def mlp_kernel(
    dims, n_in, cot_far, cotangent, wg, wu, wd, gu_pre, d_pre,
    dn_out, out_out, mine_out, got_out, g_hbm, r_hbm,
    n2, cot, wgu_v, wd_v, hid, dgu, left_t, gt, st, ost, fin, away,
    x_own, x_send, x_recv, a_send, a_recv, g_sem, s_sem, rs_send, rs_recv, fx_send, fx_recv, o_sem, c_sem,
):
    shards, ctx, tensor, chunks, kept, fc, rows_own, d_own = dims
    rows, width = n2.shape
    dz = ctx * d_own
    ff = chunks * fc
    z = lax.axis_index("shard")
    x = lax.axis_index("ctx")
    t = lax.axis_index("tensor")
    p = Place(shards, ctx, tensor)
    above, below = p.above, p.below
    p.meet([1, tensor])

    here_too = (z, x, flip(t, 1))

    def remote(src, dst, send, recv, where):
        return pltpu.make_async_remote_copy(
            src_ref=src, dst_ref=dst, send_sem=send, recv_sem=recv, device_id=where, device_id_type=pl.DeviceIdType.MESH
        )

    def x_copies(c, own):
        half = x if own else 1 - x
        low_c = pl.multiple_of(half * ff + c * fc, fc)
        d_at = pl.ds(pl.multiple_of((z * ctx + x) * d_own, d_own), d_own)
        pairs = [
            (wg.at[:, pl.ds(low_c, fc)], wgu_v.at[c, d_at, pl.ds(0, fc)]),
            (wu.at[:, pl.ds(low_c, fc)], wgu_v.at[c, d_at, pl.ds(fc, fc)]),
            (wd.at[pl.ds(low_c, fc), :], wd_v.at[pl.ds(pl.multiple_of(c * fc, fc), fc), d_at]),
        ]
        if own:
            return [pltpu.make_async_copy(a, b, x_own.at[c, i]) for i, (a, b) in enumerate(pairs)]
        return [remote(a, b, x_send.at[c, i], x_recv.at[c, i], (z, 1 - x, t)) for i, (a, b) in enumerate(pairs)]

    def x_landed(c):
        d_at = pl.ds(pl.multiple_of((z * ctx + 1 - x) * d_own, d_own), d_own)
        lands = [
            wgu_v.at[c, d_at, pl.ds(0, fc)],
            wgu_v.at[c, d_at, pl.ds(fc, fc)],
            wd_v.at[pl.ds(pl.multiple_of(c * fc, fc), fc), d_at],
        ]
        return [remote(a, a, x_send.at[c, i], x_recv.at[c, i], here_too) for i, a in enumerate(lands)]

    def hop(c, way, k, b, wait=False):
        at = pl.ds(pl.multiple_of(b * dz, dz), dz)
        parts = [wgu_v.at[c, at, :], wd_v.at[pl.ds(pl.multiple_of(c * fc, fc), fc), at]]
        where = here_too if wait else above() if way == 0 else below()
        return [remote(p, p, a_send.at[c, way, k, i], a_recv.at[c, way, k, i], where) for i, p in enumerate(parts)]

    def hop_start(c, k):
        @pl.when((z >= k - 1) & (z < shards - 1))
        def _():
            for d in hop(c, 0, k - 1, z - (k - 1)):
                d.start()

        @pl.when((z + k - 1 <= shards - 1) & (z > 0))
        def _():
            for d in hop(c, 1, k - 1, z + (k - 1)):
                d.start()

    def hop_sent(c, k):
        @pl.when((z >= k - 1) & (z < shards - 1))
        def _():
            for d in hop(c, 0, k - 1, z - (k - 1)):
                d.wait_send()

        @pl.when((z + k - 1 <= shards - 1) & (z > 0))
        def _():
            for d in hop(c, 1, k - 1, z + (k - 1)):
                d.wait_send()

    def hop_wait(c, k):
        @pl.when(z >= k)
        def _():
            for d in hop(c, 0, k - 1, z - k, True):
                d.wait_recv()

        @pl.when(z + k <= shards - 1)
        def _():
            for d in hop(c, 1, k - 1, z + k, True):
                d.wait_recv()

    def x_start(c):
        for d in x_copies(c, False):
            d.start()
        for d in x_copies(c, True):
            d.start()

    if chunks > PRE:
        x_start(PRE)
    pre_copies = [
        pltpu.make_async_copy(gu_pre, wgu_v.at[pl.ds(0, PRE)], x_own.at[0, 0]),
        pltpu.make_async_copy(d_pre, wd_v.at[pl.ds(0, PRE * fc), :], x_own.at[0, 1]),
    ]
    for d in pre_copies:
        d.start()

    near = tensor * rows_own
    cot_copies = [pltpu.make_async_copy(cot_far.at[pl.ds(near, near), :], cot.at[pl.ds(near, near), :], c_sem.at[0])]
    for k in range(tensor):
        _, tt = p.peer(k)
        src = cotangent.at[pl.ds(pl.multiple_of(tt * rows_own, rows_own), rows_own), :]
        cot_copies.append(pltpu.make_async_copy(src, cot.at[pl.ds(k * rows_own, rows_own), :], c_sem.at[3 + k]))
    cot_copies.append(pltpu.make_async_copy(n_in, n2, c_sem.at[1]))
    for d in cot_copies:
        d.start()
    for c in range(PRE + 1, chunks):
        x_start(c)
    if chunks > PRE:
        for d in x_copies(PRE, True):
            d.wait()
        for d in x_landed(PRE):
            d.wait_recv()
        hop_start(PRE, 1)

    def ag_round(r, top):
        for k in range(shards - 1, 0, -1):
            if k > top:
                continue
            c = r - k + 1

            @pl.when((c >= PRE) & (c < chunks))
            def _(c=c, k=k):
                if k == 1:
                    for d in x_copies(c, True):
                        d.wait()
                    for d in x_landed(c):
                        d.wait_recv()
                else:
                    hop_wait(c, k - 1)
                hop_start(c, k)

    for d in cot_copies:
        d.wait()
    for d in pre_copies:
        d.wait()

    def block_of(i):
        down = shards - 1 - i
        down = down - jnp.where(down <= z, 1, 0)
        up = i + jnp.where(i >= z, 1, 0)
        return jnp.where(i == shards - 1, z, jnp.where(2 * z < shards, down, up))

    def g_copy(c, d, slot):
        return pltpu.make_async_copy(gt.at[slot], g_hbm.at[c, d], g_sem.at[slot])

    def rs_send_copy(src, c, way, d, wait=False):
        where = here_too if wait else above() if way == 0 else below()
        return remote(src, r_hbm.at[c, way, d], rs_send.at[c, way, d], rs_recv.at[c, way, d], where)

    combos = [(way, k) for k in range(2, shards) for way in (0, 1)]

    def target(way, k):
        return z + shards - k if way == 0 else z - (shards - k)

    def sends(way, k):
        if way == 0:
            return z < k
        return z >= shards - k

    def starts(way):
        return z == 0 if way == 0 else z == shards - 1

    def runs(way):
        return z != 0 if way == 0 else z != shards - 1

    def at_slot(first):
        return first // 2, (first >= 0) & (first % 2 == 0) & (first // 2 < kept)

    def rs_step(s):
        for way in (0, 1):
            for k in range(1, shards):
                c, due = at_slot(s - (k - 1))

                @pl.when(due & starts(way))
                def _(c=c, way=way, k=k):
                    d = target(way, k)
                    rs_send_copy(g_hbm.at[c, d], c, way, d).start()

        for i, (way, k) in enumerate(combos):
            c, due = at_slot(s - (k - 1))

            @pl.when(due & sends(way, k) & runs(way))
            def _(c=c, way=way, k=k, i=i):
                d = target(way, k)

                @pl.when(c >= 1)
                def _():
                    rs_send_copy(st.at[2 * i], c - 1, way, d).wait_send()

                rs_send_copy(st.at[2 * i], c, way, d, True).wait_recv()
                pltpu.make_async_copy(g_hbm.at[c, d], st.at[2 * i], s_sem.at[2 * i]).start()
                pltpu.make_async_copy(r_hbm.at[c, way, d], st.at[2 * i + 1], s_sem.at[2 * i + 1]).start()

        last = 2 * len(combos)
        c_fin, due_fin = at_slot(s - (shards - 1))

        @pl.when(due_fin)
        def _():
            pltpu.make_async_copy(g_hbm.at[c_fin, z], st.at[last], s_sem.at[last]).start()
            for way in (0, 1):
                slot = last + 1 + way

                @pl.when(runs(way))
                def _(way=way, slot=slot):
                    rs_send_copy(st.at[slot], c_fin, way, z, True).wait_recv()
                    pltpu.make_async_copy(r_hbm.at[c_fin, way, z], st.at[slot], s_sem.at[slot]).start()

                @pl.when(starts(way))
                def _(slot=slot):
                    st[slot] = jnp.zeros(st.shape[1:], BF)

        for i, (way, k) in enumerate(combos):
            c, due = at_slot(s - (k - 1))

            @pl.when(due & sends(way, k) & runs(way))
            def _(c=c, way=way, k=k, i=i):
                d = target(way, k)
                pltpu.make_async_copy(g_hbm.at[c, d], st.at[2 * i], s_sem.at[2 * i]).wait()
                pltpu.make_async_copy(r_hbm.at[c, way, d], st.at[2 * i + 1], s_sem.at[2 * i + 1]).wait()
                st[2 * i] = (st[2 * i].astype(F32) + st[2 * i + 1].astype(F32)).astype(BF)
                rs_send_copy(st.at[2 * i], c, way, d).start()

        @pl.when(due_fin)
        def _():
            pltpu.make_async_copy(g_hbm.at[c_fin, z], st.at[last], s_sem.at[last]).wait()
            for way in (0, 1):
                slot = last + 1 + way

                @pl.when(runs(way))
                def _(way=way, slot=slot):
                    pltpu.make_async_copy(r_hbm.at[c_fin, way, z], st.at[slot], s_sem.at[slot]).wait()

            @pl.when(c_fin >= 1)
            def _():
                pltpu.make_async_copy(fin, mine_out.at[c_fin - 1], c_sem.at[2]).wait()
                fin_copy(c_fin - 1).wait_send()

            total = st[last].astype(F32) + st[last + 1].astype(F32) + st[last + 2].astype(F32)
            low, high = total[:, :d_own], total[:, d_own:]
            fin[...] = jnp.where(x == 0, low, high)
            away[...] = jnp.where(x == 0, high, low).astype(BF)
            pltpu.make_async_copy(fin, mine_out.at[c_fin], c_sem.at[2]).start()
            fin_copy(c_fin).start()

    def fin_copy(c):
        return remote(away, got_out.at[c], fx_send.at[c], fx_recv.at[c], (z, 1 - x, t))

    tile = 512

    def phase_one(c):
        def body(r, carry):
            at = pl.ds(pl.multiple_of(r * tile, tile), tile)
            gu = mm(n2[at, :], wgu_v[c])
            dh = mm(cot[at, :], wd_v[pl.ds(pl.multiple_of(c * fc, fc), fc), :], NT)
            gate, up = gu[:, :fc], gu[:, fc:]
            sig = 1.0 / (1.0 + jnp.exp(-gate))
            act = gate * sig
            h = (act * up).astype(BF)
            dg = (dh * up * sig * (1.0 + gate * (1.0 - sig))).astype(BF)
            du = (dh * act).astype(BF)
            hid[c, at, :] = h
            dgu[c, at, 0:fc] = dg
            dgu[c, at, fc : 2 * fc] = du
            left_t[0:fc, at] = h.T
            left_t[fc : 2 * fc, at] = dg.T
            left_t[2 * fc : 3 * fc, at] = du.T
            return carry

        lax.fori_loop(0, rows // tile, body, 0)

    def phase_two(c):
        def body(i, carry):
            d = block_of(i)
            slot = i % 2
            at = pl.ds(pl.multiple_of(d * dz, dz), dz)

            @pl.when(i >= 2)
            def _():
                g_copy(c, block_of(i - 2), slot).wait()

            gt[slot, 0:fc, :] = mm(left_t[0:fc, :], cot[:, at]).astype(BF)
            gt[slot, fc : 3 * fc, :] = mm(left_t[fc : 3 * fc, :], n2[:, at]).astype(BF)
            g_copy(c, d, slot).start()
            return carry

        lax.fori_loop(0, shards, body, 0)
        for i in (shards - 2, shards - 1):
            g_copy(c, block_of(jnp.int32(i)), i % 2).wait()

    ot = 256
    units = rows // ot

    def tail_unit(u):
        at = pl.ds(pl.multiple_of((u % units) * ot, ot), ot)
        slot = u % 2

        @pl.when(u >= 2)
        def _():
            pltpu.make_async_copy(ost.at[slot], dn_out.at[at, :], o_sem.at[slot]).wait()

        @pl.when(u < units)
        def _():
            for n in range(width // 512):
                cols = slice(n * 512, (n + 1) * 512)
                acc = jnp.zeros((ot, 512), F32)
                for c in range(chunks):
                    acc = acc + mm(dgu[c, at, :], wgu_v[c, cols, :], NT)
                ost[slot, :, cols] = acc.astype(BF)
            pltpu.make_async_copy(ost.at[slot], dn_out.at[at, :], o_sem.at[slot]).start()

        @pl.when(u >= units)
        def _():
            for n in range(width // 512):
                cols = slice(n * 512, (n + 1) * 512)
                acc = jnp.zeros((ot, 512), F32)
                for c in range(chunks):
                    acc = acc + mm(hid[c, at, :], wd_v[c * fc : (c + 1) * fc, cols])
                ost[slot, :, cols] = acc.astype(BF)
            pltpu.make_async_copy(ost.at[slot], out_out.at[at, :], o_sem.at[slot]).start()

    tail_slots = 2 * (kept - 1) + shards - chunks if 2 * (kept - 1) + shards > chunks else 1
    per_slot = -(-2 * units // tail_slots)

    def slot_body(s, carry):
        @pl.when(s < chunks)
        def _():
            @pl.when(s >= PRE)
            def _():
                hop_wait(s, shards - 1)

            phase_one(s)
            phase_two(s)
            for i in range(shards - 3):
                ag_round(PRE + 1 + s * (shards - 3) + i, shards - 1)

        @pl.when(s >= chunks)
        def _():
            first_u = (s - chunks) * per_slot
            last_u = jnp.minimum(first_u + per_slot, 2 * units)

            def body(u, carry):
                tail_unit(u)
                return carry

            lax.fori_loop(first_u, last_u, body, 0)

        rs_step(s)
        return carry

    lax.fori_loop(0, chunks + tail_slots, slot_body, 0)

    for u in (2 * units - 2, 2 * units - 1):
        at = pl.ds((u % units) * ot, ot)
        pltpu.make_async_copy(ost.at[u % 2], out_out.at[at, :], o_sem.at[u % 2]).wait()
    for c in range(PRE, chunks):
        for d in x_copies(c, False):
            d.wait_send()
        for k in range(1, shards):
            hop_sent(c, k)
    for way in (0, 1):
        for k in range(1, shards):

            @pl.when(starts(way))
            def _(way=way, k=k):
                d = target(way, k)
                for c in range(kept):
                    rs_send_copy(g_hbm.at[c, d], c, way, d).wait_send()

    for i, (way, k) in enumerate(combos):

        @pl.when(sends(way, k) & runs(way))
        def _(way=way, k=k, i=i):
            rs_send_copy(st.at[2 * i], kept - 1, way, target(way, k)).wait_send()

    pltpu.make_async_copy(fin, mine_out.at[kept - 1], c_sem.at[2]).wait()
    fin_copy(kept - 1).wait_send()
    for c in range(kept):
        fin_copy(c).wait_recv()


def mlp_call(shards, ctx, tensor, n_all, cot, cotangent, wg, wu, wd, gu_pre, d_pre):
    rows, width = n_all.shape
    rows_own = rows // (ctx * tensor)
    d_own = wg.shape[0]
    ff = wg.shape[1] // ctx
    fc = gu_pre.shape[2] // 2
    chunks = ff // fc
    dz = ctx * d_own
    any_spec = pl.BlockSpec(memory_space=pl.ANY)
    stage = 4 * (shards - 2) + 3
    kept = chunks - chunks // 2
    dims = (shards, ctx, tensor, chunks, kept, fc, rows_own, d_own)
    dma = pltpu.SemaphoreType.DMA
    return pl.pallas_call(
        functools.partial(mlp_kernel, dims),
        in_specs=[any_spec] * 8,
        out_specs=[any_spec] * 6,
        out_shape=[
            jax.ShapeDtypeStruct((rows, width), BF),
            jax.ShapeDtypeStruct((rows, width), BF),
            jax.ShapeDtypeStruct((kept, 3 * fc, d_own), F32),
            jax.ShapeDtypeStruct((kept, 3 * fc, d_own), BF),
            jax.ShapeDtypeStruct((chunks, shards, 3 * fc, dz), BF),
            jax.ShapeDtypeStruct((kept, 2, shards, 3 * fc, dz), BF),
        ],
        scratch_shapes=[
            pltpu.VMEM((rows, width), BF),
            pltpu.VMEM((rows, width), BF),
            pltpu.VMEM((chunks, width, 2 * fc), BF),
            pltpu.VMEM((ff, width), BF),
            pltpu.VMEM((chunks, rows, fc), BF),
            pltpu.VMEM((chunks, rows, 2 * fc), BF),
            pltpu.VMEM((3 * fc, rows), BF),
            pltpu.VMEM((2, 3 * fc, dz), BF),
            pltpu.VMEM((stage, 3 * fc, dz), BF),
            pltpu.VMEM((2, 256, width), BF),
            pltpu.VMEM((3 * fc, d_own), F32),
            pltpu.VMEM((3 * fc, d_own), BF),
            dma((chunks, 3)),
            dma((chunks, 3)),
            dma((chunks, 3)),
            dma((chunks, 2, shards - 1, 2)),
            dma((chunks, 2, shards - 1, 2)),
            dma((2,)),
            dma((stage,)),
            dma((chunks, 2, shards)),
            dma((chunks, 2, shards)),
            dma((chunks,)),
            dma((chunks,)),
            dma((2,)),
            dma((3 + tensor,)),
        ],
        compiler_params=pltpu.CompilerParams(
            collective_id=1, has_side_effects=True, vmem_limit_bytes=63 * 1024 * 1024
        ),
        cost_estimate=pl.CostEstimate(
            flops=18 * rows * width * ff, bytes_accessed=100 * 1024 * 1024, transcendentals=rows * ff
        ),
        name="feed_forward",
    )(n_all, cot, cotangent, wg, wu, wd, gu_pre, d_pre)


def last_kernel(
    dims, place_s, at_s, live_s, g_late, dn_part, out_part, h_in, cot_in, tokens, gains_in, n_one, w_qkv_in, w_o_in, o_rel_in,
    os_in, qs, ks, vs, stats, cos_ref, sin_ref,
    result, grad_x, mine_o, got_o, mine_w, got_w, gain_out, mine_late, got_late, dh_all, dh_keep, o_land, o_parts, r_late,
    big, w_qkv, chip, c_land, parts_land, stage_own, tile_h, gains, dh_low, go_rel, go, delta, dq,
    d_rel, left_o, left_w, g_o, r_o, g_w, r_w, away_o, g_sum, g_land, g_chain, half_sum, fin_late, away_late,
    send_sems, recv_sems, own_sems,
):
    shards, ctx, tensor, own_rows, d_own, kept = dims
    p = Place(shards, ctx, tensor)
    z, x, t = p.z, p.x, p.t
    group = p.group
    rows, cols = qs.shape
    width = dh_low.shape[1]
    heads = cols // HDIM
    dz = ctx * d_own
    half = own_rows // 2
    d_seq = big.at[pl.ds(0, rows), pl.ds(0, 3 * cols)]
    links = Links(p, send_sems, recv_sems)
    count = [0]

    def own(src, dst):
        i = count[0]
        count[0] += 1
        c = pltpu.make_async_copy(src, dst, own_sems.at[i])
        c.start()
        return c

    p.meet(list(range(1, group)))

    def block(k):
        return pl.ds(k * own_rows, own_rows)

    def mine(k=0):
        _, tt = p.peer(k)
        return pl.ds(pl.multiple_of(tt * own_rows, own_rows), own_rows)

    orders = [p.bits_x + p.bits_y, p.bits_y + p.bits_x]

    def halves(land, in_hbm=False):
        have = [list(range(0, group, 2)), list(range(0, group, 2))]
        spot = 0
        for stage in range(len(orders[0])):
            step = []
            for h in (0, 1):
                bit = orders[h][stage]
                leave = [k for k in have[h] if k & bit]
                for i, k in enumerate(leave):
                    at = pl.ds(h * half, half)
                    dst = land.at[h, spot + i]
                    step.append((h, k, bit, spot + i, links.send(chip.at[k // 2, at, :], dst, p.peer_id(bit))))
                have[h] = [k for k in have[h] if not k & bit]
            spot += len(leave)
            yield
            for h, k, bit, i, m in step:
                m.come()
                at = pl.ds(h * half, half)
                keep = (k ^ bit) // 2
                if in_hbm:
                    own(land.at[h, i], stage_own.at[pl.ds(0, half), :]).wait()
                    came = stage_own[0:half, :].astype(F32)
                else:
                    came = land[h, i].astype(F32)
                total = chip[keep, at, :].astype(F32) + came
                if stage == len(orders[0]) - 1:
                    half_sum[at, :] = total
                else:
                    chip[keep, at, :] = total.astype(BF)
            for h, k, bit, i, m in step:
                m.sent()
                done_moves.append(m)

    done_moves = []

    late = r_late.shape[0]
    late_moves = {}

    def late_wait(copies, conds):
        for c, cond in zip(copies, conds):
            pl.when(cond)(c.wait)

    def tile_copy(src, slot, sem):
        return pltpu.make_async_copy(src, g_w.at[slot], own_sems.at[sem])

    for c in range(late):
        for k in range(1, shards):
            for way in (0, 1):
                d = z + shards - k if way == 0 else z - (shards - k)
                came = z + shards - (k + 1) if way == 0 else z - (shards - (k + 1))
                last = way == 1 and k == shards - 1
                dst = r_late.at[c, shards] if last else r_late.at[c, d]
                land = r_late.at[c, shards] if last else r_late.at[c, came]
                end = z == 0 if way == 0 else z == shards - 1
                mid = (z >= 1) & (z < k) if way == 0 else (z <= shards - 2) & (z >= shards - k)
                comes = (z >= 1) & (z <= k) if way == 0 else (z <= shards - 2) & (z >= shards - 1 - k)
                where = p.above() if way == 0 else p.below()
                src = g_late.at[kept + c, d]
                move = links.send(src, dst, where, land, end, comes)
                pair = g_w.at[2 * way]
                add = Move(
                    pltpu.make_async_remote_copy(
                        src_ref=pair,
                        dst_ref=dst,
                        send_sem=links.send_sems.at[move.place],
                        recv_sem=links.recv_sems.at[move.place],
                        device_id=where,
                        device_id_type=pl.DeviceIdType.MESH,
                    ),
                    move.due,
                    mid,
                    comes,
                )
                late_moves[c, k, way] = (move, add, d, mid)

    def late_sums():
        sent = []
        sem = late_sem
        for c in range(late):
            for k in range(2, shards):
                copies = []
                for m in sent:
                    m.sent()
                sent = []
                for way in (0, 1):
                    late_moves[c, k - 1, way][0].come()
                    _, add, d, mid = late_moves[c, k, way]
                    pair = [
                        tile_copy(g_late.at[kept + c, d], 2 * way, sem),
                        tile_copy(r_late.at[c, d], 2 * way + 1, sem + 1),
                    ]
                    sem += 2
                    for cp in pair:
                        pl.when(mid)(cp.start)
                    copies.append((way, add, mid, pair))
                for way, add, mid, pair in copies:

                    @pl.when(mid)
                    def _(way=way, pair=pair):
                        for cp in pair:
                            cp.wait()
                        g_w[2 * way] = plus(g_w[2 * way], g_w[2 * way + 1])

                    add.start()
                    sent.append(add)
                yield
            for m in sent:
                m.sent()
            sent = []
            for way in (0, 1):
                late_moves[c, shards - 1, way][0].come()
            has_low, has_high = z > 0, z < shards - 1
            loads = [
                (tile_copy(g_late.at[kept + c, z], 0, sem), None),
                (tile_copy(r_late.at[c, z], 1, sem + 1), has_low),
                (tile_copy(r_late.at[c, shards], 2, sem + 2), has_high),
            ]
            sem += 3
            for cp, cond in loads:
                cp.start() if cond is None else pl.when(cond)(cp.start)
            for cp, cond in loads:
                cp.wait() if cond is None else pl.when(cond)(cp.wait)

            fin = fin_late.at[pl.ds(0, 3 * cols), :]

            def half_of(xx):
                at = pl.ds(pl.multiple_of(xx * d_own, d_own), d_own)
                fin[...] = g_w[0, :, at].astype(F32)

                @pl.when(has_low)
                def _():
                    fin[...] += g_w[1, :, at].astype(F32)

                @pl.when(has_high)
                def _():
                    fin[...] += g_w[2, :, at].astype(F32)

            half_of(1 - x)
            if c > 0:
                across_late[-1].sent()
                done_moves.append(across_late[-1])
            away_late[...] = fin[...].astype(BF)
            across_late.append(links.send(away_late, got_late.at[c], p.peer_id(tensor)))
            half_of(x)
            keep = tile_out(c, sem)
            sem += 1
            keep.start()
            keep.wait()
            yield

    def tile_out(c, sem):
        return pltpu.make_async_copy(fin_late.at[pl.ds(0, 3 * cols), :], mine_late.at[c], own_sems.at[sem])

    across_late = []
    late_sem = 120
    late_steps = late_sums()

    odd = list(range(1, group, 2))
    core = [links.send(dn_part.at[block(k), :], c_land.at[k // 2], p.peer_id(1)) for k in odd]
    even = [own(dn_part.at[block(k - 1), :], chip.at[k // 2]) for k in odd]
    load_gain = own(gains_in, gains)
    load_h = [
        own(h_in.at[:, j * cols : (j + 1) * cols], dq.at[j * own_rows : (j + 1) * own_rows, :]) for j in range(width // cols)
    ]
    load_cot = own(cot_in.at[mine(), :], stage_own)
    load_o = own(w_o_in, big)
    load_w = own(w_qkv_in, w_qkv)
    core_out = [links.send(out_part.at[block(k), :], o_land.at[k // 2], p.peer_id(1), start=False) for k in odd]
    for i in range(group // 2):
        even[i].wait()
        core[i].come()
        chip[i] = plus(chip[i], c_land[i])
    sums = halves(parts_land)
    next(sums)
    next(late_steps, None)
    for m in core_out:
        m.start()
    load_gain.wait()
    for _ in sums:
        pass

    per = tile_h.shape[1]
    spans = [(slice(j * own_rows, (j + 1) * own_rows), slice(j * cols, (j + 1) * cols)) for j in range(width // cols)]

    def spread_out(r):
        return jnp.concatenate([dq[j * own_rows + r * per : j * own_rows + (r + 1) * per, :] for j in range(len(spans))], axis=1)

    for c in load_h:
        c.wait()
    load_cot.wait()
    for r in range(own_rows // per):
        at = pl.ds(r * per, per)
        h = spread_out(r)
        dn = half_sum[at, :]
        scale = lax.rsqrt(jnp.mean(h * h, axis=-1, keepdims=True) + EPS)
        normed = h * scale
        scaled = dn * gains[1:2, :]
        inner = jnp.mean(scaled * normed, axis=-1, keepdims=True)
        d_h = stage_own[at, :].astype(F32) + scale * (scaled - normed * inner)
        part = jnp.sum(dn * normed, axis=0, keepdims=True)
        g_sum[0, 0:1, :] = part if r == 0 else g_sum[0, 0:1, :] + part
        dh_low[at, :] = d_h.astype(BF)
        for j, (_, c) in enumerate(spans):
            dq[j * own_rows + r * per : j * own_rows + (r + 1) * per, :] = d_h[:, c]
    keep_dh = [own(dq.at[a, :], dh_keep.at[:, c]) for a, c in spans]
    own(dh_low, dh_all.at[block(0), :]).wait()
    next(late_steps, None)

    def dh_part(k, h):
        if h is None:
            return dh_all.at[block(k), :]
        return dh_all.at[pl.ds(k * own_rows + h * half, half), :]

    load_o.wait()
    wo_rows = width // tensor
    for tt in range(tensor):
        acc = jnp.zeros((own_rows, wo_rows), F32)
        for xx in range(ctx):
            left = jnp.concatenate(
                [dh_low[:, (zz * ctx + xx) * d_own : (zz * ctx + xx + 1) * d_own] for zz in range(shards)], axis=1
            )
            acc = acc + mm(left, big[xx * width + tt * wo_rows : xx * width + (tt + 1) * wo_rows, :], NT)
        stage_own[:, tt * wo_rows : (tt + 1) * wo_rows] = acc.astype(BF)

    def heads_of(k):
        xx, tt = p.peer(k)
        return stage_own.at[:, pl.ds(pl.multiple_of((tt * ctx + xx) * cols, cols), cols)]

    swaps = [links.send(heads_of(k), go_rel.at[block(k), :], p.peer_id(k)) for k in range(1, group)]
    own_heads = own(heads_of(0), go_rel.at[block(0), :])
    dh_rows = links.spread(dh_part)
    next(dh_rows)
    load_left = own(o_rel_in, d_rel.at[:, 0:cols])
    load_tok = own(tokens.at[mine(), :], dh_low)

    def output():
        for i in range(group // 2):
            even_copy = own(out_part.at[block(2 * i), :], chip.at[i])
            core_out[i].come()
            land_copy = own(o_land.at[i], stage_own)
            even_copy.wait()
            land_copy.wait()
            chip[i] = plus(chip[i], stage_own[...])
        steps = halves(o_parts, True)
        for _ in steps:
            yield
        loads = [own(h_in.at[pl.ds(r * per, per), :], tile_h.at[r]) for r in range(2)]
        for r in range(own_rows // per):
            at = pl.ds(r * per, per)
            loads[r].wait()
            stage_own[at, :] = (tile_h[r % 2] + half_sum[at, :]).astype(BF)
            if r + 2 < own_rows // per:
                loads.append(own(h_in.at[pl.ds((r + 2) * per, per), :], tile_h.at[r % 2]))
        own(stage_own, result.at[mine(), :]).wait()
        yield from everywhere(result)

    def everywhere(ref):
        def put(k, bit):
            return links.send(ref.at[mine(k), :], ref.at[mine(k), :], p.peer_id(bit), ref.at[mine(k | bit), :])

        cores = [put(0, 1)]
        have = [0]
        for bit in p.bits_y:
            step = [put(k, bit) for k in have]
            yield
            for m in step:
                m.come()
            new = [k | bit for k in have]
            cores += [put(k, 1) for k in new]
            have = have + new
        yield
        for m in cores:
            m.come()

    next(late_steps, None)
    own_heads.wait()
    for m in swaps:
        m.come()
    for m in swaps:
        m.sent()
        done_moves.append(m)

    def fill(b, carry):
        go[pl.ds(pl.multiple_of(b * BLK, BLK), BLK), :] = picked(go_rel, place_s[b])
        return carry

    lax.fori_loop(0, rows // BLK, fill, 0)
    load_os = own(os_in, go_rel)
    load_left.wait()
    for k in range(group):
        left_o[:, k * own_rows : (k + 1) * own_rows] = d_rel[k * own_rows : (k + 1) * own_rows, 0:cols].T
    load_os.wait()
    head_row = lax.broadcasted_iota(jnp.int32, (8, cols), 0)
    head_col = lax.broadcasted_iota(jnp.int32, (8, cols), 1) // HDIM
    pick = jnp.where(head_row == head_col, 1.0, 0.0)
    for i in range(rows // QT):
        part = slice(i * QT, (i + 1) * QT)
        both = go[part, :].astype(F32) * go_rel[part, :].astype(F32)
        delta[:, part] = lax.dot_general(pick, both, NT, precision=lax.Precision.HIGHEST, preferred_element_type=F32)
    for c in keep_dh:
        c.wait()
    dq[...] = jnp.zeros_like(dq)
    live = live_s[0]
    tiles = rows // QT

    def store(i, column, value, turned):
        at = slice(i * QT, (i + 1) * QT)
        if turned:
            value = turn(value, wide(cos_ref[at, :], cols), -wide(sin_ref[at, :], cols))
        d_seq[at, column * cols : (column + 1) * cols] = value.astype(BF)

    out_steps = output()

    def grads_o():
        steps = sums_along(g_o, r_o, fin_late.at[pl.ds(0, cols), :], away_o, got_o, mine_o)
        dh_block = d_rel.at[:, pl.ds(0, dz)]
        for i in range(shards):
            d = far_first(i)
            own(dh_all.at[:, pl.ds(pl.multiple_of(d * dz, dz), dz)], dh_block).wait()
            g_o[d] = mm(left_o[...], d_rel[:, 0:dz]).astype(BF)
            if i < shards - 2:
                next(steps)
                yield
        for _ in steps:
            yield

    def far_first(i):
        down = shards - 1 - i
        down = down - jnp.where(down <= z, 1, 0)
        up = i + jnp.where(i >= z, 1, 0)
        return z if i == shards - 1 else jnp.where(2 * z < shards, down, up)

    def sums_along(g, r, fin, away, got_ref, mine_ref):
        before = [None, None]
        for k in range(1, shards):
            now = []
            for way in (0, 1):
                d = z + shards - k if way == 0 else z - (shards - k)
                came = z + shards - (k + 1) if way == 0 else z - (shards - (k + 1))
                goes = z < k if way == 0 else z >= shards - k
                comes = (z >= 1) & (z <= k) if way == 0 else (z <= shards - 2) & (z >= shards - 1 - k)
                if k > 1:
                    before[way].come()
                    mid = (z >= 1) & (z < k) if way == 0 else (z <= shards - 2) & (z >= shards - k)

                    @pl.when(mid)
                    def _(d=d):
                        g[d] = plus(g[d], r[d])

                last = way == 1 and k == shards - 1
                dst = r.at[shards] if last else r.at[d]
                land = r.at[shards] if last else r.at[came]
                now.append(links.send(g.at[d], dst, p.above() if way == 0 else p.below(), land, goes, comes))
            before = now
            yield
        for m in before:
            m.come()

        def half_of(xx):
            at = pl.ds(pl.multiple_of(xx * d_own, d_own), d_own)
            fin[...] = g[z, :, at].astype(F32)

            @pl.when(z > 0)
            def _():
                fin[...] += r[z, :, at].astype(F32)

            @pl.when(z < shards - 1)
            def _():
                fin[...] += r[shards, :, at].astype(F32)

        half_of(1 - x)
        away[...] = fin[...].astype(BF)
        across = links.send(away, got_ref, p.peer_id(tensor))
        half_of(x)
        keep = own(fin, mine_ref)
        yield
        across.come()
        keep.wait()

    o_steps = None
    next(dh_rows)
    next(out_steps)
    for i in range(tiles):
        begin = i * QT

        def head(h, carry):
            dk, dv = carry
            kt = ks[begin : begin + QT, :]
            lane = lax.broadcasted_iota(jnp.int32, (QT, cols), 1) // HDIM
            km = jnp.where(lane == h, kt * BF(0.125), BF(0))
            dead = jnp.where(lax.broadcasted_iota(jnp.int32, (QT, 1), 0) + begin < live, 0.0, NEG)
            for j in range(i, tiles):
                at = slice(j * QT, (j + 1) * QT)
                qm = jnp.where(lane == h, qs[at, :] * BF(0.125), BF(0))
                gm = jnp.where(lane == h, go[at, :], BF(0))
                s = mm(kt, qm, NT) + dead
                if j == i:
                    kpos = lax.broadcasted_iota(jnp.int32, (QT, QT), 0)
                    qpos = lax.broadcasted_iota(jnp.int32, (QT, QT), 1)
                    s = s + jnp.where(kpos <= qpos, 0.0, NEG)
                e = jnp.exp(s - stats[pl.ds(h, 1), at])
                dp = mm(vs[begin : begin + QT, :], gm, NT)
                ds = (e * (dp - delta[pl.ds(h, 1), at])).astype(BF)
                dq[at, :] += mm(ds, km, TN)
                dk = dk + mm(ds, qm)
                dv = dv + mm(e.astype(BF), gm)
            return dk, dv

        zero = jnp.zeros((QT, cols), F32)
        dk, dv = lax.fori_loop(0, heads, head, (zero, zero))
        store(i, 1, dk, True)
        store(i, 2, dv, False)
        store(i, 0, dq[begin : begin + QT, :], True)
        next(late_steps, None)
        if i == 0:
            next(dh_rows, None)
        else:
            next(out_steps, None)
        if i == 1:
            drain(dh_rows)
            o_steps = grads_o()
        if i >= 1:
            next(o_steps, None)

    def back_to_rows(j, carry):
        dst = pl.ds(pl.multiple_of(j * BLK, BLK), BLK)
        d_rel[dst, :] = picked(d_seq, at_s[j])
        return carry

    lax.fori_loop(0, rows // BLK, back_to_rows, 0)
    drain(late_steps)
    for m in across_late:
        m.come()
    across_late[-1].sent()
    done_moves.append(across_late[-1])
    drain(out_steps)
    load_w.wait()

    def d_n_one(k, c):
        return mm(d_rel[k * own_rows : (k + 1) * own_rows, :], w_qkv[c, :], NT)

    quarters = [slice(c, c + width // 4) for c in range(0, width, width // 4)]

    load_n = []
    per_n = shards // ctx
    for d in range(shards):
        load_n.append(
            own(
                n_one.at[:, d * dz : (d + 1) * dz],
                big.at[(d // per_n) * rows : (d // per_n + 1) * rows, (d % per_n) * dz : (d % per_n + 1) * dz],
            )
        )
    load_dh = [own(dh_keep.at[:, c], dq.at[a, :]) for a, c in spans]
    core = []
    for i, k in enumerate(odd):
        for c in quarters:
            chip[i, :, c] = d_n_one(k, c).astype(BF)
        core.append(links.send(chip.at[i], c_land.at[i], p.peer_id(1)))
    next(o_steps, None)
    for k in range(group):
        left_w[:, k * own_rows : (k + 1) * own_rows] = d_rel[k * own_rows : (k + 1) * own_rows, :].T
    for c in load_n:
        c.wait()

    def n_block(d):
        row = pl.ds(pl.multiple_of((d // per_n) * rows, rows), rows)
        return big[row, pl.ds(pl.multiple_of((d % per_n) * dz, dz), dz)]

    w_steps = sums_along(g_w, r_w, fin_late.at[pl.ds(0, 3 * cols), :], away_late, got_w, mine_w)

    def grad_w(i):
        d = far_first(i)
        for i in range(3):
            at = slice(i * cols, (i + 1) * cols)
            g_w[d, at, :] = mm(left_w[at, :], n_block(d)).astype(BF)

    grad_w(0)
    next(w_steps)
    grad_w(1)
    for i in range(group // 2):
        core[i].sent()
        done_moves.append(core[i])
        core[i].come()
        for c in quarters:
            chip[i, :, c] = (d_n_one(2 * i, c) + c_land[i, :, c].astype(F32)).astype(BF)
    sums = halves(parts_land)
    next(sums)
    next(w_steps, None)
    for i in range(2, shards):
        grad_w(i)
        if i < shards - 1:
            next(w_steps, None)
    next(o_steps, None)
    for _ in sums:
        pass
    for c in load_dh:
        c.wait()
    load_tok.wait()
    for r in range(own_rows // per):
        at = pl.ds(r * per, per)
        v = dh_low[at, :].astype(F32)
        dn = half_sum[at, :]
        scale = lax.rsqrt(jnp.mean(v * v, axis=-1, keepdims=True) + EPS)
        normed = v * scale
        scaled = dn * gains[0:1, :]
        inner = jnp.mean(scaled * normed, axis=-1, keepdims=True)
        stage_own[at, :] = (spread_out(r) + scale * (scaled - normed * inner)).astype(BF)
        part = jnp.sum(dn * normed, axis=0, keepdims=True)
        g_sum[0, 1:2, :] = part if r == 0 else g_sum[0, 1:2, :] + part
    g_sum[0, 2:8, :] = jnp.zeros((6, width), F32)
    own(stage_own, grad_x.at[mine(), :]).wait()
    x_steps = everywhere(grad_x)
    next(x_steps)
    bit, i = 1, 0
    while bit < group:
        m = links.send(g_sum.at[i], g_land.at[i], p.peer_id(bit))
        m.come()
        g_sum[i + 1] = g_sum[i] + g_land[i]
        bit, i = bit * 2, i + 1
    own(g_sum.at[i], g_chain.at[z]).wait()
    g_steps = links.chain(lambda b: [g_chain.at[b]])
    next(g_steps)
    next(w_steps, None)
    next(x_steps, None)
    drain(g_steps)
    total = g_chain[0]
    for b in range(1, shards):
        total = total + g_chain[b]
    g_land[0] = total
    own(g_land.at[0, :, pl.ds(pl.multiple_of((z * ctx + x) * d_own, d_own), d_own)], gain_out).wait()
    drain(o_steps, x_steps, w_steps)
    for m in links.moves:
        if m not in done_moves:
            m.sent()


def last_call(
    shards, ctx, tensor, place, at, live, g_late, dn_part, out_part, hidden, cot, tokens, gains, n_one, w_qkv, w_o, o_rel,
    os, qs, ks, vs, stats, cos, sin,
):
    rows, cols = qs.shape
    width = hidden.shape[1]
    own_rows = hidden.shape[0]
    group = ctx * tensor
    d_own = width // (shards * ctx)
    dz = ctx * d_own
    chunks = g_late.shape[0]
    late = chunks // 2
    dims = (shards, ctx, tensor, own_rows, d_own, chunks - late)
    any_spec = pl.BlockSpec(memory_space=pl.ANY)
    smem = pl.BlockSpec(memory_space=pltpu.SMEM)
    vmem = pl.BlockSpec(memory_space=pltpu.VMEM)
    dma = pltpu.SemaphoreType.DMA
    half = own_rows // 2
    per = min(32, own_rows)
    bits = group.bit_length() - 1

    def out(shape, kind=BF):
        return jax.ShapeDtypeStruct(shape, kind)

    parts = (2, group // 2 - 1, half, width)
    return pl.pallas_call(
        functools.partial(last_kernel, dims),
        in_specs=[smem] * 3 + [any_spec] * 12 + [vmem] * 6,
        out_specs=[any_spec] * 14,
        out_shape=[
            out((tensor * own_rows, width)),
            out((tensor * own_rows, width)),
            out((cols, d_own), F32),
            out((cols, d_own)),
            out((3 * cols, d_own), F32),
            out((3 * cols, d_own)),
            out((8, d_own), F32),
            out((late, 3 * cols, d_own), F32),
            out((late, 3 * cols, d_own)),
            out((rows, width)),
            out((own_rows, width), F32),
            out((group // 2, own_rows, width)),
            out(parts),
            out((late, shards + 1, 3 * cols, dz)),
        ],
        scratch_shapes=[
            pltpu.VMEM((ctx * width, shards * d_own), BF),
            pltpu.VMEM((width, 3 * cols), BF),
            pltpu.VMEM((group // 2, own_rows, width), BF),
            pltpu.VMEM((group // 2, own_rows, width), BF),
            pltpu.VMEM(parts, BF),
            pltpu.VMEM((own_rows, width), BF),
            pltpu.VMEM((2, per, width), F32),
            pltpu.VMEM((8, width), F32),
            pltpu.VMEM((own_rows, width), BF),
            pltpu.VMEM((rows, cols), BF),
            pltpu.VMEM((rows, cols), BF),
            pltpu.VMEM((8, rows), F32),
            pltpu.VMEM((rows, cols), F32),
            pltpu.VMEM((rows, 3 * cols), BF),
            pltpu.VMEM((cols, rows), BF),
            pltpu.VMEM((3 * cols, rows), BF),
            pltpu.VMEM((shards, cols, dz), BF),
            pltpu.VMEM((shards + 1, cols, dz), BF),
            pltpu.VMEM((shards, 3 * cols, dz), BF),
            pltpu.VMEM((shards + 1, 3 * cols, dz), BF),
            pltpu.VMEM((cols, d_own), BF),
            pltpu.VMEM((bits + 1, 8, width), F32),
            pltpu.VMEM((bits, 8, width), F32),
            pltpu.VMEM((shards, 8, width), F32),
            pltpu.VMEM((own_rows, width), F32),
            pltpu.VMEM((3 * cols, d_own), F32),
            pltpu.VMEM((3 * cols, d_own), BF),
            dma((300,)),
            dma((300,)),
            dma((240,)),
        ],
        compiler_params=pltpu.CompilerParams(
            collective_id=2, has_side_effects=True, vmem_limit_bytes=63 * 1024 * 1024
        ),
        cost_estimate=pl.CostEstimate(
            flops=2 * rows * width * cols * 8, bytes_accessed=64 * 1024 * 1024, transcendentals=rows * rows * cols // HDIM
        ),
        name="last",
    )(place, at, live, g_late, dn_part, out_part, hidden, cot, tokens, gains, n_one, w_qkv, w_o, o_rel, os, qs, ks, vs, stats, cos, sin)


def per_device(
    shards, ctx, tensor, tokens, cotangent, seq_len, block_slot, attn_gain, w_query, w_key, w_value, w_out, mlp_gain, w_gate, w_up, w_down
):
    group = ctx * tensor
    my_x = lax.axis_index("ctx")
    my_t = lax.axis_index("tensor")
    me = my_x * tensor + my_t
    width = tokens.shape[1]
    own_rows = tokens.shape[0] // tensor
    level_rows = own_rows * group
    slots_each = own_rows // BLK
    d_own = w_query.shape[0]
    cols = w_query.shape[1] // ctx
    ff = w_gate.shape[1] // ctx
    slot = block_slot[0]
    place = ((slot // slots_each) ^ me) * slots_each + slot % slots_each
    order = jnp.arange(slot.shape[0], dtype=jnp.int32)
    at = jnp.sum(jnp.where(place[:, None] == order[None, :], order[:, None], 0), axis=0).astype(jnp.int32)

    def x_join(mine, got, axis):
        return jnp.where(
            my_x == 0, jnp.concatenate([mine, got], axis=axis), jnp.concatenate([got, mine], axis=axis)
        )

    angle_at = jnp.arange(level_rows, dtype=F32)
    lane = jnp.arange(128)
    freqs = THETA ** (-(lane % (HDIM // 2)).astype(F32) / (HDIM // 2))
    angles = angle_at[:, None] * freqs[None, :]
    cos = jnp.cos(angles)
    sin = jnp.sin(angles) * jnp.where(lane % HDIM < HDIM // 2, -1.0, 1.0)
    at_pos = (at[:, None] * BLK + jnp.arange(BLK)[None, :]).reshape(-1).astype(F32)
    angles = at_pos[:, None] * freqs[None, :]
    cos_rel = jnp.cos(angles)
    sin_rel = jnp.sin(angles) * jnp.where(lane % HDIM < HDIM // 2, -1.0, 1.0)
    gains = jnp.concatenate([jnp.stack([attn_gain, mlp_gain], axis=0).astype(F32), jnp.zeros((6, d_own), F32)], axis=0)
    n_one, w_qkv, w_o, cot, gu_pre, d_pre, n_two_own, hidden_res, gains, qs, ks, vs, os, stats, o_slot = first_call(
        shards, ctx, tensor, place.astype(jnp.int32), at, seq_len, tokens, cotangent, gains,
        w_query, w_key, w_value, w_out, w_gate, w_up, w_down, cos_rel, sin_rel,
    )
    dn_part, out_part, ff_mine, ff_got, g_late, _ = mlp_call(
        shards, ctx, tensor, n_two_own, cot, cotangent, w_gate, w_up, w_down, gu_pre, d_pre
    )

    result, grad_x, mine_o, got_o, mine_w, got_w, gain_sums, late_mine, late_got, *_ = last_call(
        shards, ctx, tensor, place.astype(jnp.int32), at, seq_len, g_late, dn_part, out_part, hidden_res, cotangent, tokens, gains,
        n_one, w_qkv, w_o.reshape(ctx * width, shards * d_own), o_slot, os, qs, ks, vs, stats, cos, sin,
    )
    ff_mine = jnp.concatenate([ff_mine, late_mine], axis=0)
    ff_got = jnp.concatenate([ff_got, late_got], axis=0)
    chunks = ff_mine.shape[0]
    fc = ff // chunks
    mine = ff_mine.reshape(chunks, 3, fc, d_own)
    got = ff_got.reshape(chunks, 3, fc, d_own).astype(F32)

    def spread(i):
        return x_join(mine[:, i].reshape(ff, d_own), got[:, i].reshape(ff, d_own), 0)

    grad_down = spread(0)
    grad_gate = spread(1).T
    grad_up = spread(2).T

    grad_out = x_join(mine_o, got_o.astype(F32), 0)
    mine = mine_w.reshape(3, cols, d_own)
    got = got_w.reshape(3, cols, d_own).astype(F32)
    grad_q, grad_k, grad_v = (x_join(mine[i], got[i], 0).T for i in range(3))
    grad_gain_two, grad_gain_one = gain_sums[0], gain_sums[1]
    return (
        result,
        grad_x,
        grad_gain_one,
        grad_q,
        grad_k,
        grad_v,
        grad_out,
        grad_gain_two,
        grad_gate,
        grad_up,
        grad_down,
    )


def solution(mesh):
    rows = P(("shard", "ctx"), None)
    gain = P(("shard", "ctx"))
    into = P(("shard", "ctx"), "tensor")
    back = P("tensor", ("shard", "ctx"))
    sizes = mesh.shape
    return jax.shard_map(
        functools.partial(per_device, sizes["shard"], sizes["ctx"], sizes["tensor"]),
        mesh=mesh,
        in_specs=(rows, rows, P("shard"), P("shard", None), gain, into, into, into, back, gain, into, into, back),
        out_specs=(rows, rows, gain, into, into, into, back, gain, into, into, back),
        check_vma=False,
    )
```

```python
import functools

import jax
import jax.numpy as jnp
from jax import lax
from jax.experimental import pallas as pl
from jax.experimental.pallas import tpu as pltpu
from jax.sharding import PartitionSpec as P

HDIM = 64
BLK = 128
EPS = 1e-05
THETA = 130000.0
NEG = -1e30
LEVEL = ("ctx", "tensor")
BF = jnp.bfloat16
F32 = jnp.float32
QT = 512
PRE = 2

NT = (((1,), (1,)), ((), ()))
TN = (((0,), (0,)), ((), ()))


def mm(left, right, dims=None):
    if dims is None:
        return jnp.dot(left, right, preferred_element_type=F32)
    return lax.dot_general(left, right, dims, preferred_element_type=F32)


def level_bits(ctx, tensor):
    bits_y = []
    bit = 2
    while bit < tensor:
        bits_y.append(bit)
        bit *= 2
    bits_x = []
    bit = tensor
    while bit < ctx * tensor:
        bits_x.append(bit)
        bit *= 2
    return bits_y, bits_x


def plus(a, b):
    return (a.astype(F32) + b.astype(F32)).astype(BF)


def turn(u, cos, sin):
    lane = lax.broadcasted_iota(jnp.int32, u.shape, 1)
    width = u.shape[1]
    ahead = pltpu.roll(u, width - HDIM // 2, axis=1)
    behind = pltpu.roll(u, HDIM // 2, axis=1)
    other = jnp.where(lane % HDIM < HDIM // 2, ahead, behind)
    return u * cos + other * sin


def wide(table, cols):
    reps = cols // table.shape[1]
    return jnp.concatenate([table] * reps, axis=1) if reps > 1 else table


def flip(index, bit):
    return index + bit - 2 * bit * ((index // bit) % 2)


class Place:
    def __init__(self, shards, ctx, tensor):
        self.shards, self.ctx, self.tensor = shards, ctx, tensor
        self.group = ctx * tensor
        self.z = lax.axis_index("shard")
        self.x = lax.axis_index("ctx")
        self.t = lax.axis_index("tensor")
        self.bits_y, self.bits_x = level_bits(ctx, tensor)

    def peer(self, offset):
        t, x = self.t, self.x
        bit = 1
        while bit < self.group:
            if offset & bit:
                if bit < self.tensor:
                    t = flip(t, bit)
                else:
                    x = 1 - x
            bit *= 2
        return x, t

    def peer_id(self, offset):
        x, t = self.peer(offset)
        return (self.z, x, t)

    def above(self):
        return (self.z + 1, self.x, self.t)

    def below(self):
        return (self.z - 1, self.x, self.t)

    def meet(self, offsets, chain=True):
        barrier = pltpu.get_barrier_semaphore()
        z, shards = self.z, self.shards
        for k in offsets:
            pl.semaphore_signal(barrier, inc=1, device_id=self.peer_id(k), device_id_type=pl.DeviceIdType.MESH)
        peers = len(offsets)
        if chain:

            @pl.when(z < shards - 1)
            def _():
                pl.semaphore_signal(barrier, inc=1, device_id=self.above(), device_id_type=pl.DeviceIdType.MESH)

            @pl.when(z > 0)
            def _():
                pl.semaphore_signal(barrier, inc=1, device_id=self.below(), device_id_type=pl.DeviceIdType.MESH)

            peers = peers + (z + shards - 1) // shards + (2 * shards - 2 - z) // shards
        pl.semaphore_wait(barrier, peers)


class Move:
    def __init__(self, out, due, goes, comes, place=None):
        self.out, self.due, self.goes, self.comes, self.place = out, due, goes, comes, place

    def _run(self, cond, fn):
        if cond is None:
            fn()
        else:
            pl.when(cond)(fn)

    def start(self):
        self._run(self.goes, self.out.start)

    def come(self):
        self._run(self.comes, self.due.wait_recv)

    def sent(self):
        self._run(self.goes, self.out.wait_send)


class Links:
    def __init__(self, place, send_sems, recv_sems):
        self.place, self.send_sems, self.recv_sems = place, send_sems, recv_sems
        self.moves = []

    def send(self, src, dst, where, land=None, goes=None, comes=None, start=True):
        i = len(self.moves)
        land = dst if land is None else land
        safe = self.place.peer_id(1)

        def copy(a, b, w):
            return pltpu.make_async_remote_copy(
                src_ref=a,
                dst_ref=b,
                send_sem=self.send_sems.at[i],
                recv_sem=self.recv_sems.at[i],
                device_id=w,
                device_id_type=pl.DeviceIdType.MESH,
            )

        move = Move(copy(src, dst, where), copy(land, land, safe), goes, comes, i)
        self.moves.append(move)
        if start:
            move.start()
        return move

    def all_sent(self):
        for m in self.moves:
            m.sent()


    def chain(self, parts):
        p = self.place
        z, shards = p.z, p.shards
        due = []
        for k in range(1, shards):
            for m in due:
                m.come()
            due = []
            up = zip(parts(z - (k - 1)), parts(z - k))
            for src, land in up:
                due.append(self.send(src, src, p.above(), land, (z >= k - 1) & (z < shards - 1), z >= k))
            down = zip(parts(z + (k - 1)), parts(z + k))
            for src, land in down:
                due.append(
                    self.send(src, src, p.below(), land, (z + k - 1 <= shards - 1) & (z > 0), z + k <= shards - 1)
                )
            yield
        for m in due:
            m.come()

    def spread(self, part, absolute=False):
        p = self.place

        def put(k, bit, h):
            return self.send(part(k, h), part(k if absolute else k | bit, h), p.peer_id(bit), part(k | bit, h))

        cores = [put(0, 1, None)]
        have = [[0], [0]]
        found = {}
        orders = [p.bits_x + p.bits_y, p.bits_y + p.bits_x]
        for stage in range(len(orders[0])):
            step = []
            for h in (0, 1):
                bit = orders[h][stage]
                step += [(k | bit, put(k, bit, h)) for k in have[h]]
                have[h] = have[h] + [k | bit for k in have[h]]
            yield
            for k, m in step:
                m.come()
                found[k] = found.get(k, 0) + 1
                if found[k] == 2:
                    cores.append(put(k, 1, None))
        yield
        for m in cores:
            m.come()

    def rows(self, source, keep, own_rows, log):
        p = self.place

        def slot(k):
            return keep.at[pl.ds(k * own_rows, own_rows), :]

        mine = source.at[pl.ds(pl.multiple_of(p.t * own_rows, own_rows), own_rows), :]
        first = self.send(mine, slot(p.tensor), p.peer_id(p.tensor))
        log.append(first)
        yield
        first.come()
        far = [p.tensor]
        for bit in p.bits_y:
            step = [self.send(slot(k), slot(k | bit), p.peer_id(bit)) for k in far]
            log += step
            yield
            for m in step:
                m.come()
            far = far + [k | bit for k in far]
        last = [self.send(slot(k), slot(k | 1), p.peer_id(1)) for k in far]
        log += last
        yield
        for m in last:
            m.come()


def drain(*gens):
    for g in gens:
        for _ in g:
            pass


def first_kernel(
    dims, place_s, at_s, live_s, tokens, cotangent, gains_in, wq, wk, wv, w_out, wg, wu, wd, cos_ref, sin_ref,
    n_one_out, w_qkv_out, w_o_out, cot_out, gu_out, d_out, n_all, h_out, gains, qs, ks, vs, os, stats, o_rel,
    n_one, w_qkv, w_o, qkv_rel, attn_rows, h_own, n_own, x_keep, gu_v, d_v, cos_v, sin_v,
    send_sems, recv_sems, own_sems,
):
    shards, ctx, tensor, fc, own_rows, d_own = dims
    p = Place(shards, ctx, tensor)
    z, x, t = p.z, p.x, p.t
    group = p.group
    rows, width = n_one.shape
    cols = qs.shape[1]
    heads = cols // HDIM
    ff = wg.shape[1] // ctx
    dz = ctx * d_own
    links = Links(p, send_sems, recv_sems)
    own_count = [0]

    def own(src, dst):
        i = own_count[0]
        own_count[0] += 1
        c = pltpu.make_async_copy(src, dst, own_sems.at[i])
        c.start()
        return c

    p.meet(list(range(1, group)))

    def d_at(xx):
        return pl.ds(pl.multiple_of((z * ctx + xx) * d_own, d_own), d_own)

    def z_at(b):
        return pl.ds(pl.multiple_of(b * dz, dz), dz)

    def part_cols(xx, size):
        return pl.ds(pl.multiple_of(xx * size, size), size)

    across = p.peer_id(tensor)

    wo_rows = w_out.shape[0]

    def o_at(tt, xx, zz):
        return w_o.at[xx, pl.ds(pl.multiple_of(tt * wo_rows, wo_rows), wo_rows), pl.ds(pl.multiple_of(zz * d_own, d_own), d_own)]

    own_o = own(w_out, o_at(t, x, z))
    own_gain = own(gains_in, gains.at[:, d_at(x)])
    own_w = [own(w.at[:, part_cols(x, cols)], w_qkv.at[d_at(x), i * cols : (i + 1) * cols]) for i, w in enumerate((wq, wk, wv))]
    own_gain.wait()
    gain_x = links.send(gains.at[:, d_at(x)], gains.at[:, d_at(x)], across, gains.at[:, d_at(1 - x)])
    qkv_x = [
        links.send(
            w.at[:, part_cols(1 - x, cols)],
            w_qkv.at[d_at(x), i * cols : (i + 1) * cols],
            across,
            w_qkv.at[d_at(1 - x), i * cols : (i + 1) * cols],
        )
        for i, w in enumerate((wq, wk, wv))
    ]
    tok_log = []
    tok_rows = links.rows(tokens, n_one, own_rows, tok_log)
    next(tok_rows)
    own_tok = []
    for k in range(tensor):
        _, tt = p.peer(k)
        src = tokens.at[pl.ds(pl.multiple_of(tt * own_rows, own_rows), own_rows), :]
        own_tok.append(own(src, n_one.at[pl.ds(k * own_rows, own_rows), :]))
    own_o.wait()
    o_chain = links.chain(lambda b: [o_at(t, x, b)])
    next(o_chain)
    gain_x.come()
    gain_chain = links.chain(lambda b: [gains.at[:, z_at(b)]])
    next(gain_chain)
    next(o_chain, None)
    for c in own_w:
        c.wait()
    for m in qkv_x:
        m.come()
    next(gain_chain, None)
    qkv_chain = links.chain(lambda b: [w_qkv.at[z_at(b), :]])
    next(qkv_chain)

    gu_pairs = [(wg, 0), (wu, 1)]

    def gu_place(c, xx, i):
        return gu_v.at[c, d_at(xx), i * fc : (i + 1) * fc]

    def ff_begin(c):
        at = [pl.ds(pl.multiple_of(xx * ff + c * fc, fc), fc) for xx in (x, 1 - x)]
        d_rows = slice(c * fc, (c + 1) * fc)
        mine = [own(w.at[:, at[0]], gu_place(c, x, i)) for w, i in gu_pairs]
        mine.append(own(wd.at[at[0], :], d_v.at[d_rows, d_at(x)]))
        came = [links.send(w.at[:, at[1]], gu_place(c, x, i), across, gu_place(c, 1 - x, i)) for w, i in gu_pairs]
        came.append(links.send(wd.at[at[1], :], d_v.at[d_rows, d_at(x)], across, d_v.at[d_rows, d_at(1 - x)]))
        return mine, came

    def ff_moves():
        running = []
        for c in range(PRE + shards):
            if c < PRE:
                mine, came = begun[c]
                for m in mine:
                    m.wait()
                for m in came:
                    m.come()
                running.append(links.chain(lambda b, c=c: [gu_v.at[c, z_at(b), :], d_v.at[c * fc : (c + 1) * fc, z_at(b)]]))
            for g in running:
                next(g, None)
            yield

    begun = [ff_begin(0)]
    drain(gain_chain)
    drain(o_chain)
    for c in own_tok:
        c.wait()
    x_keep[...] = n_one[0:own_rows, :]
    next(tok_rows, None)

    def o_part(k, h):
        xx, tt = p.peer(k)
        size = wo_rows if h is None else wo_rows // 2
        start = tt * wo_rows + (0 if h is None else h * size)
        return w_o.at[xx, pl.ds(pl.multiple_of(start, size), size), :]

    o_spread = links.spread(o_part, absolute=True)
    next(o_spread)

    def norm(r, carry):
        at = pl.ds(pl.multiple_of(r * own_rows, own_rows), own_rows)
        v = n_one[at, :].astype(F32)
        scale = lax.rsqrt(jnp.mean(v * v, axis=-1, keepdims=True) + EPS)
        n_one[at, :] = (v * scale * gains[0:1, :]).astype(BF)
        return carry

    next(qkv_chain, None)

    def tables(j, carry):
        dst = pl.ds(pl.multiple_of(j * BLK, BLK), BLK)
        cos_v[dst, :] = picked(cos_ref, at_s[j])
        sin_v[dst, :] = picked(sin_ref, at_s[j])
        return carry

    lax.fori_loop(0, rows // BLK, tables, 0)
    lax.fori_loop(0, tensor, norm, 0)
    next(tok_rows, None)
    next(qkv_chain, None)
    for c in range(1, PRE):
        begun.append(ff_begin(c))
    ff_chain = ff_moves()
    next(ff_chain)
    cot_rows = links.rows(cotangent, cot_out, own_rows, [])
    next(cot_rows)
    drain(tok_rows)
    for m in tok_log:
        m.sent()
    lax.fori_loop(tensor, group, norm, 0)
    out_n = own(n_one, n_one_out)
    next(o_spread, None)
    drain(qkv_chain)
    out_w = own(w_qkv, w_qkv_out)

    def project(r, carry):
        at = pl.ds(pl.multiple_of(r * own_rows, own_rows), own_rows)
        lin = mm(n_one[at, :], w_qkv[...])
        per = own_rows // BLK
        for i in range(per):
            where = pl.ds(pl.multiple_of(r * own_rows + i * BLK, BLK), BLK)
            cos, sin = wide(cos_v[where, :], cols), wide(sin_v[where, :], cols)
            part = lin[i * BLK : (i + 1) * BLK, :]
            dst = pl.ds(pl.multiple_of(r * own_rows + i * BLK, BLK), BLK)
            qkv_rel[dst, 0:cols] = turn(part[:, 0:cols], cos, sin).astype(BF)
            qkv_rel[dst, cols : 2 * cols] = turn(part[:, cols : 2 * cols], cos, sin).astype(BF)
            qkv_rel[dst, 2 * cols : 3 * cols] = part[:, 2 * cols : 3 * cols].astype(BF)
        return carry

    lax.fori_loop(0, group, project, 0)

    def fill(b, carry):
        dst = pl.ds(pl.multiple_of(b * BLK, BLK), BLK)
        found = picked(qkv_rel, place_s[b])
        qs[dst, :] = found[:, 0:cols]
        ks[dst, :] = found[:, cols : 2 * cols]
        vs[dst, :] = found[:, 2 * cols : 3 * cols]
        return carry

    lax.fori_loop(0, rows // BLK, fill, 0)
    next(ff_chain, None)
    live = live_s[0]
    tiles = rows // QT
    for tile in range(tiles):
        attend_tile(tile, live, qs, ks, vs, os, stats)
        if tile == 1:
            next(cot_rows, None)
        if tile == 2:
            next(o_spread, None)
    next(ff_chain, None)

    def back_to_rows(j, carry):
        dst = pl.ds(pl.multiple_of(j * BLK, BLK), BLK)
        o_rel[dst, :] = picked(os, at_s[j])
        return carry

    lax.fori_loop(0, rows // BLK, back_to_rows, 0)

    def head_at(k):
        xx, tt = p.peer(k)
        return attn_rows.at[:, pl.ds(pl.multiple_of((tt * ctx + xx) * cols, cols), cols)]

    swaps = [
        links.send(o_rel.at[pl.ds(k * own_rows, own_rows), :], head_at(0), p.peer_id(k), head_at(k)) for k in range(1, group)
    ]
    own_heads = own(o_rel.at[pl.ds(0, own_rows), :], head_at(0))
    drain(o_spread)
    out_o = own(w_o, w_o_out)
    next(cot_rows, None)
    own_heads.wait()
    for m in swaps:
        m.come()
    for xx in range(ctx):
        span = shards * d_own
        mixed = mm(attn_rows[...], w_o[xx])
        for zz in range(shards):
            at = slice((zz * ctx + xx) * d_own, (zz * ctx + xx + 1) * d_own)
            h_own[:, at] = x_keep[:, at].astype(F32) + mixed[:, zz * d_own : (zz + 1) * d_own]
    h = h_own[...]
    scale = lax.rsqrt(jnp.mean(h * h, axis=-1, keepdims=True) + EPS)
    n_own[...] = (h * scale * gains[1:2, :]).astype(BF)
    out_h = own(h_own, h_out)
    own(n_own, n_all.at[pl.ds(0, own_rows), :]).wait()

    def n_part(k, h):
        if h is None:
            return n_all.at[pl.ds(k * own_rows, own_rows), :]
        return n_all.at[pl.ds(k * own_rows + h * (own_rows // 2), own_rows // 2), :]

    n_spread = links.spread(n_part)
    next(n_spread)
    next(ff_chain, None)
    next(n_spread, None)
    next(cot_rows, None)
    next(n_spread, None)
    drain(ff_chain)
    out_gu = own(gu_v, gu_out)
    out_d = own(d_v, d_out)
    drain(cot_rows)
    drain(n_spread)
    for m in links.moves:
        if m not in tok_log:
            m.sent()
    for c in (out_n, out_w, out_o, out_h, out_gu, out_d):
        c.wait()


def picked(ref, block):
    found = ref[0:BLK, :]
    for j in range(1, ref.shape[0] // BLK):
        found = jnp.where(block == j, ref[j * BLK : (j + 1) * BLK, :], found)
    return found


def attend_tile(t, live, qs, ks, vs, os, stats):
    rows, cols = qs.shape
    heads = cols // HDIM
    ext = (t + 1) * QT
    lane = lax.broadcasted_iota(jnp.int32, (QT, cols), 1) // HDIM
    qpos = lax.broadcasted_iota(jnp.int32, (QT, QT), 0)
    kpos = lax.broadcasted_iota(jnp.int32, (QT, QT), 1)
    diag = jnp.where(kpos <= qpos, 0.0, NEG)
    dead = jnp.where(lax.broadcasted_iota(jnp.int32, (1, ext), 1) < live, 0.0, NEG)

    def head(h, acc):
        q = jnp.where(lane == h, qs[t * QT : ext, :] * BF(0.125), BF(0))
        s = mm(q, ks[0:ext, :], NT) + dead
        last = s[:, t * QT :] + diag
        s = jnp.concatenate([s[:, : t * QT], last], axis=1) if t else last
        top = jnp.max(s, axis=1, keepdims=True)
        e = jnp.exp(s - top)
        total = jnp.sum(e, axis=1, keepdims=True)
        mixed = mm(e.astype(BF), vs[0:ext, :]) / total
        note = jnp.broadcast_to(top + jnp.log(total), (QT, 128))
        stats[pl.ds(h, 1), t * QT : ext] = jnp.transpose(note)[0:1, :]
        return jnp.where(lane == h, mixed, acc)

    acc = lax.fori_loop(0, heads, head, jnp.zeros((QT, cols), F32))
    os[t * QT : ext, :] = acc.astype(BF)


def first_call(shards, ctx, tensor, place, at, live, tokens, cotangent, gains, wq, wk, wv, w_out, wg, wu, wd, cos, sin):
    width = tokens.shape[1]
    own_rows = tokens.shape[0] // tensor
    group = ctx * tensor
    rows = own_rows * group
    d_own = wq.shape[0]
    cols = wq.shape[1] // ctx
    fc = cols
    dims = (shards, ctx, tensor, fc, own_rows, d_own)
    any_spec = pl.BlockSpec(memory_space=pl.ANY)
    smem = pl.BlockSpec(memory_space=pltpu.SMEM)
    vmem = pl.BlockSpec(memory_space=pltpu.VMEM)
    piece = jax.ShapeDtypeStruct((rows, cols), BF)
    moves = 400
    dma = pltpu.SemaphoreType.DMA
    return pl.pallas_call(
        functools.partial(first_kernel, dims),
        in_specs=[smem] * 3 + [any_spec] * 10 + [vmem] * 2,
        out_specs=[any_spec] * 8 + [vmem] * 7,
        out_shape=[
            jax.ShapeDtypeStruct((rows, width), BF),
            jax.ShapeDtypeStruct((width, 3 * cols), BF),
            jax.ShapeDtypeStruct((ctx, width, shards * d_own), BF),
            jax.ShapeDtypeStruct((rows, width), BF),
            jax.ShapeDtypeStruct((PRE, width, 2 * fc), BF),
            jax.ShapeDtypeStruct((PRE * fc, width), BF),
            jax.ShapeDtypeStruct((rows, width), BF),
            jax.ShapeDtypeStruct((own_rows, width), F32),
            jax.ShapeDtypeStruct((8, width), F32),
            piece,
            piece,
            piece,
            piece,
            jax.ShapeDtypeStruct((8, rows), F32),
            piece,
        ],
        scratch_shapes=[
            pltpu.VMEM((rows, width), BF),
            pltpu.VMEM((width, 3 * cols), BF),
            pltpu.VMEM((ctx, width, shards * d_own), BF),
            pltpu.VMEM((rows, 3 * cols), BF),
            pltpu.VMEM((own_rows, width), BF),
            pltpu.VMEM((own_rows, width), F32),
            pltpu.VMEM((own_rows, width), BF),
            pltpu.VMEM((own_rows, width), BF),
            pltpu.VMEM((PRE, width, 2 * fc), BF),
            pltpu.VMEM((PRE * fc, width), BF),
            pltpu.VMEM((rows, 128), F32),
            pltpu.VMEM((rows, 128), F32),
            dma((moves,)),
            dma((moves,)),
            dma((40,)),
        ],
        compiler_params=pltpu.CompilerParams(
            collective_id=0, has_side_effects=True, vmem_limit_bytes=62 * 1024 * 1024
        ),
        cost_estimate=pl.CostEstimate(
            flops=2 * rows * width * cols * 4, bytes_accessed=64 * 1024 * 1024, transcendentals=rows * rows * cols // HDIM
        ),
        name="first",
    )(place, at, live, tokens, cotangent, gains, wq, wk, wv, w_out, wg, wu, wd, cos, sin)


def mlp_kernel(
    dims, n_in, cot_far, cotangent, wg, wu, wd, gu_pre, d_pre,
    dn_out, out_out, mine_out, got_out, g_hbm, r_hbm,
    n2, cot, wgu_v, wd_v, hid, dgu, left_t, gt, st, ost, fin, away,
    x_own, x_send, x_recv, a_send, a_recv, g_sem, s_sem, rs_send, rs_recv, fx_send, fx_recv, o_sem, c_sem,
):
    shards, ctx, tensor, chunks, kept, fc, rows_own, d_own = dims
    rows, width = n2.shape
    dz = ctx * d_own
    ff = chunks * fc
    z = lax.axis_index("shard")
    x = lax.axis_index("ctx")
    t = lax.axis_index("tensor")
    p = Place(shards, ctx, tensor)
    above, below = p.above, p.below
    p.meet([1, tensor])

    here_too = (z, x, flip(t, 1))

    def remote(src, dst, send, recv, where):
        return pltpu.make_async_remote_copy(
            src_ref=src, dst_ref=dst, send_sem=send, recv_sem=recv, device_id=where, device_id_type=pl.DeviceIdType.MESH
        )

    def x_copies(c, own):
        half = x if own else 1 - x
        low_c = pl.multiple_of(half * ff + c * fc, fc)
        d_at = pl.ds(pl.multiple_of((z * ctx + x) * d_own, d_own), d_own)
        pairs = [
            (wg.at[:, pl.ds(low_c, fc)], wgu_v.at[c, d_at, pl.ds(0, fc)]),
            (wu.at[:, pl.ds(low_c, fc)], wgu_v.at[c, d_at, pl.ds(fc, fc)]),
            (wd.at[pl.ds(low_c, fc), :], wd_v.at[pl.ds(pl.multiple_of(c * fc, fc), fc), d_at]),
        ]
        if own:
            return [pltpu.make_async_copy(a, b, x_own.at[c, i]) for i, (a, b) in enumerate(pairs)]
        return [remote(a, b, x_send.at[c, i], x_recv.at[c, i], (z, 1 - x, t)) for i, (a, b) in enumerate(pairs)]

    def x_landed(c):
        d_at = pl.ds(pl.multiple_of((z * ctx + 1 - x) * d_own, d_own), d_own)
        lands = [
            wgu_v.at[c, d_at, pl.ds(0, fc)],
            wgu_v.at[c, d_at, pl.ds(fc, fc)],
            wd_v.at[pl.ds(pl.multiple_of(c * fc, fc), fc), d_at],
        ]
        return [remote(a, a, x_send.at[c, i], x_recv.at[c, i], here_too) for i, a in enumerate(lands)]

    def hop(c, way, k, b, wait=False):
        at = pl.ds(pl.multiple_of(b * dz, dz), dz)
        parts = [wgu_v.at[c, at, :], wd_v.at[pl.ds(pl.multiple_of(c * fc, fc), fc), at]]
        where = here_too if wait else above() if way == 0 else below()
        return [remote(p, p, a_send.at[c, way, k, i], a_recv.at[c, way, k, i], where) for i, p in enumerate(parts)]

    def hop_start(c, k):
        @pl.when((z >= k - 1) & (z < shards - 1))
        def _():
            for d in hop(c, 0, k - 1, z - (k - 1)):
                d.start()

        @pl.when((z + k - 1 <= shards - 1) & (z > 0))
        def _():
            for d in hop(c, 1, k - 1, z + (k - 1)):
                d.start()

    def hop_sent(c, k):
        @pl.when((z >= k - 1) & (z < shards - 1))
        def _():
            for d in hop(c, 0, k - 1, z - (k - 1)):
                d.wait_send()

        @pl.when((z + k - 1 <= shards - 1) & (z > 0))
        def _():
            for d in hop(c, 1, k - 1, z + (k - 1)):
                d.wait_send()

    def hop_wait(c, k):
        @pl.when(z >= k)
        def _():
            for d in hop(c, 0, k - 1, z - k, True):
                d.wait_recv()

        @pl.when(z + k <= shards - 1)
        def _():
            for d in hop(c, 1, k - 1, z + k, True):
                d.wait_recv()

    def x_start(c):
        for d in x_copies(c, False):
            d.start()
        for d in x_copies(c, True):
            d.start()

    if chunks > PRE:
        x_start(PRE)
    pre_copies = [
        pltpu.make_async_copy(gu_pre, wgu_v.at[pl.ds(0, PRE)], x_own.at[0, 0]),
        pltpu.make_async_copy(d_pre, wd_v.at[pl.ds(0, PRE * fc), :], x_own.at[0, 1]),
    ]
    for d in pre_copies:
        d.start()

    near = tensor * rows_own
    cot_copies = [pltpu.make_async_copy(cot_far.at[pl.ds(near, near), :], cot.at[pl.ds(near, near), :], c_sem.at[0])]
    for k in range(tensor):
        _, tt = p.peer(k)
        src = cotangent.at[pl.ds(pl.multiple_of(tt * rows_own, rows_own), rows_own), :]
        cot_copies.append(pltpu.make_async_copy(src, cot.at[pl.ds(k * rows_own, rows_own), :], c_sem.at[3 + k]))
    cot_copies.append(pltpu.make_async_copy(n_in, n2, c_sem.at[1]))
    for d in cot_copies:
        d.start()
    for c in range(PRE + 1, chunks):
        x_start(c)
    if chunks > PRE:
        for d in x_copies(PRE, True):
            d.wait()
        for d in x_landed(PRE):
            d.wait_recv()
        hop_start(PRE, 1)

    def ag_round(r, top):
        for k in range(shards - 1, 0, -1):
            if k > top:
                continue
            c = r - k + 1

            @pl.when((c >= PRE) & (c < chunks))
            def _(c=c, k=k):
                if k == 1:
                    for d in x_copies(c, True):
                        d.wait()
                    for d in x_landed(c):
                        d.wait_recv()
                else:
                    hop_wait(c, k - 1)
                hop_start(c, k)

    for d in cot_copies:
        d.wait()
    for d in pre_copies:
        d.wait()

    def block_of(i):
        down = shards - 1 - i
        down = down - jnp.where(down <= z, 1, 0)
        up = i + jnp.where(i >= z, 1, 0)
        return jnp.where(i == shards - 1, z, jnp.where(2 * z < shards, down, up))

    def g_copy(c, d, slot):
        return pltpu.make_async_copy(gt.at[slot], g_hbm.at[c, d], g_sem.at[slot])

    def rs_send_copy(src, c, way, d, wait=False):
        where = here_too if wait else above() if way == 0 else below()
        return remote(src, r_hbm.at[c, way, d], rs_send.at[c, way, d], rs_recv.at[c, way, d], where)

    combos = [(way, k) for k in range(2, shards) for way in (0, 1)]

    def target(way, k):
        return z + shards - k if way == 0 else z - (shards - k)

    def sends(way, k):
        if way == 0:
            return z < k
        return z >= shards - k

    def starts(way):
        return z == 0 if way == 0 else z == shards - 1

    def runs(way):
        return z != 0 if way == 0 else z != shards - 1

    def at_slot(first):
        return first // 2, (first >= 0) & (first % 2 == 0) & (first // 2 < kept)

    def rs_step(s):
        for way in (0, 1):
            for k in range(1, shards):
                c, due = at_slot(s - (k - 1))

                @pl.when(due & starts(way))
                def _(c=c, way=way, k=k):
                    d = target(way, k)
                    rs_send_copy(g_hbm.at[c, d], c, way, d).start()

        for i, (way, k) in enumerate(combos):
            c, due = at_slot(s - (k - 1))

            @pl.when(due & sends(way, k) & runs(way))
            def _(c=c, way=way, k=k, i=i):
                d = target(way, k)

                @pl.when(c >= 1)
                def _():
                    rs_send_copy(st.at[2 * i], c - 1, way, d).wait_send()

                rs_send_copy(st.at[2 * i], c, way, d, True).wait_recv()
                pltpu.make_async_copy(g_hbm.at[c, d], st.at[2 * i], s_sem.at[2 * i]).start()
                pltpu.make_async_copy(r_hbm.at[c, way, d], st.at[2 * i + 1], s_sem.at[2 * i + 1]).start()

        last = 2 * len(combos)
        c_fin, due_fin = at_slot(s - (shards - 1))

        @pl.when(due_fin)
        def _():
            pltpu.make_async_copy(g_hbm.at[c_fin, z], st.at[last], s_sem.at[last]).start()
            for way in (0, 1):
                slot = last + 1 + way

                @pl.when(runs(way))
                def _(way=way, slot=slot):
                    rs_send_copy(st.at[slot], c_fin, way, z, True).wait_recv()
                    pltpu.make_async_copy(r_hbm.at[c_fin, way, z], st.at[slot], s_sem.at[slot]).start()

                @pl.when(starts(way))
                def _(slot=slot):
                    st[slot] = jnp.zeros(st.shape[1:], BF)

        for i, (way, k) in enumerate(combos):
            c, due = at_slot(s - (k - 1))

            @pl.when(due & sends(way, k) & runs(way))
            def _(c=c, way=way, k=k, i=i):
                d = target(way, k)
                pltpu.make_async_copy(g_hbm.at[c, d], st.at[2 * i], s_sem.at[2 * i]).wait()
                pltpu.make_async_copy(r_hbm.at[c, way, d], st.at[2 * i + 1], s_sem.at[2 * i + 1]).wait()
                st[2 * i] = (st[2 * i].astype(F32) + st[2 * i + 1].astype(F32)).astype(BF)
                rs_send_copy(st.at[2 * i], c, way, d).start()

        @pl.when(due_fin)
        def _():
            pltpu.make_async_copy(g_hbm.at[c_fin, z], st.at[last], s_sem.at[last]).wait()
            for way in (0, 1):
                slot = last + 1 + way

                @pl.when(runs(way))
                def _(way=way, slot=slot):
                    pltpu.make_async_copy(r_hbm.at[c_fin, way, z], st.at[slot], s_sem.at[slot]).wait()

            @pl.when(c_fin >= 1)
            def _():
                pltpu.make_async_copy(fin, mine_out.at[c_fin - 1], c_sem.at[2]).wait()
                fin_copy(c_fin - 1).wait_send()

            total = st[last].astype(F32) + st[last + 1].astype(F32) + st[last + 2].astype(F32)
            low, high = total[:, :d_own], total[:, d_own:]
            fin[...] = jnp.where(x == 0, low, high)
            away[...] = jnp.where(x == 0, high, low).astype(BF)
            pltpu.make_async_copy(fin, mine_out.at[c_fin], c_sem.at[2]).start()
            fin_copy(c_fin).start()

    def fin_copy(c):
        return remote(away, got_out.at[c], fx_send.at[c], fx_recv.at[c], (z, 1 - x, t))

    tile = 512

    def phase_one(c):
        def body(r, carry):
            at = pl.ds(pl.multiple_of(r * tile, tile), tile)
            gu = mm(n2[at, :], wgu_v[c])
            dh = mm(cot[at, :], wd_v[pl.ds(pl.multiple_of(c * fc, fc), fc), :], NT)
            gate, up = gu[:, :fc], gu[:, fc:]
            sig = 1.0 / (1.0 + jnp.exp(-gate))
            act = gate * sig
            h = (act * up).astype(BF)
            dg = (dh * up * sig * (1.0 + gate * (1.0 - sig))).astype(BF)
            du = (dh * act).astype(BF)
            hid[c, at, :] = h
            dgu[c, at, 0:fc] = dg
            dgu[c, at, fc : 2 * fc] = du
            left_t[0:fc, at] = h.T
            left_t[fc : 2 * fc, at] = dg.T
            left_t[2 * fc : 3 * fc, at] = du.T
            return carry

        lax.fori_loop(0, rows // tile, body, 0)

    def phase_two(c):
        def body(i, carry):
            d = block_of(i)
            slot = i % 2
            at = pl.ds(pl.multiple_of(d * dz, dz), dz)

            @pl.when(i >= 2)
            def _():
                g_copy(c, block_of(i - 2), slot).wait()

            gt[slot, 0:fc, :] = mm(left_t[0:fc, :], cot[:, at]).astype(BF)
            gt[slot, fc : 3 * fc, :] = mm(left_t[fc : 3 * fc, :], n2[:, at]).astype(BF)
            g_copy(c, d, slot).start()
            return carry

        lax.fori_loop(0, shards, body, 0)
        for i in (shards - 2, shards - 1):
            g_copy(c, block_of(jnp.int32(i)), i % 2).wait()

    ot = 256
    units = rows // ot

    def tail_unit(u):
        at = pl.ds(pl.multiple_of((u % units) * ot, ot), ot)
        slot = u % 2

        @pl.when(u >= 2)
        def _():
            pltpu.make_async_copy(ost.at[slot], dn_out.at[at, :], o_sem.at[slot]).wait()

        @pl.when(u < units)
        def _():
            for n in range(width // 512):
                cols = slice(n * 512, (n + 1) * 512)
                acc = jnp.zeros((ot, 512), F32)
                for c in range(chunks):
                    acc = acc + mm(dgu[c, at, :], wgu_v[c, cols, :], NT)
                ost[slot, :, cols] = acc.astype(BF)
            pltpu.make_async_copy(ost.at[slot], dn_out.at[at, :], o_sem.at[slot]).start()

        @pl.when(u >= units)
        def _():
            for n in range(width // 512):
                cols = slice(n * 512, (n + 1) * 512)
                acc = jnp.zeros((ot, 512), F32)
                for c in range(chunks):
                    acc = acc + mm(hid[c, at, :], wd_v[c * fc : (c + 1) * fc, cols])
                ost[slot, :, cols] = acc.astype(BF)
            pltpu.make_async_copy(ost.at[slot], out_out.at[at, :], o_sem.at[slot]).start()

    tail_slots = 2 * (kept - 1) + shards - chunks if 2 * (kept - 1) + shards > chunks else 1
    per_slot = -(-2 * units // tail_slots)

    def slot_body(s, carry):
        @pl.when(s < chunks)
        def _():
            @pl.when(s >= PRE)
            def _():
                hop_wait(s, shards - 1)

            phase_one(s)
            phase_two(s)
            for i in range(shards - 3):
                ag_round(PRE + 1 + s * (shards - 3) + i, shards - 1)

        @pl.when(s >= chunks)
        def _():
            first_u = (s - chunks) * per_slot
            last_u = jnp.minimum(first_u + per_slot, 2 * units)

            def body(u, carry):
                tail_unit(u)
                return carry

            lax.fori_loop(first_u, last_u, body, 0)

        rs_step(s)
        return carry

    lax.fori_loop(0, chunks + tail_slots, slot_body, 0)

    for u in (2 * units - 2, 2 * units - 1):
        at = pl.ds((u % units) * ot, ot)
        pltpu.make_async_copy(ost.at[u % 2], out_out.at[at, :], o_sem.at[u % 2]).wait()
    for c in range(PRE, chunks):
        for d in x_copies(c, False):
            d.wait_send()
        for k in range(1, shards):
            hop_sent(c, k)
    for way in (0, 1):
        for k in range(1, shards):

            @pl.when(starts(way))
            def _(way=way, k=k):
                d = target(way, k)
                for c in range(kept):
                    rs_send_copy(g_hbm.at[c, d], c, way, d).wait_send()

    for i, (way, k) in enumerate(combos):

        @pl.when(sends(way, k) & runs(way))
        def _(way=way, k=k, i=i):
            rs_send_copy(st.at[2 * i], kept - 1, way, target(way, k)).wait_send()

    pltpu.make_async_copy(fin, mine_out.at[kept - 1], c_sem.at[2]).wait()
    fin_copy(kept - 1).wait_send()
    for c in range(kept):
        fin_copy(c).wait_recv()


def mlp_call(shards, ctx, tensor, n_all, cot, cotangent, wg, wu, wd, gu_pre, d_pre):
    rows, width = n_all.shape
    rows_own = rows // (ctx * tensor)
    d_own = wg.shape[0]
    ff = wg.shape[1] // ctx
    fc = gu_pre.shape[2] // 2
    chunks = ff // fc
    dz = ctx * d_own
    any_spec = pl.BlockSpec(memory_space=pl.ANY)
    stage = 4 * (shards - 2) + 3
    kept = chunks - chunks // 2
    dims = (shards, ctx, tensor, chunks, kept, fc, rows_own, d_own)
    dma = pltpu.SemaphoreType.DMA
    return pl.pallas_call(
        functools.partial(mlp_kernel, dims),
        in_specs=[any_spec] * 8,
        out_specs=[any_spec] * 6,
        out_shape=[
            jax.ShapeDtypeStruct((rows, width), BF),
            jax.ShapeDtypeStruct((rows, width), BF),
            jax.ShapeDtypeStruct((kept, 3 * fc, d_own), F32),
            jax.ShapeDtypeStruct((kept, 3 * fc, d_own), BF),
            jax.ShapeDtypeStruct((chunks, shards, 3 * fc, dz), BF),
            jax.ShapeDtypeStruct((kept, 2, shards, 3 * fc, dz), BF),
        ],
        scratch_shapes=[
            pltpu.VMEM((rows, width), BF),
            pltpu.VMEM((rows, width), BF),
            pltpu.VMEM((chunks, width, 2 * fc), BF),
            pltpu.VMEM((ff, width), BF),
            pltpu.VMEM((chunks, rows, fc), BF),
            pltpu.VMEM((chunks, rows, 2 * fc), BF),
            pltpu.VMEM((3 * fc, rows), BF),
            pltpu.VMEM((2, 3 * fc, dz), BF),
            pltpu.VMEM((stage, 3 * fc, dz), BF),
            pltpu.VMEM((2, 256, width), BF),
            pltpu.VMEM((3 * fc, d_own), F32),
            pltpu.VMEM((3 * fc, d_own), BF),
            dma((chunks, 3)),
            dma((chunks, 3)),
            dma((chunks, 3)),
            dma((chunks, 2, shards - 1, 2)),
            dma((chunks, 2, shards - 1, 2)),
            dma((2,)),
            dma((stage,)),
            dma((chunks, 2, shards)),
            dma((chunks, 2, shards)),
            dma((chunks,)),
            dma((chunks,)),
            dma((2,)),
            dma((3 + tensor,)),
        ],
        compiler_params=pltpu.CompilerParams(
            collective_id=1, has_side_effects=True, vmem_limit_bytes=63 * 1024 * 1024
        ),
        cost_estimate=pl.CostEstimate(
            flops=18 * rows * width * ff, bytes_accessed=100 * 1024 * 1024, transcendentals=rows * ff
        ),
        name="feed_forward",
    )(n_all, cot, cotangent, wg, wu, wd, gu_pre, d_pre)


def last_kernel(
    dims, place_s, at_s, live_s, g_late, dn_part, out_part, h_in, cot_in, tokens, gains_in, n_one, w_qkv_in, w_o_in, o_rel_in,
    os_in, qs, ks, vs, stats, cos_ref, sin_ref,
    result, grad_x, mine_o, got_o, mine_w, got_w, gain_out, mine_late, got_late, dh_all, dh_keep, o_land, o_parts, r_late,
    big, w_qkv, chip, c_land, parts_land, stage_own, tile_h, gains, dh_low, go_rel, go, delta, dq,
    d_rel, left_o, left_w, g_o, r_o, g_w, r_w, away_o, g_sum, g_land, g_chain, half_sum, fin_late, away_late,
    send_sems, recv_sems, own_sems,
):
    shards, ctx, tensor, own_rows, d_own, kept = dims
    p = Place(shards, ctx, tensor)
    z, x, t = p.z, p.x, p.t
    group = p.group
    rows, cols = qs.shape
    width = dh_low.shape[1]
    heads = cols // HDIM
    dz = ctx * d_own
    half = own_rows // 2
    d_seq = big.at[pl.ds(0, rows), pl.ds(0, 3 * cols)]
    links = Links(p, send_sems, recv_sems)
    count = [0]

    def own(src, dst):
        i = count[0]
        count[0] += 1
        c = pltpu.make_async_copy(src, dst, own_sems.at[i])
        c.start()
        return c

    p.meet(list(range(1, group)))

    def block(k):
        return pl.ds(k * own_rows, own_rows)

    def mine(k=0):
        _, tt = p.peer(k)
        return pl.ds(pl.multiple_of(tt * own_rows, own_rows), own_rows)

    orders = [p.bits_x + p.bits_y, p.bits_y + p.bits_x]

    def halves(land, in_hbm=False):
        have = [list(range(0, group, 2)), list(range(0, group, 2))]
        spot = 0
        for stage in range(len(orders[0])):
            step = []
            for h in (0, 1):
                bit = orders[h][stage]
                leave = [k for k in have[h] if k & bit]
                for i, k in enumerate(leave):
                    at = pl.ds(h * half, half)
                    dst = land.at[h, spot + i]
                    step.append((h, k, bit, spot + i, links.send(chip.at[k // 2, at, :], dst, p.peer_id(bit))))
                have[h] = [k for k in have[h] if not k & bit]
            spot += len(leave)
            yield
            for h, k, bit, i, m in step:
                m.come()
                at = pl.ds(h * half, half)
                keep = (k ^ bit) // 2
                if in_hbm:
                    own(land.at[h, i], stage_own.at[pl.ds(0, half), :]).wait()
                    came = stage_own[0:half, :].astype(F32)
                else:
                    came = land[h, i].astype(F32)
                total = chip[keep, at, :].astype(F32) + came
                if stage == len(orders[0]) - 1:
                    half_sum[at, :] = total
                else:
                    chip[keep, at, :] = total.astype(BF)
            for h, k, bit, i, m in step:
                m.sent()
                done_moves.append(m)

    done_moves = []

    late = r_late.shape[0]
    late_moves = {}

    def late_wait(copies, conds):
        for c, cond in zip(copies, conds):
            pl.when(cond)(c.wait)

    def tile_copy(src, slot, sem):
        return pltpu.make_async_copy(src, g_w.at[slot], own_sems.at[sem])

    for c in range(late):
        for k in range(1, shards):
            for way in (0, 1):
                d = z + shards - k if way == 0 else z - (shards - k)
                came = z + shards - (k + 1) if way == 0 else z - (shards - (k + 1))
                last = way == 1 and k == shards - 1
                dst = r_late.at[c, shards] if last else r_late.at[c, d]
                land = r_late.at[c, shards] if last else r_late.at[c, came]
                end = z == 0 if way == 0 else z == shards - 1
                mid = (z >= 1) & (z < k) if way == 0 else (z <= shards - 2) & (z >= shards - k)
                comes = (z >= 1) & (z <= k) if way == 0 else (z <= shards - 2) & (z >= shards - 1 - k)
                where = p.above() if way == 0 else p.below()
                src = g_late.at[kept + c, d]
                move = links.send(src, dst, where, land, end, comes)
                pair = g_w.at[2 * way]
                add = Move(
                    pltpu.make_async_remote_copy(
                        src_ref=pair,
                        dst_ref=dst,
                        send_sem=links.send_sems.at[move.place],
                        recv_sem=links.recv_sems.at[move.place],
                        device_id=where,
                        device_id_type=pl.DeviceIdType.MESH,
                    ),
                    move.due,
                    mid,
                    comes,
                )
                late_moves[c, k, way] = (move, add, d, mid)

    def late_sums():
        sent = []
        sem = late_sem
        for c in range(late):
            for k in range(2, shards):
                copies = []
                for m in sent:
                    m.sent()
                sent = []
                for way in (0, 1):
                    late_moves[c, k - 1, way][0].come()
                    _, add, d, mid = late_moves[c, k, way]
                    pair = [
                        tile_copy(g_late.at[kept + c, d], 2 * way, sem),
                        tile_copy(r_late.at[c, d], 2 * way + 1, sem + 1),
                    ]
                    sem += 2
                    for cp in pair:
                        pl.when(mid)(cp.start)
                    copies.append((way, add, mid, pair))
                for way, add, mid, pair in copies:

                    @pl.when(mid)
                    def _(way=way, pair=pair):
                        for cp in pair:
                            cp.wait()
                        g_w[2 * way] = plus(g_w[2 * way], g_w[2 * way + 1])

                    add.start()
                    sent.append(add)
                yield
            for m in sent:
                m.sent()
            sent = []
            for way in (0, 1):
                late_moves[c, shards - 1, way][0].come()
            has_low, has_high = z > 0, z < shards - 1
            loads = [
                (tile_copy(g_late.at[kept + c, z], 0, sem), None),
                (tile_copy(r_late.at[c, z], 1, sem + 1), has_low),
                (tile_copy(r_late.at[c, shards], 2, sem + 2), has_high),
            ]
            sem += 3
            for cp, cond in loads:
                cp.start() if cond is None else pl.when(cond)(cp.start)
            for cp, cond in loads:
                cp.wait() if cond is None else pl.when(cond)(cp.wait)

            fin = fin_late.at[pl.ds(0, 3 * cols), :]

            def half_of(xx):
                at = pl.ds(pl.multiple_of(xx * d_own, d_own), d_own)
                fin[...] = g_w[0, :, at].astype(F32)

                @pl.when(has_low)
                def _():
                    fin[...] += g_w[1, :, at].astype(F32)

                @pl.when(has_high)
                def _():
                    fin[...] += g_w[2, :, at].astype(F32)

            half_of(1 - x)
            if c > 0:
                across_late[-1].sent()
                done_moves.append(across_late[-1])
            away_late[...] = fin[...].astype(BF)
            across_late.append(links.send(away_late, got_late.at[c], p.peer_id(tensor)))
            half_of(x)
            keep = tile_out(c, sem)
            sem += 1
            keep.start()
            keep.wait()
            yield

    def tile_out(c, sem):
        return pltpu.make_async_copy(fin_late.at[pl.ds(0, 3 * cols), :], mine_late.at[c], own_sems.at[sem])

    across_late = []
    late_sem = 120
    late_steps = late_sums()

    odd = list(range(1, group, 2))
    core = [links.send(dn_part.at[block(k), :], c_land.at[k // 2], p.peer_id(1)) for k in odd]
    even = [own(dn_part.at[block(k - 1), :], chip.at[k // 2]) for k in odd]
    load_gain = own(gains_in, gains)
    load_h = [
        own(h_in.at[:, j * cols : (j + 1) * cols], dq.at[j * own_rows : (j + 1) * own_rows, :]) for j in range(width // cols)
    ]
    load_cot = own(cot_in.at[mine(), :], stage_own)
    load_left = own(o_rel_in, d_rel.at[:, 0:cols])
    load_o = own(w_o_in, big)
    load_w = own(w_qkv_in, w_qkv)
    core_out = [links.send(out_part.at[block(k), :], o_land.at[k // 2], p.peer_id(1), start=False) for k in odd]
    for i in range(group // 2):
        even[i].wait()
        core[i].come()
        chip[i] = plus(chip[i], c_land[i])
    sums = halves(parts_land)
    next(sums)
    next(late_steps, None)
    for m in core_out:
        m.start()
    load_gain.wait()
    load_left.wait()
    for k in range(group):
        left_o[:, k * own_rows : (k + 1) * own_rows] = d_rel[k * own_rows : (k + 1) * own_rows, 0:cols].T
    for _ in sums:
        pass

    per = tile_h.shape[1]
    spans = [(slice(j * own_rows, (j + 1) * own_rows), slice(j * cols, (j + 1) * cols)) for j in range(width // cols)]

    def spread_out(r):
        return jnp.concatenate([dq[j * own_rows + r * per : j * own_rows + (r + 1) * per, :] for j in range(len(spans))], axis=1)

    for c in load_h:
        c.wait()
    load_cot.wait()
    for r in range(own_rows // per):
        at = pl.ds(r * per, per)
        h = spread_out(r)
        dn = half_sum[at, :]
        scale = lax.rsqrt(jnp.mean(h * h, axis=-1, keepdims=True) + EPS)
        normed = h * scale
        scaled = dn * gains[1:2, :]
        inner = jnp.mean(scaled * normed, axis=-1, keepdims=True)
        d_h = stage_own[at, :].astype(F32) + scale * (scaled - normed * inner)
        part = jnp.sum(dn * normed, axis=0, keepdims=True)
        g_sum[0, 0:1, :] = part if r == 0 else g_sum[0, 0:1, :] + part
        dh_low[at, :] = d_h.astype(BF)
        for j, (_, c) in enumerate(spans):
            dq[j * own_rows + r * per : j * own_rows + (r + 1) * per, :] = d_h[:, c]
    keep_dh = [own(dq.at[a, :], dh_keep.at[:, c]) for a, c in spans]
    copy_dh = own(dh_low, dh_all.at[block(0), :])

    def dh_part(k, h):
        if h is None:
            return dh_all.at[block(k), :]
        return dh_all.at[pl.ds(k * own_rows + h * half, half), :]

    load_o.wait()
    wo_rows = width // tensor
    lefts = [
        jnp.concatenate([dh_low[:, (zz * ctx + xx) * d_own : (zz * ctx + xx + 1) * d_own] for zz in range(shards)], axis=1)
        for xx in range(ctx)
    ]
    for tt in range(tensor):
        acc = jnp.zeros((own_rows, wo_rows), F32)
        for xx in range(ctx):
            acc = acc + mm(lefts[xx], big[xx * width + tt * wo_rows : xx * width + (tt + 1) * wo_rows, :], NT)
        stage_own[:, tt * wo_rows : (tt + 1) * wo_rows] = acc.astype(BF)

    def heads_of(k):
        xx, tt = p.peer(k)
        return stage_own.at[:, pl.ds(pl.multiple_of((tt * ctx + xx) * cols, cols), cols)]

    swaps = [links.send(heads_of(k), go_rel.at[block(k), :], p.peer_id(k)) for k in range(1, group)]
    own_heads = own(heads_of(0), go_rel.at[block(0), :])
    copy_dh.wait()
    dh_rows = links.spread(dh_part)
    next(dh_rows)
    load_tok = own(tokens.at[mine(), :], dh_low)

    def output():
        for i in range(group // 2):
            even_copy = own(out_part.at[block(2 * i), :], chip.at[i])
            core_out[i].come()
            land_copy = own(o_land.at[i], stage_own)
            even_copy.wait()
            land_copy.wait()
            chip[i] = plus(chip[i], stage_own[...])
        steps = halves(o_parts, True)
        for _ in steps:
            yield
        loads = [own(h_in.at[pl.ds(r * per, per), :], tile_h.at[r]) for r in range(2)]
        for r in range(own_rows // per):
            at = pl.ds(r * per, per)
            loads[r].wait()
            stage_own[at, :] = (tile_h[r % 2] + half_sum[at, :]).astype(BF)
            if r + 2 < own_rows // per:
                loads.append(own(h_in.at[pl.ds((r + 2) * per, per), :], tile_h.at[r % 2]))
        own(stage_own, result.at[mine(), :]).wait()
        yield from everywhere(result)

    def everywhere(ref):
        def put(k, bit):
            return links.send(ref.at[mine(k), :], ref.at[mine(k), :], p.peer_id(bit), ref.at[mine(k | bit), :])

        cores = [put(0, 1)]
        have = [0]
        for bit in p.bits_y:
            step = [put(k, bit) for k in have]
            yield
            for m in step:
                m.come()
            new = [k | bit for k in have]
            cores += [put(k, 1) for k in new]
            have = have + new
        yield
        for m in cores:
            m.come()

    next(late_steps, None)
    next(late_steps, None)
    own_heads.wait()
    for m in swaps:
        m.come()
    for m in swaps:
        m.sent()
        done_moves.append(m)

    def fill(b, carry):
        go[pl.ds(pl.multiple_of(b * BLK, BLK), BLK), :] = picked(go_rel, place_s[b])
        return carry

    lax.fori_loop(0, rows // BLK, fill, 0)
    load_os = own(os_in, go_rel)
    load_os.wait()
    head_row = lax.broadcasted_iota(jnp.int32, (8, cols), 0)
    head_col = lax.broadcasted_iota(jnp.int32, (8, cols), 1) // HDIM
    pick = jnp.where(head_row == head_col, 1.0, 0.0).astype(BF)
    for i in range(rows // QT):
        part = slice(i * QT, (i + 1) * QT)
        both = go[part, :].astype(F32) * go_rel[part, :].astype(F32)
        coarse = both.astype(BF)
        fine = (both - coarse.astype(F32)).astype(BF)
        delta[:, part] = mm(pick, coarse, NT) + mm(pick, fine, NT)
    for c in keep_dh:
        c.wait()
    dq[...] = jnp.zeros_like(dq)
    live = live_s[0]
    tiles = rows // QT

    def store(i, column, value, turned):
        at = slice(i * QT, (i + 1) * QT)
        if turned:
            value = turn(value, wide(cos_ref[at, :], cols), -wide(sin_ref[at, :], cols))
        d_seq[at, column * cols : (column + 1) * cols] = value.astype(BF)

    out_steps = output()

    def grads_o():
        steps = sums_along(g_o, r_o, fin_late.at[pl.ds(0, cols), :], away_o, got_o, mine_o)
        dh_block = d_rel.at[:, pl.ds(0, dz)]
        for i in range(shards):
            d = far_first(i)
            own(dh_all.at[:, pl.ds(pl.multiple_of(d * dz, dz), dz)], dh_block).wait()
            g_o[d] = mm(left_o[...], d_rel[:, 0:dz]).astype(BF)
            if i < shards - 2:
                next(steps)
                yield
        for _ in steps:
            yield

    def far_first(i):
        down = shards - 1 - i
        down = down - jnp.where(down <= z, 1, 0)
        up = i + jnp.where(i >= z, 1, 0)
        return z if i == shards - 1 else jnp.where(2 * z < shards, down, up)

    def sums_along(g, r, fin, away, got_ref, mine_ref):
        before = [None, None]
        for k in range(1, shards):
            now = []
            for way in (0, 1):
                d = z + shards - k if way == 0 else z - (shards - k)
                came = z + shards - (k + 1) if way == 0 else z - (shards - (k + 1))
                goes = z < k if way == 0 else z >= shards - k
                comes = (z >= 1) & (z <= k) if way == 0 else (z <= shards - 2) & (z >= shards - 1 - k)
                if k > 1:
                    before[way].come()
                    mid = (z >= 1) & (z < k) if way == 0 else (z <= shards - 2) & (z >= shards - k)

                    @pl.when(mid)
                    def _(d=d):
                        g[d] = plus(g[d], r[d])

                last = way == 1 and k == shards - 1
                dst = r.at[shards] if last else r.at[d]
                land = r.at[shards] if last else r.at[came]
                now.append(links.send(g.at[d], dst, p.above() if way == 0 else p.below(), land, goes, comes))
            before = now
            yield
        for m in before:
            m.come()

        def half_of(xx):
            at = pl.ds(pl.multiple_of(xx * d_own, d_own), d_own)
            fin[...] = g[z, :, at].astype(F32)

            @pl.when(z > 0)
            def _():
                fin[...] += r[z, :, at].astype(F32)

            @pl.when(z < shards - 1)
            def _():
                fin[...] += r[shards, :, at].astype(F32)

        half_of(1 - x)
        away[...] = fin[...].astype(BF)
        across = links.send(away, got_ref, p.peer_id(tensor))
        half_of(x)
        keep = own(fin, mine_ref)
        yield
        across.come()
        keep.wait()

    o_steps = None
    next(dh_rows)
    next(out_steps)
    for i in range(tiles):
        begin = i * QT

        def head(h, carry):
            dk, dv = carry
            kt = ks[begin : begin + QT, :]
            lane = lax.broadcasted_iota(jnp.int32, (QT, cols), 1) // HDIM
            km = jnp.where(lane == h, kt * BF(0.125), BF(0))
            dead = jnp.where(lax.broadcasted_iota(jnp.int32, (QT, 1), 0) + begin < live, 0.0, NEG)
            for j in range(i, tiles):
                at = slice(j * QT, (j + 1) * QT)
                qm = jnp.where(lane == h, qs[at, :] * BF(0.125), BF(0))
                gm = jnp.where(lane == h, go[at, :], BF(0))
                s = mm(kt, qm, NT) + dead
                if j == i:
                    kpos = lax.broadcasted_iota(jnp.int32, (QT, QT), 0)
                    qpos = lax.broadcasted_iota(jnp.int32, (QT, QT), 1)
                    s = s + jnp.where(kpos <= qpos, 0.0, NEG)
                e = jnp.exp(s - stats[pl.ds(h, 1), at])
                dp = mm(vs[begin : begin + QT, :], gm, NT)
                ds = (e * (dp - delta[pl.ds(h, 1), at])).astype(BF)
                dq[at, :] += mm(ds, km, TN)
                dk = dk + mm(ds, qm)
                dv = dv + mm(e.astype(BF), gm)
            return dk, dv

        zero = jnp.zeros((QT, cols), F32)
        dk, dv = lax.fori_loop(0, heads, head, (zero, zero))
        store(i, 1, dk, True)
        store(i, 2, dv, False)
        store(i, 0, dq[begin : begin + QT, :], True)
        next(late_steps, None)
        if i == 0:
            next(dh_rows, None)
        else:
            next(out_steps, None)
        if i == 1:
            drain(dh_rows)
            o_steps = grads_o()
        if i >= 1:
            next(o_steps, None)

    def back_to_rows(j, carry):
        dst = pl.ds(pl.multiple_of(j * BLK, BLK), BLK)
        d_rel[dst, :] = picked(d_seq, at_s[j])
        return carry

    lax.fori_loop(0, rows // BLK, back_to_rows, 0)
    drain(late_steps)
    for m in across_late:
        m.come()
    across_late[-1].sent()
    done_moves.append(across_late[-1])
    drain(out_steps)
    load_w.wait()

    def d_n_one(k, c):
        return mm(d_rel[k * own_rows : (k + 1) * own_rows, :], w_qkv[c, :], NT)

    quarters = [slice(c, c + width // 4) for c in range(0, width, width // 4)]

    load_n = []
    per_n = shards // ctx
    for d in range(shards):
        load_n.append(
            own(
                n_one.at[:, d * dz : (d + 1) * dz],
                big.at[(d // per_n) * rows : (d // per_n + 1) * rows, (d % per_n) * dz : (d % per_n + 1) * dz],
            )
        )
    load_dh = [own(dh_keep.at[:, c], dq.at[a, :]) for a, c in spans]
    core = []
    for i, k in enumerate(odd):
        for c in quarters:
            chip[i, :, c] = d_n_one(k, c).astype(BF)
        core.append(links.send(chip.at[i], c_land.at[i], p.peer_id(1)))
    for k in range(group):
        left_w[:, k * own_rows : (k + 1) * own_rows] = d_rel[k * own_rows : (k + 1) * own_rows, :].T
    for c in load_n:
        c.wait()

    def n_block(d):
        row = pl.ds(pl.multiple_of((d // per_n) * rows, rows), rows)
        return big[row, pl.ds(pl.multiple_of((d % per_n) * dz, dz), dz)]

    w_steps = sums_along(g_w, r_w, fin_late.at[pl.ds(0, 3 * cols), :], away_late, got_w, mine_w)

    def grad_w(i):
        d = far_first(i)
        for j in range(3):
            at = slice(j * cols, (j + 1) * cols)
            g_w[d, at, :] = mm(left_w[at, :], n_block(d)).astype(BF)

    grad_w(0)
    next(w_steps)
    for i in range(1, shards):
        grad_w(i)
    next(o_steps, None)
    for i in range(group // 2):
        core[i].sent()
        done_moves.append(core[i])
        core[i].come()
        for c in quarters:
            chip[i, :, c] = (d_n_one(2 * i, c) + c_land[i, :, c].astype(F32)).astype(BF)
    sums = halves(parts_land)
    next(sums)
    next(w_steps, None)
    next(sums)
    next(w_steps, None)
    drain(o_steps)
    for _ in sums:
        pass
    for c in load_dh:
        c.wait()
    load_tok.wait()
    for r in range(own_rows // per):
        at = pl.ds(r * per, per)
        v = dh_low[at, :].astype(F32)
        dn = half_sum[at, :]
        scale = lax.rsqrt(jnp.mean(v * v, axis=-1, keepdims=True) + EPS)
        normed = v * scale
        scaled = dn * gains[0:1, :]
        inner = jnp.mean(scaled * normed, axis=-1, keepdims=True)
        stage_own[at, :] = (spread_out(r) + scale * (scaled - normed * inner)).astype(BF)
        part = jnp.sum(dn * normed, axis=0, keepdims=True)
        g_sum[0, 1:2, :] = part if r == 0 else g_sum[0, 1:2, :] + part
    g_sum[0, 2:8, :] = jnp.zeros((6, width), F32)
    own(stage_own, grad_x.at[mine(), :]).wait()
    x_steps = everywhere(grad_x)
    next(x_steps)
    bit, i = 1, 0
    while bit < group:
        m = links.send(g_sum.at[i], g_land.at[i], p.peer_id(bit))
        m.come()
        g_sum[i + 1] = g_sum[i] + g_land[i]
        bit, i = bit * 2, i + 1
    own(g_sum.at[i], g_chain.at[z]).wait()
    g_steps = links.chain(lambda b: [g_chain.at[b]])
    next(g_steps)
    next(w_steps, None)
    next(x_steps, None)
    drain(g_steps)
    total = g_chain[0]
    for b in range(1, shards):
        total = total + g_chain[b]
    g_land[0] = total
    own(g_land.at[0, :, pl.ds(pl.multiple_of((z * ctx + x) * d_own, d_own), d_own)], gain_out).wait()
    drain(x_steps, w_steps)
    for m in links.moves:
        if m not in done_moves:
            m.sent()


def last_call(
    shards, ctx, tensor, place, at, live, g_late, dn_part, out_part, hidden, cot, tokens, gains, n_one, w_qkv, w_o, o_rel,
    os, qs, ks, vs, stats, cos, sin,
):
    rows, cols = qs.shape
    width = hidden.shape[1]
    own_rows = hidden.shape[0]
    group = ctx * tensor
    d_own = width // (shards * ctx)
    dz = ctx * d_own
    chunks = g_late.shape[0]
    late = chunks // 2
    dims = (shards, ctx, tensor, own_rows, d_own, chunks - late)
    any_spec = pl.BlockSpec(memory_space=pl.ANY)
    smem = pl.BlockSpec(memory_space=pltpu.SMEM)
    vmem = pl.BlockSpec(memory_space=pltpu.VMEM)
    dma = pltpu.SemaphoreType.DMA
    half = own_rows // 2
    per = min(32, own_rows)
    bits = group.bit_length() - 1

    def out(shape, kind=BF):
        return jax.ShapeDtypeStruct(shape, kind)

    parts = (2, group // 2 - 1, half, width)
    return pl.pallas_call(
        functools.partial(last_kernel, dims),
        in_specs=[smem] * 3 + [any_spec] * 12 + [vmem] * 6,
        out_specs=[any_spec] * 14,
        out_shape=[
            out((tensor * own_rows, width)),
            out((tensor * own_rows, width)),
            out((cols, d_own), F32),
            out((cols, d_own)),
            out((3 * cols, d_own), F32),
            out((3 * cols, d_own)),
            out((8, d_own), F32),
            out((late, 3 * cols, d_own), F32),
            out((late, 3 * cols, d_own)),
            out((rows, width)),
            out((own_rows, width), F32),
            out((group // 2, own_rows, width)),
            out(parts),
            out((late, shards + 1, 3 * cols, dz)),
        ],
        scratch_shapes=[
            pltpu.VMEM((ctx * width, shards * d_own), BF),
            pltpu.VMEM((width, 3 * cols), BF),
            pltpu.VMEM((group // 2, own_rows, width), BF),
            pltpu.VMEM((group // 2, own_rows, width), BF),
            pltpu.VMEM(parts, BF),
            pltpu.VMEM((own_rows, width), BF),
            pltpu.VMEM((2, per, width), F32),
            pltpu.VMEM((8, width), F32),
            pltpu.VMEM((own_rows, width), BF),
            pltpu.VMEM((rows, cols), BF),
            pltpu.VMEM((rows, cols), BF),
            pltpu.VMEM((8, rows), F32),
            pltpu.VMEM((rows, cols), F32),
            pltpu.VMEM((rows, 3 * cols), BF),
            pltpu.VMEM((cols, rows), BF),
            pltpu.VMEM((3 * cols, rows), BF),
            pltpu.VMEM((shards, cols, dz), BF),
            pltpu.VMEM((shards + 1, cols, dz), BF),
            pltpu.VMEM((shards, 3 * cols, dz), BF),
            pltpu.VMEM((shards + 1, 3 * cols, dz), BF),
            pltpu.VMEM((cols, d_own), BF),
            pltpu.VMEM((bits + 1, 8, width), F32),
            pltpu.VMEM((bits, 8, width), F32),
            pltpu.VMEM((shards, 8, width), F32),
            pltpu.VMEM((own_rows, width), F32),
            pltpu.VMEM((3 * cols, d_own), F32),
            pltpu.VMEM((3 * cols, d_own), BF),
            dma((300,)),
            dma((300,)),
            dma((240,)),
        ],
        compiler_params=pltpu.CompilerParams(
            collective_id=2, has_side_effects=True, vmem_limit_bytes=63 * 1024 * 1024
        ),
        cost_estimate=pl.CostEstimate(
            flops=2 * rows * width * cols * 8, bytes_accessed=64 * 1024 * 1024, transcendentals=rows * rows * cols // HDIM
        ),
        name="last",
    )(place, at, live, g_late, dn_part, out_part, hidden, cot, tokens, gains, n_one, w_qkv, w_o, o_rel, os, qs, ks, vs, stats, cos, sin)


def per_device(
    shards, ctx, tensor, tokens, cotangent, seq_len, block_slot, attn_gain, w_query, w_key, w_value, w_out, mlp_gain, w_gate, w_up, w_down
):
    group = ctx * tensor
    my_x = lax.axis_index("ctx")
    my_t = lax.axis_index("tensor")
    me = my_x * tensor + my_t
    width = tokens.shape[1]
    own_rows = tokens.shape[0] // tensor
    level_rows = own_rows * group
    slots_each = own_rows // BLK
    d_own = w_query.shape[0]
    cols = w_query.shape[1] // ctx
    ff = w_gate.shape[1] // ctx
    slot = block_slot[0]
    place = ((slot // slots_each) ^ me) * slots_each + slot % slots_each
    order = jnp.arange(slot.shape[0], dtype=jnp.int32)
    at = jnp.sum(jnp.where(place[:, None] == order[None, :], order[:, None], 0), axis=0).astype(jnp.int32)

    def x_join(mine, got, axis):
        return jnp.where(
            my_x == 0, jnp.concatenate([mine, got], axis=axis), jnp.concatenate([got, mine], axis=axis)
        )

    angle_at = jnp.arange(level_rows, dtype=F32)
    lane = jnp.arange(128)
    freqs = THETA ** (-(lane % (HDIM // 2)).astype(F32) / (HDIM // 2))
    angles = angle_at[:, None] * freqs[None, :]
    cos = jnp.cos(angles)
    sin = jnp.sin(angles) * jnp.where(lane % HDIM < HDIM // 2, -1.0, 1.0)
    gains = jnp.concatenate([jnp.stack([attn_gain, mlp_gain], axis=0).astype(F32), jnp.zeros((6, d_own), F32)], axis=0)
    n_one, w_qkv, w_o, cot, gu_pre, d_pre, n_two_own, hidden_res, gains, qs, ks, vs, os, stats, o_slot = first_call(
        shards, ctx, tensor, place.astype(jnp.int32), at, seq_len, tokens, cotangent, gains,
        w_query, w_key, w_value, w_out, w_gate, w_up, w_down, cos, sin,
    )
    dn_part, out_part, ff_mine, ff_got, g_late, _ = mlp_call(
        shards, ctx, tensor, n_two_own, cot, cotangent, w_gate, w_up, w_down, gu_pre, d_pre
    )

    result, grad_x, mine_o, got_o, mine_w, got_w, gain_sums, late_mine, late_got, *_ = last_call(
        shards, ctx, tensor, place.astype(jnp.int32), at, seq_len, g_late, dn_part, out_part, hidden_res, cotangent, tokens, gains,
        n_one, w_qkv, w_o.reshape(ctx * width, shards * d_own), o_slot, os, qs, ks, vs, stats, cos, sin,
    )
    ff_mine = jnp.concatenate([ff_mine, late_mine], axis=0)
    ff_got = jnp.concatenate([ff_got, late_got], axis=0)
    chunks = ff_mine.shape[0]
    fc = ff // chunks
    mine = ff_mine.reshape(chunks, 3, fc, d_own)
    got = ff_got.reshape(chunks, 3, fc, d_own).astype(F32)

    def spread(i):
        return x_join(mine[:, i].reshape(ff, d_own), got[:, i].reshape(ff, d_own), 0)

    grad_down = spread(0)
    grad_gate = spread(1).T
    grad_up = spread(2).T

    grad_out = x_join(mine_o, got_o.astype(F32), 0)
    mine = mine_w.reshape(3, cols, d_own)
    got = got_w.reshape(3, cols, d_own).astype(F32)
    grad_q, grad_k, grad_v = (x_join(mine[i], got[i], 0).T for i in range(3))
    grad_gain_two, grad_gain_one = gain_sums[0], gain_sums[1]
    return (
        result,
        grad_x,
        grad_gain_one,
        grad_q,
        grad_k,
        grad_v,
        grad_out,
        grad_gain_two,
        grad_gate,
        grad_up,
        grad_down,
    )


def solution(mesh):
    rows = P(("shard", "ctx"), None)
    gain = P(("shard", "ctx"))
    into = P(("shard", "ctx"), "tensor")
    back = P("tensor", ("shard", "ctx"))
    sizes = mesh.shape
    return jax.shard_map(
        functools.partial(per_device, sizes["shard"], sizes["ctx"], sizes["tensor"]),
        mesh=mesh,
        in_specs=(rows, rows, P("shard"), P("shard", None), gain, into, into, into, back, gain, into, into, back),
        out_specs=(rows, rows, gain, into, into, into, back, gain, into, into, back),
        check_vma=False,
    )
```
